32 devices in a mesh: depth: 8 (over y, x, core), lat: 4 (over z).
Axes of the slice: x: 2, y: 2, z: 4, core: 2. Of those that a mesh axis runs over, the one named last changes fastest.
Arguments:
- inflow: float32 [8, 16, 128, 256], P('depth', 'lat'), may hold values from -6 to 6
- source: bfloat16 [3, 16, 128, 256], P(None, 'lat'), may hold values from -6 to 6
- operators: bfloat16 [8, 16, 6, 2, 128, 128], P('depth', 'lat'), may hold values from -0.15625 to 0.15625
- transmission: float32 [8, 16, 128], P('depth', 'lat'), may hold values from 0.5 to 1
- reflectivity: float32 [8, 16, 128], P('depth', 'lat'), may hold values from -1 to 1
- send_ids: int32 [4, 2, 2], P('lat'), may hold values from 0 to 3, as said below
- send_count: int32 [4, 2], P('lat'), may hold values from 1 to 2, as said below
- pattern: int32 [16, 6], P('lat'), may hold values from 0 to 7, as said below
Outputs:
- reflected: bfloat16 [4, 8, 16, 128, 256], P(None, 'depth', 'lat')
- transmitted: float32 [8, 16, 128, 256], P('depth', 'lat')
The draws below stay inside these ranges and needn't reach their ends.
Inputs may be any that keep to these rules, and one draw needn't show every extreme that they name: `send_ids`: the 2 numbers of one list are distinct block numbers of the tile that holds the list. `send_count`: some list holds 2 live entries in every draw. `pattern`: entry 0 of block b names b's own local number (b modulo 4). Other entries name a local block or a live received slot: slots 4 + i for i below the lower tile's count for its upper list, slots 4 + 2 + i for i below the upper tile's count for its lower list; tile 0 names no lower slot, tile 4 - 1 no upper slot. Every live received slot of a tile is named by some entry of that tile.
All inputs are finite; a program needn't handle non-finite values.
Results may differ from the reference program's by a relative error of at most 0.0061.
Values may be sent and summed in bfloat16 or wider, within the bound.
No kernel may reach another device: no remote copies, remote signals or barrier semaphores. Data moves between devices by JAX's collectives and lax.ppermute only.
A program may use at most 64 MiB of HBM per device.

```python
import math
import jax
import jax.numpy as jnp
from jax import lax

BLK = 128
BLK_DEV = 4
SEND = 2
K = 6
SHOTS = 128
TICKS = 4
TILES = 4
DEPTHS = 8
BLOCKS = 16


def lateral_layout(key):
    base = jax.random.fold_in(key, 11)
    subkeys = jax.random.split(base, 7)
    perm_keys = jax.random.split(subkeys[0], TILES * 2)
    shuffled = jax.vmap(lambda single: jax.random.permutation(single, BLK_DEV))(perm_keys)
    chosen = shuffled[:, :SEND].reshape(TILES, 2, SEND).astype(jnp.int32)
    heavy = jax.random.randint(subkeys[1], (TILES, 2), 0, 4) == 0
    heavy_count = jax.random.randint(subkeys[2], (TILES, 2), 1, SEND + 1)
    counts = jnp.where(heavy, heavy_count, 1)
    heavy_tile = jax.random.randint(subkeys[3], (), 0, TILES)
    heavy_side = jax.random.randint(subkeys[4], (), 0, 2)
    counts = counts.at[heavy_tile, heavy_side].set(SEND).astype(jnp.int32)
    tile_number = jnp.arange(TILES, dtype=jnp.int32)
    left_count = jnp.where(tile_number > 0, jnp.roll(counts[:, 1], 1), 0)
    right_count = jnp.where(tile_number < TILES - 1, jnp.roll(counts[:, 0], -1), 0)
    live_total = BLK_DEV + left_count + right_count
    drawn = jax.random.randint(subkeys[5], (TILES, BLK_DEV, K), 0, 1 << 20) % live_total[:, None, None]
    left_wide = left_count[:, None, None]
    entries = jnp.where(drawn < BLK_DEV + left_wide, drawn, drawn - left_wide + SEND)
    block_number = jnp.arange(BLK_DEV, dtype=jnp.int32)[None, :]
    forced_raw = BLK_DEV + block_number
    left_flat = left_count[:, None]
    forced = jnp.where(forced_raw < BLK_DEV + left_flat, forced_raw, forced_raw - left_flat + SEND)
    covered = block_number < (left_count + right_count)[:, None]
    position = jax.random.randint(subkeys[6], (TILES, BLK_DEV), 1, K)
    entry_number = jnp.arange(K, dtype=jnp.int32)[None, None, :]
    entries = jnp.where((entry_number == position[:, :, None]) & covered[:, :, None], forced[:, :, None], entries)
    entries = jnp.where(entry_number == 0, jnp.broadcast_to(block_number[:, :, None], entries.shape), entries)
    return (chosen, counts, entries.reshape(TILES * BLK_DEV, K).astype(jnp.int32))


def draw_send_ids(key, part):
    return lateral_layout(key)[0]


def draw_send_count(key, part):
    return lateral_layout(key)[1]


def draw_pattern(key, part):
    return lateral_layout(key)[2]


def steps_of(own_key, extent, cuts, low, largest):
    gain, own = 1.0, jax.random.fold_in(own_key, 6)
    for dim, parts in cuts:
        draws = jnp.exp(jax.random.uniform(jax.random.fold_in(own, dim), (parts,), jnp.float32, low / len(cuts), largest / len(cuts)))
        gain = gain * jnp.repeat(draws, extent[dim] // parts).reshape([-1 if axis == dim else 1 for axis in range(len(extent))])
    return gain


def centred(rng, dims, width, limit, pieces=(), kind=jnp.bfloat16):
    values = jax.random.normal(rng, dims, jnp.float32) * width
    if len(pieces) > 0:
        values = steps_of(rng, dims, pieces, -0.22, 0.18) * values
    return jnp.clip(values, min=-limit, max=limit).astype(kind)


def setup_inputs(seed: int = 0) -> dict:
    seeds = jax.random.split(jax.random.key(seed), 9)
    return {
        "inflow": centred(seeds[0], (DEPTHS, BLOCKS, BLK, 2 * SHOTS), 1.0, 6.0, ((0, 8), (1, 4)), jnp.float32),
        "source": centred(seeds[1], (TICKS - 1, BLOCKS, BLK, 2 * SHOTS), 1.0, 6.0, ((1, 4),)),
        "operators": centred(seeds[2], (DEPTHS, BLOCKS, K, 2, BLK, BLK), (2 * K * BLK) ** -0.5, 0.15625, ((0, 8), (1, 4))),
        "transmission": jnp.clip(jnp.exp(math.log(1.0) - 0.6931472 * jax.random.uniform(seeds[3], (DEPTHS, BLOCKS, BLK), jnp.float32) ** steps_of(seeds[3], (DEPTHS, BLOCKS, BLK), ((0, 8), (1, 4)), -0.2, 0.2)), 0.5, 1.0),
        "reflectivity": jnp.clip(jax.random.uniform(seeds[4], (DEPTHS, BLOCKS, BLK), jnp.float32, -1.0, 1.0) * steps_of(seeds[4], (DEPTHS, BLOCKS, BLK), ((0, 8), (1, 4)), -0.4, 0.0), -1.0, 1.0),
        "send_ids": draw_send_ids(jax.random.fold_in(seeds[8], 71), 0),
        "send_count": draw_send_count(jax.random.fold_in(seeds[8], 71), 0),
        "pattern": draw_pattern(jax.random.fold_in(seeds[8], 71), 0),
    }


def build_buffer(wavefield, send_ids, send_count):
    columns = wavefield.shape[-1]
    tile_blocks = wavefield.reshape(TILES, BLK_DEV, BLK, columns)
    flat_ids = send_ids.reshape(TILES, 2 * SEND)
    tile_number = jnp.arange(TILES, dtype=jnp.int32)[:, None]
    listed = tile_blocks[tile_number, flat_ids].reshape(TILES, 2, SEND, BLK, columns)
    live_slots = jnp.arange(SEND, dtype=jnp.int32)[None, None, :] < send_count[:, :, None]
    listed = jnp.where(live_slots[:, :, :, None, None], listed, jnp.zeros_like(listed))
    zero_rim = jnp.zeros_like(listed[:1, 0])
    from_lower = jnp.concatenate([zero_rim, listed[:-1, 1]], axis=0)
    from_upper = jnp.concatenate([listed[1:, 0], zero_rim], axis=0)
    return jnp.concatenate([tile_blocks, from_lower, from_upper], axis=1)


def extrapolate(section_ops, wavefield, send_ids, send_count, pattern):
    columns = wavefield.shape[-1]
    shots_half = columns // 2
    buffer = build_buffer(wavefield, send_ids, send_count)
    picked_index = pattern.reshape(TILES, BLK_DEV * K)
    tile_number = jnp.arange(TILES, dtype=jnp.int32)[:, None]
    picked = buffer[tile_number, picked_index].reshape(TILES * BLK_DEV, K, BLK, columns)
    products = jnp.einsum('bkrpq,bkqc->brpc', section_ops.astype(jnp.float32), picked.astype(jnp.float32),
                          precision=lax.Precision.HIGHEST)
    real_part = products[:, 0, :, :shots_half] - products[:, 1, :, shots_half:]
    imag_part = products[:, 0, :, shots_half:] + products[:, 1, :, :shots_half]
    return jnp.concatenate([real_part, imag_part], axis=-1)


def reference(inflow, source, operators, transmission, reflectivity, send_ids, send_count, pattern):
    wavefield = inflow.astype(jnp.bfloat16)
    echoes = []
    onward = None
    for tick_index in range(TICKS):
        def run_section(section_args):
            section_ops, section_wave, passing, reflect_coef = section_args
            extrapolated = extrapolate(section_ops, section_wave, send_ids, send_count, pattern)
            leaving = passing[:, :, None] * extrapolated
            echoed = (reflect_coef[:, :, None] * extrapolated).astype(jnp.bfloat16)
            return leaving, echoed

        onward, echoed = lax.map(run_section, (operators, wavefield, transmission, reflectivity))
        echoes.append(echoed)
        if tick_index + 1 < TICKS:
            wavefield = jnp.concatenate([source[tick_index][None], onward[:-1].astype(jnp.bfloat16)], axis=0)
    return jnp.stack(echoes), onward
```

```python
import functools

import jax
import jax.numpy as jnp
from jax import lax
from jax.experimental import pallas as pl
from jax.experimental.pallas import tpu as pltpu
from jax.sharding import PartitionSpec as P

WAVE = jnp.bfloat16
SMEM_SPEC = pl.BlockSpec(memory_space=pltpu.SMEM)
VMEM_SPEC = pl.BlockSpec(memory_space=pltpu.VMEM)
ANY_SPEC = pl.BlockSpec(memory_space=pl.ANY)
VMEM_LIMIT = 8 * 1024 * 1024


def in_vmem(array):
    return pltpu.with_memory_space_constraint(array, pltpu.VMEM)


def write_lists(ids_ref, count_ref, blocks_ref, lists):
    for side, list_ref in enumerate(lists):
        for slot in range(list_ref.shape[0]):
            live = slot < count_ref[0, side]

            @pl.when(live)
            def _():
                list_ref[slot] = blocks_ref[ids_ref[0, side, slot]]

            @pl.when(jnp.logical_not(live))
            def _():
                list_ref[slot] = jnp.zeros(list_ref.shape[1:], list_ref.dtype)


def prepare_kernel(ids_ref, count_ref, inflow_ref, wave_ref, down_ref, up_ref, landed, sems):
    blocks = wave_ref.shape[0]
    copies = [
        pltpu.make_async_copy(inflow_ref.at[0, b], landed.at[b], sems.at[b]) for b in range(blocks)
    ]
    for copy in copies:
        copy.start()
    for b, copy in enumerate(copies):
        copy.wait()
        wave_ref[b] = landed[b].astype(wave_ref.dtype)
    write_lists(ids_ref, count_ref, wave_ref, (down_ref, up_ref))


def columns_of(rows_ref, b):
    row = rows_ref[0, pl.ds(b, 1), :]
    points = row.shape[1]
    return jnp.broadcast_to(row, (points, points)).T


def extrapolate_block(pattern_ref, ops_ref, buffer, b):
    slots = ops_ref.shape[2]
    points = ops_ref.shape[5]
    left = jnp.concatenate(
        [ops_ref[0, b, k].reshape(2 * points, points) for k in range(slots)], axis=1
    )
    right = jnp.concatenate([buffer[pattern_ref[b, k]] for k in range(slots)], axis=0)
    products = jnp.dot(left, right, preferred_element_type=jnp.float32)
    half = products.shape[1] // 2
    real_part = products[:points, :half] - products[points:, half:]
    imag_part = products[:points, half:] + products[points:, :half]
    return real_part, imag_part


def fill_buffer(section, tick, source_ref, wave_ref, lower_ref, upper_ref, buffer):
    blocks = wave_ref.shape[0]
    slots = lower_ref.shape[0]
    if tick == 0:
        buffer[:blocks] = wave_ref[...]
    else:
        @pl.when(section == 0)
        def _():
            buffer[:blocks] = source_ref[tick - 1]

        @pl.when(section != 0)
        def _():
            buffer[:blocks] = wave_ref[...]
    buffer[blocks : blocks + slots] = lower_ref[...]
    buffer[blocks + slots :] = upper_ref[...]


def tick_kernel(
    tick, sections, ids_ref, count_ref, pattern_ref, ops_ref, pass_ref, reflect_ref, source_ref,
    wave_ref, lower_ref, upper_ref, echo_ref, onward_ref, down_ref, up_ref, buffer,
):
    section = lax.axis_index("depth")
    fill_buffer(section, tick, source_ref, wave_ref, lower_ref, upper_ref, buffer)
    for b in range(wave_ref.shape[0]):
        parts = extrapolate_block(pattern_ref, ops_ref, buffer, b)
        passing = columns_of(pass_ref, b)
        reflect = columns_of(reflect_ref, b)
        for i, part in enumerate(parts):
            cols = pl.ds(i * part.shape[1], part.shape[1])
            onward_ref[b, :, cols] = (passing * part).astype(onward_ref.dtype)
            echo_ref[b, :, cols] = (reflect * part).astype(echo_ref.dtype)

    @pl.when(section != sections - 1)
    def _():
        write_lists(ids_ref, count_ref, onward_ref, (down_ref, up_ref))

    @pl.when(section == sections - 1)
    def _():
        write_lists(ids_ref, count_ref, source_ref.at[tick], (down_ref, up_ref))


def last_kernel(
    tick, pattern_ref, ops_ref, pass_ref, reflect_ref, source_ref,
    wave_ref, lower_ref, upper_ref, *rest,
):
    earlier = rest[:tick]
    reflected_ref, transmitted_ref, buffer, echo, leaving, early_sems, echo_sems, leave_sems = rest[tick:]
    section = lax.axis_index("depth")
    copies = [
        pltpu.make_async_copy(earlier[t], reflected_ref.at[t, 0], early_sems.at[t])
        for t in range(tick)
    ]
    for copy in copies:
        copy.start()
    fill_buffer(section, tick, source_ref, wave_ref, lower_ref, upper_ref, buffer)
    for b in range(wave_ref.shape[0]):
        parts = extrapolate_block(pattern_ref, ops_ref, buffer, b)
        passing = columns_of(pass_ref, b)
        reflect = columns_of(reflect_ref, b)
        for i, part in enumerate(parts):
            cols = pl.ds(i * part.shape[1], part.shape[1])
            leaving[b, :, cols] = passing * part
            echo[b, :, cols] = (reflect * part).astype(echo.dtype)
        for copy in (
            pltpu.make_async_copy(leaving.at[b], transmitted_ref.at[0, b], leave_sems.at[b]),
            pltpu.make_async_copy(echo.at[b], reflected_ref.at[tick, 0, b], echo_sems.at[b]),
        ):
            copy.start()
            copies.append(copy)
    for copy in copies:
        copy.wait()


def per_device(
    inflow, source, operators, transmission, reflectivity, send_ids, send_count, pattern
):
    sections, tiles = lax.axis_size("depth"), lax.axis_size("lat")
    ticks = source.shape[0] + 1
    _, blocks, points, columns = inflow.shape
    listed = send_ids.shape[-1]
    taken = operators.shape[2]
    wave_type = pltpu.VMEM((blocks, points, columns), WAVE)
    list_type = pltpu.VMEM((listed, points, columns), WAVE)
    params = pltpu.CompilerParams(vmem_limit_bytes=VMEM_LIMIT)
    tick_cost = pl.CostEstimate(
        flops=blocks * taken * 4 * points * points * columns,
        bytes_accessed=2 * operators.size + 8 * blocks * points * columns,
        transcendentals=0,
    )

    deeper = [(s, s + 1) for s in range(sections - 1)]
    beside = {
        way: [(j, j + way) for j in range(tiles) if 0 <= j + way < tiles] for way in (1, -1)
    }
    deeper_beside = {
        way: [
            (s * tiles + j, ((s + 1) % sections) * tiles + to)
            for s in range(sections)
            for j, to in beside[way]
        ]
        for way in (1, -1)
    }

    wave, down, up = pl.pallas_call(
        prepare_kernel,
        out_shape=(wave_type, list_type, list_type),
        in_specs=[SMEM_SPEC, SMEM_SPEC, ANY_SPEC],
        out_specs=(VMEM_SPEC,) * 3,
        scratch_shapes=[
            pltpu.VMEM((blocks, points, columns), inflow.dtype),
            pltpu.SemaphoreType.DMA((blocks,)),
        ],
        compiler_params=params,
        cost_estimate=pl.CostEstimate(
            flops=inflow.size, bytes_accessed=8 * inflow.size, transcendentals=0
        ),
        name="prepare",
    )(send_ids, send_count, inflow)
    lower = lax.ppermute(up, "lat", beside[1])
    upper = lax.ppermute(down, "lat", beside[-1])

    fixed = [in_vmem(a) for a in (operators, transmission, reflectivity, source)]
    buffer_type = pltpu.VMEM((blocks + 2 * listed, points, columns), WAVE)
    echoes = []
    for tick in range(ticks - 1):
        echo, onward, down, up = pl.pallas_call(
            functools.partial(tick_kernel, tick, sections),
            out_shape=(wave_type, wave_type, list_type, list_type),
            in_specs=[SMEM_SPEC] * 3 + [VMEM_SPEC] * 7,
            out_specs=(VMEM_SPEC,) * 4,
            scratch_shapes=[buffer_type],
            compiler_params=params,
            cost_estimate=tick_cost,
            name=f"tick{tick}",
        )(send_ids, send_count, pattern, *fixed, in_vmem(wave), in_vmem(lower), in_vmem(upper))
        echoes.append(echo)
        wave = lax.ppermute(onward, "depth", deeper)
        lower = lax.ppermute(up, ("depth", "lat"), deeper_beside[1])
        upper = lax.ppermute(down, ("depth", "lat"), deeper_beside[-1])

    tick = ticks - 1
    reflected, transmitted = pl.pallas_call(
        functools.partial(last_kernel, tick),
        out_shape=(
            jax.ShapeDtypeStruct((ticks, 1, blocks, points, columns), WAVE),
            jax.ShapeDtypeStruct((1, blocks, points, columns), jnp.float32),
        ),
        in_specs=[SMEM_SPEC] + [VMEM_SPEC] * (7 + tick),
        out_specs=(ANY_SPEC, ANY_SPEC),
        scratch_shapes=[
            buffer_type,
            pltpu.VMEM((blocks, points, columns), WAVE),
            pltpu.VMEM((blocks, points, columns), jnp.float32),
            pltpu.SemaphoreType.DMA((tick,)),
            pltpu.SemaphoreType.DMA((blocks,)),
            pltpu.SemaphoreType.DMA((blocks,)),
        ],
        compiler_params=params,
        cost_estimate=tick_cost,
        name="last_tick",
    )(pattern, *fixed, in_vmem(wave), in_vmem(lower), in_vmem(upper), *map(in_vmem, echoes))
    return reflected, transmitted


def solution(mesh):
    return jax.shard_map(
        per_device,
        mesh=mesh,
        in_specs=(
            P("depth", "lat", None, None),
            P(None, "lat", None, None),
            P("depth", "lat", None, None, None, None),
            P("depth", "lat", None),
            P("depth", "lat", None),
            P("lat", None, None),
            P("lat", None),
            P("lat", None),
        ),
        out_specs=(P(None, "depth", "lat", None, None), P("depth", "lat", None, None)),
        check_vma=False,
    )
```

```python
import functools

import jax
import jax.numpy as jnp
from jax import lax
from jax.experimental import pallas as pl
from jax.experimental.pallas import tpu as pltpu
from jax.sharding import PartitionSpec as P

WAVE = jnp.bfloat16
SMEM_SPEC = pl.BlockSpec(memory_space=pltpu.SMEM)
VMEM_SPEC = pl.BlockSpec(memory_space=pltpu.VMEM)
ANY_SPEC = pl.BlockSpec(memory_space=pl.ANY)
VMEM_LIMIT = 8 * 1024 * 1024
LOWER, UPPER = 0, 1


def in_vmem(array):
    return pltpu.with_memory_space_constraint(array, pltpu.VMEM)


def in_hbm(array):
    return pltpu.with_memory_space_constraint(array, pltpu.HBM)


def write_lists(section, plan_ref, blocks_ref, lists):
    listed = lists[0].shape[0]
    parity = lax.rem(section, 2)
    for list_ref, side in zip(lists, (UPPER - parity, parity)):
        count = plan_ref[2 * listed + side]
        for slot in range(listed):
            live = slot < count

            @pl.when(live)
            def _():
                list_ref[slot] = blocks_ref[plan_ref[side * listed + slot]]

            @pl.when(jnp.logical_not(live))
            def _():
                list_ref[slot] = jnp.zeros(list_ref.shape[1:], list_ref.dtype)


def prepare_kernel(
    ids_hbm, count_hbm, pattern_hbm, inflow_hbm, plan_ref, wave_ref, first_ref, second_ref,
    ids, count, pattern, landed, small_sems, sems,
):
    blocks = wave_ref.shape[0]
    small = [
        pltpu.make_async_copy(source, target, small_sems.at[i])
        for i, (source, target) in enumerate(
            ((ids_hbm, ids), (count_hbm, count), (pattern_hbm, pattern))
        )
    ]
    large = [
        pltpu.make_async_copy(inflow_hbm.at[0, b], landed.at[b], sems.at[b]) for b in range(blocks)
    ]
    for copy in small + large:
        copy.start()
    for copy in small:
        copy.wait()
    _, sides, listed = ids.shape
    taken = pattern.shape[1]
    for side in range(sides):
        for slot in range(listed):
            plan_ref[side * listed + slot] = ids[0, side, slot]
        plan_ref[sides * listed + side] = count[0, side]
    for b in range(blocks):
        for k in range(taken):
            plan_ref[sides * (listed + 1) + b * taken + k] = pattern[b, k]
    for b, copy in enumerate(large):
        copy.wait()
        wave_ref[b] = landed[b].astype(wave_ref.dtype)
    write_lists(lax.axis_index("depth"), plan_ref, wave_ref, (first_ref, second_ref))


def load_kernel(
    ops_hbm, source_hbm, pass_hbm, reflect_hbm, after_ref,
    ops_ref, source_ref, pass_ref, reflect_ref, pass_rows, reflect_rows, sems,
):
    del after_ref
    copies = [
        pltpu.make_async_copy(source, target, sems.at[i])
        for i, (source, target) in enumerate(
            (
                (pass_hbm, pass_rows),
                (reflect_hbm, reflect_rows),
                (ops_hbm, ops_ref),
                (source_hbm, source_ref),
            )
        )
    ]
    for copy in copies:
        copy.start()
    for copy, rows, columns_ref in zip(copies, (pass_rows, reflect_rows), (pass_ref, reflect_ref)):
        copy.wait()
        for b in range(columns_ref.shape[0]):
            row = rows[0, pl.ds(b, 1), :]
            columns_ref[b] = jnp.broadcast_to(row, columns_ref.shape[1:]).T
    for copy in copies[2:]:
        copy.wait()


def fill_buffer(section, sections, tick, source_ref, wave_ref, first_ref, second_ref, buffer):
    blocks, listed = wave_ref.shape[0], first_ref.shape[0]
    if tick == 0:
        sender = section
        buffer[:blocks] = wave_ref[...]
    else:
        sender = lax.rem(section + sections - 1, sections)

        @pl.when(section == 0)
        def _():
            buffer[:blocks] = source_ref[tick - 1]

        @pl.when(section != 0)
        def _():
            buffer[:blocks] = wave_ref[...]
    parity = lax.rem(sender, 2)
    buffer[pl.ds(blocks + parity * listed, listed)] = first_ref[...]
    buffer[pl.ds(blocks + (1 - parity) * listed, listed)] = second_ref[...]


def extrapolate_block(plan_ref, pattern_start, ops_ref, buffer, b):
    taken = ops_ref.shape[2]
    points = ops_ref.shape[5]
    left = jnp.concatenate(
        [ops_ref[0, b, k].reshape(2 * points, points) for k in range(taken)], axis=1
    )
    right = jnp.concatenate(
        [buffer[plan_ref[pattern_start + b * taken + k]] for k in range(taken)], axis=0
    )
    products = jnp.dot(left, right, preferred_element_type=jnp.float32)
    half = products.shape[1] // 2
    real_part = products[:points, :half] - products[points:, half:]
    imag_part = products[:points, half:] + products[points:, :half]
    return real_part, imag_part


def tick_kernel(
    tick, sections, plan_ref, ops_ref, source_ref, pass_ref, reflect_ref,
    wave_ref, first_in_ref, second_in_ref, echo_ref, onward_ref, first_ref, second_ref, buffer,
):
    section = lax.axis_index("depth")
    listed = first_ref.shape[0]
    fill_buffer(
        section, sections, tick, source_ref, wave_ref, first_in_ref, second_in_ref, buffer
    )
    for b in range(wave_ref.shape[0]):
        parts = extrapolate_block(plan_ref, 2 * (listed + 1), ops_ref, buffer, b)
        for i, part in enumerate(parts):
            cols = pl.ds(i * part.shape[1], part.shape[1])
            onward_ref[b, :, cols] = (pass_ref[b] * part).astype(onward_ref.dtype)
            echo_ref[b, :, cols] = (reflect_ref[b] * part).astype(echo_ref.dtype)

    @pl.when(section != sections - 1)
    def _():
        write_lists(section, plan_ref, onward_ref, (first_ref, second_ref))

    @pl.when(section == sections - 1)
    def _():
        write_lists(section, plan_ref, source_ref.at[tick], (first_ref, second_ref))


def last_kernel(
    tick, sections, plan_ref, ops_ref, source_ref, pass_ref, reflect_ref,
    wave_ref, first_in_ref, second_in_ref, *rest,
):
    earlier = rest[:tick]
    (reflected_ref, transmitted_ref, buffer, echo, leaving,
     early_sems, echo_sems, leave_sems) = rest[tick:]
    section = lax.axis_index("depth")
    listed = first_in_ref.shape[0]
    copies = [
        pltpu.make_async_copy(earlier[t], reflected_ref.at[t, 0], early_sems.at[t])
        for t in range(tick)
    ]
    for copy in copies:
        copy.start()
    fill_buffer(
        section, sections, tick, source_ref, wave_ref, first_in_ref, second_in_ref, buffer
    )
    for b in range(wave_ref.shape[0]):
        parts = extrapolate_block(plan_ref, 2 * (listed + 1), ops_ref, buffer, b)
        for i, part in enumerate(parts):
            cols = pl.ds(i * part.shape[1], part.shape[1])
            leaving[b, :, cols] = pass_ref[b] * part
            echo[b, :, cols] = (reflect_ref[b] * part).astype(echo.dtype)
        for copy in (
            pltpu.make_async_copy(leaving.at[b], transmitted_ref.at[0, b], leave_sems.at[b]),
            pltpu.make_async_copy(echo.at[b], reflected_ref.at[tick, 0, b], echo_sems.at[b]),
        ):
            copy.start()
            copies.append(copy)
    for copy in copies:
        copy.wait()


def halo_routes(sections, tiles, deeper):
    routes = []
    for turn in (0, 1):
        route = []
        for s in range(sections):
            way = 1 if (s + turn) % 2 == 0 else -1
            to_section = (s + 1) % sections if deeper else s
            route += [
                (s * tiles + j, to_section * tiles + j + way)
                for j in range(tiles)
                if 0 <= j + way < tiles
            ]
        routes.append(route)
    return routes


def per_device(
    inflow, source, operators, transmission, reflectivity, send_ids, send_count, pattern
):
    sections, tiles = lax.axis_size("depth"), lax.axis_size("lat")
    ticks = source.shape[0] + 1
    _, blocks, points, columns = inflow.shape
    listed = send_ids.shape[-1]
    taken = operators.shape[2]
    wave_type = pltpu.VMEM((blocks, points, columns), WAVE)
    list_type = pltpu.VMEM((listed, points, columns), WAVE)
    params = pltpu.CompilerParams(vmem_limit_bytes=VMEM_LIMIT)
    tick_cost = pl.CostEstimate(
        flops=blocks * taken * 4 * points * points * columns,
        bytes_accessed=2 * operators.size + 8 * blocks * points * columns,
        transcendentals=0,
    )
    both = ("depth", "lat")
    deeper = [(s, s + 1) for s in range(sections - 1)]

    plan, wave, first, second = pl.pallas_call(
        prepare_kernel,
        out_shape=(
            pltpu.SMEM((2 * (listed + 1) + blocks * taken,), jnp.int32),
            wave_type,
            list_type,
            list_type,
        ),
        in_specs=[ANY_SPEC] * 4,
        out_specs=(SMEM_SPEC,) + (VMEM_SPEC,) * 3,
        scratch_shapes=[
            pltpu.SMEM(send_ids.shape, jnp.int32),
            pltpu.SMEM(send_count.shape, jnp.int32),
            pltpu.SMEM(pattern.shape, jnp.int32),
            pltpu.VMEM((blocks, points, columns), inflow.dtype),
            pltpu.SemaphoreType.DMA((3,)),
            pltpu.SemaphoreType.DMA((blocks,)),
        ],
        compiler_params=params,
        cost_estimate=pl.CostEstimate(
            flops=inflow.size, bytes_accessed=8 * inflow.size, transcendentals=0
        ),
        name="prepare",
    )(*map(in_hbm, (send_ids, send_count, pattern, inflow)))
    routes = halo_routes(sections, tiles, False)
    loaded_first = first
    first = lax.ppermute(first, both, routes[0])
    second = lax.ppermute(second, both, routes[1])

    column_type = pltpu.VMEM((blocks, points, columns // 2), jnp.float32)
    fixed = pl.pallas_call(
        load_kernel,
        out_shape=(
            pltpu.VMEM(operators.shape, operators.dtype),
            pltpu.VMEM(source.shape, source.dtype),
            column_type,
            column_type,
        ),
        in_specs=[ANY_SPEC] * 4 + [VMEM_SPEC],
        out_specs=(VMEM_SPEC,) * 4,
        scratch_shapes=[
            pltpu.VMEM(transmission.shape, transmission.dtype),
            pltpu.VMEM(reflectivity.shape, reflectivity.dtype),
            pltpu.SemaphoreType.DMA((4,)),
        ],
        compiler_params=params,
        cost_estimate=pl.CostEstimate(
            flops=0, bytes_accessed=4 * (operators.size + source.size), transcendentals=0
        ),
        name="load",
    )(*map(in_hbm, (operators, source, transmission, reflectivity)), in_vmem(loaded_first))
    fixed = [plan, *map(in_vmem, fixed)]

    buffer_type = pltpu.VMEM((blocks + 2 * listed, points, columns), WAVE)
    routes = halo_routes(sections, tiles, True)
    echoes = []
    for tick in range(ticks - 1):
        echo, onward, first, second = pl.pallas_call(
            functools.partial(tick_kernel, tick, sections),
            out_shape=(wave_type, wave_type, list_type, list_type),
            in_specs=[SMEM_SPEC] + [VMEM_SPEC] * 7,
            out_specs=(VMEM_SPEC,) * 4,
            scratch_shapes=[buffer_type],
            compiler_params=params,
            cost_estimate=tick_cost,
            name=f"tick{tick}",
        )(*fixed, in_vmem(wave), in_vmem(first), in_vmem(second))
        echoes.append(echo)
        wave = lax.ppermute(onward, "depth", deeper)
        first = lax.ppermute(first, both, routes[0])
        second = lax.ppermute(second, both, routes[1])

    tick = ticks - 1
    reflected, transmitted = pl.pallas_call(
        functools.partial(last_kernel, tick, sections),
        out_shape=(
            jax.ShapeDtypeStruct((ticks, 1, blocks, points, columns), WAVE),
            jax.ShapeDtypeStruct((1, blocks, points, columns), jnp.float32),
        ),
        in_specs=[SMEM_SPEC] + [VMEM_SPEC] * (7 + tick),
        out_specs=(ANY_SPEC, ANY_SPEC),
        scratch_shapes=[
            buffer_type,
            pltpu.VMEM((blocks, points, columns), WAVE),
            pltpu.VMEM((blocks, points, columns), jnp.float32),
            pltpu.SemaphoreType.DMA((tick,)),
            pltpu.SemaphoreType.DMA((blocks,)),
            pltpu.SemaphoreType.DMA((blocks,)),
        ],
        compiler_params=params,
        cost_estimate=tick_cost,
        name="last_tick",
    )(*fixed, in_vmem(wave), in_vmem(first), in_vmem(second), *map(in_vmem, echoes))
    return reflected, transmitted


def solution(mesh):
    return jax.shard_map(
        per_device,
        mesh=mesh,
        in_specs=(
            P("depth", "lat", None, None),
            P(None, "lat", None, None),
            P("depth", "lat", None, None, None, None),
            P("depth", "lat", None),
            P("depth", "lat", None),
            P("lat", None, None),
            P("lat", None),
            P("lat", None),
        ),
        out_specs=(P(None, "depth", "lat", None, None), P("depth", "lat", None, None)),
        check_vma=False,
    )
```

```python
import functools

import jax
import jax.numpy as jnp
from jax import lax
from jax.experimental import pallas as pl
from jax.experimental.pallas import tpu as pltpu
from jax.sharding import PartitionSpec as P

WAVE = jnp.bfloat16
SMEM_SPEC = pl.BlockSpec(memory_space=pltpu.SMEM)
VMEM_SPEC = pl.BlockSpec(memory_space=pltpu.VMEM)
ANY_SPEC = pl.BlockSpec(memory_space=pl.ANY)
VMEM_LIMIT = 8 * 1024 * 1024
LOWER, UPPER = 0, 1
ORDER = ((1, 0), (0, 1))


def in_vmem(array):
    return pltpu.with_memory_space_constraint(array, pltpu.VMEM)


def in_hbm(array):
    return pltpu.with_memory_space_constraint(array, pltpu.HBM)


def write_list(plan_ref, side, blocks_ref, list_ref):
    listed = list_ref.shape[0]
    for slot in range(listed):
        live = slot < plan_ref[2 * listed + side]

        @pl.when(live)
        def _():
            list_ref[slot] = blocks_ref[plan_ref[side * listed + slot]]

        @pl.when(jnp.logical_not(live))
        def _():
            list_ref[slot] = jnp.zeros(list_ref.shape[1:], list_ref.dtype)


def prepare_kernel(
    ids_hbm, count_hbm, pattern_hbm, inflow_hbm, plan_ref, wave_ref, first_ref, second_ref,
    ids, count, pattern, landed, small_sems, sems,
):
    blocks = wave_ref.shape[0]
    small = [
        pltpu.make_async_copy(source, target, small_sems.at[i])
        for i, (source, target) in enumerate(
            ((ids_hbm, ids), (count_hbm, count), (pattern_hbm, pattern))
        )
    ]
    large = [
        pltpu.make_async_copy(inflow_hbm.at[0, b], landed.at[b], sems.at[b]) for b in range(blocks)
    ]
    for copy in small + large:
        copy.start()
    for copy in small:
        copy.wait()
    _, sides, listed = ids.shape
    taken = pattern.shape[1]
    for side in range(sides):
        for slot in range(listed):
            plan_ref[side * listed + slot] = ids[0, side, slot]
        plan_ref[sides * listed + side] = count[0, side]
    for b in range(blocks):
        for k in range(taken):
            plan_ref[sides * (listed + 1) + b * taken + k] = pattern[b, k]
    for b, copy in enumerate(large):
        copy.wait()
        wave_ref[b] = landed[b].astype(wave_ref.dtype)
    parity = lax.rem(lax.axis_index("depth"), 2)
    write_list(plan_ref, UPPER - parity, wave_ref, first_ref)
    write_list(plan_ref, parity, wave_ref, second_ref)


def load_kernel(
    ops_hbm, source_hbm, pass_hbm, reflect_hbm, after_ref,
    ops_ref, source_ref, pass_ref, reflect_ref, pass_rows, reflect_rows, sems,
):
    del after_ref
    copies = [
        pltpu.make_async_copy(source, target, sems.at[i])
        for i, (source, target) in enumerate(
            (
                (pass_hbm, pass_rows),
                (reflect_hbm, reflect_rows),
                (ops_hbm, ops_ref),
                (source_hbm, source_ref),
            )
        )
    ]
    for copy in copies:
        copy.start()
    for copy, rows, columns_ref in zip(copies, (pass_rows, reflect_rows), (pass_ref, reflect_ref)):
        copy.wait()
        for b in range(columns_ref.shape[0]):
            row = rows[0, pl.ds(b, 1), :]
            columns_ref[b] = jnp.broadcast_to(row, columns_ref.shape[1:]).T
    for copy in copies[2:]:
        copy.wait()


def fill_buffer(section, tick, source_ref, wave_ref, lower_ref, upper_ref, buffer):
    blocks, listed = wave_ref.shape[0], lower_ref.shape[0]
    if tick == 0:
        buffer[:blocks] = wave_ref[...]
    else:
        @pl.when(section == 0)
        def _():
            buffer[:blocks] = source_ref[tick - 1]

        @pl.when(section != 0)
        def _():
            buffer[:blocks] = wave_ref[...]
    buffer[blocks : blocks + listed] = lower_ref[...]
    buffer[blocks + listed :] = upper_ref[...]


def extrapolate_block(plan_ref, pattern_start, ops_ref, buffer, b):
    taken = ops_ref.shape[2]
    points = ops_ref.shape[5]
    left = jnp.concatenate(
        [ops_ref[0, b, k].reshape(2 * points, points) for k in range(taken)], axis=1
    )
    right = jnp.concatenate(
        [buffer[plan_ref[pattern_start + b * taken + k]] for k in range(taken)], axis=0
    )
    products = jnp.dot(left, right, preferred_element_type=jnp.float32)
    half = products.shape[1] // 2
    real_part = products[:points, :half] - products[points:, half:]
    imag_part = products[:points, half:] + products[points:, :half]
    return real_part, imag_part


def tick_kernel(
    parity, tick, sections, plan_ref, ops_ref, source_ref, pass_ref, reflect_ref,
    wave_ref, lower_ref, upper_ref, *rest,
):
    echo_ref, onward_ref, down_ref, up_ref, buffer = rest[-5:]
    section = lax.axis_index("depth")
    listed = lower_ref.shape[0]

    @pl.when(lax.rem(section, 2) == parity)
    def _():
        fill_buffer(section, tick, source_ref, wave_ref, lower_ref, upper_ref, buffer)
        for b in range(wave_ref.shape[0]):
            parts = extrapolate_block(plan_ref, 2 * (listed + 1), ops_ref, buffer, b)
            for i, part in enumerate(parts):
                cols = pl.ds(i * part.shape[1], part.shape[1])
                onward_ref[b, :, cols] = (pass_ref[b] * part).astype(onward_ref.dtype)
                echo_ref[b, :, cols] = (reflect_ref[b] * part).astype(echo_ref.dtype)

        @pl.when(section != sections - 1)
        def _():
            write_list(plan_ref, UPPER, onward_ref, up_ref)
            write_list(plan_ref, LOWER, onward_ref, down_ref)

        @pl.when(section == sections - 1)
        def _():
            write_list(plan_ref, UPPER, source_ref.at[tick], up_ref)
            write_list(plan_ref, LOWER, source_ref.at[tick], down_ref)


def last_kernel(
    parity, tick, plan_ref, ops_ref, source_ref, pass_ref, reflect_ref,
    wave_ref, lower_ref, upper_ref, *rest,
):
    earlier = rest[:tick]
    (reflected_ref, transmitted_ref, buffer, echo, leaving,
     early_sems, echo_sems, leave_sems) = rest[-8:]
    section = lax.axis_index("depth")
    listed = lower_ref.shape[0]

    @pl.when(lax.rem(section, 2) == parity)
    def _():
        copies = [
            pltpu.make_async_copy(earlier[t], reflected_ref.at[t, 0], early_sems.at[t])
            for t in range(tick)
        ]
        for copy in copies:
            copy.start()
        fill_buffer(section, tick, source_ref, wave_ref, lower_ref, upper_ref, buffer)
        for b in range(wave_ref.shape[0]):
            parts = extrapolate_block(plan_ref, 2 * (listed + 1), ops_ref, buffer, b)
            for i, part in enumerate(parts):
                cols = pl.ds(i * part.shape[1], part.shape[1])
                leaving[b, :, cols] = pass_ref[b] * part
                echo[b, :, cols] = (reflect_ref[b] * part).astype(echo.dtype)
            for copy in (
                pltpu.make_async_copy(leaving.at[b], transmitted_ref.at[0, b], leave_sems.at[b]),
                pltpu.make_async_copy(echo.at[b], reflected_ref.at[tick, 0, b], echo_sems.at[b]),
            ):
                copy.start()
                copies.append(copy)
        for copy in copies:
            copy.wait()


def beside(sections, tiles, ways, deeper):
    return [
        (s * tiles + j, ((s + 1) % sections if deeper else s) * tiles + j + ways[s % 2])
        for s in range(sections)
        if s % 2 in ways
        for j in range(tiles)
        if 0 <= j + ways[s % 2] < tiles
    ]


def per_device(
    inflow, source, operators, transmission, reflectivity, send_ids, send_count, pattern
):
    sections, tiles = lax.axis_size("depth"), lax.axis_size("lat")
    ticks = source.shape[0] + 1
    _, blocks, points, columns = inflow.shape
    listed = send_ids.shape[-1]
    taken = operators.shape[2]
    wave_type = pltpu.VMEM((blocks, points, columns), WAVE)
    list_type = pltpu.VMEM((listed, points, columns), WAVE)
    params = pltpu.CompilerParams(vmem_limit_bytes=VMEM_LIMIT)
    tick_cost = pl.CostEstimate(
        flops=blocks * taken * 4 * points * points * columns,
        bytes_accessed=2 * operators.size + 8 * blocks * points * columns,
        transcendentals=0,
    )
    both = ("depth", "lat")

    plan, wave, first, second = pl.pallas_call(
        prepare_kernel,
        out_shape=(
            pltpu.SMEM((2 * (listed + 1) + blocks * taken,), jnp.int32),
            wave_type,
            list_type,
            list_type,
        ),
        in_specs=[ANY_SPEC] * 4,
        out_specs=(SMEM_SPEC,) + (VMEM_SPEC,) * 3,
        scratch_shapes=[
            pltpu.SMEM(send_ids.shape, jnp.int32),
            pltpu.SMEM(send_count.shape, jnp.int32),
            pltpu.SMEM(pattern.shape, jnp.int32),
            pltpu.VMEM((blocks, points, columns), inflow.dtype),
            pltpu.SemaphoreType.DMA((3,)),
            pltpu.SemaphoreType.DMA((blocks,)),
        ],
        compiler_params=params,
        cost_estimate=pl.CostEstimate(
            flops=inflow.size, bytes_accessed=8 * inflow.size, transcendentals=0
        ),
        name="prepare",
    )(*map(in_hbm, (send_ids, send_count, pattern, inflow)))
    loaded_first = first
    first = lax.ppermute(first, both, beside(sections, tiles, {0: 1, 1: -1}, False))
    second = lax.ppermute(second, both, beside(sections, tiles, {0: -1, 1: 1}, False))

    column_type = pltpu.VMEM((blocks, points, columns // 2), jnp.float32)
    fixed = pl.pallas_call(
        load_kernel,
        out_shape=(
            pltpu.VMEM(operators.shape, operators.dtype),
            pltpu.VMEM(source.shape, source.dtype),
            column_type,
            column_type,
        ),
        in_specs=[ANY_SPEC] * 4 + [VMEM_SPEC],
        out_specs=(VMEM_SPEC,) * 4,
        scratch_shapes=[
            pltpu.VMEM(transmission.shape, transmission.dtype),
            pltpu.VMEM(reflectivity.shape, reflectivity.dtype),
            pltpu.SemaphoreType.DMA((4,)),
        ],
        compiler_params=params,
        cost_estimate=pl.CostEstimate(
            flops=0, bytes_accessed=4 * (operators.size + source.size), transcendentals=0
        ),
        name="load",
    )(*map(in_hbm, (operators, source, transmission, reflectivity)), in_vmem(loaded_first))
    fixed = [plan, *map(in_vmem, fixed)]
    buffer_type = pltpu.VMEM((blocks + 2 * listed, points, columns), WAVE)

    arrived = {0: (wave, first, second), 1: (wave, second, first)}
    echoes = []
    for tick in range(ticks - 1):
        leaving = {}
        echo = None
        for parity in ORDER[tick % 2]:
            known = [] if echo is None else [in_vmem(echo)]
            echo, onward, down, up = pl.pallas_call(
                functools.partial(tick_kernel, parity, tick, sections),
                out_shape=(wave_type, wave_type, list_type, list_type),
                in_specs=[SMEM_SPEC] + [VMEM_SPEC] * (7 + len(known)),
                out_specs=(VMEM_SPEC,) * 4,
                input_output_aliases={8: 0} if known else {},
                scratch_shapes=[buffer_type],
                compiler_params=params,
                cost_estimate=tick_cost,
                name=f"tick{tick}_{parity}",
            )(*fixed, *map(in_vmem, arrived[parity]), *known)
            deeper = [(s, s + 1) for s in range(parity, sections - 1, 2)]
            up = lax.ppermute(up, both, beside(sections, tiles, {parity: 1}, True))
            down = lax.ppermute(down, both, beside(sections, tiles, {parity: -1}, True))
            wave = lax.ppermute(onward, "depth", deeper)
            leaving[1 - parity] = (wave, up, down)
        arrived = leaving
        echoes.append(echo)

    tick = ticks - 1
    results = []
    result_types = (
        jax.ShapeDtypeStruct((ticks, 1, blocks, points, columns), WAVE),
        jax.ShapeDtypeStruct((1, blocks, points, columns), jnp.float32),
    )
    for parity in ORDER[tick % 2]:
        results = pl.pallas_call(
            functools.partial(last_kernel, parity, tick),
            out_shape=result_types,
            in_specs=[SMEM_SPEC] + [VMEM_SPEC] * (7 + tick) + [ANY_SPEC] * len(results),
            out_specs=(ANY_SPEC, ANY_SPEC),
            input_output_aliases={8 + tick: 0, 9 + tick: 1} if results else {},
            scratch_shapes=[
                buffer_type,
                pltpu.VMEM((blocks, points, columns), WAVE),
                pltpu.VMEM((blocks, points, columns), jnp.float32),
                pltpu.SemaphoreType.DMA((tick,)),
                pltpu.SemaphoreType.DMA((blocks,)),
                pltpu.SemaphoreType.DMA((blocks,)),
            ],
            compiler_params=params,
            cost_estimate=tick_cost,
            name=f"last_tick_{parity}",
        )(*fixed, *map(in_vmem, arrived[parity]), *map(in_vmem, echoes), *results)
    return tuple(results)


def solution(mesh):
    return jax.shard_map(
        per_device,
        mesh=mesh,
        in_specs=(
            P("depth", "lat", None, None),
            P(None, "lat", None, None),
            P("depth", "lat", None, None, None, None),
            P("depth", "lat", None),
            P("depth", "lat", None),
            P("lat", None, None),
            P("lat", None),
            P("lat", None),
        ),
        out_specs=(P(None, "depth", "lat", None, None), P("depth", "lat", None, None)),
        check_vma=False,
    )
```

```python
import functools

import jax
import jax.numpy as jnp
from jax import lax
from jax.experimental import pallas as pl
from jax.experimental.pallas import tpu as pltpu
from jax.sharding import PartitionSpec as P

WAVE = jnp.bfloat16
SMEM_SPEC = pl.BlockSpec(memory_space=pltpu.SMEM)
VMEM_SPEC = pl.BlockSpec(memory_space=pltpu.VMEM)
ANY_SPEC = pl.BlockSpec(memory_space=pl.ANY)
VMEM_LIMIT = 8 * 1024 * 1024
LOWER, UPPER = 0, 1


def in_vmem(array):
    return pltpu.with_memory_space_constraint(array, pltpu.VMEM)


def in_hbm(array):
    return pltpu.with_memory_space_constraint(array, pltpu.HBM)


def write_lists(position, plan_ref, blocks_ref, lists):
    listed = lists[0].shape[0]
    parity = lax.rem(position, 2)
    for list_ref, side in zip(lists, (UPPER - parity, parity)):
        count = plan_ref[2 * listed + side]
        for slot in range(listed):
            live = slot < count

            @pl.when(live)
            def _():
                list_ref[slot] = blocks_ref[plan_ref[side * listed + slot]]

            @pl.when(jnp.logical_not(live))
            def _():
                list_ref[slot] = jnp.zeros(list_ref.shape[1:], list_ref.dtype)


def prepare_kernel(
    ids_hbm, count_hbm, pattern_hbm, inflow_hbm, plan_ref, wave_ref, first_ref, second_ref,
    ids, count, pattern, landed, small_sems, sems,
):
    blocks = wave_ref.shape[0]
    small = [
        pltpu.make_async_copy(source, target, small_sems.at[i])
        for i, (source, target) in enumerate(
            ((ids_hbm, ids), (count_hbm, count), (pattern_hbm, pattern))
        )
    ]
    large = [
        pltpu.make_async_copy(inflow_hbm.at[0, b], landed.at[b], sems.at[b]) for b in range(blocks)
    ]
    for copy in small + large:
        copy.start()
    for copy in small:
        copy.wait()
    _, sides, listed = ids.shape
    taken = pattern.shape[1]
    for side in range(sides):
        for slot in range(listed):
            plan_ref[side * listed + slot] = ids[0, side, slot]
        plan_ref[sides * listed + side] = count[0, side]
    for b in range(blocks):
        for k in range(taken):
            plan_ref[sides * (listed + 1) + b * taken + k] = pattern[b, k]
    for b, copy in enumerate(large):
        copy.wait()
        wave_ref[b] = landed[b].astype(wave_ref.dtype)
    write_lists(lax.axis_index("lat"), plan_ref, wave_ref, (first_ref, second_ref))


def load_kernel(
    ops_hbm, source_hbm, pass_hbm, reflect_hbm, after_ref,
    ops_ref, source_ref, pass_ref, reflect_ref, pass_rows, reflect_rows, sems,
):
    del after_ref
    copies = [
        pltpu.make_async_copy(source, target, sems.at[i])
        for i, (source, target) in enumerate(
            (
                (pass_hbm, pass_rows),
                (reflect_hbm, reflect_rows),
                (ops_hbm, ops_ref),
                (source_hbm, source_ref),
            )
        )
    ]
    for copy in copies:
        copy.start()
    for copy, rows, columns_ref in zip(copies, (pass_rows, reflect_rows), (pass_ref, reflect_ref)):
        copy.wait()
        for b in range(columns_ref.shape[0]):
            row = rows[0, pl.ds(b, 1), :]
            columns_ref[b] = jnp.broadcast_to(row, columns_ref.shape[1:]).T
    for copy in copies[2:]:
        copy.wait()


def fill_buffer(section, sections, tick, source_ref, wave_ref, first_ref, second_ref, buffer):
    blocks, listed = wave_ref.shape[0], first_ref.shape[0]
    if tick == 0:
        sender = lax.axis_index("lat") + 1
        buffer[:blocks] = wave_ref[...]
    else:
        sender = lax.rem(section + sections - 1, sections)

        @pl.when(section == 0)
        def _():
            buffer[:blocks] = source_ref[tick - 1]

        @pl.when(section != 0)
        def _():
            buffer[:blocks] = wave_ref[...]
    parity = lax.rem(sender, 2)
    buffer[pl.ds(blocks + parity * listed, listed)] = first_ref[...]
    buffer[pl.ds(blocks + (1 - parity) * listed, listed)] = second_ref[...]


def extrapolate_block(plan_ref, pattern_start, ops_ref, buffer, b):
    taken = ops_ref.shape[2]
    points = ops_ref.shape[5]
    left = jnp.concatenate(
        [ops_ref[0, b, k].reshape(2 * points, points) for k in range(taken)], axis=1
    )
    right = jnp.concatenate(
        [buffer[plan_ref[pattern_start + b * taken + k]] for k in range(taken)], axis=0
    )
    products = jnp.dot(left, right, preferred_element_type=jnp.float32)
    half = products.shape[1] // 2
    real_part = products[:points, :half] - products[points:, half:]
    imag_part = products[:points, half:] + products[points:, :half]
    return real_part, imag_part


def tick_kernel(
    tick, sections, plan_ref, ops_ref, source_ref, pass_ref, reflect_ref,
    wave_ref, first_in_ref, second_in_ref, echo_ref, onward_ref, first_ref, second_ref, buffer,
):
    section = lax.axis_index("depth")
    listed = first_ref.shape[0]
    fill_buffer(
        section, sections, tick, source_ref, wave_ref, first_in_ref, second_in_ref, buffer
    )
    for b in range(wave_ref.shape[0]):
        parts = extrapolate_block(plan_ref, 2 * (listed + 1), ops_ref, buffer, b)
        for i, part in enumerate(parts):
            cols = pl.ds(i * part.shape[1], part.shape[1])
            onward_ref[b, :, cols] = (pass_ref[b] * part).astype(onward_ref.dtype)
            echo_ref[b, :, cols] = (reflect_ref[b] * part).astype(echo_ref.dtype)

    @pl.when(section != sections - 1)
    def _():
        write_lists(section, plan_ref, onward_ref, (first_ref, second_ref))

    @pl.when(section == sections - 1)
    def _():
        write_lists(section, plan_ref, source_ref.at[tick], (first_ref, second_ref))


def last_kernel(
    tick, sections, plan_ref, ops_ref, source_ref, pass_ref, reflect_ref,
    wave_ref, first_in_ref, second_in_ref, *rest,
):
    earlier = rest[:tick]
    (reflected_ref, transmitted_ref, buffer, echo, leaving,
     early_sems, echo_sems, leave_sems) = rest[tick:]
    section = lax.axis_index("depth")
    listed = first_in_ref.shape[0]
    copies = [
        pltpu.make_async_copy(earlier[t], reflected_ref.at[t, 0], early_sems.at[t])
        for t in range(tick)
    ]
    for copy in copies:
        copy.start()
    fill_buffer(
        section, sections, tick, source_ref, wave_ref, first_in_ref, second_in_ref, buffer
    )
    for b in range(wave_ref.shape[0]):
        parts = extrapolate_block(plan_ref, 2 * (listed + 1), ops_ref, buffer, b)
        for i, part in enumerate(parts):
            cols = pl.ds(i * part.shape[1], part.shape[1])
            leaving[b, :, cols] = pass_ref[b] * part
            echo[b, :, cols] = (reflect_ref[b] * part).astype(echo.dtype)
        for copy in (
            pltpu.make_async_copy(leaving.at[b], transmitted_ref.at[0, b], leave_sems.at[b]),
            pltpu.make_async_copy(echo.at[b], reflected_ref.at[tick, 0, b], echo_sems.at[b]),
        ):
            copy.start()
            copies.append(copy)
    for copy in copies:
        copy.wait()


def swaps(tiles, start):
    pairs = [(j, j + 1) for j in range(start, tiles - 1, 2)]
    return pairs + [(to, j) for j, to in pairs]


def halo_routes(sections, tiles):
    return [
        [
            (s * tiles + j, (s + 1) % sections * tiles + j + way)
            for s in range(sections)
            for way in (1 if (s + turn) % 2 == 0 else -1,)
            for j in range(tiles)
            if 0 <= j + way < tiles
        ]
        for turn in (0, 1)
    ]


def per_device(
    inflow, source, operators, transmission, reflectivity, send_ids, send_count, pattern
):
    sections, tiles = lax.axis_size("depth"), lax.axis_size("lat")
    ticks = source.shape[0] + 1
    _, blocks, points, columns = inflow.shape
    listed = send_ids.shape[-1]
    taken = operators.shape[2]
    wave_type = pltpu.VMEM((blocks, points, columns), WAVE)
    list_type = pltpu.VMEM((listed, points, columns), WAVE)
    params = pltpu.CompilerParams(vmem_limit_bytes=VMEM_LIMIT)
    tick_cost = pl.CostEstimate(
        flops=blocks * taken * 4 * points * points * columns,
        bytes_accessed=2 * operators.size + 8 * blocks * points * columns,
        transcendentals=0,
    )
    both = ("depth", "lat")
    deeper = [(s, (s + 1) % sections) for s in range(sections)]

    plan, wave, first, second = pl.pallas_call(
        prepare_kernel,
        out_shape=(
            pltpu.SMEM((2 * (listed + 1) + blocks * taken,), jnp.int32),
            wave_type,
            list_type,
            list_type,
        ),
        in_specs=[ANY_SPEC] * 4,
        out_specs=(SMEM_SPEC,) + (VMEM_SPEC,) * 3,
        scratch_shapes=[
            pltpu.SMEM(send_ids.shape, jnp.int32),
            pltpu.SMEM(send_count.shape, jnp.int32),
            pltpu.SMEM(pattern.shape, jnp.int32),
            pltpu.VMEM((blocks, points, columns), inflow.dtype),
            pltpu.SemaphoreType.DMA((3,)),
            pltpu.SemaphoreType.DMA((blocks,)),
        ],
        compiler_params=params,
        cost_estimate=pl.CostEstimate(
            flops=inflow.size, bytes_accessed=8 * inflow.size, transcendentals=0
        ),
        name="prepare",
    )(*map(in_hbm, (send_ids, send_count, pattern, inflow)))
    loaded_first = first
    first = lax.ppermute(first, "lat", swaps(tiles, 0))
    second = lax.ppermute(second, "lat", swaps(tiles, 1))

    column_type = pltpu.VMEM((blocks, points, columns // 2), jnp.float32)
    fixed = pl.pallas_call(
        load_kernel,
        out_shape=(
            pltpu.VMEM(operators.shape, operators.dtype),
            pltpu.VMEM(source.shape, source.dtype),
            column_type,
            column_type,
        ),
        in_specs=[ANY_SPEC] * 4 + [VMEM_SPEC],
        out_specs=(VMEM_SPEC,) * 4,
        scratch_shapes=[
            pltpu.VMEM(transmission.shape, transmission.dtype),
            pltpu.VMEM(reflectivity.shape, reflectivity.dtype),
            pltpu.SemaphoreType.DMA((4,)),
        ],
        compiler_params=params,
        cost_estimate=pl.CostEstimate(
            flops=0, bytes_accessed=4 * (operators.size + source.size), transcendentals=0
        ),
        name="load",
    )(*map(in_hbm, (operators, source, transmission, reflectivity)), in_vmem(loaded_first))
    fixed = [plan, *map(in_vmem, fixed)]

    buffer_type = pltpu.VMEM((blocks + 2 * listed, points, columns), WAVE)
    routes = halo_routes(sections, tiles)
    echoes = []
    for tick in range(ticks - 1):
        echo, onward, first, second = pl.pallas_call(
            functools.partial(tick_kernel, tick, sections),
            out_shape=(wave_type, wave_type, list_type, list_type),
            in_specs=[SMEM_SPEC] + [VMEM_SPEC] * 7,
            out_specs=(VMEM_SPEC,) * 4,
            scratch_shapes=[buffer_type],
            compiler_params=params,
            cost_estimate=tick_cost,
            name=f"tick{tick}",
        )(*fixed, in_vmem(wave), in_vmem(first), in_vmem(second))
        echoes.append(echo)
        wave = lax.ppermute(onward, "depth", deeper)
        first = lax.ppermute(first, both, routes[0])
        second = lax.ppermute(second, both, routes[1])

    tick = ticks - 1
    reflected, transmitted = pl.pallas_call(
        functools.partial(last_kernel, tick, sections),
        out_shape=(
            jax.ShapeDtypeStruct((ticks, 1, blocks, points, columns), WAVE),
            jax.ShapeDtypeStruct((1, blocks, points, columns), jnp.float32),
        ),
        in_specs=[SMEM_SPEC] + [VMEM_SPEC] * (7 + tick),
        out_specs=(ANY_SPEC, ANY_SPEC),
        scratch_shapes=[
            buffer_type,
            pltpu.VMEM((blocks, points, columns), WAVE),
            pltpu.VMEM((blocks, points, columns), jnp.float32),
            pltpu.SemaphoreType.DMA((tick,)),
            pltpu.SemaphoreType.DMA((blocks,)),
            pltpu.SemaphoreType.DMA((blocks,)),
        ],
        compiler_params=params,
        cost_estimate=tick_cost,
        name="last_tick",
    )(*fixed, in_vmem(wave), in_vmem(first), in_vmem(second), *map(in_vmem, echoes))
    return reflected, transmitted


def solution(mesh):
    return jax.shard_map(
        per_device,
        mesh=mesh,
        in_specs=(
            P("depth", "lat", None, None),
            P(None, "lat", None, None),
            P("depth", "lat", None, None, None, None),
            P("depth", "lat", None),
            P("depth", "lat", None),
            P("lat", None, None),
            P("lat", None),
            P("lat", None),
        ),
        out_specs=(P(None, "depth", "lat", None, None), P("depth", "lat", None, None)),
        check_vma=False,
    )
```

```python
import functools

import jax
import jax.numpy as jnp
from jax import lax
from jax.experimental import pallas as pl
from jax.experimental.pallas import tpu as pltpu
from jax.sharding import PartitionSpec as P

WAVE = jnp.bfloat16
SMEM_SPEC = pl.BlockSpec(memory_space=pltpu.SMEM)
VMEM_SPEC = pl.BlockSpec(memory_space=pltpu.VMEM)
ANY_SPEC = pl.BlockSpec(memory_space=pl.ANY)
VMEM_LIMIT = 8 * 1024 * 1024
LOWER, UPPER = 0, 1


def in_vmem(array):
    return pltpu.with_memory_space_constraint(array, pltpu.VMEM)


def in_hbm(array):
    return pltpu.with_memory_space_constraint(array, pltpu.HBM)


def write_lists(position, plan_ref, blocks_ref, lists):
    listed = lists[0].shape[0]
    parity = lax.rem(position, 2)
    for list_ref, side in zip(lists, (UPPER - parity, parity)):
        count = plan_ref[2 * listed + side]
        for slot in range(listed):
            live = slot < count

            @pl.when(live)
            def _():
                list_ref[slot] = blocks_ref[plan_ref[side * listed + slot]]

            @pl.when(jnp.logical_not(live))
            def _():
                list_ref[slot] = jnp.zeros(list_ref.shape[1:], list_ref.dtype)


def prepare_kernel(
    ids_hbm, count_hbm, pattern_hbm, inflow_hbm, plan_ref, wave_ref, first_ref, second_ref,
    ids, count, pattern, landed, small_sems, sems,
):
    blocks = wave_ref.shape[0]
    small = [
        pltpu.make_async_copy(source, target, small_sems.at[i])
        for i, (source, target) in enumerate(
            ((ids_hbm, ids), (count_hbm, count), (pattern_hbm, pattern))
        )
    ]
    large = [
        pltpu.make_async_copy(inflow_hbm.at[0, b], landed.at[b], sems.at[b]) for b in range(blocks)
    ]
    for copy in small + large:
        copy.start()
    for copy in small:
        copy.wait()
    _, sides, listed = ids.shape
    taken = pattern.shape[1]
    for side in range(sides):
        for slot in range(listed):
            plan_ref[side * listed + slot] = ids[0, side, slot]
        plan_ref[sides * listed + side] = count[0, side]
    for b in range(blocks):
        for k in range(taken):
            plan_ref[sides * (listed + 1) + b * taken + k] = pattern[b, k]
    for b, copy in enumerate(large):
        copy.wait()
        wave_ref[b] = landed[b].astype(wave_ref.dtype)
    position = lax.axis_index("lat") + lax.axis_index("depth")
    write_lists(position, plan_ref, wave_ref, (first_ref, second_ref))


def load_kernel(
    ops_hbm, source_hbm, pass_hbm, reflect_hbm, after_ref,
    ops_ref, source_ref, pass_ref, reflect_ref, pass_rows, reflect_rows, sems,
):
    del after_ref
    copies = [
        pltpu.make_async_copy(source, target, sems.at[i])
        for i, (source, target) in enumerate(
            (
                (pass_hbm, pass_rows),
                (reflect_hbm, reflect_rows),
                (ops_hbm, ops_ref),
                (source_hbm, source_ref),
            )
        )
    ]
    for copy in copies:
        copy.start()
    for copy, rows, columns_ref in zip(copies, (pass_rows, reflect_rows), (pass_ref, reflect_ref)):
        copy.wait()
        for b in range(columns_ref.shape[0]):
            row = rows[0, pl.ds(b, 1), :]
            columns_ref[b] = jnp.broadcast_to(row, columns_ref.shape[1:]).T
    for copy in copies[2:]:
        copy.wait()


def fill_buffer(section, sections, tick, source_ref, wave_ref, first_ref, second_ref, buffer):
    blocks, listed = wave_ref.shape[0], first_ref.shape[0]
    if tick == 0:
        sender = section + lax.axis_index("lat") + 1
        buffer[:blocks] = wave_ref[...]
    else:
        sender = lax.rem(section + sections - 1, sections)

        @pl.when(section == 0)
        def _():
            buffer[:blocks] = source_ref[tick - 1]

        @pl.when(section != 0)
        def _():
            buffer[:blocks] = wave_ref[...]
    parity = lax.rem(sender, 2)
    buffer[pl.ds(blocks + parity * listed, listed)] = first_ref[...]
    buffer[pl.ds(blocks + (1 - parity) * listed, listed)] = second_ref[...]


def extrapolate_block(plan_ref, pattern_start, ops_ref, buffer, b):
    taken = ops_ref.shape[2]
    points = ops_ref.shape[5]
    left = jnp.concatenate(
        [ops_ref[0, b, k].reshape(2 * points, points) for k in range(taken)], axis=1
    )
    right = jnp.concatenate(
        [buffer[plan_ref[pattern_start + b * taken + k]] for k in range(taken)], axis=0
    )
    products = jnp.dot(left, right, preferred_element_type=jnp.float32)
    half = products.shape[1] // 2
    real_part = products[:points, :half] - products[points:, half:]
    imag_part = products[:points, half:] + products[points:, :half]
    return real_part, imag_part


def tick_kernel(
    tick, sections, plan_ref, ops_ref, source_ref, pass_ref, reflect_ref,
    wave_ref, first_in_ref, second_in_ref, echo_ref, onward_ref, first_ref, second_ref, buffer,
):
    section = lax.axis_index("depth")
    listed = first_ref.shape[0]
    fill_buffer(
        section, sections, tick, source_ref, wave_ref, first_in_ref, second_in_ref, buffer
    )
    for b in range(wave_ref.shape[0]):
        parts = extrapolate_block(plan_ref, 2 * (listed + 1), ops_ref, buffer, b)
        for i, part in enumerate(parts):
            cols = pl.ds(i * part.shape[1], part.shape[1])
            onward_ref[b, :, cols] = (pass_ref[b] * part).astype(onward_ref.dtype)
            echo_ref[b, :, cols] = (reflect_ref[b] * part).astype(echo_ref.dtype)

    @pl.when(section != sections - 1)
    def _():
        write_lists(section, plan_ref, onward_ref, (first_ref, second_ref))

    @pl.when(section == sections - 1)
    def _():
        write_lists(section, plan_ref, source_ref.at[tick], (first_ref, second_ref))


def last_kernel(
    tick, sections, plan_ref, ops_ref, source_ref, pass_ref, reflect_ref,
    wave_ref, first_in_ref, second_in_ref, *rest,
):
    earlier = rest[:tick]
    (reflected_ref, transmitted_ref, buffer, echo, leaving,
     early_sems, echo_sems, leave_sems) = rest[tick:]
    section = lax.axis_index("depth")
    listed = first_in_ref.shape[0]
    copies = [
        pltpu.make_async_copy(earlier[t], reflected_ref.at[t, 0], early_sems.at[t])
        for t in range(tick)
    ]
    for copy in copies:
        copy.start()
    fill_buffer(
        section, sections, tick, source_ref, wave_ref, first_in_ref, second_in_ref, buffer
    )
    for b in range(wave_ref.shape[0]):
        parts = extrapolate_block(plan_ref, 2 * (listed + 1), ops_ref, buffer, b)
        for i, part in enumerate(parts):
            cols = pl.ds(i * part.shape[1], part.shape[1])
            leaving[b, :, cols] = pass_ref[b] * part
            echo[b, :, cols] = (reflect_ref[b] * part).astype(echo.dtype)
        for copy in (
            pltpu.make_async_copy(leaving.at[b], transmitted_ref.at[0, b], leave_sems.at[b]),
            pltpu.make_async_copy(echo.at[b], reflected_ref.at[tick, 0, b], echo_sems.at[b]),
        ):
            copy.start()
            copies.append(copy)
    for copy in copies:
        copy.wait()


def closed(route, devices):
    target = dict(route)
    source = {to: at for at, to in route}
    for end in [d for d in range(devices) if d not in target]:
        start = end
        while start in source:
            start = source[start]
        target[end], source[start] = start, end
    return sorted(target.items())


def swap_routes(sections, tiles):
    return [
        closed(
            [
                (s * tiles + at, s * tiles + to)
                for s in range(sections)
                for j in range((s + turn) % 2, tiles - 1, 2)
                for at, to in ((j, j + 1), (j + 1, j))
            ],
            sections * tiles,
        )
        for turn in (0, 1)
    ]


def halo_routes(sections, tiles):
    return [
        [
            (s * tiles + j, (s + 1) % sections * tiles + j + way)
            if 0 <= j + way < tiles
            else (s * tiles + j, s * tiles + j)
            for s in range(sections)
            for way in (1 if (s + turn) % 2 == 0 else -1,)
            for j in range(tiles)
        ]
        for turn in (0, 1)
    ]


def per_device(
    inflow, source, operators, transmission, reflectivity, send_ids, send_count, pattern
):
    sections, tiles = lax.axis_size("depth"), lax.axis_size("lat")
    ticks = source.shape[0] + 1
    _, blocks, points, columns = inflow.shape
    listed = send_ids.shape[-1]
    taken = operators.shape[2]
    wave_type = pltpu.VMEM((blocks, points, columns), WAVE)
    list_type = pltpu.VMEM((listed, points, columns), WAVE)
    params = pltpu.CompilerParams(vmem_limit_bytes=VMEM_LIMIT)
    tick_cost = pl.CostEstimate(
        flops=blocks * taken * 4 * points * points * columns,
        bytes_accessed=2 * operators.size + 8 * blocks * points * columns,
        transcendentals=0,
    )
    both = ("depth", "lat")
    deeper = [(s, (s + 1) % sections) for s in range(sections)]

    plan, wave, first, second = pl.pallas_call(
        prepare_kernel,
        out_shape=(
            pltpu.SMEM((2 * (listed + 1) + blocks * taken,), jnp.int32),
            wave_type,
            list_type,
            list_type,
        ),
        in_specs=[ANY_SPEC] * 4,
        out_specs=(SMEM_SPEC,) + (VMEM_SPEC,) * 3,
        scratch_shapes=[
            pltpu.SMEM(send_ids.shape, jnp.int32),
            pltpu.SMEM(send_count.shape, jnp.int32),
            pltpu.SMEM(pattern.shape, jnp.int32),
            pltpu.VMEM((blocks, points, columns), inflow.dtype),
            pltpu.SemaphoreType.DMA((3,)),
            pltpu.SemaphoreType.DMA((blocks,)),
        ],
        compiler_params=params,
        cost_estimate=pl.CostEstimate(
            flops=inflow.size, bytes_accessed=8 * inflow.size, transcendentals=0
        ),
        name="prepare",
    )(*map(in_hbm, (send_ids, send_count, pattern, inflow)))
    loaded_first = first
    routes = swap_routes(sections, tiles)
    first = lax.ppermute(first, both, routes[0])
    second = lax.ppermute(second, both, routes[1])

    column_type = pltpu.VMEM((blocks, points, columns // 2), jnp.float32)
    fixed = pl.pallas_call(
        load_kernel,
        out_shape=(
            pltpu.VMEM(operators.shape, operators.dtype),
            pltpu.VMEM(source.shape, source.dtype),
            column_type,
            column_type,
        ),
        in_specs=[ANY_SPEC] * 4 + [VMEM_SPEC],
        out_specs=(VMEM_SPEC,) * 4,
        scratch_shapes=[
            pltpu.VMEM(transmission.shape, transmission.dtype),
            pltpu.VMEM(reflectivity.shape, reflectivity.dtype),
            pltpu.SemaphoreType.DMA((4,)),
        ],
        compiler_params=params,
        cost_estimate=pl.CostEstimate(
            flops=0, bytes_accessed=4 * (operators.size + source.size), transcendentals=0
        ),
        name="load",
    )(*map(in_hbm, (operators, source, transmission, reflectivity)), in_vmem(loaded_first))
    fixed = [plan, *map(in_vmem, fixed)]

    buffer_type = pltpu.VMEM((blocks + 2 * listed, points, columns), WAVE)
    routes = halo_routes(sections, tiles)
    echoes = []
    for tick in range(ticks - 1):
        echo, onward, first, second = pl.pallas_call(
            functools.partial(tick_kernel, tick, sections),
            out_shape=(wave_type, wave_type, list_type, list_type),
            in_specs=[SMEM_SPEC] + [VMEM_SPEC] * 7,
            out_specs=(VMEM_SPEC,) * 4,
            scratch_shapes=[buffer_type],
            compiler_params=params,
            cost_estimate=tick_cost,
            name=f"tick{tick}",
        )(*fixed, in_vmem(wave), in_vmem(first), in_vmem(second))
        echoes.append(echo)
        wave = lax.ppermute(onward, "depth", deeper)
        first = lax.ppermute(first, both, routes[0])
        second = lax.ppermute(second, both, routes[1])

    tick = ticks - 1
    reflected, transmitted = pl.pallas_call(
        functools.partial(last_kernel, tick, sections),
        out_shape=(
            jax.ShapeDtypeStruct((ticks, 1, blocks, points, columns), WAVE),
            jax.ShapeDtypeStruct((1, blocks, points, columns), jnp.float32),
        ),
        in_specs=[SMEM_SPEC] + [VMEM_SPEC] * (7 + tick),
        out_specs=(ANY_SPEC, ANY_SPEC),
        scratch_shapes=[
            buffer_type,
            pltpu.VMEM((blocks, points, columns), WAVE),
            pltpu.VMEM((blocks, points, columns), jnp.float32),
            pltpu.SemaphoreType.DMA((tick,)),
            pltpu.SemaphoreType.DMA((blocks,)),
            pltpu.SemaphoreType.DMA((blocks,)),
        ],
        compiler_params=params,
        cost_estimate=tick_cost,
        name="last_tick",
    )(*fixed, in_vmem(wave), in_vmem(first), in_vmem(second), *map(in_vmem, echoes))
    return reflected, transmitted


def solution(mesh):
    return jax.shard_map(
        per_device,
        mesh=mesh,
        in_specs=(
            P("depth", "lat", None, None),
            P(None, "lat", None, None),
            P("depth", "lat", None, None, None, None),
            P("depth", "lat", None),
            P("depth", "lat", None),
            P("lat", None, None),
            P("lat", None),
            P("lat", None),
        ),
        out_specs=(P(None, "depth", "lat", None, None), P("depth", "lat", None, None)),
        check_vma=False,
    )
```

```python
import functools

import jax
import jax.numpy as jnp
from jax import lax
from jax.experimental import pallas as pl
from jax.experimental.pallas import tpu as pltpu
from jax.sharding import PartitionSpec as P

WAVE = jnp.bfloat16
SMEM_SPEC = pl.BlockSpec(memory_space=pltpu.SMEM)
VMEM_SPEC = pl.BlockSpec(memory_space=pltpu.VMEM)
ANY_SPEC = pl.BlockSpec(memory_space=pl.ANY)
VMEM_LIMIT = 8 * 1024 * 1024
LOWER, UPPER = 0, 1


def in_vmem(array):
    return pltpu.with_memory_space_constraint(array, pltpu.VMEM)


def in_hbm(array):
    return pltpu.with_memory_space_constraint(array, pltpu.HBM)


def write_lists(tile, plan_ref, blocks_ref, lists):
    listed = lists[0].shape[0]
    parity = lax.rem(tile, 2)
    for list_ref, side in zip(lists, (UPPER - parity, parity)):
        count = plan_ref[2 * listed + side]
        for slot in range(listed):
            live = slot < count

            @pl.when(live)
            def _():
                list_ref[slot] = blocks_ref[plan_ref[side * listed + slot]]

            @pl.when(jnp.logical_not(live))
            def _():
                list_ref[slot] = jnp.zeros(list_ref.shape[1:], list_ref.dtype)


def prepare_kernel(
    ids_hbm, count_hbm, pattern_hbm, inflow_hbm, plan_ref, wave_ref, first_ref, second_ref,
    ids, count, pattern, landed, small_sems, sems,
):
    blocks = wave_ref.shape[0]
    small = [
        pltpu.make_async_copy(source, target, small_sems.at[i])
        for i, (source, target) in enumerate(
            ((ids_hbm, ids), (count_hbm, count), (pattern_hbm, pattern))
        )
    ]
    large = [
        pltpu.make_async_copy(inflow_hbm.at[0, b], landed.at[b], sems.at[b]) for b in range(blocks)
    ]
    for copy in small + large:
        copy.start()
    for copy in small:
        copy.wait()
    _, sides, listed = ids.shape
    taken = pattern.shape[1]
    for side in range(sides):
        for slot in range(listed):
            plan_ref[side * listed + slot] = ids[0, side, slot]
        plan_ref[sides * listed + side] = count[0, side]
    for b in range(blocks):
        for k in range(taken):
            plan_ref[sides * (listed + 1) + b * taken + k] = pattern[b, k]
    for b, copy in enumerate(large):
        copy.wait()
        wave_ref[b] = landed[b].astype(wave_ref.dtype)
    write_lists(lax.axis_index("lat"), plan_ref, wave_ref, (first_ref, second_ref))


def load_kernel(
    ops_hbm, source_hbm, pass_hbm, reflect_hbm, after_ref,
    ops_ref, source_ref, pass_ref, reflect_ref, pass_rows, reflect_rows, sems,
):
    del after_ref
    copies = [
        pltpu.make_async_copy(source, target, sems.at[i])
        for i, (source, target) in enumerate(
            (
                (pass_hbm, pass_rows),
                (reflect_hbm, reflect_rows),
                (ops_hbm, ops_ref),
                (source_hbm, source_ref),
            )
        )
    ]
    for copy in copies:
        copy.start()
    for copy, rows, columns_ref in zip(copies, (pass_rows, reflect_rows), (pass_ref, reflect_ref)):
        copy.wait()
        for b in range(columns_ref.shape[0]):
            row = rows[0, pl.ds(b, 1), :]
            columns_ref[b] = jnp.broadcast_to(row, columns_ref.shape[1:]).T
    for copy in copies[2:]:
        copy.wait()


def fill_buffer(section, tick, source_ref, wave_ref, first_ref, second_ref, buffer):
    blocks, listed = wave_ref.shape[0], first_ref.shape[0]
    if tick == 0:
        buffer[:blocks] = wave_ref[...]
    else:
        @pl.when(section == 0)
        def _():
            buffer[:blocks] = source_ref[tick - 1]

        @pl.when(section != 0)
        def _():
            buffer[:blocks] = wave_ref[...]
    parity = lax.rem(lax.axis_index("lat"), 2)
    buffer[pl.ds(blocks + (1 - parity) * listed, listed)] = first_ref[...]
    buffer[pl.ds(blocks + parity * listed, listed)] = second_ref[...]


def extrapolate_block(plan_ref, pattern_start, ops_ref, buffer, b):
    taken = ops_ref.shape[2]
    points = ops_ref.shape[5]
    left = jnp.concatenate(
        [ops_ref[0, b, k].reshape(2 * points, points) for k in range(taken)], axis=1
    )
    right = jnp.concatenate(
        [buffer[plan_ref[pattern_start + b * taken + k]] for k in range(taken)], axis=0
    )
    products = jnp.dot(left, right, preferred_element_type=jnp.float32)
    half = products.shape[1] // 2
    real_part = products[:points, :half] - products[points:, half:]
    imag_part = products[:points, half:] + products[points:, :half]
    return real_part, imag_part


def tick_kernel(
    tick, sections, plan_ref, ops_ref, source_ref, pass_ref, reflect_ref,
    wave_ref, first_in_ref, second_in_ref, echo_ref, onward_ref, first_ref, second_ref, buffer,
):
    section = lax.axis_index("depth")
    tile = lax.axis_index("lat")
    listed = first_ref.shape[0]
    fill_buffer(section, tick, source_ref, wave_ref, first_in_ref, second_in_ref, buffer)
    for b in range(wave_ref.shape[0]):
        parts = extrapolate_block(plan_ref, 2 * (listed + 1), ops_ref, buffer, b)
        for i, part in enumerate(parts):
            cols = pl.ds(i * part.shape[1], part.shape[1])
            onward_ref[b, :, cols] = (pass_ref[b] * part).astype(onward_ref.dtype)
            echo_ref[b, :, cols] = (reflect_ref[b] * part).astype(echo_ref.dtype)

    @pl.when(section != sections - 1)
    def _():
        write_lists(tile, plan_ref, onward_ref, (first_ref, second_ref))

    @pl.when(section == sections - 1)
    def _():
        write_lists(tile, plan_ref, source_ref.at[tick], (first_ref, second_ref))


def last_kernel(
    tick, plan_ref, ops_ref, source_ref, pass_ref, reflect_ref,
    wave_ref, first_in_ref, second_in_ref, *rest,
):
    earlier = rest[:tick]
    (reflected_ref, transmitted_ref, buffer, echo, leaving,
     early_sems, echo_sems, leave_sems) = rest[tick:]
    section = lax.axis_index("depth")
    listed = first_in_ref.shape[0]
    copies = [
        pltpu.make_async_copy(earlier[t], reflected_ref.at[t, 0], early_sems.at[t])
        for t in range(tick)
    ]
    for copy in copies:
        copy.start()
    fill_buffer(section, tick, source_ref, wave_ref, first_in_ref, second_in_ref, buffer)
    for b in range(wave_ref.shape[0]):
        parts = extrapolate_block(plan_ref, 2 * (listed + 1), ops_ref, buffer, b)
        for i, part in enumerate(parts):
            cols = pl.ds(i * part.shape[1], part.shape[1])
            leaving[b, :, cols] = pass_ref[b] * part
            echo[b, :, cols] = (reflect_ref[b] * part).astype(echo.dtype)
        for copy in (
            pltpu.make_async_copy(leaving.at[b], transmitted_ref.at[0, b], leave_sems.at[b]),
            pltpu.make_async_copy(echo.at[b], reflected_ref.at[tick, 0, b], echo_sems.at[b]),
        ):
            copy.start()
            copies.append(copy)
    for copy in copies:
        copy.wait()


def neighbour(j, turn, tiles):
    to = j + (1 if (j + turn) % 2 == 0 else -1)
    return to if 0 <= to < tiles else None


def swap_routes(sections, tiles):
    routes = []
    for turn in (0, 1):
        route = []
        for s in range(sections):
            for j in range(tiles):
                to = neighbour(j, turn, tiles)
                end = ((s ^ 1) * tiles + j) if to is None else (s * tiles + to)
                route.append((s * tiles + j, end))
        routes.append(route)
    return routes


def halo_routes(sections, tiles):
    routes = []
    for turn in (0, 1):
        route = []
        for s in range(sections):
            for j in range(tiles):
                to = neighbour(j, turn, tiles)
                to = j if to is None else to
                route.append((s * tiles + j, (s + 1) % sections * tiles + to))
        routes.append(route)
    return routes


def per_device(
    inflow, source, operators, transmission, reflectivity, send_ids, send_count, pattern
):
    sections, tiles = lax.axis_size("depth"), lax.axis_size("lat")
    ticks = source.shape[0] + 1
    _, blocks, points, columns = inflow.shape
    listed = send_ids.shape[-1]
    taken = operators.shape[2]
    wave_type = pltpu.VMEM((blocks, points, columns), WAVE)
    list_type = pltpu.VMEM((listed, points, columns), WAVE)
    params = pltpu.CompilerParams(vmem_limit_bytes=VMEM_LIMIT)
    tick_cost = pl.CostEstimate(
        flops=blocks * taken * 4 * points * points * columns,
        bytes_accessed=2 * operators.size + 8 * blocks * points * columns,
        transcendentals=0,
    )
    both = ("depth", "lat")
    deeper = [(s, (s + 1) % sections) for s in range(sections)]

    plan, wave, first, second = pl.pallas_call(
        prepare_kernel,
        out_shape=(
            pltpu.SMEM((2 * (listed + 1) + blocks * taken,), jnp.int32),
            wave_type,
            list_type,
            list_type,
        ),
        in_specs=[ANY_SPEC] * 4,
        out_specs=(SMEM_SPEC,) + (VMEM_SPEC,) * 3,
        scratch_shapes=[
            pltpu.SMEM(send_ids.shape, jnp.int32),
            pltpu.SMEM(send_count.shape, jnp.int32),
            pltpu.SMEM(pattern.shape, jnp.int32),
            pltpu.VMEM((blocks, points, columns), inflow.dtype),
            pltpu.SemaphoreType.DMA((3,)),
            pltpu.SemaphoreType.DMA((blocks,)),
        ],
        compiler_params=params,
        cost_estimate=pl.CostEstimate(
            flops=inflow.size, bytes_accessed=8 * inflow.size, transcendentals=0
        ),
        name="prepare",
    )(*map(in_hbm, (send_ids, send_count, pattern, inflow)))
    loaded_first = first
    routes = swap_routes(sections, tiles)
    first = lax.ppermute(first, both, routes[0])
    second = lax.ppermute(second, both, routes[1])

    column_type = pltpu.VMEM((blocks, points, columns // 2), jnp.float32)
    fixed = pl.pallas_call(
        load_kernel,
        out_shape=(
            pltpu.VMEM(operators.shape, operators.dtype),
            pltpu.VMEM(source.shape, source.dtype),
            column_type,
            column_type,
        ),
        in_specs=[ANY_SPEC] * 4 + [VMEM_SPEC],
        out_specs=(VMEM_SPEC,) * 4,
        scratch_shapes=[
            pltpu.VMEM(transmission.shape, transmission.dtype),
            pltpu.VMEM(reflectivity.shape, reflectivity.dtype),
            pltpu.SemaphoreType.DMA((4,)),
        ],
        compiler_params=params,
        cost_estimate=pl.CostEstimate(
            flops=0, bytes_accessed=4 * (operators.size + source.size), transcendentals=0
        ),
        name="load",
    )(*map(in_hbm, (operators, source, transmission, reflectivity)), in_vmem(loaded_first))
    fixed = [plan, *map(in_vmem, fixed)]

    buffer_type = pltpu.VMEM((blocks + 2 * listed, points, columns), WAVE)
    routes = halo_routes(sections, tiles)
    echoes = []
    for tick in range(ticks - 1):
        echo, onward, first, second = pl.pallas_call(
            functools.partial(tick_kernel, tick, sections),
            out_shape=(wave_type, wave_type, list_type, list_type),
            in_specs=[SMEM_SPEC] + [VMEM_SPEC] * 7,
            out_specs=(VMEM_SPEC,) * 4,
            scratch_shapes=[buffer_type],
            compiler_params=params,
            cost_estimate=tick_cost,
            name=f"tick{tick}",
        )(*fixed, in_vmem(wave), in_vmem(first), in_vmem(second))
        echoes.append(echo)
        wave = lax.ppermute(onward, "depth", deeper)
        first = lax.ppermute(first, both, routes[0])
        second = lax.ppermute(second, both, routes[1])

    tick = ticks - 1
    reflected, transmitted = pl.pallas_call(
        functools.partial(last_kernel, tick),
        out_shape=(
            jax.ShapeDtypeStruct((ticks, 1, blocks, points, columns), WAVE),
            jax.ShapeDtypeStruct((1, blocks, points, columns), jnp.float32),
        ),
        in_specs=[SMEM_SPEC] + [VMEM_SPEC] * (7 + tick),
        out_specs=(ANY_SPEC, ANY_SPEC),
        scratch_shapes=[
            buffer_type,
            pltpu.VMEM((blocks, points, columns), WAVE),
            pltpu.VMEM((blocks, points, columns), jnp.float32),
            pltpu.SemaphoreType.DMA((tick,)),
            pltpu.SemaphoreType.DMA((blocks,)),
            pltpu.SemaphoreType.DMA((blocks,)),
        ],
        compiler_params=params,
        cost_estimate=tick_cost,
        name="last_tick",
    )(*fixed, in_vmem(wave), in_vmem(first), in_vmem(second), *map(in_vmem, echoes))
    return reflected, transmitted


def solution(mesh):
    return jax.shard_map(
        per_device,
        mesh=mesh,
        in_specs=(
            P("depth", "lat", None, None),
            P(None, "lat", None, None),
            P("depth", "lat", None, None, None, None),
            P("depth", "lat", None),
            P("depth", "lat", None),
            P("lat", None, None),
            P("lat", None),
            P("lat", None),
        ),
        out_specs=(P(None, "depth", "lat", None, None), P("depth", "lat", None, None)),
        check_vma=False,
    )
```

```python
import functools

import jax
import jax.numpy as jnp
from jax import lax
from jax.experimental import pallas as pl
from jax.experimental.pallas import tpu as pltpu
from jax.sharding import PartitionSpec as P

WAVE = jnp.bfloat16
SMEM_SPEC = pl.BlockSpec(memory_space=pltpu.SMEM)
VMEM_SPEC = pl.BlockSpec(memory_space=pltpu.VMEM)
ANY_SPEC = pl.BlockSpec(memory_space=pl.ANY)
VMEM_LIMIT = 8 * 1024 * 1024
LOWER, UPPER = 0, 1


def in_vmem(array):
    return pltpu.with_memory_space_constraint(array, pltpu.VMEM)


def in_hbm(array):
    return pltpu.with_memory_space_constraint(array, pltpu.HBM)


def write_lists(tile, plan_ref, blocks_ref, lists):
    listed = lists[0].shape[0]
    parity = lax.rem(tile, 2)
    for list_ref, side in zip(lists, (UPPER - parity, parity)):
        count = plan_ref[2 * listed + side]
        for slot in range(listed):
            live = slot < count

            @pl.when(live)
            def _():
                list_ref[slot] = blocks_ref[plan_ref[side * listed + slot]]

            @pl.when(jnp.logical_not(live))
            def _():
                list_ref[slot] = jnp.zeros(list_ref.shape[1:], list_ref.dtype)


def prepare_kernel(
    ids_hbm, count_hbm, pattern_hbm, inflow_hbm, plan_ref, wave_ref, first_ref, second_ref,
    ids, count, pattern, landed, small_sems, sems,
):
    blocks = wave_ref.shape[0]
    small = [
        pltpu.make_async_copy(source, target, small_sems.at[i])
        for i, (source, target) in enumerate(
            ((ids_hbm, ids), (count_hbm, count), (pattern_hbm, pattern))
        )
    ]
    large = [
        pltpu.make_async_copy(inflow_hbm.at[0, b], landed.at[b], sems.at[b]) for b in range(blocks)
    ]
    for copy in small + large:
        copy.start()
    for copy in small:
        copy.wait()
    _, sides, listed = ids.shape
    taken = pattern.shape[1]
    for side in range(sides):
        for slot in range(listed):
            plan_ref[side * listed + slot] = ids[0, side, slot]
        plan_ref[sides * listed + side] = count[0, side]
    for b in range(blocks):
        for k in range(taken):
            plan_ref[sides * (listed + 1) + b * taken + k] = pattern[b, k]
    for b, copy in enumerate(large):
        copy.wait()
        wave_ref[b] = landed[b].astype(wave_ref.dtype)
    write_lists(lax.axis_index("lat"), plan_ref, wave_ref, (first_ref, second_ref))


def load_kernel(
    ops_hbm, source_hbm, pass_hbm, reflect_hbm, after_ref,
    ops_ref, source_ref, pass_ref, reflect_ref, pass_rows, reflect_rows, sems,
):
    del after_ref
    copies = [
        pltpu.make_async_copy(source, target, sems.at[i])
        for i, (source, target) in enumerate(
            (
                (pass_hbm, pass_rows),
                (reflect_hbm, reflect_rows),
                (ops_hbm, ops_ref),
                (source_hbm, source_ref),
            )
        )
    ]
    for copy in copies:
        copy.start()
    for copy, rows, columns_ref in zip(copies, (pass_rows, reflect_rows), (pass_ref, reflect_ref)):
        copy.wait()
        for b in range(columns_ref.shape[0]):
            row = rows[0, pl.ds(b, 1), :]
            columns_ref[b] = jnp.broadcast_to(row, columns_ref.shape[1:]).T
    for copy in copies[2:]:
        copy.wait()


def fill_buffer(section, tick, source_ref, wave_refs, first_ref, second_ref, buffer):
    blocks, listed = source_ref.shape[1], first_ref.shape[0]

    def fill_wave():
        start = 0
        for wave_ref in wave_refs:
            buffer[start : start + wave_ref.shape[0]] = wave_ref[...]
            start += wave_ref.shape[0]

    if tick == 0:
        fill_wave()
    else:
        pl.when(section != 0)(fill_wave)

        @pl.when(section == 0)
        def _():
            buffer[:blocks] = source_ref[tick - 1]

    parity = lax.rem(lax.axis_index("lat"), 2)
    buffer[pl.ds(blocks + (1 - parity) * listed, listed)] = first_ref[...]
    buffer[pl.ds(blocks + parity * listed, listed)] = second_ref[...]


def extrapolate_block(plan_ref, pattern_start, ops_ref, buffer, b):
    taken = ops_ref.shape[2]
    points = ops_ref.shape[5]
    left = jnp.concatenate(
        [ops_ref[0, b, k].reshape(2 * points, points) for k in range(taken)], axis=1
    )
    right = jnp.concatenate(
        [buffer[plan_ref[pattern_start + b * taken + k]] for k in range(taken)], axis=0
    )
    products = jnp.dot(left, right, preferred_element_type=jnp.float32)
    half = products.shape[1] // 2
    real_part = products[:points, :half] - products[points:, half:]
    imag_part = products[:points, half:] + products[points:, :half]
    return real_part, imag_part


def acts(section, parity):
    return True if parity is None else lax.rem(section, 2) == parity


def tick_kernel(
    parity, tick, sections, plan_ref, ops_ref, source_ref, pass_ref, reflect_ref,
    wave_refs, first_in_ref, second_in_ref, known_refs, out_refs, buffer, onward,
):
    del known_refs
    echo_ref, first_ref, second_ref, *onward_refs = out_refs
    section = lax.axis_index("depth")
    tile = lax.axis_index("lat")
    listed = first_ref.shape[0]

    @pl.when(acts(section, parity))
    def _():
        fill_buffer(section, tick, source_ref, wave_refs, first_in_ref, second_in_ref, buffer)
        for b in range(echo_ref.shape[0]):
            parts = extrapolate_block(plan_ref, 2 * (listed + 1), ops_ref, buffer, b)
            for i, part in enumerate(parts):
                cols = pl.ds(i * part.shape[1], part.shape[1])
                onward[b, :, cols] = (pass_ref[b] * part).astype(onward.dtype)
                echo_ref[b, :, cols] = (reflect_ref[b] * part).astype(echo_ref.dtype)
        start = 0
        for onward_ref in onward_refs:
            if start == onward.shape[0]:
                start = 0
            onward_ref[...] = onward[start : start + onward_ref.shape[0]]
            start += onward_ref.shape[0]

        @pl.when(section != sections - 1)
        def _():
            write_lists(tile, plan_ref, onward, (first_ref, second_ref))

        @pl.when(section == sections - 1)
        def _():
            write_lists(tile, plan_ref, source_ref.at[tick], (first_ref, second_ref))


def last_kernel(
    parity, tick, plan_ref, ops_ref, source_ref, pass_ref, reflect_ref,
    wave_refs, first_in_ref, second_in_ref, earlier, known_refs, out_refs,
    buffer, echo, leaving, early_sems, echo_sems, leave_sems,
):
    del known_refs
    reflected_ref, transmitted_ref = out_refs
    section = lax.axis_index("depth")
    listed = first_in_ref.shape[0]

    @pl.when(acts(section, parity))
    def _():
        copies = [
            pltpu.make_async_copy(earlier[t], reflected_ref.at[t, 0], early_sems.at[t])
            for t in range(tick)
        ]
        for copy in copies:
            copy.start()
        fill_buffer(section, tick, source_ref, wave_refs, first_in_ref, second_in_ref, buffer)
        for b in range(echo.shape[0]):
            parts = extrapolate_block(plan_ref, 2 * (listed + 1), ops_ref, buffer, b)
            for i, part in enumerate(parts):
                cols = pl.ds(i * part.shape[1], part.shape[1])
                leaving[b, :, cols] = pass_ref[b] * part
                echo[b, :, cols] = (reflect_ref[b] * part).astype(echo.dtype)
            for copy in (
                pltpu.make_async_copy(leaving.at[b], transmitted_ref.at[0, b], leave_sems.at[b]),
                pltpu.make_async_copy(echo.at[b], reflected_ref.at[tick, 0, b], echo_sems.at[b]),
            ):
                copy.start()
                copies.append(copy)
        for copy in copies:
            copy.wait()


def grouped_call(kernel, groups, outs, out_specs, known, **options):
    flat = [array for group in groups for array in (group if isinstance(group, list) else [group])]

    def body(*refs):
        refs = list(refs)
        take = lambda count: [refs.pop(0) for _ in range(count)]
        inputs = [take(len(g)) if isinstance(g, list) else refs.pop(0) for g in groups]
        kernel(*inputs, take(len(known)), take(len(outs)), *refs)

    return pl.pallas_call(
        body,
        out_shape=tuple(outs),
        in_specs=[SMEM_SPEC] + [VMEM_SPEC] * (len(flat) - 1) + list(out_specs[: len(known)]),
        out_specs=tuple(out_specs),
        input_output_aliases={len(flat) + i: i for i in range(len(known))},
        **options,
    )(flat[0], *map(in_vmem, flat[1:]), *known)


def neighbour(j, turn, tiles):
    to = j + (1 if (j + turn) % 2 == 0 else -1)
    return to if 0 <= to < tiles else None


def swap_routes(sections, tiles):
    routes = []
    for turn in (0, 1):
        route = []
        for s in range(sections):
            for j in range(tiles):
                to = neighbour(j, turn, tiles)
                end = ((s ^ 1) * tiles + j) if to is None else (s * tiles + to)
                route.append((s * tiles + j, end))
        routes.append(route)
    return routes


def halo_routes(sections, tiles):
    routes = []
    for turn in (0, 1):
        route = []
        for s in range(sections):
            for j in range(tiles):
                to = neighbour(j, turn, tiles)
                end = (s ^ 1) * tiles + j if to is None else (s + 1) % sections * tiles + to
                route.append((s * tiles + j, end))
        routes.append(route)
    return routes


def per_device(
    inflow, source, operators, transmission, reflectivity, send_ids, send_count, pattern
):
    sections, tiles = lax.axis_size("depth"), lax.axis_size("lat")
    ticks = source.shape[0] + 1
    _, blocks, points, columns = inflow.shape
    listed = send_ids.shape[-1]
    taken = operators.shape[2]
    wave_type = pltpu.VMEM((blocks, points, columns), WAVE)
    list_type = pltpu.VMEM((listed, points, columns), WAVE)
    params = pltpu.CompilerParams(vmem_limit_bytes=VMEM_LIMIT)
    tick_cost = pl.CostEstimate(
        flops=blocks * taken * 4 * points * points * columns,
        bytes_accessed=2 * operators.size + 8 * blocks * points * columns,
        transcendentals=0,
    )
    both = ("depth", "lat")
    deeper = [(s, (s + 1) % sections) for s in range(sections)]

    plan, wave, first, second = pl.pallas_call(
        prepare_kernel,
        out_shape=(
            pltpu.SMEM((2 * (listed + 1) + blocks * taken,), jnp.int32),
            wave_type,
            list_type,
            list_type,
        ),
        in_specs=[ANY_SPEC] * 4,
        out_specs=(SMEM_SPEC,) + (VMEM_SPEC,) * 3,
        scratch_shapes=[
            pltpu.SMEM(send_ids.shape, jnp.int32),
            pltpu.SMEM(send_count.shape, jnp.int32),
            pltpu.SMEM(pattern.shape, jnp.int32),
            pltpu.VMEM((blocks, points, columns), inflow.dtype),
            pltpu.SemaphoreType.DMA((3,)),
            pltpu.SemaphoreType.DMA((blocks,)),
        ],
        compiler_params=params,
        cost_estimate=pl.CostEstimate(
            flops=inflow.size, bytes_accessed=8 * inflow.size, transcendentals=0
        ),
        name="prepare",
    )(*map(in_hbm, (send_ids, send_count, pattern, inflow)))
    loaded_first = first
    routes = swap_routes(sections, tiles)
    first = lax.ppermute(first, both, routes[0])
    second = lax.ppermute(second, both, routes[1])

    column_type = pltpu.VMEM((blocks, points, columns // 2), jnp.float32)
    fixed = pl.pallas_call(
        load_kernel,
        out_shape=(
            pltpu.VMEM(operators.shape, operators.dtype),
            pltpu.VMEM(source.shape, source.dtype),
            column_type,
            column_type,
        ),
        in_specs=[ANY_SPEC] * 4 + [VMEM_SPEC],
        out_specs=(VMEM_SPEC,) * 4,
        scratch_shapes=[
            pltpu.VMEM(transmission.shape, transmission.dtype),
            pltpu.VMEM(reflectivity.shape, reflectivity.dtype),
            pltpu.SemaphoreType.DMA((4,)),
        ],
        compiler_params=params,
        cost_estimate=pl.CostEstimate(
            flops=0, bytes_accessed=4 * (operators.size + source.size), transcendentals=0
        ),
        name="load",
    )(*map(in_hbm, (operators, source, transmission, reflectivity)), in_vmem(loaded_first))
    fixed = [plan, *fixed]

    buffer_type = pltpu.VMEM((blocks + 2 * listed, points, columns), WAVE)

    ODD, EVEN = 1, 0
    halves = [blocks // 2, blocks - blocks // 2]
    half_types = [pltpu.VMEM((n, points, columns), WAVE) for n in halves]
    crossing = [(s, (s + 1) % sections) for s in range(sections)]
    inside = [(s, s ^ 1) for s in range(sections)]
    routes = halo_routes(sections, tiles)

    waves = {None: [wave]}
    echoes = []
    for tick in range(ticks - 1):
        known = []
        sent = {}
        for parity in (None,) if tick == 0 else (ODD, EVEN):
            to_next = ([wave_type] if parity != EVEN else []) + (half_types if parity != ODD else [])
            outs = [wave_type, list_type, list_type] + to_next
            known = grouped_call(
                functools.partial(tick_kernel, parity, tick, sections),
                [*fixed, waves[parity], first, second],
                outs,
                [VMEM_SPEC] * len(outs),
                known[:3] and [in_vmem(a) for a in known[:3]],
                scratch_shapes=[buffer_type, pltpu.VMEM(wave_type.shape, WAVE)],
                compiler_params=params,
                cost_estimate=tick_cost,
                name=f"tick{tick}" + ("" if parity is None else "_odd" if parity else "_even"),
            )
            if parity != EVEN:
                sent[EVEN] = [lax.ppermute(known[3], "depth", crossing)]
            if parity != ODD:
                sent[ODD] = [lax.ppermute(a, "depth", inside) for a in known[-2:]]
        waves = sent
        echo, first, second = known[:3]
        first = lax.ppermute(first, both, routes[0])
        second = lax.ppermute(second, both, routes[1])
        echoes.append(echo)

    tick = ticks - 1
    results = []
    result_types = (
        jax.ShapeDtypeStruct((ticks, 1, blocks, points, columns), WAVE),
        jax.ShapeDtypeStruct((1, blocks, points, columns), jnp.float32),
    )
    for parity in (ODD, EVEN):
        results = grouped_call(
            functools.partial(last_kernel, parity, tick),
            [*fixed, waves[parity], first, second, echoes],
            result_types,
            [ANY_SPEC] * 2,
            list(results),
            scratch_shapes=[
                buffer_type,
                pltpu.VMEM((blocks, points, columns), WAVE),
                pltpu.VMEM((blocks, points, columns), jnp.float32),
                pltpu.SemaphoreType.DMA((tick,)),
                pltpu.SemaphoreType.DMA((blocks,)),
                pltpu.SemaphoreType.DMA((blocks,)),
            ],
            compiler_params=params,
            cost_estimate=tick_cost,
            name="last_tick" + ("_odd" if parity else "_even"),
        )
    return tuple(results)


def solution(mesh):
    return jax.shard_map(
        per_device,
        mesh=mesh,
        in_specs=(
            P("depth", "lat", None, None),
            P(None, "lat", None, None),
            P("depth", "lat", None, None, None, None),
            P("depth", "lat", None),
            P("depth", "lat", None),
            P("lat", None, None),
            P("lat", None),
            P("lat", None),
        ),
        out_specs=(P(None, "depth", "lat", None, None), P("depth", "lat", None, None)),
        check_vma=False,
    )
```

```python
import functools

import jax
import jax.numpy as jnp
from jax import lax
from jax.experimental import pallas as pl
from jax.experimental.pallas import tpu as pltpu
from jax.sharding import PartitionSpec as P

WAVE = jnp.bfloat16
SMEM_SPEC = pl.BlockSpec(memory_space=pltpu.SMEM)
VMEM_SPEC = pl.BlockSpec(memory_space=pltpu.VMEM)
ANY_SPEC = pl.BlockSpec(memory_space=pl.ANY)
VMEM_LIMIT = 8 * 1024 * 1024
LOWER, UPPER = 0, 1


def in_vmem(array):
    return pltpu.with_memory_space_constraint(array, pltpu.VMEM)


def in_hbm(array):
    return pltpu.with_memory_space_constraint(array, pltpu.HBM)


def write_lists(tile, plan_ref, blocks_ref, lists):
    listed = lists[0].shape[0]
    parity = lax.rem(tile, 2)
    for list_ref, side in zip(lists, (UPPER - parity, parity)):
        count = plan_ref[2 * listed + side]
        for slot in range(listed):
            live = slot < count

            @pl.when(live)
            def _():
                list_ref[slot] = blocks_ref[plan_ref[side * listed + slot]]

            @pl.when(jnp.logical_not(live))
            def _():
                list_ref[slot] = jnp.zeros(list_ref.shape[1:], list_ref.dtype)


def prepare_kernel(
    ids_hbm, count_hbm, pattern_hbm, inflow_hbm, plan_ref, wave_ref, first_ref, second_ref,
    ids, count, pattern, landed, small_sems, sems,
):
    blocks = wave_ref.shape[0]
    small = [
        pltpu.make_async_copy(source, target, small_sems.at[i])
        for i, (source, target) in enumerate(
            ((ids_hbm, ids), (count_hbm, count), (pattern_hbm, pattern))
        )
    ]
    large = [
        pltpu.make_async_copy(inflow_hbm.at[0, b], landed.at[b], sems.at[b]) for b in range(blocks)
    ]
    for copy in small + large:
        copy.start()
    for copy in small:
        copy.wait()
    _, sides, listed = ids.shape
    taken = pattern.shape[1]
    for side in range(sides):
        for slot in range(listed):
            plan_ref[side * listed + slot] = ids[0, side, slot]
        plan_ref[sides * listed + side] = count[0, side]
    for b in range(blocks):
        for k in range(taken):
            plan_ref[sides * (listed + 1) + b * taken + k] = pattern[b, k]
    for b, copy in enumerate(large):
        copy.wait()
        wave_ref[b] = landed[b].astype(wave_ref.dtype)
    write_lists(lax.axis_index("lat"), plan_ref, wave_ref, (first_ref, second_ref))


def load_kernel(
    ops_hbm, source_hbm, pass_hbm, reflect_hbm, after_ref,
    ops_ref, source_ref, pass_ref, reflect_ref, pass_rows, reflect_rows, sems,
):
    del after_ref
    copies = [
        pltpu.make_async_copy(source, target, sems.at[i])
        for i, (source, target) in enumerate(
            (
                (pass_hbm, pass_rows),
                (reflect_hbm, reflect_rows),
                (ops_hbm, ops_ref),
                (source_hbm, source_ref),
            )
        )
    ]
    for copy in copies:
        copy.start()
    for copy, rows, columns_ref in zip(copies, (pass_rows, reflect_rows), (pass_ref, reflect_ref)):
        copy.wait()
        for b in range(columns_ref.shape[0]):
            row = rows[0, pl.ds(b, 1), :]
            columns_ref[b] = jnp.broadcast_to(row, columns_ref.shape[1:]).T
    for copy in copies[2:]:
        copy.wait()


def fill_buffer(section, tick, source_ref, wave_refs, first_ref, second_ref, buffer):
    blocks, listed = source_ref.shape[1], first_ref.shape[0]

    def fill_wave():
        start = 0
        for wave_ref in wave_refs:
            buffer[start : start + wave_ref.shape[0]] = wave_ref[...]
            start += wave_ref.shape[0]

    if tick == 0:
        fill_wave()
    else:
        pl.when(section != 0)(fill_wave)

        @pl.when(section == 0)
        def _():
            buffer[:blocks] = source_ref[tick - 1]

    parity = lax.rem(lax.axis_index("lat"), 2)
    buffer[pl.ds(blocks + (1 - parity) * listed, listed)] = first_ref[...]
    buffer[pl.ds(blocks + parity * listed, listed)] = second_ref[...]


def extrapolate_block(plan_ref, pattern_start, ops_ref, buffer, b):
    taken = ops_ref.shape[2]
    points = ops_ref.shape[5]
    left = jnp.concatenate(
        [ops_ref[0, b, k].reshape(2 * points, points) for k in range(taken)], axis=1
    )
    right = jnp.concatenate(
        [buffer[plan_ref[pattern_start + b * taken + k]] for k in range(taken)], axis=0
    )
    products = jnp.dot(left, right, preferred_element_type=jnp.float32)
    half = products.shape[1] // 2
    real_part = products[:points, :half] - products[points:, half:]
    imag_part = products[:points, half:] + products[points:, :half]
    return real_part, imag_part


def acts(section, parity):
    return True if parity is None else lax.rem(section, 2) == parity


def tick_kernel(
    parity, tick, sections, plan_ref, ops_ref, source_ref, pass_ref, reflect_ref,
    wave_refs, first_in_ref, second_in_ref, known_refs, out_refs, buffer, onward,
):
    del known_refs
    echo_ref, first_ref, second_ref, *onward_refs = out_refs
    section = lax.axis_index("depth")
    tile = lax.axis_index("lat")
    listed = first_ref.shape[0]

    @pl.when(acts(section, parity))
    def _():
        fill_buffer(section, tick, source_ref, wave_refs, first_in_ref, second_in_ref, buffer)
        for b in range(echo_ref.shape[0]):
            parts = extrapolate_block(plan_ref, 2 * (listed + 1), ops_ref, buffer, b)
            for i, part in enumerate(parts):
                cols = pl.ds(i * part.shape[1], part.shape[1])
                onward[b, :, cols] = (pass_ref[b] * part).astype(onward.dtype)
                echo_ref[b, :, cols] = (reflect_ref[b] * part).astype(echo_ref.dtype)
        start = 0
        for onward_ref in onward_refs:
            if start == onward.shape[0]:
                start = 0
            onward_ref[...] = onward[start : start + onward_ref.shape[0]]
            start += onward_ref.shape[0]

        @pl.when(section != sections - 1)
        def _():
            write_lists(tile, plan_ref, onward, (first_ref, second_ref))

        @pl.when(section == sections - 1)
        def _():
            write_lists(tile, plan_ref, source_ref.at[tick], (first_ref, second_ref))


def last_kernel(
    parity, tick, plan_ref, ops_ref, source_ref, pass_ref, reflect_ref,
    wave_refs, first_in_ref, second_in_ref, earlier, known_refs, out_refs,
    buffer, echo, leaving, early_sems, echo_sems, leave_sems,
):
    del known_refs
    reflected_ref, transmitted_ref = out_refs
    section = lax.axis_index("depth")
    listed = first_in_ref.shape[0]

    @pl.when(acts(section, parity))
    def _():
        copies = [
            pltpu.make_async_copy(earlier[t], reflected_ref.at[t, 0], early_sems.at[t])
            for t in range(tick)
        ]
        for copy in copies:
            copy.start()
        fill_buffer(section, tick, source_ref, wave_refs, first_in_ref, second_in_ref, buffer)
        for b in range(echo.shape[0]):
            parts = extrapolate_block(plan_ref, 2 * (listed + 1), ops_ref, buffer, b)
            for i, part in enumerate(parts):
                cols = pl.ds(i * part.shape[1], part.shape[1])
                leaving[b, :, cols] = pass_ref[b] * part
                echo[b, :, cols] = (reflect_ref[b] * part).astype(echo.dtype)
            for copy in (
                pltpu.make_async_copy(leaving.at[b], transmitted_ref.at[0, b], leave_sems.at[b]),
                pltpu.make_async_copy(echo.at[b], reflected_ref.at[tick, 0, b], echo_sems.at[b]),
            ):
                copy.start()
                copies.append(copy)
        for copy in copies:
            copy.wait()


def grouped_call(kernel, groups, outs, out_specs, known, **options):
    flat = [array for group in groups for array in (group if isinstance(group, list) else [group])]

    def body(*refs):
        refs = list(refs)
        take = lambda count: [refs.pop(0) for _ in range(count)]
        inputs = [take(len(g)) if isinstance(g, list) else refs.pop(0) for g in groups]
        kernel(*inputs, take(len(known)), take(len(outs)), *refs)

    return pl.pallas_call(
        body,
        out_shape=tuple(outs),
        in_specs=[SMEM_SPEC] + [VMEM_SPEC] * (len(flat) - 1) + list(out_specs[: len(known)]),
        out_specs=tuple(out_specs),
        input_output_aliases={len(flat) + i: i for i in range(len(known))},
        **options,
    )(flat[0], *map(in_vmem, flat[1:]), *known)


def neighbour(j, turn, tiles):
    to = j + (1 if (j + turn) % 2 == 0 else -1)
    return to if 0 <= to < tiles else None


def swap_routes(sections, tiles):
    routes = []
    for turn in (0, 1):
        route = []
        for s in range(sections):
            for j in range(tiles):
                to = neighbour(j, turn, tiles)
                end = ((s ^ 1) * tiles + j) if to is None else (s * tiles + to)
                route.append((s * tiles + j, end))
        routes.append(route)
    return routes


def halo_routes(sections, tiles):
    routes = []
    for turn in (0, 1):
        route = []
        for s in range(sections):
            for j in range(tiles):
                to = neighbour(j, turn, tiles)
                end = (s ^ 1) * tiles + j if to is None else (s + 1) % sections * tiles + to
                route.append((s * tiles + j, end))
        routes.append(route)
    return routes


def per_device(
    inflow, source, operators, transmission, reflectivity, send_ids, send_count, pattern
):
    sections, tiles = lax.axis_size("depth"), lax.axis_size("lat")
    ticks = source.shape[0] + 1
    _, blocks, points, columns = inflow.shape
    listed = send_ids.shape[-1]
    taken = operators.shape[2]
    wave_type = pltpu.VMEM((blocks, points, columns), WAVE)
    list_type = pltpu.VMEM((listed, points, columns), WAVE)
    params = pltpu.CompilerParams(vmem_limit_bytes=VMEM_LIMIT)
    tick_cost = pl.CostEstimate(
        flops=blocks * taken * 4 * points * points * columns,
        bytes_accessed=2 * operators.size + 8 * blocks * points * columns,
        transcendentals=0,
    )
    both = ("depth", "lat")
    deeper = [(s, (s + 1) % sections) for s in range(sections)]

    plan, wave, first, second = pl.pallas_call(
        prepare_kernel,
        out_shape=(
            pltpu.SMEM((2 * (listed + 1) + blocks * taken,), jnp.int32),
            wave_type,
            list_type,
            list_type,
        ),
        in_specs=[ANY_SPEC] * 4,
        out_specs=(SMEM_SPEC,) + (VMEM_SPEC,) * 3,
        scratch_shapes=[
            pltpu.SMEM(send_ids.shape, jnp.int32),
            pltpu.SMEM(send_count.shape, jnp.int32),
            pltpu.SMEM(pattern.shape, jnp.int32),
            pltpu.VMEM((blocks, points, columns), inflow.dtype),
            pltpu.SemaphoreType.DMA((3,)),
            pltpu.SemaphoreType.DMA((blocks,)),
        ],
        compiler_params=params,
        cost_estimate=pl.CostEstimate(
            flops=inflow.size, bytes_accessed=8 * inflow.size, transcendentals=0
        ),
        name="prepare",
    )(*map(in_hbm, (send_ids, send_count, pattern, inflow)))
    loaded_first = first
    routes = swap_routes(sections, tiles)
    first = lax.ppermute(first, both, routes[0])
    second = lax.ppermute(second, both, routes[1])

    column_type = pltpu.VMEM((blocks, points, columns // 2), jnp.float32)
    fixed = pl.pallas_call(
        load_kernel,
        out_shape=(
            pltpu.VMEM(operators.shape, operators.dtype),
            pltpu.VMEM(source.shape, source.dtype),
            column_type,
            column_type,
        ),
        in_specs=[ANY_SPEC] * 4 + [VMEM_SPEC],
        out_specs=(VMEM_SPEC,) * 4,
        scratch_shapes=[
            pltpu.VMEM(transmission.shape, transmission.dtype),
            pltpu.VMEM(reflectivity.shape, reflectivity.dtype),
            pltpu.SemaphoreType.DMA((4,)),
        ],
        compiler_params=params,
        cost_estimate=pl.CostEstimate(
            flops=0, bytes_accessed=4 * (operators.size + source.size), transcendentals=0
        ),
        name="load",
    )(*map(in_hbm, (operators, source, transmission, reflectivity)), in_vmem(loaded_first))
    fixed = [plan, *fixed]

    buffer_type = pltpu.VMEM((blocks + 2 * listed, points, columns), WAVE)

    ODD, EVEN = 1, 0
    halves = [blocks // 2, blocks - blocks // 2]
    half_types = [pltpu.VMEM((n, points, columns), WAVE) for n in halves]
    crossing = [(s, (s + 1) % sections) for s in range(sections)]
    inside = [(s, s ^ 1) for s in range(sections)]
    routes = halo_routes(sections, tiles)

    waves = {None: [wave]}
    echoes = []
    for tick in range(ticks - 1):
        known = []
        sent = {}
        for parity in (None,) if tick == 0 else (ODD, EVEN):
            to_next = ([wave_type] if parity != EVEN else []) + (half_types if parity != ODD else [])
            outs = [wave_type, list_type, list_type] + to_next
            known = grouped_call(
                functools.partial(tick_kernel, parity, tick, sections),
                [*fixed, waves[parity], first, second],
                outs,
                [VMEM_SPEC] * len(outs),
                known[:3] and [in_vmem(a) for a in known[:3]],
                scratch_shapes=[buffer_type, pltpu.VMEM(wave_type.shape, WAVE)],
                compiler_params=params,
                cost_estimate=tick_cost,
                name=f"tick{tick}" + ("" if parity is None else "_odd" if parity else "_even"),
            )
            if parity is None:
                sent[EVEN] = [lax.ppermute(a, "depth", crossing) for a in known[-2:]]
                sent[ODD] = [lax.ppermute(known[3], "depth", inside)]
            elif parity == ODD:
                sent[EVEN] = [lax.ppermute(known[3], "depth", crossing)]
            else:
                sent[ODD] = [lax.ppermute(a, "depth", inside) for a in known[-2:]]
        waves = sent
        echo, first, second = known[:3]
        first = lax.ppermute(first, both, routes[0])
        second = lax.ppermute(second, both, routes[1])
        echoes.append(echo)

    tick = ticks - 1
    results = []
    result_types = (
        jax.ShapeDtypeStruct((ticks, 1, blocks, points, columns), WAVE),
        jax.ShapeDtypeStruct((1, blocks, points, columns), jnp.float32),
    )
    for parity in (ODD, EVEN):
        results = grouped_call(
            functools.partial(last_kernel, parity, tick),
            [*fixed, waves[parity], first, second, echoes],
            result_types,
            [ANY_SPEC] * 2,
            list(results),
            scratch_shapes=[
                buffer_type,
                pltpu.VMEM((blocks, points, columns), WAVE),
                pltpu.VMEM((blocks, points, columns), jnp.float32),
                pltpu.SemaphoreType.DMA((tick,)),
                pltpu.SemaphoreType.DMA((blocks,)),
                pltpu.SemaphoreType.DMA((blocks,)),
            ],
            compiler_params=params,
            cost_estimate=tick_cost,
            name="last_tick" + ("_odd" if parity else "_even"),
        )
    return tuple(results)


def solution(mesh):
    return jax.shard_map(
        per_device,
        mesh=mesh,
        in_specs=(
            P("depth", "lat", None, None),
            P(None, "lat", None, None),
            P("depth", "lat", None, None, None, None),
            P("depth", "lat", None),
            P("depth", "lat", None),
            P("lat", None, None),
            P("lat", None),
            P("lat", None),
        ),
        out_specs=(P(None, "depth", "lat", None, None), P("depth", "lat", None, None)),
        check_vma=False,
    )
```

```python
import functools

import jax
import jax.numpy as jnp
from jax import lax
from jax.experimental import pallas as pl
from jax.experimental.pallas import tpu as pltpu
from jax.sharding import PartitionSpec as P

WAVE = jnp.bfloat16
SMEM_SPEC = pl.BlockSpec(memory_space=pltpu.SMEM)
VMEM_SPEC = pl.BlockSpec(memory_space=pltpu.VMEM)
ANY_SPEC = pl.BlockSpec(memory_space=pl.ANY)
VMEM_LIMIT = 8 * 1024 * 1024
LOWER, UPPER = 0, 1


def in_vmem(array):
    return pltpu.with_memory_space_constraint(array, pltpu.VMEM)


def in_hbm(array):
    return pltpu.with_memory_space_constraint(array, pltpu.HBM)


def write_lists(tile, plan_ref, blocks_ref, lists):
    listed = lists[0].shape[0]
    parity = lax.rem(tile, 2)
    for list_ref, side in zip(lists, (UPPER - parity, parity)):
        count = plan_ref[2 * listed + side]
        for slot in range(listed):
            live = slot < count

            @pl.when(live)
            def _():
                list_ref[slot] = blocks_ref[plan_ref[side * listed + slot]]

            @pl.when(jnp.logical_not(live))
            def _():
                list_ref[slot] = jnp.zeros(list_ref.shape[1:], list_ref.dtype)


def start_load(hbm_refs, refs, rows, sems):
    ops_hbm, source_hbm, pass_hbm, reflect_hbm = hbm_refs
    pairs = ((pass_hbm, rows[0]), (reflect_hbm, rows[1]), (ops_hbm, refs[0]), (source_hbm, refs[1]))
    copies = [
        pltpu.make_async_copy(source, target, sems.at[i]) for i, (source, target) in enumerate(pairs)
    ]
    for copy in copies:
        copy.start()
    return copies


def finish_load(copies, refs, rows):
    for copy, coefficient, columns_ref in zip(copies, rows, refs[2:]):
        copy.wait()
        for b in range(columns_ref.shape[0]):
            row = coefficient[0, pl.ds(b, 1), :]
            columns_ref[b] = jnp.broadcast_to(row, columns_ref.shape[1:]).T
    for copy in copies[2:]:
        copy.wait()


def prepare_kernel(
    ids_hbm, count_hbm, pattern_hbm, inflow_hbm, ops_hbm, source_hbm, pass_hbm, reflect_hbm,
    plan_ref, wave_ref, first_ref, second_ref, ops_ref, source_ref, pass_ref, reflect_ref,
    ids, count, pattern, landed, small_sems, sems, pass_rows, reflect_rows, load_sems,
):
    blocks = wave_ref.shape[0]
    small = [
        pltpu.make_async_copy(source, target, small_sems.at[i])
        for i, (source, target) in enumerate(
            ((ids_hbm, ids), (count_hbm, count), (pattern_hbm, pattern))
        )
    ]
    large = [
        pltpu.make_async_copy(inflow_hbm.at[0, b], landed.at[b], sems.at[b]) for b in range(blocks)
    ]
    for copy in small + large:
        copy.start()
    for copy in small:
        copy.wait()
    _, sides, listed = ids.shape
    taken = pattern.shape[1]
    for side in range(sides):
        for slot in range(listed):
            plan_ref[side * listed + slot] = ids[0, side, slot]
        plan_ref[sides * listed + side] = count[0, side]
    for b in range(blocks):
        for k in range(taken):
            plan_ref[sides * (listed + 1) + b * taken + k] = pattern[b, k]
    for b, copy in enumerate(large):
        copy.wait()
        wave_ref[b] = landed[b].astype(wave_ref.dtype)
    write_lists(lax.axis_index("lat"), plan_ref, wave_ref, (first_ref, second_ref))

    @pl.when(lax.rem(lax.axis_index("depth"), 2) == 1)
    def _():
        refs = (ops_ref, source_ref, pass_ref, reflect_ref)
        rows = (pass_rows, reflect_rows)
        copies = start_load((ops_hbm, source_hbm, pass_hbm, reflect_hbm), refs, rows, load_sems)
        finish_load(copies, refs, rows)


def load_kernel(ops_hbm, source_hbm, pass_hbm, reflect_hbm, *rest):
    refs, (pass_rows, reflect_rows, sems) = rest[4:8], rest[8:]

    @pl.when(lax.rem(lax.axis_index("depth"), 2) == 0)
    def _():
        rows = (pass_rows, reflect_rows)
        copies = start_load((ops_hbm, source_hbm, pass_hbm, reflect_hbm), refs, rows, sems)
        finish_load(copies, refs, rows)


def fill_buffer(section, tick, source_ref, wave_refs, first_ref, second_ref, buffer):
    blocks, listed = source_ref.shape[1], first_ref.shape[0]

    def fill_wave():
        start = 0
        for wave_ref in wave_refs:
            buffer[start : start + wave_ref.shape[0]] = wave_ref[...]
            start += wave_ref.shape[0]

    if tick == 0:
        fill_wave()
    else:
        pl.when(section != 0)(fill_wave)

        @pl.when(section == 0)
        def _():
            buffer[:blocks] = source_ref[tick - 1]

    parity = lax.rem(lax.axis_index("lat"), 2)
    buffer[pl.ds(blocks + (1 - parity) * listed, listed)] = first_ref[...]
    buffer[pl.ds(blocks + parity * listed, listed)] = second_ref[...]


def extrapolate_block(plan_ref, pattern_start, ops_ref, buffer, b):
    taken = ops_ref.shape[2]
    points = ops_ref.shape[5]
    left = jnp.concatenate(
        [ops_ref[0, b, k].reshape(2 * points, points) for k in range(taken)], axis=1
    )
    right = jnp.concatenate(
        [buffer[plan_ref[pattern_start + b * taken + k]] for k in range(taken)], axis=0
    )
    products = jnp.dot(left, right, preferred_element_type=jnp.float32)
    half = products.shape[1] // 2
    real_part = products[:points, :half] - products[points:, half:]
    imag_part = products[:points, half:] + products[points:, :half]
    return real_part, imag_part


def acts(section, parity):
    return True if parity is None else lax.rem(section, 2) == parity


def tick_kernel(
    parity, tick, sections, plan_ref, ops_ref, source_ref, pass_ref, reflect_ref,
    wave_refs, first_in_ref, second_in_ref, known_refs, out_refs, buffer, onward,
):
    del known_refs
    echo_ref, first_ref, second_ref, *onward_refs = out_refs
    section = lax.axis_index("depth")
    tile = lax.axis_index("lat")
    listed = first_ref.shape[0]

    @pl.when(acts(section, parity))
    def _():
        fill_buffer(section, tick, source_ref, wave_refs, first_in_ref, second_in_ref, buffer)
        for b in range(echo_ref.shape[0]):
            parts = extrapolate_block(plan_ref, 2 * (listed + 1), ops_ref, buffer, b)
            for i, part in enumerate(parts):
                cols = pl.ds(i * part.shape[1], part.shape[1])
                onward[b, :, cols] = (pass_ref[b] * part).astype(onward.dtype)
                echo_ref[b, :, cols] = (reflect_ref[b] * part).astype(echo_ref.dtype)
        start = 0
        for onward_ref in onward_refs:
            if start == onward.shape[0]:
                start = 0
            onward_ref[...] = onward[start : start + onward_ref.shape[0]]
            start += onward_ref.shape[0]

        @pl.when(section != sections - 1)
        def _():
            write_lists(tile, plan_ref, onward, (first_ref, second_ref))

        @pl.when(section == sections - 1)
        def _():
            write_lists(tile, plan_ref, source_ref.at[tick], (first_ref, second_ref))


def last_kernel(
    parity, tick, plan_ref, ops_ref, source_ref, pass_ref, reflect_ref,
    wave_refs, first_in_ref, second_in_ref, earlier, known_refs, out_refs,
    buffer, echo, leaving, early_sems, echo_sems, leave_sems,
):
    del known_refs
    reflected_ref, transmitted_ref = out_refs
    section = lax.axis_index("depth")
    listed = first_in_ref.shape[0]

    @pl.when(acts(section, parity))
    def _():
        copies = [
            pltpu.make_async_copy(earlier[t], reflected_ref.at[t, 0], early_sems.at[t])
            for t in range(tick)
        ]
        for copy in copies:
            copy.start()
        fill_buffer(section, tick, source_ref, wave_refs, first_in_ref, second_in_ref, buffer)
        for b in range(echo.shape[0]):
            parts = extrapolate_block(plan_ref, 2 * (listed + 1), ops_ref, buffer, b)
            for i, part in enumerate(parts):
                cols = pl.ds(i * part.shape[1], part.shape[1])
                leaving[b, :, cols] = pass_ref[b] * part
                echo[b, :, cols] = (reflect_ref[b] * part).astype(echo.dtype)
            for copy in (
                pltpu.make_async_copy(leaving.at[b], transmitted_ref.at[0, b], leave_sems.at[b]),
                pltpu.make_async_copy(echo.at[b], reflected_ref.at[tick, 0, b], echo_sems.at[b]),
            ):
                copy.start()
                copies.append(copy)
        for copy in copies:
            copy.wait()


def grouped_call(kernel, groups, outs, out_specs, known, **options):
    flat = [array for group in groups for array in (group if isinstance(group, list) else [group])]

    def body(*refs):
        refs = list(refs)
        take = lambda count: [refs.pop(0) for _ in range(count)]
        inputs = [take(len(g)) if isinstance(g, list) else refs.pop(0) for g in groups]
        kernel(*inputs, take(len(known)), take(len(outs)), *refs)

    return pl.pallas_call(
        body,
        out_shape=tuple(outs),
        in_specs=[SMEM_SPEC] + [VMEM_SPEC] * (len(flat) - 1) + list(out_specs[: len(known)]),
        out_specs=tuple(out_specs),
        input_output_aliases={len(flat) + i: i for i in range(len(known))},
        **options,
    )(flat[0], *map(in_vmem, flat[1:]), *known)


def neighbour(j, turn, tiles):
    to = j + (1 if (j + turn) % 2 == 0 else -1)
    return to if 0 <= to < tiles else None


def swap_routes(sections, tiles):
    routes = []
    for turn in (0, 1):
        route = []
        for s in range(sections):
            for j in range(tiles):
                to = neighbour(j, turn, tiles)
                end = ((s ^ 1) * tiles + j) if to is None else (s * tiles + to)
                route.append((s * tiles + j, end))
        routes.append(route)
    return routes


def halo_routes(sections, tiles):
    routes = []
    for turn in (0, 1):
        route = []
        for s in range(sections):
            for j in range(tiles):
                to = neighbour(j, turn, tiles)
                end = (s ^ 1) * tiles + j if to is None else (s + 1) % sections * tiles + to
                route.append((s * tiles + j, end))
        routes.append(route)
    return routes


def per_device(
    inflow, source, operators, transmission, reflectivity, send_ids, send_count, pattern
):
    sections, tiles = lax.axis_size("depth"), lax.axis_size("lat")
    ticks = source.shape[0] + 1
    _, blocks, points, columns = inflow.shape
    listed = send_ids.shape[-1]
    taken = operators.shape[2]
    wave_type = pltpu.VMEM((blocks, points, columns), WAVE)
    list_type = pltpu.VMEM((listed, points, columns), WAVE)
    params = pltpu.CompilerParams(vmem_limit_bytes=VMEM_LIMIT)
    tick_cost = pl.CostEstimate(
        flops=blocks * taken * 4 * points * points * columns,
        bytes_accessed=2 * operators.size + 8 * blocks * points * columns,
        transcendentals=0,
    )
    both = ("depth", "lat")
    deeper = [(s, (s + 1) % sections) for s in range(sections)]

    column_type = pltpu.VMEM((blocks, points, columns // 2), jnp.float32)
    fixed_types = (
        pltpu.VMEM(operators.shape, operators.dtype),
        pltpu.VMEM(source.shape, source.dtype),
        column_type,
        column_type,
    )
    load_scratch = [
        pltpu.VMEM(transmission.shape, transmission.dtype),
        pltpu.VMEM(reflectivity.shape, reflectivity.dtype),
        pltpu.SemaphoreType.DMA((4,)),
    ]
    load_cost = pl.CostEstimate(
        flops=0, bytes_accessed=4 * (operators.size + source.size), transcendentals=0
    )
    stored = [in_hbm(a) for a in (operators, source, transmission, reflectivity)]
    plan, wave, first, second, *fixed = pl.pallas_call(
        prepare_kernel,
        out_shape=(
            pltpu.SMEM((2 * (listed + 1) + blocks * taken,), jnp.int32),
            wave_type,
            list_type,
            list_type,
            *fixed_types,
        ),
        in_specs=[ANY_SPEC] * 8,
        out_specs=(SMEM_SPEC,) + (VMEM_SPEC,) * 7,
        scratch_shapes=[
            pltpu.SMEM(send_ids.shape, jnp.int32),
            pltpu.SMEM(send_count.shape, jnp.int32),
            pltpu.SMEM(pattern.shape, jnp.int32),
            pltpu.VMEM((blocks, points, columns), inflow.dtype),
            pltpu.SemaphoreType.DMA((3,)),
            pltpu.SemaphoreType.DMA((blocks,)),
            *load_scratch,
        ],
        compiler_params=params,
        cost_estimate=pl.CostEstimate(
            flops=inflow.size, bytes_accessed=8 * inflow.size, transcendentals=0
        ),
        name="prepare",
    )(*map(in_hbm, (send_ids, send_count, pattern, inflow)), *stored)
    routes = swap_routes(sections, tiles)
    first = lax.ppermute(first, both, routes[0])
    second = lax.ppermute(second, both, routes[1])

    fixed = pl.pallas_call(
        load_kernel,
        out_shape=fixed_types,
        in_specs=[ANY_SPEC] * 4 + [VMEM_SPEC] * 4,
        out_specs=(VMEM_SPEC,) * 4,
        input_output_aliases={4: 0, 5: 1, 6: 2, 7: 3},
        scratch_shapes=load_scratch,
        compiler_params=params,
        cost_estimate=load_cost,
        name="load",
    )(*stored, *map(in_vmem, fixed))
    fixed = [plan, *fixed]

    buffer_type = pltpu.VMEM((blocks + 2 * listed, points, columns), WAVE)

    ODD, EVEN = 1, 0
    halves = [blocks // 2, blocks - blocks // 2]
    half_types = [pltpu.VMEM((n, points, columns), WAVE) for n in halves]
    crossing = [(s, (s + 1) % sections) for s in range(sections)]
    inside = [(s, s ^ 1) for s in range(sections)]
    routes = halo_routes(sections, tiles)

    waves = {None: [wave]}
    echoes = []
    for tick in range(ticks - 1):
        known = []
        sent = {}
        for parity in (None,) if tick == 0 else (ODD, EVEN):
            to_next = ([wave_type] if parity != EVEN else []) + (half_types if parity != ODD else [])
            outs = [wave_type, list_type, list_type] + to_next
            known = grouped_call(
                functools.partial(tick_kernel, parity, tick, sections),
                [*fixed, waves[parity], first, second],
                outs,
                [VMEM_SPEC] * len(outs),
                known[:3] and [in_vmem(a) for a in known[:3]],
                scratch_shapes=[buffer_type, pltpu.VMEM(wave_type.shape, WAVE)],
                compiler_params=params,
                cost_estimate=tick_cost,
                name=f"tick{tick}" + ("" if parity is None else "_odd" if parity else "_even"),
            )
            if parity != EVEN:
                sent[EVEN] = [lax.ppermute(known[3], "depth", crossing)]
            if parity != ODD:
                echo, first, second = known[:3]
                first = lax.ppermute(first, both, routes[0])
                second = lax.ppermute(second, both, routes[1])
                sent[ODD] = [lax.ppermute(a, "depth", inside) for a in known[-2:]]
        waves = sent
        echoes.append(echo)

    tick = ticks - 1
    results = []
    result_types = (
        jax.ShapeDtypeStruct((ticks, 1, blocks, points, columns), WAVE),
        jax.ShapeDtypeStruct((1, blocks, points, columns), jnp.float32),
    )
    for parity in (ODD, EVEN):
        results = grouped_call(
            functools.partial(last_kernel, parity, tick),
            [*fixed, waves[parity], first, second, echoes],
            result_types,
            [ANY_SPEC] * 2,
            list(results),
            scratch_shapes=[
                buffer_type,
                pltpu.VMEM((blocks, points, columns), WAVE),
                pltpu.VMEM((blocks, points, columns), jnp.float32),
                pltpu.SemaphoreType.DMA((tick,)),
                pltpu.SemaphoreType.DMA((blocks,)),
                pltpu.SemaphoreType.DMA((blocks,)),
            ],
            compiler_params=params,
            cost_estimate=tick_cost,
            name="last_tick" + ("_odd" if parity else "_even"),
        )
    return tuple(results)


def solution(mesh):
    return jax.shard_map(
        per_device,
        mesh=mesh,
        in_specs=(
            P("depth", "lat", None, None),
            P(None, "lat", None, None),
            P("depth", "lat", None, None, None, None),
            P("depth", "lat", None),
            P("depth", "lat", None),
            P("lat", None, None),
            P("lat", None),
            P("lat", None),
        ),
        out_specs=(P(None, "depth", "lat", None, None), P("depth", "lat", None, None)),
        check_vma=False,
    )
```

```python
import functools

import jax
import jax.numpy as jnp
from jax import lax
from jax.experimental import pallas as pl
from jax.experimental.pallas import tpu as pltpu
from jax.sharding import PartitionSpec as P

WAVE = jnp.bfloat16
SMEM_SPEC = pl.BlockSpec(memory_space=pltpu.SMEM)
VMEM_SPEC = pl.BlockSpec(memory_space=pltpu.VMEM)
ANY_SPEC = pl.BlockSpec(memory_space=pl.ANY)
VMEM_LIMIT = 8 * 1024 * 1024
LOWER, UPPER = 0, 1


def in_vmem(array):
    return pltpu.with_memory_space_constraint(array, pltpu.VMEM)


def in_hbm(array):
    return pltpu.with_memory_space_constraint(array, pltpu.HBM)


def write_lists(section, plan_ref, blocks_ref, lists):
    listed = lists[0].shape[0]
    parity = lax.rem(section + lax.axis_index("lat"), 2)
    for list_ref, side in zip(lists, (UPPER - parity, parity)):
        count = plan_ref[2 * listed + side]
        for slot in range(listed):
            live = slot < count

            @pl.when(live)
            def _():
                list_ref[slot] = blocks_ref[plan_ref[side * listed + slot]]

            @pl.when(jnp.logical_not(live))
            def _():
                list_ref[slot] = jnp.zeros(list_ref.shape[1:], list_ref.dtype)


def prepare_kernel(
    ids_hbm, count_hbm, pattern_hbm, inflow_hbm, plan_ref, wave_ref, first_ref, second_ref,
    ids, count, pattern, landed, small_sems, sems,
):
    blocks = wave_ref.shape[0]
    small = [
        pltpu.make_async_copy(source, target, small_sems.at[i])
        for i, (source, target) in enumerate(
            ((ids_hbm, ids), (count_hbm, count), (pattern_hbm, pattern))
        )
    ]
    large = [
        pltpu.make_async_copy(inflow_hbm.at[0, b], landed.at[b], sems.at[b]) for b in range(blocks)
    ]
    for copy in small + large:
        copy.start()
    for copy in small:
        copy.wait()
    _, sides, listed = ids.shape
    taken = pattern.shape[1]
    for side in range(sides):
        for slot in range(listed):
            plan_ref[side * listed + slot] = ids[0, side, slot]
        plan_ref[sides * listed + side] = count[0, side]
    for b in range(blocks):
        for k in range(taken):
            plan_ref[sides * (listed + 1) + b * taken + k] = pattern[b, k]
    for b, copy in enumerate(large):
        copy.wait()
        wave_ref[b] = landed[b].astype(wave_ref.dtype)
    write_lists(lax.axis_index("depth"), plan_ref, wave_ref, (first_ref, second_ref))


def load_kernel(
    ops_hbm, source_hbm, pass_hbm, reflect_hbm, after_ref,
    ops_ref, source_ref, pass_ref, reflect_ref, pass_rows, reflect_rows, sems,
):
    del after_ref
    copies = [
        pltpu.make_async_copy(source, target, sems.at[i])
        for i, (source, target) in enumerate(
            (
                (pass_hbm, pass_rows),
                (reflect_hbm, reflect_rows),
                (ops_hbm, ops_ref),
                (source_hbm, source_ref),
            )
        )
    ]
    for copy in copies:
        copy.start()
    for copy, rows, columns_ref in zip(copies, (pass_rows, reflect_rows), (pass_ref, reflect_ref)):
        copy.wait()
        for b in range(columns_ref.shape[0]):
            row = rows[0, pl.ds(b, 1), :]
            columns_ref[b] = jnp.broadcast_to(row, columns_ref.shape[1:]).T
    for copy in copies[2:]:
        copy.wait()


def fill_buffer(section, tick, source_ref, wave_refs, first_ref, second_ref, buffer):
    blocks, listed = source_ref.shape[1], first_ref.shape[0]

    def fill_wave():
        start = 0
        for wave_ref in wave_refs:
            buffer[start : start + wave_ref.shape[0]] = wave_ref[...]
            start += wave_ref.shape[0]

    if tick == 0:
        fill_wave()
    else:
        pl.when(section != 0)(fill_wave)

        @pl.when(section == 0)
        def _():
            buffer[:blocks] = source_ref[tick - 1]

    sender = section if tick == 0 else section + 1
    parity = lax.rem(sender + lax.axis_index("lat"), 2)
    buffer[pl.ds(blocks + (1 - parity) * listed, listed)] = first_ref[...]
    buffer[pl.ds(blocks + parity * listed, listed)] = second_ref[...]


def extrapolate_block(plan_ref, pattern_start, ops_ref, buffer, b):
    taken = ops_ref.shape[2]
    points = ops_ref.shape[5]
    left = jnp.concatenate(
        [ops_ref[0, b, k].reshape(2 * points, points) for k in range(taken)], axis=1
    )
    right = jnp.concatenate(
        [buffer[plan_ref[pattern_start + b * taken + k]] for k in range(taken)], axis=0
    )
    products = jnp.dot(left, right, preferred_element_type=jnp.float32)
    half = products.shape[1] // 2
    real_part = products[:points, :half] - products[points:, half:]
    imag_part = products[:points, half:] + products[points:, :half]
    return real_part, imag_part


def acts(section, parity):
    return True if parity is None else lax.rem(section, 2) == parity


def tick_kernel(
    parity, tick, sections, plan_ref, ops_ref, source_ref, pass_ref, reflect_ref,
    wave_refs, first_in_ref, second_in_ref, known_refs, out_refs, buffer, onward,
):
    del known_refs
    echo_ref, first_ref, second_ref, *onward_refs = out_refs
    section = lax.axis_index("depth")
    listed = first_ref.shape[0]

    @pl.when(acts(section, parity))
    def _():
        fill_buffer(section, tick, source_ref, wave_refs, first_in_ref, second_in_ref, buffer)
        for b in range(echo_ref.shape[0]):
            parts = extrapolate_block(plan_ref, 2 * (listed + 1), ops_ref, buffer, b)
            for i, part in enumerate(parts):
                cols = pl.ds(i * part.shape[1], part.shape[1])
                onward[b, :, cols] = (pass_ref[b] * part).astype(onward.dtype)
                echo_ref[b, :, cols] = (reflect_ref[b] * part).astype(echo_ref.dtype)
        start = 0
        for onward_ref in onward_refs:
            if start == onward.shape[0]:
                start = 0
            onward_ref[...] = onward[start : start + onward_ref.shape[0]]
            start += onward_ref.shape[0]

        @pl.when(section != sections - 1)
        def _():
            write_lists(section, plan_ref, onward, (first_ref, second_ref))

        @pl.when(section == sections - 1)
        def _():
            write_lists(section, plan_ref, source_ref.at[tick], (first_ref, second_ref))


def last_kernel(
    parity, tick, plan_ref, ops_ref, source_ref, pass_ref, reflect_ref,
    wave_refs, first_in_ref, second_in_ref, earlier, known_refs, out_refs,
    buffer, echo, leaving, early_sems, echo_sems, leave_sems,
):
    del known_refs
    reflected_ref, transmitted_ref = out_refs
    section = lax.axis_index("depth")
    listed = first_in_ref.shape[0]

    @pl.when(acts(section, parity))
    def _():
        copies = [
            pltpu.make_async_copy(earlier[t], reflected_ref.at[t, 0], early_sems.at[t])
            for t in range(tick)
        ]
        for copy in copies:
            copy.start()
        fill_buffer(section, tick, source_ref, wave_refs, first_in_ref, second_in_ref, buffer)
        for b in range(echo.shape[0]):
            parts = extrapolate_block(plan_ref, 2 * (listed + 1), ops_ref, buffer, b)
            for i, part in enumerate(parts):
                cols = pl.ds(i * part.shape[1], part.shape[1])
                leaving[b, :, cols] = pass_ref[b] * part
                echo[b, :, cols] = (reflect_ref[b] * part).astype(echo.dtype)
            for copy in (
                pltpu.make_async_copy(leaving.at[b], transmitted_ref.at[0, b], leave_sems.at[b]),
                pltpu.make_async_copy(echo.at[b], reflected_ref.at[tick, 0, b], echo_sems.at[b]),
            ):
                copy.start()
                copies.append(copy)
        for copy in copies:
            copy.wait()


def grouped_call(kernel, groups, outs, out_specs, known, **options):
    flat = [array for group in groups for array in (group if isinstance(group, list) else [group])]

    def body(*refs):
        refs = list(refs)
        take = lambda count: [refs.pop(0) for _ in range(count)]
        inputs = [take(len(g)) if isinstance(g, list) else refs.pop(0) for g in groups]
        kernel(*inputs, take(len(known)), take(len(outs)), *refs)

    return pl.pallas_call(
        body,
        out_shape=tuple(outs),
        in_specs=[SMEM_SPEC] + [VMEM_SPEC] * (len(flat) - 1) + list(out_specs[: len(known)]),
        out_specs=tuple(out_specs),
        input_output_aliases={len(flat) + i: i for i in range(len(known))},
        **options,
    )(flat[0], *map(in_vmem, flat[1:]), *known)


def neighbour(s, j, turn, tiles):
    to = j + (1 if (s + j + turn) % 2 == 0 else -1)
    return to if 0 <= to < tiles else None


def swap_routes(sections, tiles):
    routes = []
    for turn in (0, 1):
        route = []
        for s in range(sections):
            for j in range(tiles):
                to = neighbour(s, j, turn, tiles)
                end = (s + 2) % sections * tiles + j if to is None else s * tiles + to
                route.append((s * tiles + j, end))
        routes.append(route)
    return routes


def halo_routes(sections, tiles):
    routes = []
    for turn in (0, 1):
        route = []
        for s in range(sections):
            for j in range(tiles):
                to = neighbour(s, j, turn, tiles)
                end = (s ^ 1) * tiles + j if to is None else (s + 1) % sections * tiles + to
                route.append((s * tiles + j, end))
        routes.append(route)
    return routes


def per_device(
    inflow, source, operators, transmission, reflectivity, send_ids, send_count, pattern
):
    sections, tiles = lax.axis_size("depth"), lax.axis_size("lat")
    ticks = source.shape[0] + 1
    _, blocks, points, columns = inflow.shape
    listed = send_ids.shape[-1]
    taken = operators.shape[2]
    wave_type = pltpu.VMEM((blocks, points, columns), WAVE)
    list_type = pltpu.VMEM((listed, points, columns), WAVE)
    params = pltpu.CompilerParams(vmem_limit_bytes=VMEM_LIMIT)
    tick_cost = pl.CostEstimate(
        flops=blocks * taken * 4 * points * points * columns,
        bytes_accessed=2 * operators.size + 8 * blocks * points * columns,
        transcendentals=0,
    )
    both = ("depth", "lat")
    deeper = [(s, (s + 1) % sections) for s in range(sections)]

    plan, wave, first, second = pl.pallas_call(
        prepare_kernel,
        out_shape=(
            pltpu.SMEM((2 * (listed + 1) + blocks * taken,), jnp.int32),
            wave_type,
            list_type,
            list_type,
        ),
        in_specs=[ANY_SPEC] * 4,
        out_specs=(SMEM_SPEC,) + (VMEM_SPEC,) * 3,
        scratch_shapes=[
            pltpu.SMEM(send_ids.shape, jnp.int32),
            pltpu.SMEM(send_count.shape, jnp.int32),
            pltpu.SMEM(pattern.shape, jnp.int32),
            pltpu.VMEM((blocks, points, columns), inflow.dtype),
            pltpu.SemaphoreType.DMA((3,)),
            pltpu.SemaphoreType.DMA((blocks,)),
        ],
        compiler_params=params,
        cost_estimate=pl.CostEstimate(
            flops=inflow.size, bytes_accessed=8 * inflow.size, transcendentals=0
        ),
        name="prepare",
    )(*map(in_hbm, (send_ids, send_count, pattern, inflow)))
    loaded_first = first
    routes = swap_routes(sections, tiles)
    first = lax.ppermute(first, both, routes[0])
    second = lax.ppermute(second, both, routes[1])

    column_type = pltpu.VMEM((blocks, points, columns // 2), jnp.float32)
    fixed = pl.pallas_call(
        load_kernel,
        out_shape=(
            pltpu.VMEM(operators.shape, operators.dtype),
            pltpu.VMEM(source.shape, source.dtype),
            column_type,
            column_type,
        ),
        in_specs=[ANY_SPEC] * 4 + [VMEM_SPEC],
        out_specs=(VMEM_SPEC,) * 4,
        scratch_shapes=[
            pltpu.VMEM(transmission.shape, transmission.dtype),
            pltpu.VMEM(reflectivity.shape, reflectivity.dtype),
            pltpu.SemaphoreType.DMA((4,)),
        ],
        compiler_params=params,
        cost_estimate=pl.CostEstimate(
            flops=0, bytes_accessed=4 * (operators.size + source.size), transcendentals=0
        ),
        name="load",
    )(*map(in_hbm, (operators, source, transmission, reflectivity)), in_vmem(loaded_first))
    fixed = [plan, *fixed]

    buffer_type = pltpu.VMEM((blocks + 2 * listed, points, columns), WAVE)

    ODD, EVEN = 1, 0
    halves = [blocks // 2, blocks - blocks // 2]
    half_types = [pltpu.VMEM((n, points, columns), WAVE) for n in halves]
    crossing = [(s, (s + 1) % sections) for s in range(sections)]
    inside = [(s, s ^ 1) for s in range(sections)]
    routes = halo_routes(sections, tiles)

    waves = {None: [wave]}
    echoes = []
    for tick in range(ticks - 1):
        known = []
        sent = {}
        for parity in (None,) if tick == 0 else (ODD, EVEN):
            to_next = ([wave_type] if parity != EVEN else []) + (half_types if parity != ODD else [])
            outs = [wave_type, list_type, list_type] + to_next
            known = grouped_call(
                functools.partial(tick_kernel, parity, tick, sections),
                [*fixed, waves[parity], first, second],
                outs,
                [VMEM_SPEC] * len(outs),
                known[:3] and [in_vmem(a) for a in known[:3]],
                scratch_shapes=[buffer_type, pltpu.VMEM(wave_type.shape, WAVE)],
                compiler_params=params,
                cost_estimate=tick_cost,
                name=f"tick{tick}" + ("" if parity is None else "_odd" if parity else "_even"),
            )
            if parity != EVEN:
                sent[EVEN] = [lax.ppermute(known[3], "depth", crossing)]
            if parity != ODD:
                sent[ODD] = [lax.ppermute(a, "depth", inside) for a in known[-2:]]
        waves = sent
        echo, first, second = known[:3]
        first = lax.ppermute(first, both, routes[0])
        second = lax.ppermute(second, both, routes[1])
        echoes.append(echo)

    tick = ticks - 1
    results = []
    result_types = (
        jax.ShapeDtypeStruct((ticks, 1, blocks, points, columns), WAVE),
        jax.ShapeDtypeStruct((1, blocks, points, columns), jnp.float32),
    )
    for parity in (ODD, EVEN):
        results = grouped_call(
            functools.partial(last_kernel, parity, tick),
            [*fixed, waves[parity], first, second, echoes],
            result_types,
            [ANY_SPEC] * 2,
            list(results),
            scratch_shapes=[
                buffer_type,
                pltpu.VMEM((blocks, points, columns), WAVE),
                pltpu.VMEM((blocks, points, columns), jnp.float32),
                pltpu.SemaphoreType.DMA((tick,)),
                pltpu.SemaphoreType.DMA((blocks,)),
                pltpu.SemaphoreType.DMA((blocks,)),
            ],
            compiler_params=params,
            cost_estimate=tick_cost,
            name="last_tick" + ("_odd" if parity else "_even"),
        )
    return tuple(results)


def solution(mesh):
    return jax.shard_map(
        per_device,
        mesh=mesh,
        in_specs=(
            P("depth", "lat", None, None),
            P(None, "lat", None, None),
            P("depth", "lat", None, None, None, None),
            P("depth", "lat", None),
            P("depth", "lat", None),
            P("lat", None, None),
            P("lat", None),
            P("lat", None),
        ),
        out_specs=(P(None, "depth", "lat", None, None), P("depth", "lat", None, None)),
        check_vma=False,
    )
```

```python
import functools

import jax
import jax.numpy as jnp
from jax import lax
from jax.experimental import pallas as pl
from jax.experimental.pallas import tpu as pltpu
from jax.sharding import PartitionSpec as P

WAVE = jnp.bfloat16
SMEM_SPEC = pl.BlockSpec(memory_space=pltpu.SMEM)
VMEM_SPEC = pl.BlockSpec(memory_space=pltpu.VMEM)
ANY_SPEC = pl.BlockSpec(memory_space=pl.ANY)
VMEM_LIMIT = 8 * 1024 * 1024
LOWER, UPPER = 0, 1


def in_vmem(array):
    return pltpu.with_memory_space_constraint(array, pltpu.VMEM)


def in_hbm(array):
    return pltpu.with_memory_space_constraint(array, pltpu.HBM)


def write_lists(tile, plan_ref, blocks_ref, lists):
    listed = lists[0].shape[0]
    parity = lax.rem(tile, 2)
    for list_ref, side in zip(lists, (UPPER - parity, parity)):
        count = plan_ref[2 * listed + side]
        for slot in range(listed):
            live = slot < count

            @pl.when(live)
            def _():
                list_ref[slot] = blocks_ref[plan_ref[side * listed + slot]]

            @pl.when(jnp.logical_not(live))
            def _():
                list_ref[slot] = jnp.zeros(list_ref.shape[1:], list_ref.dtype)


def prepare_kernel(
    ids_hbm, count_hbm, pattern_hbm, inflow_hbm, plan_ref, wave_ref, first_ref, second_ref,
    ids, count, pattern, landed, small_sems, sems,
):
    blocks = wave_ref.shape[0]
    small = [
        pltpu.make_async_copy(source, target, small_sems.at[i])
        for i, (source, target) in enumerate(
            ((ids_hbm, ids), (count_hbm, count), (pattern_hbm, pattern))
        )
    ]
    large = [
        pltpu.make_async_copy(inflow_hbm.at[0, b], landed.at[b], sems.at[b]) for b in range(blocks)
    ]
    for copy in small + large:
        copy.start()
    for copy in small:
        copy.wait()
    _, sides, listed = ids.shape
    taken = pattern.shape[1]
    for side in range(sides):
        for slot in range(listed):
            plan_ref[side * listed + slot] = ids[0, side, slot]
        plan_ref[sides * listed + side] = count[0, side]
    for b in range(blocks):
        for k in range(taken):
            plan_ref[sides * (listed + 1) + b * taken + k] = pattern[b, k]
    for b, copy in enumerate(large):
        copy.wait()
        wave_ref[b] = landed[b].astype(wave_ref.dtype)
    write_lists(lax.axis_index("lat"), plan_ref, wave_ref, (first_ref, second_ref))


def load_kernel(
    ops_hbm, source_hbm, pass_hbm, reflect_hbm, after_ref,
    ops_ref, source_ref, pass_ref, reflect_ref, pass_rows, reflect_rows, sems,
):
    del after_ref
    copies = [
        pltpu.make_async_copy(source, target, sems.at[i])
        for i, (source, target) in enumerate(
            (
                (pass_hbm, pass_rows),
                (reflect_hbm, reflect_rows),
                (ops_hbm, ops_ref),
                (source_hbm, source_ref),
            )
        )
    ]
    for copy in copies:
        copy.start()
    for copy, rows, columns_ref in zip(copies, (pass_rows, reflect_rows), (pass_ref, reflect_ref)):
        copy.wait()
        for b in range(columns_ref.shape[0]):
            row = rows[0, pl.ds(b, 1), :]
            columns_ref[b] = jnp.broadcast_to(row, columns_ref.shape[1:]).T
    for copy in copies[2:]:
        copy.wait()


def fill_buffer(section, tick, source_ref, wave_refs, first_ref, second_ref, buffer):
    blocks, listed = source_ref.shape[1], first_ref.shape[0]

    def fill_wave():
        start = 0
        for wave_ref in wave_refs:
            buffer[start : start + wave_ref.shape[0]] = wave_ref[...]
            start += wave_ref.shape[0]

    if tick == 0:
        fill_wave()
    else:
        pl.when(section != 0)(fill_wave)

        @pl.when(section == 0)
        def _():
            buffer[:blocks] = source_ref[tick - 1]

    parity = lax.rem(lax.axis_index("lat"), 2)
    buffer[pl.ds(blocks + (1 - parity) * listed, listed)] = first_ref[...]
    buffer[pl.ds(blocks + parity * listed, listed)] = second_ref[...]


def extrapolate_block(plan_ref, pattern_start, ops_ref, buffer, b):
    taken = ops_ref.shape[2]
    points = ops_ref.shape[5]
    left = jnp.concatenate(
        [ops_ref[0, b, k].reshape(2 * points, points) for k in range(taken)], axis=1
    )
    right = jnp.concatenate(
        [buffer[plan_ref[pattern_start + b * taken + k]] for k in range(taken)], axis=0
    )
    products = jnp.dot(left, right, preferred_element_type=jnp.float32)
    half = products.shape[1] // 2
    real_part = products[:points, :half] - products[points:, half:]
    imag_part = products[:points, half:] + products[points:, :half]
    return real_part, imag_part


def acts(section, parity):
    return lax.rem(section, 2) == parity


def tick_kernel(
    parity, tick, sections, plan_ref, ops_ref, source_ref, pass_ref, reflect_ref,
    wave_refs, first_in_ref, second_in_ref, known_refs, out_refs, buffer, onward,
):
    del known_refs
    echo_ref, first_ref, second_ref, *onward_refs = out_refs
    section = lax.axis_index("depth")
    tile = lax.axis_index("lat")
    listed = first_ref.shape[0]

    @pl.when(acts(section, parity))
    def _():
        fill_buffer(section, tick, source_ref, wave_refs, first_in_ref, second_in_ref, buffer)
        for b in range(echo_ref.shape[0]):
            parts = extrapolate_block(plan_ref, 2 * (listed + 1), ops_ref, buffer, b)
            for i, part in enumerate(parts):
                cols = pl.ds(i * part.shape[1], part.shape[1])
                onward[b, :, cols] = (pass_ref[b] * part).astype(onward.dtype)
                echo_ref[b, :, cols] = (reflect_ref[b] * part).astype(echo_ref.dtype)
        start = 0
        for onward_ref in onward_refs:
            onward_ref[...] = onward[start : start + onward_ref.shape[0]]
            start += onward_ref.shape[0]

        @pl.when(section != sections - 1)
        def _():
            write_lists(tile, plan_ref, onward, (first_ref, second_ref))

        @pl.when(section == sections - 1)
        def _():
            write_lists(tile, plan_ref, source_ref.at[tick], (first_ref, second_ref))


def last_kernel(
    parity, tick, plan_ref, ops_ref, source_ref, pass_ref, reflect_ref,
    wave_refs, first_in_ref, second_in_ref, earlier, known_refs, out_refs,
    buffer, echo, leaving, early_sems, echo_sems, leave_sems,
):
    del known_refs
    reflected_ref, transmitted_ref = out_refs
    section = lax.axis_index("depth")
    listed = first_in_ref.shape[0]

    @pl.when(acts(section, parity))
    def _():
        copies = [
            pltpu.make_async_copy(earlier[t], reflected_ref.at[t, 0], early_sems.at[t])
            for t in range(tick)
        ]
        for copy in copies:
            copy.start()
        fill_buffer(section, tick, source_ref, wave_refs, first_in_ref, second_in_ref, buffer)
        for b in range(echo.shape[0]):
            parts = extrapolate_block(plan_ref, 2 * (listed + 1), ops_ref, buffer, b)
            for i, part in enumerate(parts):
                cols = pl.ds(i * part.shape[1], part.shape[1])
                leaving[b, :, cols] = pass_ref[b] * part
                echo[b, :, cols] = (reflect_ref[b] * part).astype(echo.dtype)
            for copy in (
                pltpu.make_async_copy(leaving.at[b], transmitted_ref.at[0, b], leave_sems.at[b]),
                pltpu.make_async_copy(echo.at[b], reflected_ref.at[tick, 0, b], echo_sems.at[b]),
            ):
                copy.start()
                copies.append(copy)
        for copy in copies:
            copy.wait()


def grouped_call(kernel, groups, outs, out_specs, known, **options):
    flat = [array for group in groups for array in (group if isinstance(group, list) else [group])]

    def body(*refs):
        refs = list(refs)
        take = lambda count: [refs.pop(0) for _ in range(count)]
        inputs = [take(len(g)) if isinstance(g, list) else refs.pop(0) for g in groups]
        kernel(*inputs, take(len(known)), take(len(outs)), *refs)

    return pl.pallas_call(
        body,
        out_shape=tuple(outs),
        in_specs=[SMEM_SPEC] + [VMEM_SPEC] * (len(flat) - 1) + list(out_specs[: len(known)]),
        out_specs=tuple(out_specs),
        input_output_aliases={len(flat) + i: i for i in range(len(known))},
        **options,
    )(flat[0], *map(in_vmem, flat[1:]), *known)


def neighbour(j, turn, tiles):
    to = j + (1 if (j + turn) % 2 == 0 else -1)
    return to if 0 <= to < tiles else None


def swap_routes(sections, tiles):
    routes = []
    for turn in (0, 1):
        route = []
        for s in range(sections):
            for j in range(tiles):
                to = neighbour(j, turn, tiles)
                end = ((s ^ 1) * tiles + j) if to is None else (s * tiles + to)
                route.append((s * tiles + j, end))
        routes.append(route)
    return routes


def halo_routes(sections, tiles):
    routes = []
    for turn in (0, 1):
        route = []
        for s in range(sections):
            for j in range(tiles):
                to = neighbour(j, turn, tiles)
                end = (s ^ 1) * tiles + j if to is None else (s + 1) % sections * tiles + to
                route.append((s * tiles + j, end))
        routes.append(route)
    return routes


def per_device(
    inflow, source, operators, transmission, reflectivity, send_ids, send_count, pattern
):
    sections, tiles = lax.axis_size("depth"), lax.axis_size("lat")
    ticks = source.shape[0] + 1
    _, blocks, points, columns = inflow.shape
    listed = send_ids.shape[-1]
    taken = operators.shape[2]
    wave_type = pltpu.VMEM((blocks, points, columns), WAVE)
    list_type = pltpu.VMEM((listed, points, columns), WAVE)
    params = pltpu.CompilerParams(vmem_limit_bytes=VMEM_LIMIT)
    tick_cost = pl.CostEstimate(
        flops=blocks * taken * 4 * points * points * columns,
        bytes_accessed=2 * operators.size + 8 * blocks * points * columns,
        transcendentals=0,
    )
    both = ("depth", "lat")
    deeper = [(s, (s + 1) % sections) for s in range(sections)]

    plan, wave, first, second = pl.pallas_call(
        prepare_kernel,
        out_shape=(
            pltpu.SMEM((2 * (listed + 1) + blocks * taken,), jnp.int32),
            wave_type,
            list_type,
            list_type,
        ),
        in_specs=[ANY_SPEC] * 4,
        out_specs=(SMEM_SPEC,) + (VMEM_SPEC,) * 3,
        scratch_shapes=[
            pltpu.SMEM(send_ids.shape, jnp.int32),
            pltpu.SMEM(send_count.shape, jnp.int32),
            pltpu.SMEM(pattern.shape, jnp.int32),
            pltpu.VMEM((blocks, points, columns), inflow.dtype),
            pltpu.SemaphoreType.DMA((3,)),
            pltpu.SemaphoreType.DMA((blocks,)),
        ],
        compiler_params=params,
        cost_estimate=pl.CostEstimate(
            flops=inflow.size, bytes_accessed=8 * inflow.size, transcendentals=0
        ),
        name="prepare",
    )(*map(in_hbm, (send_ids, send_count, pattern, inflow)))
    loaded_first = first
    routes = swap_routes(sections, tiles)
    first = lax.ppermute(first, both, routes[0])
    second = lax.ppermute(second, both, routes[1])

    column_type = pltpu.VMEM((blocks, points, columns // 2), jnp.float32)
    fixed = pl.pallas_call(
        load_kernel,
        out_shape=(
            pltpu.VMEM(operators.shape, operators.dtype),
            pltpu.VMEM(source.shape, source.dtype),
            column_type,
            column_type,
        ),
        in_specs=[ANY_SPEC] * 4 + [VMEM_SPEC],
        out_specs=(VMEM_SPEC,) * 4,
        scratch_shapes=[
            pltpu.VMEM(transmission.shape, transmission.dtype),
            pltpu.VMEM(reflectivity.shape, reflectivity.dtype),
            pltpu.SemaphoreType.DMA((4,)),
        ],
        compiler_params=params,
        cost_estimate=pl.CostEstimate(
            flops=0, bytes_accessed=4 * (operators.size + source.size), transcendentals=0
        ),
        name="load",
    )(*map(in_hbm, (operators, source, transmission, reflectivity)), in_vmem(loaded_first))
    fixed = [plan, *fixed]

    buffer_type = pltpu.VMEM((blocks + 2 * listed, points, columns), WAVE)

    ODD, EVEN = 1, 0
    halves = [blocks // 2, blocks - blocks // 2]
    half_types = [pltpu.VMEM((n, points, columns), WAVE) for n in halves]
    crossing = [(s, (s + 1) % sections) for s in range(sections)]
    inside = [(s, s ^ 1) for s in range(sections)]
    routes = halo_routes(sections, tiles)

    waves = {ODD: [wave], EVEN: [wave]}
    echoes = []
    for tick in range(ticks - 1):
        known = []
        sent = {}
        for parity in (ODD, EVEN):
            to_next = [wave_type] if parity == ODD else half_types
            outs = [wave_type, list_type, list_type] + to_next
            known = grouped_call(
                functools.partial(tick_kernel, parity, tick, sections),
                [*fixed, waves[parity], first, second],
                outs,
                [VMEM_SPEC] * len(outs),
                known[:3] and [in_vmem(a) for a in known[:3]],
                scratch_shapes=[buffer_type, pltpu.VMEM(wave_type.shape, WAVE)],
                compiler_params=params,
                cost_estimate=tick_cost,
                name=f"tick{tick}" + ("_odd" if parity else "_even"),
            )
            if parity == ODD:
                sent[EVEN] = [lax.ppermute(known[3], "depth", crossing)]
            else:
                sent[ODD] = [lax.ppermute(a, "depth", inside) for a in known[-2:]]
        waves = sent
        echo, first, second = known[:3]
        first = lax.ppermute(first, both, routes[0])
        second = lax.ppermute(second, both, routes[1])
        echoes.append(echo)

    tick = ticks - 1
    results = []
    result_types = (
        jax.ShapeDtypeStruct((ticks, 1, blocks, points, columns), WAVE),
        jax.ShapeDtypeStruct((1, blocks, points, columns), jnp.float32),
    )
    for parity in (ODD, EVEN):
        results = grouped_call(
            functools.partial(last_kernel, parity, tick),
            [*fixed, waves[parity], first, second, echoes],
            result_types,
            [ANY_SPEC] * 2,
            list(results),
            scratch_shapes=[
                buffer_type,
                pltpu.VMEM((blocks, points, columns), WAVE),
                pltpu.VMEM((blocks, points, columns), jnp.float32),
                pltpu.SemaphoreType.DMA((tick,)),
                pltpu.SemaphoreType.DMA((blocks,)),
                pltpu.SemaphoreType.DMA((blocks,)),
            ],
            compiler_params=params,
            cost_estimate=tick_cost,
            name="last_tick" + ("_odd" if parity else "_even"),
        )
    return tuple(results)


def solution(mesh):
    return jax.shard_map(
        per_device,
        mesh=mesh,
        in_specs=(
            P("depth", "lat", None, None),
            P(None, "lat", None, None),
            P("depth", "lat", None, None, None, None),
            P("depth", "lat", None),
            P("depth", "lat", None),
            P("lat", None, None),
            P("lat", None),
            P("lat", None),
        ),
        out_specs=(P(None, "depth", "lat", None, None), P("depth", "lat", None, None)),
        check_vma=False,
    )
```

```python
import functools

import jax
import jax.numpy as jnp
from jax import lax
from jax.experimental import pallas as pl
from jax.experimental.pallas import tpu as pltpu
from jax.sharding import PartitionSpec as P

WAVE = jnp.bfloat16
SMEM_SPEC = pl.BlockSpec(memory_space=pltpu.SMEM)
VMEM_SPEC = pl.BlockSpec(memory_space=pltpu.VMEM)
ANY_SPEC = pl.BlockSpec(memory_space=pl.ANY)
VMEM_LIMIT = 8 * 1024 * 1024
LOWER, UPPER = 0, 1


def in_vmem(array):
    return pltpu.with_memory_space_constraint(array, pltpu.VMEM)


def in_hbm(array):
    return pltpu.with_memory_space_constraint(array, pltpu.HBM)


def write_lists(tile, plan_ref, blocks_ref, lists):
    listed = lists[0].shape[0]
    points = blocks_ref.shape[1]
    parity = lax.rem(tile, 2)
    for list_ref, side in zip(lists, (UPPER - parity, parity)):
        count = plan_ref[2 * listed + side]
        for slot in range(listed):
            live = slot < count

            @pl.when(live)
            def _():
                list_ref[slot, :points] = blocks_ref[plan_ref[side * listed + slot]]

            @pl.when(jnp.logical_not(live))
            def _():
                list_ref[slot, :points] = jnp.zeros(blocks_ref.shape[1:], list_ref.dtype)


def prepare_kernel(
    ids_hbm, count_hbm, pattern_hbm, inflow_hbm, plan_ref, wave_ref, first_ref, second_ref,
    ids, count, pattern, landed, small_sems, sems,
):
    blocks = wave_ref.shape[0]
    small = [
        pltpu.make_async_copy(source, target, small_sems.at[i])
        for i, (source, target) in enumerate(
            ((ids_hbm, ids), (count_hbm, count), (pattern_hbm, pattern))
        )
    ]
    large = [
        pltpu.make_async_copy(inflow_hbm.at[0, b], landed.at[b], sems.at[b]) for b in range(blocks)
    ]
    for copy in small + large:
        copy.start()
    for copy in small:
        copy.wait()
    _, sides, listed = ids.shape
    taken = pattern.shape[1]
    for side in range(sides):
        for slot in range(listed):
            plan_ref[side * listed + slot] = ids[0, side, slot]
        plan_ref[sides * listed + side] = count[0, side]
    for b in range(blocks):
        for k in range(taken):
            plan_ref[sides * (listed + 1) + b * taken + k] = pattern[b, k]
    for b, copy in enumerate(large):
        copy.wait()
        wave_ref[b] = landed[b].astype(wave_ref.dtype)
    write_lists(lax.axis_index("lat"), plan_ref, wave_ref, (first_ref, second_ref))


def load_kernel(
    ops_hbm, source_hbm, pass_hbm, reflect_hbm, after_ref,
    ops_ref, source_ref, pass_ref, reflect_ref, pass_rows, reflect_rows, sems,
):
    del after_ref
    copies = [
        pltpu.make_async_copy(source, target, sems.at[i])
        for i, (source, target) in enumerate(
            (
                (pass_hbm, pass_rows),
                (reflect_hbm, reflect_rows),
                (ops_hbm, ops_ref),
                (source_hbm, source_ref),
            )
        )
    ]
    for copy in copies:
        copy.start()
    for copy, rows, columns_ref in zip(copies, (pass_rows, reflect_rows), (pass_ref, reflect_ref)):
        copy.wait()
        for b in range(columns_ref.shape[0]):
            row = rows[0, pl.ds(b, 1), :]
            columns_ref[b] = jnp.broadcast_to(row, columns_ref.shape[1:]).T
    for copy in copies[2:]:
        copy.wait()


def fill_buffer(section, tick, source_ref, wave_refs, first_ref, second_ref, buffer):
    blocks, listed = source_ref.shape[1], first_ref.shape[0]

    def fill_wave():
        for wave_ref in wave_refs:
            buffer[:blocks] = wave_ref[...] if len(wave_ref.shape) == 3 else wave_ref[0]

    if tick == 0:
        fill_wave()
    else:
        pl.when(section != 0)(fill_wave)

        @pl.when(section == 0)
        def _():
            buffer[:blocks] = source_ref[tick - 1]

    parity = lax.rem(lax.axis_index("lat"), 2)
    points = buffer.shape[1]
    buffer[pl.ds(blocks + (1 - parity) * listed, listed)] = first_ref[:, :points]
    buffer[pl.ds(blocks + parity * listed, listed)] = second_ref[:, :points]


def extrapolate_block(plan_ref, pattern_start, ops_ref, buffer, b):
    taken = ops_ref.shape[2]
    points = ops_ref.shape[5]
    left = jnp.concatenate(
        [ops_ref[0, b, k].reshape(2 * points, points) for k in range(taken)], axis=1
    )
    right = jnp.concatenate(
        [buffer[plan_ref[pattern_start + b * taken + k]] for k in range(taken)], axis=0
    )
    products = jnp.dot(left, right, preferred_element_type=jnp.float32)
    half = products.shape[1] // 2
    real_part = products[:points, :half] - products[points:, half:]
    imag_part = products[:points, half:] + products[points:, :half]
    return real_part, imag_part


def acts(section, parity):
    return lax.rem(section, 2) == parity


def tick_kernel(
    parity, tick, sections, plan_ref, ops_ref, source_ref, pass_ref, reflect_ref,
    wave_refs, first_in_ref, second_in_ref, known_refs, out_refs, buffer, onward,
):
    del known_refs
    echo_ref, first_ref, second_ref, *onward_refs = out_refs
    section = lax.axis_index("depth")
    tile = lax.axis_index("lat")
    listed = first_ref.shape[0]

    @pl.when(acts(section, parity))
    def _():
        fill_buffer(section, tick, source_ref, wave_refs, first_in_ref, second_in_ref, buffer)
        for b in range(echo_ref.shape[0]):
            parts = extrapolate_block(plan_ref, 2 * (listed + 1), ops_ref, buffer, b)
            for i, part in enumerate(parts):
                cols = pl.ds(i * part.shape[1], part.shape[1])
                onward[b, :, cols] = (pass_ref[b] * part).astype(onward.dtype)
                echo_ref[b, :, cols] = (reflect_ref[b] * part).astype(echo_ref.dtype)
        for onward_ref in onward_refs:
            slot = onward_ref if len(onward_ref.shape) == 3 else onward_ref.at[1]
            slot[...] = onward[...]

        @pl.when(section != sections - 1)
        def _():
            write_lists(tile, plan_ref, onward, (first_ref, second_ref))

        @pl.when(section == sections - 1)
        def _():
            write_lists(tile, plan_ref, source_ref.at[tick], (first_ref, second_ref))


def last_kernel(
    parity, tick, plan_ref, ops_ref, source_ref, pass_ref, reflect_ref,
    wave_refs, first_in_ref, second_in_ref, earlier, known_refs, out_refs,
    buffer, echo, leaving, early_sems, echo_sems, leave_sems,
):
    del known_refs
    reflected_ref, transmitted_ref = out_refs
    section = lax.axis_index("depth")
    listed = first_in_ref.shape[0]

    @pl.when(acts(section, parity))
    def _():
        copies = [
            pltpu.make_async_copy(earlier[t], reflected_ref.at[t, 0], early_sems.at[t])
            for t in range(tick)
        ]
        for copy in copies:
            copy.start()
        fill_buffer(section, tick, source_ref, wave_refs, first_in_ref, second_in_ref, buffer)
        for b in range(echo.shape[0]):
            parts = extrapolate_block(plan_ref, 2 * (listed + 1), ops_ref, buffer, b)
            for i, part in enumerate(parts):
                cols = pl.ds(i * part.shape[1], part.shape[1])
                leaving[b, :, cols] = pass_ref[b] * part
                echo[b, :, cols] = (reflect_ref[b] * part).astype(echo.dtype)
            for copy in (
                pltpu.make_async_copy(leaving.at[b], transmitted_ref.at[0, b], leave_sems.at[b]),
                pltpu.make_async_copy(echo.at[b], reflected_ref.at[tick, 0, b], echo_sems.at[b]),
            ):
                copy.start()
                copies.append(copy)
        for copy in copies:
            copy.wait()


def grouped_call(kernel, groups, outs, out_specs, known, **options):
    flat = [array for group in groups for array in (group if isinstance(group, list) else [group])]

    def body(*refs):
        refs = list(refs)
        take = lambda count: [refs.pop(0) for _ in range(count)]
        inputs = [take(len(g)) if isinstance(g, list) else refs.pop(0) for g in groups]
        kernel(*inputs, take(len(known)), take(len(outs)), *refs)

    return pl.pallas_call(
        body,
        out_shape=tuple(outs),
        in_specs=[SMEM_SPEC] + [VMEM_SPEC] * (len(flat) - 1) + list(out_specs[: len(known)]),
        out_specs=tuple(out_specs),
        input_output_aliases={len(flat) + i: i for i in range(len(known))},
        **options,
    )(flat[0], *map(in_vmem, flat[1:]), *known)


def neighbour(j, turn, tiles):
    to = j + (1 if (j + turn) % 2 == 0 else -1)
    return to if 0 <= to < tiles else None


def swap_routes(sections, tiles):
    routes = []
    for turn in (0, 1):
        route = []
        for s in range(sections):
            for j in range(tiles):
                to = neighbour(j, turn, tiles)
                end = ((s ^ 1) * tiles + j) if to is None else (s * tiles + to)
                route.append((s * tiles + j, end))
        routes.append(route)
    return routes


def halo_routes(sections, tiles, parity):
    routes = []
    for turn in (0, 1):
        route = []
        for s in range(sections):
            for j in range(tiles):
                to = neighbour(j, turn, tiles)
                real = to is not None and s % 2 == parity
                end = (s + 1) % sections * tiles + to if real else (s ^ 1) * tiles + j
                route.append((s * tiles + j, end))
        routes.append(route)
    return routes


def per_device(
    inflow, source, operators, transmission, reflectivity, send_ids, send_count, pattern
):
    sections, tiles = lax.axis_size("depth"), lax.axis_size("lat")
    ticks = source.shape[0] + 1
    _, blocks, points, columns = inflow.shape
    listed = send_ids.shape[-1]
    taken = operators.shape[2]
    wave_type = pltpu.VMEM((blocks, points, columns), WAVE)
    list_type = pltpu.VMEM((listed, points, columns), WAVE)
    params = pltpu.CompilerParams(vmem_limit_bytes=VMEM_LIMIT)
    tick_cost = pl.CostEstimate(
        flops=0,
        bytes_accessed=0,
        transcendentals=0,
    )
    both = ("depth", "lat")
    deeper = [(s, (s + 1) % sections) for s in range(sections)]

    plan, wave, first, second = pl.pallas_call(
        prepare_kernel,
        out_shape=(
            pltpu.SMEM((2 * (listed + 1) + blocks * taken,), jnp.int32),
            wave_type,
            list_type,
            list_type,
        ),
        in_specs=[ANY_SPEC] * 4,
        out_specs=(SMEM_SPEC,) + (VMEM_SPEC,) * 3,
        scratch_shapes=[
            pltpu.SMEM(send_ids.shape, jnp.int32),
            pltpu.SMEM(send_count.shape, jnp.int32),
            pltpu.SMEM(pattern.shape, jnp.int32),
            pltpu.VMEM((blocks, points, columns), inflow.dtype),
            pltpu.SemaphoreType.DMA((3,)),
            pltpu.SemaphoreType.DMA((blocks,)),
        ],
        compiler_params=params,
        cost_estimate=pl.CostEstimate(
            flops=inflow.size, bytes_accessed=8 * inflow.size, transcendentals=0
        ),
        name="prepare",
    )(*map(in_hbm, (send_ids, send_count, pattern, inflow)))
    loaded_first = first
    routes = swap_routes(sections, tiles)
    first = lax.ppermute(first, both, routes[0])
    second = lax.ppermute(second, both, routes[1])

    column_type = pltpu.VMEM((blocks, points, columns // 2), jnp.float32)
    fixed = pl.pallas_call(
        load_kernel,
        out_shape=(
            pltpu.VMEM(operators.shape, operators.dtype),
            pltpu.VMEM(source.shape, source.dtype),
            column_type,
            column_type,
        ),
        in_specs=[ANY_SPEC] * 4 + [VMEM_SPEC],
        out_specs=(VMEM_SPEC,) * 4,
        scratch_shapes=[
            pltpu.VMEM(transmission.shape, transmission.dtype),
            pltpu.VMEM(reflectivity.shape, reflectivity.dtype),
            pltpu.SemaphoreType.DMA((4,)),
        ],
        compiler_params=params,
        cost_estimate=pl.CostEstimate(
            flops=0, bytes_accessed=4 * (operators.size + source.size), transcendentals=0
        ),
        name="load",
    )(*map(in_hbm, (operators, source, transmission, reflectivity)), in_vmem(loaded_first))
    fixed = [plan, *fixed]

    buffer_type = pltpu.VMEM((blocks + 2 * listed, points, columns), WAVE)

    ODD, EVEN = 1, 0
    crossing = [(s, (s + 1) % sections) for s in range(sections)]
    pairs = [[s, s + 1] for s in range(0, sections, 2)]
    far_list_type = pltpu.VMEM((listed, points + 16, columns), WAVE)
    pair_type = pltpu.VMEM((2, blocks, points, columns), WAVE)
    routes = {parity: halo_routes(sections, tiles, parity) for parity in (ODD, EVEN)}

    arrived = {parity: ([wave], first, second) for parity in (ODD, EVEN)}
    echoes = []
    for tick in range(ticks - 1):
        echo = []
        sent = {}
        for parity in (ODD, EVEN):
            kind = list_type if parity == EVEN else far_list_type
            outs = [wave_type, kind, kind, wave_type if parity == ODD else pair_type]
            echo, first, second, onward = grouped_call(
                functools.partial(tick_kernel, parity, tick, sections),
                [*fixed, *arrived[parity]],
                outs,
                [VMEM_SPEC] * len(outs),
                [in_vmem(a) for a in echo],
                scratch_shapes=[buffer_type, pltpu.VMEM(wave_type.shape, WAVE)],
                compiler_params=params,
                cost_estimate=tick_cost,
                name=f"tick{tick}" + ("_odd" if parity else "_even"),
            )
            echo = [echo]
            if parity == ODD:
                onward = lax.ppermute(onward, "depth", crossing)
            else:
                onward = lax.all_to_all(onward, "depth", 0, 0, axis_index_groups=pairs)
            sent[1 - parity] = (
                [onward],
                lax.ppermute(first, both, routes[parity][0]),
                lax.ppermute(second, both, routes[parity][1]),
            )
        arrived = sent
        echoes += echo

    tick = ticks - 1
    results = []
    result_types = (
        jax.ShapeDtypeStruct((ticks, 1, blocks, points, columns), WAVE),
        jax.ShapeDtypeStruct((1, blocks, points, columns), jnp.float32),
    )
    for parity in (ODD, EVEN):
        results = grouped_call(
            functools.partial(last_kernel, parity, tick),
            [*fixed, *arrived[parity], echoes],
            result_types,
            [ANY_SPEC] * 2,
            list(results),
            scratch_shapes=[
                buffer_type,
                pltpu.VMEM((blocks, points, columns), WAVE),
                pltpu.VMEM((blocks, points, columns), jnp.float32),
                pltpu.SemaphoreType.DMA((tick,)),
                pltpu.SemaphoreType.DMA((blocks,)),
                pltpu.SemaphoreType.DMA((blocks,)),
            ],
            compiler_params=params,
            cost_estimate=tick_cost,
            name="last_tick" + ("_odd" if parity else "_even"),
        )
    return tuple(results)


def solution(mesh):
    return jax.shard_map(
        per_device,
        mesh=mesh,
        in_specs=(
            P("depth", "lat", None, None),
            P(None, "lat", None, None),
            P("depth", "lat", None, None, None, None),
            P("depth", "lat", None),
            P("depth", "lat", None),
            P("lat", None, None),
            P("lat", None),
            P("lat", None),
        ),
        out_specs=(P(None, "depth", "lat", None, None), P("depth", "lat", None, None)),
        check_vma=False,
    )
```

```python
import functools

import jax
import jax.numpy as jnp
from jax import lax
from jax.experimental import pallas as pl
from jax.experimental.pallas import tpu as pltpu
from jax.sharding import PartitionSpec as P

WAVE = jnp.bfloat16
SMEM_SPEC = pl.BlockSpec(memory_space=pltpu.SMEM)
VMEM_SPEC = pl.BlockSpec(memory_space=pltpu.VMEM)
ANY_SPEC = pl.BlockSpec(memory_space=pl.ANY)
VMEM_LIMIT = 8 * 1024 * 1024
LOWER, UPPER = 0, 1


def in_vmem(array):
    return pltpu.with_memory_space_constraint(array, pltpu.VMEM)


def in_hbm(array):
    return pltpu.with_memory_space_constraint(array, pltpu.HBM)


def write_lists(tile, plan_ref, blocks_ref, lists):
    listed = lists[0].shape[0]
    points = blocks_ref.shape[1]
    parity = lax.rem(tile, 2)
    for list_ref, side in zip(lists, (UPPER - parity, parity)):
        count = plan_ref[2 * listed + side]
        for slot in range(listed):
            live = slot < count

            @pl.when(live)
            def _():
                list_ref[slot, :points] = blocks_ref[plan_ref[side * listed + slot]]

            @pl.when(jnp.logical_not(live))
            def _():
                list_ref[slot, :points] = jnp.zeros(blocks_ref.shape[1:], list_ref.dtype)


def prepare_kernel(
    ids_hbm, count_hbm, pattern_hbm, inflow_hbm, plan_ref, wave_ref, first_ref, second_ref,
    ids, count, pattern, landed, small_sems, sems,
):
    blocks = wave_ref.shape[0]
    small = [
        pltpu.make_async_copy(source, target, small_sems.at[i])
        for i, (source, target) in enumerate(
            ((ids_hbm, ids), (count_hbm, count), (pattern_hbm, pattern))
        )
    ]
    large = [
        pltpu.make_async_copy(inflow_hbm.at[0, b], landed.at[b], sems.at[b]) for b in range(blocks)
    ]
    for copy in small + large:
        copy.start()
    for copy in small:
        copy.wait()
    _, sides, listed = ids.shape
    taken = pattern.shape[1]
    for side in range(sides):
        for slot in range(listed):
            plan_ref[side * listed + slot] = ids[0, side, slot]
        plan_ref[sides * listed + side] = count[0, side]
    for b in range(blocks):
        for k in range(taken):
            plan_ref[sides * (listed + 1) + b * taken + k] = pattern[b, k]
    for b, copy in enumerate(large):
        copy.wait()
        wave_ref[b] = landed[b].astype(wave_ref.dtype)
    write_lists(lax.axis_index("lat"), plan_ref, wave_ref, (first_ref, second_ref))


def load_kernel(
    ops_hbm, source_hbm, pass_hbm, reflect_hbm, after_ref,
    ops_ref, source_ref, pass_ref, reflect_ref, pass_rows, reflect_rows, sems,
):
    del after_ref
    copies = [
        pltpu.make_async_copy(source, target, sems.at[i])
        for i, (source, target) in enumerate(
            (
                (pass_hbm, pass_rows),
                (reflect_hbm, reflect_rows),
                (ops_hbm, ops_ref),
                (source_hbm, source_ref),
            )
        )
    ]
    for copy in copies:
        copy.start()
    for copy, rows, columns_ref in zip(copies, (pass_rows, reflect_rows), (pass_ref, reflect_ref)):
        copy.wait()
        for b in range(columns_ref.shape[0]):
            row = rows[0, pl.ds(b, 1), :]
            columns_ref[b] = jnp.broadcast_to(row, columns_ref.shape[1:]).T
    for copy in copies[2:]:
        copy.wait()


def fill_buffer(section, tick, source_ref, wave_refs, first_ref, second_ref, buffer):
    blocks, listed = source_ref.shape[1], first_ref.shape[0]

    def fill_wave():
        start = 0
        for wave_ref in wave_refs:
            part = wave_ref[:, : buffer.shape[1]] if len(wave_ref.shape) == 3 else wave_ref[0]
            buffer[start : start + part.shape[0]] = part
            start += part.shape[0]

    if tick == 0:
        fill_wave()
    else:
        pl.when(section != 0)(fill_wave)

        @pl.when(section == 0)
        def _():
            buffer[:blocks] = source_ref[tick - 1]

    parity = lax.rem(lax.axis_index("lat"), 2)
    points = buffer.shape[1]
    buffer[pl.ds(blocks + (1 - parity) * listed, listed)] = first_ref[:, :points]
    buffer[pl.ds(blocks + parity * listed, listed)] = second_ref[:, :points]


def extrapolate_block(plan_ref, pattern_start, ops_ref, buffer, b):
    taken = ops_ref.shape[2]
    points = ops_ref.shape[5]
    left = jnp.concatenate(
        [ops_ref[0, b, k].reshape(2 * points, points) for k in range(taken)], axis=1
    )
    right = jnp.concatenate(
        [buffer[plan_ref[pattern_start + b * taken + k]] for k in range(taken)], axis=0
    )
    products = jnp.dot(left, right, preferred_element_type=jnp.float32)
    half = products.shape[1] // 2
    real_part = products[:points, :half] - products[points:, half:]
    imag_part = products[:points, half:] + products[points:, :half]
    return real_part, imag_part


def acts(section, parity):
    return lax.rem(section, 2) == parity


def tick_kernel(
    parity, tick, sections, plan_ref, ops_ref, source_ref, pass_ref, reflect_ref,
    wave_refs, first_in_ref, second_in_ref, known_refs, out_refs, buffer, onward,
):
    del known_refs
    echo_ref, first_ref, second_ref, *onward_refs = out_refs
    section = lax.axis_index("depth")
    tile = lax.axis_index("lat")
    listed = first_ref.shape[0]

    @pl.when(acts(section, parity))
    def _():
        fill_buffer(section, tick, source_ref, wave_refs, first_in_ref, second_in_ref, buffer)
        for b in range(echo_ref.shape[0]):
            parts = extrapolate_block(plan_ref, 2 * (listed + 1), ops_ref, buffer, b)
            for i, part in enumerate(parts):
                cols = pl.ds(i * part.shape[1], part.shape[1])
                onward[b, :, cols] = (pass_ref[b] * part).astype(onward.dtype)
                echo_ref[b, :, cols] = (reflect_ref[b] * part).astype(echo_ref.dtype)
        start = 0
        for onward_ref in onward_refs:
            slot = onward_ref if len(onward_ref.shape) == 3 else onward_ref.at[1]
            slot[:, : onward.shape[1]] = onward[start : start + slot.shape[0]]
            start += slot.shape[0]

        @pl.when(section != sections - 1)
        def _():
            write_lists(tile, plan_ref, onward, (first_ref, second_ref))

        @pl.when(section == sections - 1)
        def _():
            write_lists(tile, plan_ref, source_ref.at[tick], (first_ref, second_ref))


def last_kernel(
    parity, tick, plan_ref, ops_ref, source_ref, pass_ref, reflect_ref,
    wave_refs, first_in_ref, second_in_ref, earlier, known_refs, out_refs,
    buffer, echo, leaving, early_sems, echo_sems, leave_sems,
):
    del known_refs
    reflected_ref, transmitted_ref = out_refs
    section = lax.axis_index("depth")
    listed = first_in_ref.shape[0]

    @pl.when(acts(section, parity))
    def _():
        copies = [
            pltpu.make_async_copy(earlier[t], reflected_ref.at[t, 0], early_sems.at[t])
            for t in range(tick)
        ]
        for copy in copies:
            copy.start()
        fill_buffer(section, tick, source_ref, wave_refs, first_in_ref, second_in_ref, buffer)
        for b in range(echo.shape[0]):
            parts = extrapolate_block(plan_ref, 2 * (listed + 1), ops_ref, buffer, b)
            for i, part in enumerate(parts):
                cols = pl.ds(i * part.shape[1], part.shape[1])
                leaving[b, :, cols] = pass_ref[b] * part
                echo[b, :, cols] = (reflect_ref[b] * part).astype(echo.dtype)
            for copy in (
                pltpu.make_async_copy(leaving.at[b], transmitted_ref.at[0, b], leave_sems.at[b]),
                pltpu.make_async_copy(echo.at[b], reflected_ref.at[tick, 0, b], echo_sems.at[b]),
            ):
                copy.start()
                copies.append(copy)
        for copy in copies:
            copy.wait()


def grouped_call(kernel, groups, outs, out_specs, known, **options):
    flat = [array for group in groups for array in (group if isinstance(group, list) else [group])]

    def body(*refs):
        refs = list(refs)
        take = lambda count: [refs.pop(0) for _ in range(count)]
        inputs = [take(len(g)) if isinstance(g, list) else refs.pop(0) for g in groups]
        kernel(*inputs, take(len(known)), take(len(outs)), *refs)

    return pl.pallas_call(
        body,
        out_shape=tuple(outs),
        in_specs=[SMEM_SPEC] + [VMEM_SPEC] * (len(flat) - 1) + list(out_specs[: len(known)]),
        out_specs=tuple(out_specs),
        input_output_aliases={len(flat) + i: i for i in range(len(known))},
        **options,
    )(flat[0], *map(in_vmem, flat[1:]), *known)


def neighbour(j, turn, tiles):
    to = j + (1 if (j + turn) % 2 == 0 else -1)
    return to if 0 <= to < tiles else None


def swap_routes(sections, tiles):
    routes = []
    for turn in (0, 1):
        route = []
        for s in range(sections):
            for j in range(tiles):
                to = neighbour(j, turn, tiles)
                end = ((s ^ 1) * tiles + j) if to is None else (s * tiles + to)
                route.append((s * tiles + j, end))
        routes.append(route)
    return routes


def halo_routes(sections, tiles, senders):
    routes = []
    for turn in (0, 1):
        route = []
        for s in range(sections):
            for j in range(tiles):
                to = neighbour(j, turn, tiles)
                real = to is not None and s % 2 in senders
                end = (s + 1) % sections * tiles + to if real else (s ^ 1) * tiles + j
                route.append((s * tiles + j, end))
        routes.append(route)
    return routes


def per_device(
    inflow, source, operators, transmission, reflectivity, send_ids, send_count, pattern
):
    sections, tiles = lax.axis_size("depth"), lax.axis_size("lat")
    ticks = source.shape[0] + 1
    _, blocks, points, columns = inflow.shape
    listed = send_ids.shape[-1]
    taken = operators.shape[2]
    wave_type = pltpu.VMEM((blocks, points, columns), WAVE)
    list_type = pltpu.VMEM((listed, points, columns), WAVE)
    params = pltpu.CompilerParams(vmem_limit_bytes=VMEM_LIMIT)
    tick_cost = pl.CostEstimate(
        flops=0,
        bytes_accessed=0,
        transcendentals=0,
    )
    both = ("depth", "lat")
    deeper = [(s, (s + 1) % sections) for s in range(sections)]

    plan, wave, first, second = pl.pallas_call(
        prepare_kernel,
        out_shape=(
            pltpu.SMEM((2 * (listed + 1) + blocks * taken,), jnp.int32),
            wave_type,
            list_type,
            list_type,
        ),
        in_specs=[ANY_SPEC] * 4,
        out_specs=(SMEM_SPEC,) + (VMEM_SPEC,) * 3,
        scratch_shapes=[
            pltpu.SMEM(send_ids.shape, jnp.int32),
            pltpu.SMEM(send_count.shape, jnp.int32),
            pltpu.SMEM(pattern.shape, jnp.int32),
            pltpu.VMEM((blocks, points, columns), inflow.dtype),
            pltpu.SemaphoreType.DMA((3,)),
            pltpu.SemaphoreType.DMA((blocks,)),
        ],
        compiler_params=params,
        cost_estimate=pl.CostEstimate(
            flops=inflow.size, bytes_accessed=8 * inflow.size, transcendentals=0
        ),
        name="prepare",
    )(*map(in_hbm, (send_ids, send_count, pattern, inflow)))
    loaded_first = first
    routes = swap_routes(sections, tiles)
    first = lax.ppermute(first, both, routes[0])
    second = lax.ppermute(second, both, routes[1])

    column_type = pltpu.VMEM((blocks, points, columns // 2), jnp.float32)
    fixed = pl.pallas_call(
        load_kernel,
        out_shape=(
            pltpu.VMEM(operators.shape, operators.dtype),
            pltpu.VMEM(source.shape, source.dtype),
            column_type,
            column_type,
        ),
        in_specs=[ANY_SPEC] * 4 + [VMEM_SPEC],
        out_specs=(VMEM_SPEC,) * 4,
        scratch_shapes=[
            pltpu.VMEM(transmission.shape, transmission.dtype),
            pltpu.VMEM(reflectivity.shape, reflectivity.dtype),
            pltpu.SemaphoreType.DMA((4,)),
        ],
        compiler_params=params,
        cost_estimate=pl.CostEstimate(
            flops=0, bytes_accessed=4 * (operators.size + source.size), transcendentals=0
        ),
        name="load",
    )(*map(in_hbm, (operators, source, transmission, reflectivity)), in_vmem(loaded_first))
    fixed = [plan, *fixed]

    buffer_type = pltpu.VMEM((blocks + 2 * listed, points, columns), WAVE)

    ODD, EVEN = 1, 0
    crossing = [(s, (s + 1) % sections) for s in range(sections)]
    inside = [(s, s ^ 1) for s in range(sections)]
    pairs = [[s, s + 1] for s in range(0, sections, 2)]
    pair_type = pltpu.VMEM((2, blocks, points, columns), WAVE)
    part_types = [pltpu.VMEM((blocks // 2, points, columns), WAVE)] * 2
    half_types = [pltpu.VMEM((n, points, columns), WAVE) for n in (blocks // 2, blocks - blocks // 2)]

    def lists_of(extra):
        return [pltpu.VMEM((listed, points + extra, columns), WAVE)] * 2

    def exchange(lists, senders):
        routes = halo_routes(sections, tiles, senders)
        return [lax.ppermute(a, both, route) for a, route in zip(lists, routes)]

    arrived = {parity: ([wave], first, second) for parity in (ODD, EVEN)}
    echoes = []
    for tick in range(ticks - 1):
        first_step, last_step = tick == 0, tick == ticks - 2
        known = []
        waves, halos = {}, {}
        for parity in (ODD, EVEN):
            if first_step:
                extra = 0
            elif last_step:
                extra = 16 if parity == ODD else 0
            else:
                extra = 0 if parity == ODD else 16
            if parity == ODD:
                long = 0 if first_step or last_step else 16
                to_next = [pltpu.VMEM((blocks, points + long, columns), WAVE)]
            else:
                to_next = [pair_type] if last_step else half_types if first_step else part_types
            outs = [wave_type, *lists_of(extra), *to_next]
            echo, *lists = grouped_call(
                functools.partial(tick_kernel, parity, tick, sections),
                [*fixed, *arrived[parity]],
                outs,
                [VMEM_SPEC] * len(outs),
                [in_vmem(a) for a in known],
                scratch_shapes=[buffer_type, pltpu.VMEM(wave_type.shape, WAVE)],
                compiler_params=params,
                cost_estimate=tick_cost,
                name=f"tick{tick}" + ("_odd" if parity else "_even"),
            )
            lists, onward = lists[:2], lists[2:]
            known = [echo, *lists] if first_step else [echo]
            if parity == ODD:
                waves[EVEN] = [lax.ppermute(onward[0], "depth", crossing)]
            elif last_step:
                waves[ODD] = [lax.all_to_all(onward[0], "depth", 0, 0, axis_index_groups=pairs)]
            else:
                waves[ODD] = [lax.ppermute(a, "depth", inside) for a in onward]
            if not first_step:
                halos[1 - parity] = exchange(lists, (parity,))
        if first_step:
            halos[ODD] = halos[EVEN] = exchange(lists, (ODD, EVEN))
        arrived = {parity: (waves[parity], *halos[parity]) for parity in (ODD, EVEN)}
        echoes.append(echo)

    tick = ticks - 1
    results = []
    result_types = (
        jax.ShapeDtypeStruct((ticks, 1, blocks, points, columns), WAVE),
        jax.ShapeDtypeStruct((1, blocks, points, columns), jnp.float32),
    )
    for parity in (ODD, EVEN):
        results = grouped_call(
            functools.partial(last_kernel, parity, tick),
            [*fixed, *arrived[parity], echoes],
            result_types,
            [ANY_SPEC] * 2,
            list(results),
            scratch_shapes=[
                buffer_type,
                pltpu.VMEM((blocks, points, columns), WAVE),
                pltpu.VMEM((blocks, points, columns), jnp.float32),
                pltpu.SemaphoreType.DMA((tick,)),
                pltpu.SemaphoreType.DMA((blocks,)),
                pltpu.SemaphoreType.DMA((blocks,)),
            ],
            compiler_params=params,
            cost_estimate=tick_cost,
            name="last_tick" + ("_odd" if parity else "_even"),
        )
    return tuple(results)


def solution(mesh):
    return jax.shard_map(
        per_device,
        mesh=mesh,
        in_specs=(
            P("depth", "lat", None, None),
            P(None, "lat", None, None),
            P("depth", "lat", None, None, None, None),
            P("depth", "lat", None),
            P("depth", "lat", None),
            P("lat", None, None),
            P("lat", None),
            P("lat", None),
        ),
        out_specs=(P(None, "depth", "lat", None, None), P("depth", "lat", None, None)),
        check_vma=False,
    )
```

```python
import functools

import jax
import jax.numpy as jnp
from jax import lax
from jax.experimental import pallas as pl
from jax.experimental.pallas import tpu as pltpu
from jax.sharding import PartitionSpec as P

WAVE = jnp.bfloat16
SMEM_SPEC = pl.BlockSpec(memory_space=pltpu.SMEM)
VMEM_SPEC = pl.BlockSpec(memory_space=pltpu.VMEM)
ANY_SPEC = pl.BlockSpec(memory_space=pl.ANY)
VMEM_LIMIT = 8 * 1024 * 1024
LOWER, UPPER = 0, 1


def in_vmem(array):
    return pltpu.with_memory_space_constraint(array, pltpu.VMEM)


def in_hbm(array):
    return pltpu.with_memory_space_constraint(array, pltpu.HBM)


def write_lists(tile, plan_ref, blocks_ref, lists):
    points = blocks_ref.shape[1]
    listed = lists[0].shape[0] // points
    parity = lax.rem(tile, 2)
    for list_ref, side in zip(lists, (UPPER - parity, parity)):
        count = plan_ref[2 * listed + side]
        for slot in range(listed):
            live = slot < count

            @pl.when(live)
            def _():
                list_ref[slot * points : (slot + 1) * points] = blocks_ref[
                    plan_ref[side * listed + slot]
                ]

            @pl.when(jnp.logical_not(live))
            def _():
                list_ref[slot * points : (slot + 1) * points] = jnp.zeros(
                    blocks_ref.shape[1:], list_ref.dtype
                )


def prepare_kernel(
    ids_hbm, count_hbm, pattern_hbm, inflow_hbm, plan_ref, wave_ref, first_ref, second_ref,
    ids, count, pattern, landed, small_sems, sems,
):
    blocks = wave_ref.shape[0]
    small = [
        pltpu.make_async_copy(source, target, small_sems.at[i])
        for i, (source, target) in enumerate(
            ((ids_hbm, ids), (count_hbm, count), (pattern_hbm, pattern))
        )
    ]
    large = [
        pltpu.make_async_copy(inflow_hbm.at[0, b], landed.at[b], sems.at[b]) for b in range(blocks)
    ]
    for copy in small + large:
        copy.start()
    for copy in small:
        copy.wait()
    _, sides, listed = ids.shape
    taken = pattern.shape[1]
    for side in range(sides):
        for slot in range(listed):
            plan_ref[side * listed + slot] = ids[0, side, slot]
        plan_ref[sides * listed + side] = count[0, side]
    for b in range(blocks):
        for k in range(taken):
            plan_ref[sides * (listed + 1) + b * taken + k] = pattern[b, k]
    for b, copy in enumerate(large):
        copy.wait()
        wave_ref[b] = landed[b].astype(wave_ref.dtype)
    write_lists(lax.axis_index("lat"), plan_ref, wave_ref, (first_ref, second_ref))


def load_kernel(
    ops_hbm, source_hbm, pass_hbm, reflect_hbm, after_ref,
    ops_ref, source_ref, pass_ref, reflect_ref, pass_rows, reflect_rows, sems,
):
    del after_ref
    copies = [
        pltpu.make_async_copy(source, target, sems.at[i])
        for i, (source, target) in enumerate(
            (
                (pass_hbm, pass_rows),
                (reflect_hbm, reflect_rows),
                (ops_hbm, ops_ref),
                (source_hbm, source_ref),
            )
        )
    ]
    for copy in copies:
        copy.start()
    for copy, rows, columns_ref in zip(copies, (pass_rows, reflect_rows), (pass_ref, reflect_ref)):
        copy.wait()
        for b in range(columns_ref.shape[0]):
            row = rows[0, pl.ds(b, 1), :]
            columns_ref[b] = jnp.broadcast_to(row, columns_ref.shape[1:]).T
    for copy in copies[2:]:
        copy.wait()


def fill_buffer(section, tick, source_ref, wave_refs, first_ref, second_ref, buffer):
    blocks, points = source_ref.shape[1:3]
    listed = (buffer.shape[0] - blocks) // 2

    def fill(start, ref):
        if len(ref.shape) == 2:
            count = min(ref.shape[0] // points, blocks)
            part = ref[: count * points].reshape(count, points, -1)
        else:
            part = ref[0] if len(ref.shape) == 4 else ref[...]
        buffer[pl.ds(start, part.shape[0])] = part
        return start + part.shape[0]

    def fill_wave():
        start = 0
        for wave_ref in wave_refs:
            start = fill(start, wave_ref)

    if tick == 0:
        fill_wave()
    else:
        pl.when(section != 0)(fill_wave)

        @pl.when(section == 0)
        def _():
            buffer[:blocks] = source_ref[tick - 1]

    parity = lax.rem(lax.axis_index("lat"), 2)
    fill(blocks + (1 - parity) * listed, first_ref)
    fill(blocks + parity * listed, second_ref)


def extrapolate_block(plan_ref, pattern_start, ops_ref, buffer, b):
    taken = ops_ref.shape[2]
    points = ops_ref.shape[5]
    left = jnp.concatenate(
        [ops_ref[0, b, k].reshape(2 * points, points) for k in range(taken)], axis=1
    )
    right = jnp.concatenate(
        [buffer[plan_ref[pattern_start + b * taken + k]] for k in range(taken)], axis=0
    )
    products = jnp.dot(left, right, preferred_element_type=jnp.float32)
    half = products.shape[1] // 2
    real_part = products[:points, :half] - products[points:, half:]
    imag_part = products[:points, half:] + products[points:, :half]
    return real_part, imag_part


def ids_of(plan_ref, ops_ref):
    return (plan_ref.shape[0] - ops_ref.shape[1] * ops_ref.shape[2]) // 2 - 1


def acts(section, parity):
    return lax.rem(section, 2) == parity


def tick_kernel(
    parity, tick, sections, plan_ref, ops_ref, source_ref, pass_ref, reflect_ref,
    wave_refs, first_in_ref, second_in_ref, known_refs, out_refs, buffer, onward,
):
    del known_refs
    echo_ref, first_ref, second_ref, *onward_refs = out_refs
    section = lax.axis_index("depth")
    tile = lax.axis_index("lat")
    listed = ids_of(plan_ref, ops_ref)

    @pl.when(acts(section, parity))
    def _():
        fill_buffer(section, tick, source_ref, wave_refs, first_in_ref, second_in_ref, buffer)
        for b in range(echo_ref.shape[0]):
            parts = extrapolate_block(plan_ref, 2 * (listed + 1), ops_ref, buffer, b)
            for i, part in enumerate(parts):
                cols = pl.ds(i * part.shape[1], part.shape[1])
                onward[b, :, cols] = (pass_ref[b] * part).astype(onward.dtype)
                echo_ref[b, :, cols] = (reflect_ref[b] * part).astype(echo_ref.dtype)
        start = 0
        for onward_ref in onward_refs:
            if len(onward_ref.shape) == 2:
                rows = onward.shape[0] * onward.shape[1]
                onward_ref[:rows] = onward[...].reshape(rows, onward.shape[2])
            else:
                slot = onward_ref if len(onward_ref.shape) == 3 else onward_ref.at[1]
                slot[...] = onward[start : start + slot.shape[0]]
                start += slot.shape[0]

        @pl.when(section != sections - 1)
        def _():
            write_lists(tile, plan_ref, onward, (first_ref, second_ref))

        @pl.when(section == sections - 1)
        def _():
            write_lists(tile, plan_ref, source_ref.at[tick], (first_ref, second_ref))


def last_kernel(
    parity, tick, plan_ref, ops_ref, source_ref, pass_ref, reflect_ref,
    wave_refs, first_in_ref, second_in_ref, earlier, known_refs, out_refs,
    buffer, echo, leaving, early_sems, echo_sems, leave_sems,
):
    del known_refs
    reflected_ref, transmitted_ref = out_refs
    section = lax.axis_index("depth")
    listed = ids_of(plan_ref, ops_ref)

    @pl.when(acts(section, parity))
    def _():
        copies = [
            pltpu.make_async_copy(earlier[t], reflected_ref.at[t, 0], early_sems.at[t])
            for t in range(tick)
        ]
        for copy in copies:
            copy.start()
        fill_buffer(section, tick, source_ref, wave_refs, first_in_ref, second_in_ref, buffer)
        for b in range(echo.shape[0]):
            parts = extrapolate_block(plan_ref, 2 * (listed + 1), ops_ref, buffer, b)
            for i, part in enumerate(parts):
                cols = pl.ds(i * part.shape[1], part.shape[1])
                leaving[b, :, cols] = pass_ref[b] * part
                echo[b, :, cols] = (reflect_ref[b] * part).astype(echo.dtype)
            for copy in (
                pltpu.make_async_copy(leaving.at[b], transmitted_ref.at[0, b], leave_sems.at[b]),
                pltpu.make_async_copy(echo.at[b], reflected_ref.at[tick, 0, b], echo_sems.at[b]),
            ):
                copy.start()
                copies.append(copy)
        for copy in copies:
            copy.wait()


def grouped_call(kernel, groups, outs, out_specs, known, **options):
    flat = [array for group in groups for array in (group if isinstance(group, list) else [group])]

    def body(*refs):
        refs = list(refs)
        take = lambda count: [refs.pop(0) for _ in range(count)]
        inputs = [take(len(g)) if isinstance(g, list) else refs.pop(0) for g in groups]
        kernel(*inputs, take(len(known)), take(len(outs)), *refs)

    return pl.pallas_call(
        body,
        out_shape=tuple(outs),
        in_specs=[SMEM_SPEC] + [VMEM_SPEC] * (len(flat) - 1) + list(out_specs[: len(known)]),
        out_specs=tuple(out_specs),
        input_output_aliases={len(flat) + i: i for i in range(len(known))},
        **options,
    )(flat[0], *map(in_vmem, flat[1:]), *known)


def neighbour(j, turn, tiles):
    to = j + (1 if (j + turn) % 2 == 0 else -1)
    return to if 0 <= to < tiles else None


def swap_routes(sections, tiles):
    routes = []
    for turn in (0, 1):
        route = []
        for s in range(sections):
            for j in range(tiles):
                to = neighbour(j, turn, tiles)
                end = ((s ^ 1) * tiles + j) if to is None else (s * tiles + to)
                route.append((s * tiles + j, end))
        routes.append(route)
    return routes


def halo_routes(sections, tiles, senders):
    routes = []
    for turn in (0, 1):
        route = []
        for s in range(sections):
            for j in range(tiles):
                to = neighbour(j, turn, tiles)
                real = to is not None and s % 2 in senders
                end = (s + 1) % sections * tiles + to if real else (s ^ 1) * tiles + j
                route.append((s * tiles + j, end))
        routes.append(route)
    return routes


def per_device(
    inflow, source, operators, transmission, reflectivity, send_ids, send_count, pattern
):
    sections, tiles = lax.axis_size("depth"), lax.axis_size("lat")
    ticks = source.shape[0] + 1
    _, blocks, points, columns = inflow.shape
    listed = send_ids.shape[-1]
    taken = operators.shape[2]
    wave_type = pltpu.VMEM((blocks, points, columns), WAVE)
    list_type = pltpu.VMEM((listed * points, columns), WAVE)
    params = pltpu.CompilerParams(vmem_limit_bytes=VMEM_LIMIT)
    tick_cost = pl.CostEstimate(
        flops=0,
        bytes_accessed=0,
        transcendentals=0,
    )
    both = ("depth", "lat")
    deeper = [(s, (s + 1) % sections) for s in range(sections)]

    plan, wave, first, second = pl.pallas_call(
        prepare_kernel,
        out_shape=(
            pltpu.SMEM((2 * (listed + 1) + blocks * taken,), jnp.int32),
            wave_type,
            list_type,
            list_type,
        ),
        in_specs=[ANY_SPEC] * 4,
        out_specs=(SMEM_SPEC,) + (VMEM_SPEC,) * 3,
        scratch_shapes=[
            pltpu.SMEM(send_ids.shape, jnp.int32),
            pltpu.SMEM(send_count.shape, jnp.int32),
            pltpu.SMEM(pattern.shape, jnp.int32),
            pltpu.VMEM((blocks, points, columns), inflow.dtype),
            pltpu.SemaphoreType.DMA((3,)),
            pltpu.SemaphoreType.DMA((blocks,)),
        ],
        compiler_params=params,
        cost_estimate=pl.CostEstimate(
            flops=inflow.size, bytes_accessed=8 * inflow.size, transcendentals=0
        ),
        name="prepare",
    )(*map(in_hbm, (send_ids, send_count, pattern, inflow)))
    loaded_first = first
    routes = swap_routes(sections, tiles)
    first = lax.ppermute(first, both, routes[0])
    second = lax.ppermute(second, both, routes[1])

    column_type = pltpu.VMEM((blocks, points, columns // 2), jnp.float32)
    fixed = pl.pallas_call(
        load_kernel,
        out_shape=(
            pltpu.VMEM(operators.shape, operators.dtype),
            pltpu.VMEM(source.shape, source.dtype),
            column_type,
            column_type,
        ),
        in_specs=[ANY_SPEC] * 4 + [VMEM_SPEC],
        out_specs=(VMEM_SPEC,) * 4,
        scratch_shapes=[
            pltpu.VMEM(transmission.shape, transmission.dtype),
            pltpu.VMEM(reflectivity.shape, reflectivity.dtype),
            pltpu.SemaphoreType.DMA((4,)),
        ],
        compiler_params=params,
        cost_estimate=pl.CostEstimate(
            flops=0, bytes_accessed=4 * (operators.size + source.size), transcendentals=0
        ),
        name="load",
    )(*map(in_hbm, (operators, source, transmission, reflectivity)), in_vmem(loaded_first))
    fixed = [plan, *fixed]

    buffer_type = pltpu.VMEM((blocks + 2 * listed, points, columns), WAVE)

    ODD, EVEN = 1, 0
    crossing = [(s, (s + 1) % sections) for s in range(sections)]
    inside = [(s, s ^ 1) for s in range(sections)]
    pairs = [[s, s + 1] for s in range(0, sections, 2)]
    pair_type = pltpu.VMEM((2, blocks, points, columns), WAVE)
    part_types = [pltpu.VMEM((blocks // 2, points, columns), WAVE)] * 2
    half_types = [pltpu.VMEM((n, points, columns), WAVE) for n in (blocks // 2, blocks - blocks // 2)]

    def lists_of(extra):
        return [pltpu.VMEM((listed * points + extra, columns), WAVE)] * 2

    def exchange(lists, senders):
        routes = halo_routes(sections, tiles, senders)
        return [lax.ppermute(a, both, route) for a, route in zip(lists, routes)]

    arrived = {parity: ([wave], first, second) for parity in (ODD, EVEN)}
    echoes = []
    for tick in range(ticks - 1):
        first_step, last_step = tick == 0, tick == ticks - 2
        known = []
        waves, halos = {}, {}
        for parity in (ODD, EVEN):
            if first_step:
                extra = 0
            elif last_step:
                extra = 16 if parity == ODD else 0
            else:
                extra = 0 if parity == ODD else 16
            if parity == ODD:
                long = 0 if first_step or last_step else 16
                to_next = [pltpu.VMEM((blocks * points + long, columns), WAVE)]
            else:
                to_next = [pair_type] if last_step else half_types if first_step else part_types
            outs = [wave_type, *lists_of(extra), *to_next]
            echo, *lists = grouped_call(
                functools.partial(tick_kernel, parity, tick, sections),
                [*fixed, *arrived[parity]],
                outs,
                [VMEM_SPEC] * len(outs),
                [in_vmem(a) for a in known],
                scratch_shapes=[buffer_type, pltpu.VMEM(wave_type.shape, WAVE)],
                compiler_params=params,
                cost_estimate=tick_cost,
                name=f"tick{tick}" + ("_odd" if parity else "_even"),
            )
            lists, onward = lists[:2], lists[2:]
            known = [echo, *lists] if first_step else [echo]
            if parity == ODD:
                waves[EVEN] = [lax.ppermute(onward[0], "depth", crossing)]
            elif last_step:
                waves[ODD] = [lax.all_to_all(onward[0], "depth", 0, 0, axis_index_groups=pairs)]
            else:
                waves[ODD] = [lax.ppermute(a, "depth", inside) for a in onward]
            if not first_step:
                halos[1 - parity] = exchange(lists, (parity,))
        if first_step:
            halos[ODD] = halos[EVEN] = exchange(lists, (ODD, EVEN))
        arrived = {parity: (waves[parity], *halos[parity]) for parity in (ODD, EVEN)}
        echoes.append(echo)

    tick = ticks - 1
    results = []
    result_types = (
        jax.ShapeDtypeStruct((ticks, 1, blocks, points, columns), WAVE),
        jax.ShapeDtypeStruct((1, blocks, points, columns), jnp.float32),
    )
    for parity in (ODD, EVEN):
        results = grouped_call(
            functools.partial(last_kernel, parity, tick),
            [*fixed, *arrived[parity], echoes],
            result_types,
            [ANY_SPEC] * 2,
            list(results),
            scratch_shapes=[
                buffer_type,
                pltpu.VMEM((blocks, points, columns), WAVE),
                pltpu.VMEM((blocks, points, columns), jnp.float32),
                pltpu.SemaphoreType.DMA((tick,)),
                pltpu.SemaphoreType.DMA((blocks,)),
                pltpu.SemaphoreType.DMA((blocks,)),
            ],
            compiler_params=params,
            cost_estimate=tick_cost,
            name="last_tick" + ("_odd" if parity else "_even"),
        )
    return tuple(results)


def solution(mesh):
    return jax.shard_map(
        per_device,
        mesh=mesh,
        in_specs=(
            P("depth", "lat", None, None),
            P(None, "lat", None, None),
            P("depth", "lat", None, None, None, None),
            P("depth", "lat", None),
            P("depth", "lat", None),
            P("lat", None, None),
            P("lat", None),
            P("lat", None),
        ),
        out_specs=(P(None, "depth", "lat", None, None), P("depth", "lat", None, None)),
        check_vma=False,
    )
```

```python
import functools

import jax
import jax.numpy as jnp
from jax import lax
from jax.experimental import pallas as pl
from jax.experimental.pallas import tpu as pltpu
from jax.sharding import PartitionSpec as P

WAVE = jnp.bfloat16
SMEM_SPEC = pl.BlockSpec(memory_space=pltpu.SMEM)
VMEM_SPEC = pl.BlockSpec(memory_space=pltpu.VMEM)
ANY_SPEC = pl.BlockSpec(memory_space=pl.ANY)
VMEM_LIMIT = 8 * 1024 * 1024
LOWER, UPPER = 0, 1


def in_vmem(array):
    return pltpu.with_memory_space_constraint(array, pltpu.VMEM)


def in_hbm(array):
    return pltpu.with_memory_space_constraint(array, pltpu.HBM)


def write_lists(tile, plan_ref, blocks_ref, lists):
    points = blocks_ref.shape[1]
    listed = lists[0].shape[0] // points
    parity = lax.rem(tile, 2)
    for list_ref, side in zip(lists, (UPPER - parity, parity)):
        count = plan_ref[2 * listed + side]
        for slot in range(listed):
            live = slot < count

            @pl.when(live)
            def _():
                list_ref[slot * points : (slot + 1) * points] = blocks_ref[
                    plan_ref[side * listed + slot]
                ]

            @pl.when(jnp.logical_not(live))
            def _():
                list_ref[slot * points : (slot + 1) * points] = jnp.zeros(
                    blocks_ref.shape[1:], list_ref.dtype
                )


def start_rows(hbm_refs, rows_refs, sems):
    copies = [
        pltpu.make_async_copy(source, target, sems.at[i])
        for i, (source, target) in enumerate(zip(hbm_refs, rows_refs))
    ]
    for copy in copies:
        copy.start()
    return copies


def write_columns(copies, rows_refs, columns_refs):
    for copy, rows, columns_ref in zip(copies, rows_refs, columns_refs):
        copy.wait()
        for b in range(columns_ref.shape[0]):
            row = rows[0, pl.ds(b, 1), :]
            columns_ref[b] = jnp.broadcast_to(row, columns_ref.shape[1:]).T


def prepare_kernel(
    ids_hbm, count_hbm, pattern_hbm, inflow_hbm, pass_hbm, reflect_hbm,
    plan_ref, wave_ref, first_ref, second_ref, pass_ref, reflect_ref,
    ids, count, pattern, landed, small_sems, sems, pass_rows, reflect_rows, rows_sems,
):
    blocks = wave_ref.shape[0]
    small = [
        pltpu.make_async_copy(source, target, small_sems.at[i])
        for i, (source, target) in enumerate(
            ((ids_hbm, ids), (count_hbm, count), (pattern_hbm, pattern))
        )
    ]
    large = [
        pltpu.make_async_copy(inflow_hbm.at[0, b], landed.at[b], sems.at[b]) for b in range(blocks)
    ]
    for copy in small + large:
        copy.start()
    for copy in small:
        copy.wait()
    _, sides, listed = ids.shape
    taken = pattern.shape[1]
    for side in range(sides):
        for slot in range(listed):
            plan_ref[side * listed + slot] = ids[0, side, slot]
        plan_ref[sides * listed + side] = count[0, side]
    for b in range(blocks):
        for k in range(taken):
            plan_ref[sides * (listed + 1) + b * taken + k] = pattern[b, k]
    for b, copy in enumerate(large):
        copy.wait()
        wave_ref[b] = landed[b].astype(wave_ref.dtype)
    write_lists(lax.axis_index("lat"), plan_ref, wave_ref, (first_ref, second_ref))

    @pl.when(lax.rem(lax.axis_index("depth"), 2) == 1)
    def _():
        rows = (pass_rows, reflect_rows)
        copies = start_rows((pass_hbm, reflect_hbm), rows, rows_sems)
        write_columns(copies, rows, (pass_ref, reflect_ref))


def load_kernel(
    ops_hbm, source_hbm, pass_hbm, reflect_hbm, known_pass_ref, known_reflect_ref,
    ops_ref, source_ref, pass_ref, reflect_ref, pass_rows, reflect_rows, rows_sems, sems,
):
    del known_pass_ref, known_reflect_ref
    copies = start_rows((ops_hbm, source_hbm), (ops_ref, source_ref), sems)

    @pl.when(lax.rem(lax.axis_index("depth"), 2) == 0)
    def _():
        rows = (pass_rows, reflect_rows)
        small = start_rows((pass_hbm, reflect_hbm), rows, rows_sems)
        write_columns(small, rows, (pass_ref, reflect_ref))

    for copy in copies:
        copy.wait()


def fill_buffer(section, tick, source_ref, wave_refs, first_ref, second_ref, buffer):
    blocks, points = source_ref.shape[1:3]
    listed = (buffer.shape[0] - blocks) // 2

    def fill(start, ref):
        if len(ref.shape) == 2:
            count = min(ref.shape[0] // points, blocks)
            part = ref[: count * points].reshape(count, points, -1)
        else:
            part = ref[0] if len(ref.shape) == 4 else ref[...]
        buffer[pl.ds(start, part.shape[0])] = part
        return start + part.shape[0]

    def fill_wave():
        start = 0
        for wave_ref in wave_refs:
            start = fill(start, wave_ref)

    if tick == 0:
        fill_wave()
    else:
        pl.when(section != 0)(fill_wave)

        @pl.when(section == 0)
        def _():
            buffer[:blocks] = source_ref[tick - 1]

    parity = lax.rem(lax.axis_index("lat"), 2)
    fill(blocks + (1 - parity) * listed, first_ref)
    fill(blocks + parity * listed, second_ref)


def extrapolate_block(plan_ref, pattern_start, ops_ref, buffer, b):
    taken = ops_ref.shape[2]
    points = ops_ref.shape[5]
    left = jnp.concatenate(
        [ops_ref[0, b, k].reshape(2 * points, points) for k in range(taken)], axis=1
    )
    right = jnp.concatenate(
        [buffer[plan_ref[pattern_start + b * taken + k]] for k in range(taken)], axis=0
    )
    products = jnp.dot(left, right, preferred_element_type=jnp.float32)
    half = products.shape[1] // 2
    real_part = products[:points, :half] - products[points:, half:]
    imag_part = products[:points, half:] + products[points:, :half]
    return real_part, imag_part


def ids_of(plan_ref, ops_ref):
    return (plan_ref.shape[0] - ops_ref.shape[1] * ops_ref.shape[2]) // 2 - 1


def acts(section, parity):
    return lax.rem(section, 2) == parity


def tick_kernel(
    parity, tick, sections, plan_ref, ops_ref, source_ref, pass_ref, reflect_ref,
    wave_refs, first_in_ref, second_in_ref, known_refs, out_refs, buffer, onward,
):
    del known_refs
    echo_ref, first_ref, second_ref, *onward_refs = out_refs
    section = lax.axis_index("depth")
    tile = lax.axis_index("lat")
    listed = ids_of(plan_ref, ops_ref)

    @pl.when(acts(section, parity))
    def _():
        fill_buffer(section, tick, source_ref, wave_refs, first_in_ref, second_in_ref, buffer)
        for b in range(echo_ref.shape[0]):
            parts = extrapolate_block(plan_ref, 2 * (listed + 1), ops_ref, buffer, b)
            for i, part in enumerate(parts):
                cols = pl.ds(i * part.shape[1], part.shape[1])
                onward[b, :, cols] = (pass_ref[b] * part).astype(onward.dtype)
                echo_ref[b, :, cols] = (reflect_ref[b] * part).astype(echo_ref.dtype)
        start = 0
        for onward_ref in onward_refs:
            if len(onward_ref.shape) == 2:
                rows = onward.shape[0] * onward.shape[1]
                onward_ref[:rows] = onward[...].reshape(rows, onward.shape[2])
            else:
                slot = onward_ref if len(onward_ref.shape) == 3 else onward_ref.at[1]
                slot[...] = onward[start : start + slot.shape[0]]
                start += slot.shape[0]

        @pl.when(section != sections - 1)
        def _():
            write_lists(tile, plan_ref, onward, (first_ref, second_ref))

        @pl.when(section == sections - 1)
        def _():
            write_lists(tile, plan_ref, source_ref.at[tick], (first_ref, second_ref))


def last_kernel(
    parity, tick, plan_ref, ops_ref, source_ref, pass_ref, reflect_ref,
    wave_refs, first_in_ref, second_in_ref, earlier, known_refs, out_refs,
    buffer, echo, leaving, early_sems, echo_sems, leave_sems,
):
    del known_refs
    reflected_ref, transmitted_ref = out_refs
    section = lax.axis_index("depth")
    listed = ids_of(plan_ref, ops_ref)

    @pl.when(acts(section, parity))
    def _():
        copies = [
            pltpu.make_async_copy(earlier[t], reflected_ref.at[t, 0], early_sems.at[t])
            for t in range(tick)
        ]
        for copy in copies:
            copy.start()
        fill_buffer(section, tick, source_ref, wave_refs, first_in_ref, second_in_ref, buffer)
        for b in range(echo.shape[0]):
            parts = extrapolate_block(plan_ref, 2 * (listed + 1), ops_ref, buffer, b)
            for i, part in enumerate(parts):
                cols = pl.ds(i * part.shape[1], part.shape[1])
                leaving[b, :, cols] = pass_ref[b] * part
                echo[b, :, cols] = (reflect_ref[b] * part).astype(echo.dtype)
            for copy in (
                pltpu.make_async_copy(leaving.at[b], transmitted_ref.at[0, b], leave_sems.at[b]),
                pltpu.make_async_copy(echo.at[b], reflected_ref.at[tick, 0, b], echo_sems.at[b]),
            ):
                copy.start()
                copies.append(copy)
        for copy in copies:
            copy.wait()


def grouped_call(kernel, groups, outs, out_specs, known, **options):
    flat = [array for group in groups for array in (group if isinstance(group, list) else [group])]

    def body(*refs):
        refs = list(refs)
        take = lambda count: [refs.pop(0) for _ in range(count)]
        inputs = [take(len(g)) if isinstance(g, list) else refs.pop(0) for g in groups]
        kernel(*inputs, take(len(known)), take(len(outs)), *refs)

    return pl.pallas_call(
        body,
        out_shape=tuple(outs),
        in_specs=[SMEM_SPEC] + [VMEM_SPEC] * (len(flat) - 1) + list(out_specs[: len(known)]),
        out_specs=tuple(out_specs),
        input_output_aliases={len(flat) + i: i for i in range(len(known))},
        **options,
    )(flat[0], *map(in_vmem, flat[1:]), *known)


def neighbour(j, turn, tiles):
    to = j + (1 if (j + turn) % 2 == 0 else -1)
    return to if 0 <= to < tiles else None


def swap_routes(sections, tiles):
    routes = []
    for turn in (0, 1):
        route = []
        for s in range(sections):
            for j in range(tiles):
                to = neighbour(j, turn, tiles)
                end = ((s ^ 1) * tiles + j) if to is None else (s * tiles + to)
                route.append((s * tiles + j, end))
        routes.append(route)
    return routes


def halo_routes(sections, tiles, senders):
    routes = []
    for turn in (0, 1):
        route = []
        for s in range(sections):
            for j in range(tiles):
                to = neighbour(j, turn, tiles)
                real = to is not None and s % 2 in senders
                end = (s + 1) % sections * tiles + to if real else (s ^ 1) * tiles + j
                route.append((s * tiles + j, end))
        routes.append(route)
    return routes


def per_device(
    inflow, source, operators, transmission, reflectivity, send_ids, send_count, pattern
):
    sections, tiles = lax.axis_size("depth"), lax.axis_size("lat")
    ticks = source.shape[0] + 1
    _, blocks, points, columns = inflow.shape
    listed = send_ids.shape[-1]
    taken = operators.shape[2]
    wave_type = pltpu.VMEM((blocks, points, columns), WAVE)
    list_type = pltpu.VMEM((listed * points, columns), WAVE)
    params = pltpu.CompilerParams(vmem_limit_bytes=VMEM_LIMIT)
    tick_cost = pl.CostEstimate(
        flops=0,
        bytes_accessed=0,
        transcendentals=0,
    )
    both = ("depth", "lat")
    deeper = [(s, (s + 1) % sections) for s in range(sections)]

    column_type = pltpu.VMEM((blocks, points, columns // 2), jnp.float32)
    rows_scratch = [
        pltpu.VMEM(transmission.shape, transmission.dtype),
        pltpu.VMEM(reflectivity.shape, reflectivity.dtype),
        pltpu.SemaphoreType.DMA((2,)),
    ]
    coefficients = [in_hbm(transmission), in_hbm(reflectivity)]
    plan, wave, first, second, *coefficient_columns = pl.pallas_call(
        prepare_kernel,
        out_shape=(
            pltpu.SMEM((2 * (listed + 1) + blocks * taken,), jnp.int32),
            wave_type,
            list_type,
            list_type,
            column_type,
            column_type,
        ),
        in_specs=[ANY_SPEC] * 6,
        out_specs=(SMEM_SPEC,) + (VMEM_SPEC,) * 5,
        scratch_shapes=[
            pltpu.SMEM(send_ids.shape, jnp.int32),
            pltpu.SMEM(send_count.shape, jnp.int32),
            pltpu.SMEM(pattern.shape, jnp.int32),
            pltpu.VMEM((blocks, points, columns), inflow.dtype),
            pltpu.SemaphoreType.DMA((3,)),
            pltpu.SemaphoreType.DMA((blocks,)),
            *rows_scratch,
        ],
        compiler_params=params,
        cost_estimate=pl.CostEstimate(
            flops=inflow.size, bytes_accessed=8 * inflow.size, transcendentals=0
        ),
        name="prepare",
    )(*map(in_hbm, (send_ids, send_count, pattern, inflow)), *coefficients)
    routes = swap_routes(sections, tiles)
    first = lax.ppermute(first, both, routes[0])
    second = lax.ppermute(second, both, routes[1])

    fixed = pl.pallas_call(
        load_kernel,
        out_shape=(
            pltpu.VMEM(operators.shape, operators.dtype),
            pltpu.VMEM(source.shape, source.dtype),
            column_type,
            column_type,
        ),
        in_specs=[ANY_SPEC] * 4 + [VMEM_SPEC] * 2,
        out_specs=(VMEM_SPEC,) * 4,
        input_output_aliases={4: 2, 5: 3},
        scratch_shapes=[*rows_scratch, pltpu.SemaphoreType.DMA((2,))],
        compiler_params=params,
        cost_estimate=pl.CostEstimate(
            flops=0, bytes_accessed=4 * (operators.size + source.size), transcendentals=0
        ),
        name="load",
    )(in_hbm(operators), in_hbm(source), *coefficients, *map(in_vmem, coefficient_columns))
    fixed = [plan, *fixed]

    buffer_type = pltpu.VMEM((blocks + 2 * listed, points, columns), WAVE)

    ODD, EVEN = 1, 0
    crossing = [(s, (s + 1) % sections) for s in range(sections)]
    inside = [(s, s ^ 1) for s in range(sections)]
    pairs = [[s, s + 1] for s in range(0, sections, 2)]
    pair_type = pltpu.VMEM((2, blocks, points, columns), WAVE)
    part_types = [pltpu.VMEM((blocks // 2, points, columns), WAVE)] * 2
    half_types = [pltpu.VMEM((n, points, columns), WAVE) for n in (blocks // 2, blocks - blocks // 2)]

    def lists_of(extra):
        return [pltpu.VMEM((listed * points + extra, columns), WAVE)] * 2

    def exchange(lists, senders):
        routes = halo_routes(sections, tiles, senders)
        return [lax.ppermute(a, both, route) for a, route in zip(lists, routes)]

    arrived = {parity: ([wave], first, second) for parity in (ODD, EVEN)}
    echoes = []
    for tick in range(ticks - 1):
        first_step, last_step = tick == 0, tick == ticks - 2
        known = []
        waves, halos = {}, {}
        for parity in (ODD, EVEN):
            if first_step:
                extra = 0
            elif last_step:
                extra = 16 if parity == ODD else 0
            else:
                extra = 0 if parity == ODD else 16
            if parity == ODD:
                long = 0 if first_step or last_step else 16
                to_next = [pltpu.VMEM((blocks * points + long, columns), WAVE)]
            else:
                to_next = [pair_type] if last_step else half_types if first_step else part_types
            outs = [wave_type, *lists_of(extra), *to_next]
            echo, *lists = grouped_call(
                functools.partial(tick_kernel, parity, tick, sections),
                [*fixed, *arrived[parity]],
                outs,
                [VMEM_SPEC] * len(outs),
                [in_vmem(a) for a in known],
                scratch_shapes=[buffer_type, pltpu.VMEM(wave_type.shape, WAVE)],
                compiler_params=params,
                cost_estimate=tick_cost,
                name=f"tick{tick}" + ("_odd" if parity else "_even"),
            )
            lists, onward = lists[:2], lists[2:]
            known = [echo, *lists] if first_step else [echo]
            if parity == ODD:
                waves[EVEN] = [lax.ppermute(onward[0], "depth", crossing)]
            elif last_step:
                waves[ODD] = [lax.all_to_all(onward[0], "depth", 0, 0, axis_index_groups=pairs)]
            else:
                waves[ODD] = [lax.ppermute(a, "depth", inside) for a in onward]
            if not first_step:
                halos[1 - parity] = exchange(lists, (parity,))
        if first_step:
            halos[ODD] = halos[EVEN] = exchange(lists, (ODD, EVEN))
        arrived = {parity: (waves[parity], *halos[parity]) for parity in (ODD, EVEN)}
        echoes.append(echo)

    tick = ticks - 1
    results = []
    result_types = (
        jax.ShapeDtypeStruct((ticks, 1, blocks, points, columns), WAVE),
        jax.ShapeDtypeStruct((1, blocks, points, columns), jnp.float32),
    )
    for parity in (ODD, EVEN):
        results = grouped_call(
            functools.partial(last_kernel, parity, tick),
            [*fixed, *arrived[parity], echoes],
            result_types,
            [ANY_SPEC] * 2,
            list(results),
            scratch_shapes=[
                buffer_type,
                pltpu.VMEM((blocks, points, columns), WAVE),
                pltpu.VMEM((blocks, points, columns), jnp.float32),
                pltpu.SemaphoreType.DMA((tick,)),
                pltpu.SemaphoreType.DMA((blocks,)),
                pltpu.SemaphoreType.DMA((blocks,)),
            ],
            compiler_params=params,
            cost_estimate=tick_cost,
            name="last_tick" + ("_odd" if parity else "_even"),
        )
    return tuple(results)


def solution(mesh):
    return jax.shard_map(
        per_device,
        mesh=mesh,
        in_specs=(
            P("depth", "lat", None, None),
            P(None, "lat", None, None),
            P("depth", "lat", None, None, None, None),
            P("depth", "lat", None),
            P("depth", "lat", None),
            P("lat", None, None),
            P("lat", None),
            P("lat", None),
        ),
        out_specs=(P(None, "depth", "lat", None, None), P("depth", "lat", None, None)),
        check_vma=False,
    )
```

```python
import functools

import jax
import jax.numpy as jnp
from jax import lax
from jax.experimental import pallas as pl
from jax.experimental.pallas import tpu as pltpu
from jax.sharding import PartitionSpec as P

WAVE = jnp.bfloat16
SMEM_SPEC = pl.BlockSpec(memory_space=pltpu.SMEM)
VMEM_SPEC = pl.BlockSpec(memory_space=pltpu.VMEM)
ANY_SPEC = pl.BlockSpec(memory_space=pl.ANY)
VMEM_LIMIT = 8 * 1024 * 1024
LOWER, UPPER = 0, 1


def in_vmem(array):
    return pltpu.with_memory_space_constraint(array, pltpu.VMEM)


def in_hbm(array):
    return pltpu.with_memory_space_constraint(array, pltpu.HBM)


def write_lists(tile, plan_ref, blocks_ref, lists):
    points = blocks_ref.shape[1]
    listed = lists[0].shape[0] // points
    parity = lax.rem(tile, 2)
    for list_ref, side in zip(lists, (UPPER - parity, parity)):
        count = plan_ref[2 * listed + side]
        for slot in range(listed):
            live = slot < count

            @pl.when(live)
            def _():
                list_ref[slot * points : (slot + 1) * points] = blocks_ref[
                    plan_ref[side * listed + slot]
                ]

            @pl.when(jnp.logical_not(live))
            def _():
                list_ref[slot * points : (slot + 1) * points] = jnp.zeros(
                    blocks_ref.shape[1:], list_ref.dtype
                )


def start_rows(hbm_refs, rows_refs, sems):
    copies = [
        pltpu.make_async_copy(source, target, sems.at[i])
        for i, (source, target) in enumerate(zip(hbm_refs, rows_refs))
    ]
    for copy in copies:
        copy.start()
    return copies


def write_columns(rows_refs, columns_refs):
    for rows, columns_ref in zip(rows_refs, columns_refs):
        for b in range(columns_ref.shape[0]):
            row = rows[0, pl.ds(b, 1), :]
            columns_ref[b] = jnp.broadcast_to(row, columns_ref.shape[1:]).T


def prepare_kernel(
    ids_hbm, count_hbm, pattern_hbm, inflow_hbm, pass_hbm, reflect_hbm,
    plan_ref, wave_ref, first_ref, second_ref, pass_ref, reflect_ref,
    ids, count, pattern, landed, small_sems, sems, pass_rows, reflect_rows, rows_sems,
):
    blocks = wave_ref.shape[0]
    small = [
        pltpu.make_async_copy(source, target, small_sems.at[i])
        for i, (source, target) in enumerate(
            ((ids_hbm, ids), (count_hbm, count), (pattern_hbm, pattern))
        )
    ]
    large = [
        pltpu.make_async_copy(inflow_hbm.at[0, b], landed.at[b], sems.at[b]) for b in range(blocks)
    ]
    rows = (pass_rows, reflect_rows)
    for copy in small + large:
        copy.start()
    rows_copies = start_rows((pass_hbm, reflect_hbm), rows, rows_sems)
    for copy in small:
        copy.wait()
    _, sides, listed = ids.shape
    taken = pattern.shape[1]
    for side in range(sides):
        for slot in range(listed):
            plan_ref[side * listed + slot] = ids[0, side, slot]
        plan_ref[sides * listed + side] = count[0, side]
    for b in range(blocks):
        for k in range(taken):
            plan_ref[sides * (listed + 1) + b * taken + k] = pattern[b, k]
    for b, copy in enumerate(large):
        copy.wait()
        wave_ref[b] = landed[b].astype(wave_ref.dtype)
    write_lists(lax.axis_index("lat"), plan_ref, wave_ref, (first_ref, second_ref))

    for copy in rows_copies:
        copy.wait()

    @pl.when(lax.rem(lax.axis_index("depth"), 2) == 1)
    def _():
        write_columns(rows, (pass_ref, reflect_ref))


def load_kernel(
    ops_hbm, source_hbm, pass_hbm, reflect_hbm, known_pass_ref, known_reflect_ref, after_ref,
    ops_ref, source_ref, pass_ref, reflect_ref, pass_rows, reflect_rows, rows_sems, sems,
):
    del known_pass_ref, known_reflect_ref, after_ref
    copies = start_rows((ops_hbm, source_hbm), (ops_ref, source_ref), sems)

    @pl.when(lax.rem(lax.axis_index("depth"), 2) == 0)
    def _():
        rows = (pass_rows, reflect_rows)
        for copy in start_rows((pass_hbm, reflect_hbm), rows, rows_sems):
            copy.wait()
        write_columns(rows, (pass_ref, reflect_ref))

    for copy in copies:
        copy.wait()


def fill_buffer(section, tick, source_ref, wave_refs, first_ref, second_ref, buffer):
    blocks, points = source_ref.shape[1:3]
    listed = (buffer.shape[0] - blocks) // 2

    def fill(start, ref):
        if len(ref.shape) == 2:
            count = min(ref.shape[0] // points, blocks)
            part = ref[: count * points].reshape(count, points, -1)
        else:
            part = ref[0] if len(ref.shape) == 4 else ref[...]
        buffer[pl.ds(start, part.shape[0])] = part
        return start + part.shape[0]

    def fill_wave():
        start = 0
        for wave_ref in wave_refs:
            start = fill(start, wave_ref)

    if tick == 0:
        fill_wave()
    else:
        pl.when(section != 0)(fill_wave)

        @pl.when(section == 0)
        def _():
            buffer[:blocks] = source_ref[tick - 1]

    parity = lax.rem(lax.axis_index("lat"), 2)
    fill(blocks + (1 - parity) * listed, first_ref)
    fill(blocks + parity * listed, second_ref)


def extrapolate_block(plan_ref, pattern_start, ops_ref, buffer, b):
    taken = ops_ref.shape[2]
    points = ops_ref.shape[5]
    left = jnp.concatenate(
        [ops_ref[0, b, k].reshape(2 * points, points) for k in range(taken)], axis=1
    )
    right = jnp.concatenate(
        [buffer[plan_ref[pattern_start + b * taken + k]] for k in range(taken)], axis=0
    )
    products = jnp.dot(left, right, preferred_element_type=jnp.float32)
    half = products.shape[1] // 2
    real_part = products[:points, :half] - products[points:, half:]
    imag_part = products[:points, half:] + products[points:, :half]
    return real_part, imag_part


def ids_of(plan_ref, ops_ref):
    return (plan_ref.shape[0] - ops_ref.shape[1] * ops_ref.shape[2]) // 2 - 1


def acts(section, parity):
    return lax.rem(section, 2) == parity


def tick_kernel(
    parity, tick, sections, plan_ref, ops_ref, source_ref, pass_ref, reflect_ref,
    wave_refs, first_in_ref, second_in_ref, known_refs, out_refs, buffer, onward,
):
    del known_refs
    echo_ref, first_ref, second_ref, *onward_refs = out_refs
    section = lax.axis_index("depth")
    tile = lax.axis_index("lat")
    listed = ids_of(plan_ref, ops_ref)

    @pl.when(acts(section, parity))
    def _():
        fill_buffer(section, tick, source_ref, wave_refs, first_in_ref, second_in_ref, buffer)
        for b in range(echo_ref.shape[0]):
            parts = extrapolate_block(plan_ref, 2 * (listed + 1), ops_ref, buffer, b)
            for i, part in enumerate(parts):
                cols = pl.ds(i * part.shape[1], part.shape[1])
                onward[b, :, cols] = (pass_ref[b] * part).astype(onward.dtype)
                echo_ref[b, :, cols] = (reflect_ref[b] * part).astype(echo_ref.dtype)
        start = 0
        for onward_ref in onward_refs:
            if len(onward_ref.shape) == 2:
                rows = onward.shape[0] * onward.shape[1]
                onward_ref[:rows] = onward[...].reshape(rows, onward.shape[2])
            else:
                slot = onward_ref if len(onward_ref.shape) == 3 else onward_ref.at[1]
                slot[...] = onward[start : start + slot.shape[0]]
                start += slot.shape[0]

        @pl.when(section != sections - 1)
        def _():
            write_lists(tile, plan_ref, onward, (first_ref, second_ref))

        @pl.when(section == sections - 1)
        def _():
            write_lists(tile, plan_ref, source_ref.at[tick], (first_ref, second_ref))


def last_kernel(
    parity, tick, plan_ref, ops_ref, source_ref, pass_ref, reflect_ref,
    wave_refs, first_in_ref, second_in_ref, earlier, known_refs, out_refs,
    buffer, echo, leaving, early_sems, echo_sems, leave_sems,
):
    del known_refs
    reflected_ref, transmitted_ref = out_refs
    section = lax.axis_index("depth")
    listed = ids_of(plan_ref, ops_ref)

    @pl.when(acts(section, parity))
    def _():
        copies = [
            pltpu.make_async_copy(earlier[t], reflected_ref.at[t, 0], early_sems.at[t])
            for t in range(tick)
        ]
        for copy in copies:
            copy.start()
        fill_buffer(section, tick, source_ref, wave_refs, first_in_ref, second_in_ref, buffer)
        for b in range(echo.shape[0]):
            parts = extrapolate_block(plan_ref, 2 * (listed + 1), ops_ref, buffer, b)
            for i, part in enumerate(parts):
                cols = pl.ds(i * part.shape[1], part.shape[1])
                leaving[b, :, cols] = pass_ref[b] * part
                echo[b, :, cols] = (reflect_ref[b] * part).astype(echo.dtype)
            for copy in (
                pltpu.make_async_copy(leaving.at[b], transmitted_ref.at[0, b], leave_sems.at[b]),
                pltpu.make_async_copy(echo.at[b], reflected_ref.at[tick, 0, b], echo_sems.at[b]),
            ):
                copy.start()
                copies.append(copy)
        for copy in copies:
            copy.wait()


def grouped_call(kernel, groups, outs, out_specs, known, **options):
    flat = [array for group in groups for array in (group if isinstance(group, list) else [group])]

    def body(*refs):
        refs = list(refs)
        take = lambda count: [refs.pop(0) for _ in range(count)]
        inputs = [take(len(g)) if isinstance(g, list) else refs.pop(0) for g in groups]
        kernel(*inputs, take(len(known)), take(len(outs)), *refs)

    return pl.pallas_call(
        body,
        out_shape=tuple(outs),
        in_specs=[SMEM_SPEC] + [VMEM_SPEC] * (len(flat) - 1) + list(out_specs[: len(known)]),
        out_specs=tuple(out_specs),
        input_output_aliases={len(flat) + i: i for i in range(len(known))},
        **options,
    )(flat[0], *map(in_vmem, flat[1:]), *known)


def neighbour(j, turn, tiles):
    to = j + (1 if (j + turn) % 2 == 0 else -1)
    return to if 0 <= to < tiles else None


def swap_routes(sections, tiles):
    routes = []
    for turn in (0, 1):
        route = []
        for s in range(sections):
            for j in range(tiles):
                to = neighbour(j, turn, tiles)
                end = ((s ^ 1) * tiles + j) if to is None else (s * tiles + to)
                route.append((s * tiles + j, end))
        routes.append(route)
    return routes


def halo_routes(sections, tiles, senders):
    routes = []
    for turn in (0, 1):
        route = []
        for s in range(sections):
            for j in range(tiles):
                to = neighbour(j, turn, tiles)
                real = to is not None and s % 2 in senders
                end = (s + 1) % sections * tiles + to if real else (s ^ 1) * tiles + j
                route.append((s * tiles + j, end))
        routes.append(route)
    return routes


def per_device(
    inflow, source, operators, transmission, reflectivity, send_ids, send_count, pattern
):
    sections, tiles = lax.axis_size("depth"), lax.axis_size("lat")
    ticks = source.shape[0] + 1
    _, blocks, points, columns = inflow.shape
    listed = send_ids.shape[-1]
    taken = operators.shape[2]
    wave_type = pltpu.VMEM((blocks, points, columns), WAVE)
    list_type = pltpu.VMEM((listed * points, columns), WAVE)
    params = pltpu.CompilerParams(vmem_limit_bytes=VMEM_LIMIT)
    tick_cost = pl.CostEstimate(
        flops=0,
        bytes_accessed=0,
        transcendentals=0,
    )
    both = ("depth", "lat")
    deeper = [(s, (s + 1) % sections) for s in range(sections)]

    column_type = pltpu.VMEM((blocks, points, columns // 2), jnp.float32)
    rows_scratch = [
        pltpu.VMEM(transmission.shape, transmission.dtype),
        pltpu.VMEM(reflectivity.shape, reflectivity.dtype),
        pltpu.SemaphoreType.DMA((2,)),
    ]
    coefficients = [in_hbm(transmission), in_hbm(reflectivity)]
    plan, wave, first, second, *coefficient_columns = pl.pallas_call(
        prepare_kernel,
        out_shape=(
            pltpu.SMEM((2 * (listed + 1) + blocks * taken,), jnp.int32),
            wave_type,
            list_type,
            list_type,
            column_type,
            column_type,
        ),
        in_specs=[ANY_SPEC] * 6,
        out_specs=(SMEM_SPEC,) + (VMEM_SPEC,) * 5,
        scratch_shapes=[
            pltpu.SMEM(send_ids.shape, jnp.int32),
            pltpu.SMEM(send_count.shape, jnp.int32),
            pltpu.SMEM(pattern.shape, jnp.int32),
            pltpu.VMEM((blocks, points, columns), inflow.dtype),
            pltpu.SemaphoreType.DMA((3,)),
            pltpu.SemaphoreType.DMA((blocks,)),
            *rows_scratch,
        ],
        compiler_params=params,
        cost_estimate=pl.CostEstimate(
            flops=inflow.size, bytes_accessed=8 * inflow.size, transcendentals=0
        ),
        name="prepare",
    )(*map(in_hbm, (send_ids, send_count, pattern, inflow)), *coefficients)
    listed_first = first
    routes = swap_routes(sections, tiles)
    first = lax.ppermute(first, both, routes[0])
    second = lax.ppermute(second, both, routes[1])

    fixed = pl.pallas_call(
        load_kernel,
        out_shape=(
            pltpu.VMEM(operators.shape, operators.dtype),
            pltpu.VMEM(source.shape, source.dtype),
            column_type,
            column_type,
        ),
        in_specs=[ANY_SPEC] * 4 + [VMEM_SPEC] * 3,
        out_specs=(VMEM_SPEC,) * 4,
        input_output_aliases={4: 2, 5: 3},
        scratch_shapes=[*rows_scratch, pltpu.SemaphoreType.DMA((2,))],
        compiler_params=params,
        cost_estimate=pl.CostEstimate(
            flops=0, bytes_accessed=4 * (operators.size + source.size), transcendentals=0
        ),
        name="load",
    )(in_hbm(operators), in_hbm(source), *coefficients, *map(in_vmem, [*coefficient_columns, listed_first]))
    fixed = [plan, *fixed]

    buffer_type = pltpu.VMEM((blocks + 2 * listed, points, columns), WAVE)

    ODD, EVEN = 1, 0
    crossing = [(s, (s + 1) % sections) for s in range(sections)]
    inside = [(s, s ^ 1) for s in range(sections)]
    pairs = [[s, s + 1] for s in range(0, sections, 2)]
    pair_type = pltpu.VMEM((2, blocks, points, columns), WAVE)
    part_types = [pltpu.VMEM((blocks // 2, points, columns), WAVE)] * 2
    half_types = [pltpu.VMEM((n, points, columns), WAVE) for n in (blocks // 2, blocks - blocks // 2)]

    def lists_of(extra):
        return [pltpu.VMEM((listed * points + extra, columns), WAVE)] * 2

    def exchange(lists, senders):
        routes = halo_routes(sections, tiles, senders)
        return [lax.ppermute(a, both, route) for a, route in zip(lists, routes)]

    arrived = {parity: ([wave], first, second) for parity in (ODD, EVEN)}
    echoes = []
    for tick in range(ticks - 1):
        first_step, last_step = tick == 0, tick == ticks - 2
        known = []
        waves, halos = {}, {}
        for parity in (ODD, EVEN):
            if first_step:
                extra = 0
            elif last_step:
                extra = 16 if parity == ODD else 0
            else:
                extra = 0 if parity == ODD else 16
            if parity == ODD:
                long = 0 if first_step or last_step else 16
                to_next = [pltpu.VMEM((blocks * points + long, columns), WAVE)]
            else:
                to_next = [pair_type] if last_step else half_types if first_step else part_types
            outs = [wave_type, *lists_of(extra), *to_next]
            echo, *lists = grouped_call(
                functools.partial(tick_kernel, parity, tick, sections),
                [*fixed, *arrived[parity]],
                outs,
                [VMEM_SPEC] * len(outs),
                [in_vmem(a) for a in known],
                scratch_shapes=[buffer_type, pltpu.VMEM(wave_type.shape, WAVE)],
                compiler_params=params,
                cost_estimate=tick_cost,
                name=f"tick{tick}" + ("_odd" if parity else "_even"),
            )
            lists, onward = lists[:2], lists[2:]
            known = [echo, *lists] if first_step else [echo]
            if parity == ODD:
                waves[EVEN] = [lax.ppermute(onward[0], "depth", crossing)]
            elif last_step:
                waves[ODD] = [lax.all_to_all(onward[0], "depth", 0, 0, axis_index_groups=pairs)]
            else:
                waves[ODD] = [lax.ppermute(a, "depth", inside) for a in onward]
            if not first_step:
                halos[1 - parity] = exchange(lists, (parity,))
        if first_step:
            halos[ODD] = halos[EVEN] = exchange(lists, (ODD, EVEN))
        arrived = {parity: (waves[parity], *halos[parity]) for parity in (ODD, EVEN)}
        echoes.append(echo)

    tick = ticks - 1
    results = []
    result_types = (
        jax.ShapeDtypeStruct((ticks, 1, blocks, points, columns), WAVE),
        jax.ShapeDtypeStruct((1, blocks, points, columns), jnp.float32),
    )
    for parity in (ODD, EVEN):
        results = grouped_call(
            functools.partial(last_kernel, parity, tick),
            [*fixed, *arrived[parity], echoes],
            result_types,
            [ANY_SPEC] * 2,
            list(results),
            scratch_shapes=[
                buffer_type,
                pltpu.VMEM((blocks, points, columns), WAVE),
                pltpu.VMEM((blocks, points, columns), jnp.float32),
                pltpu.SemaphoreType.DMA((tick,)),
                pltpu.SemaphoreType.DMA((blocks,)),
                pltpu.SemaphoreType.DMA((blocks,)),
            ],
            compiler_params=params,
            cost_estimate=tick_cost,
            name="last_tick" + ("_odd" if parity else "_even"),
        )
    return tuple(results)


def solution(mesh):
    return jax.shard_map(
        per_device,
        mesh=mesh,
        in_specs=(
            P("depth", "lat", None, None),
            P(None, "lat", None, None),
            P("depth", "lat", None, None, None, None),
            P("depth", "lat", None),
            P("depth", "lat", None),
            P("lat", None, None),
            P("lat", None),
            P("lat", None),
        ),
        out_specs=(P(None, "depth", "lat", None, None), P("depth", "lat", None, None)),
        check_vma=False,
    )
```

```python
import functools

import jax
import jax.numpy as jnp
from jax import lax
from jax.experimental import pallas as pl
from jax.experimental.pallas import tpu as pltpu
from jax.sharding import PartitionSpec as P

WAVE = jnp.bfloat16
SMEM_SPEC = pl.BlockSpec(memory_space=pltpu.SMEM)
VMEM_SPEC = pl.BlockSpec(memory_space=pltpu.VMEM)
ANY_SPEC = pl.BlockSpec(memory_space=pl.ANY)
VMEM_LIMIT = 8 * 1024 * 1024
LOWER, UPPER = 0, 1


def in_vmem(array):
    return pltpu.with_memory_space_constraint(array, pltpu.VMEM)


def in_hbm(array):
    return pltpu.with_memory_space_constraint(array, pltpu.HBM)


def write_lists(tile, plan_ref, blocks_ref, lists):
    points = blocks_ref.shape[1]
    listed = lists[0].shape[0] // points
    parity = lax.rem(tile, 2)
    for list_ref, side in zip(lists, (UPPER - parity, parity)):
        count = plan_ref[2 * listed + side]
        for slot in range(listed):
            live = slot < count

            @pl.when(live)
            def _():
                list_ref[slot * points : (slot + 1) * points] = blocks_ref[
                    plan_ref[side * listed + slot]
                ]

            @pl.when(jnp.logical_not(live))
            def _():
                list_ref[slot * points : (slot + 1) * points] = jnp.zeros(
                    blocks_ref.shape[1:], list_ref.dtype
                )


def copies_of(hbm_refs, refs, sems):
    return [
        pltpu.make_async_copy(source, target, sems.at[i])
        for i, (source, target) in enumerate(zip(hbm_refs, refs))
    ]


def start_copies(hbm_refs, refs, sems):
    copies = copies_of(hbm_refs, refs, sems)
    for copy in copies:
        copy.start()
    return copies


def write_columns(rows_refs, columns_refs):
    for rows, columns_ref in zip(rows_refs, columns_refs):
        for b in range(columns_ref.shape[0]):
            row = rows[0, pl.ds(b, 1), :]
            columns_ref[b] = jnp.broadcast_to(row, columns_ref.shape[1:]).T


def prepare_kernel(
    ids_hbm, count_hbm, pattern_hbm, inflow_hbm, ops_hbm, source_hbm, pass_hbm, reflect_hbm,
    plan_ref, wave_ref, first_ref, second_ref, ops_ref, source_ref, pass_ref, reflect_ref,
    ids, count, pattern, landed, small_sems, sems, pass_rows, reflect_rows, rows_sems, load_sems,
):
    odd = lax.rem(lax.axis_index("depth"), 2) == 1
    blocks = wave_ref.shape[0]
    small = [
        pltpu.make_async_copy(source, target, small_sems.at[i])
        for i, (source, target) in enumerate(
            ((ids_hbm, ids), (count_hbm, count), (pattern_hbm, pattern))
        )
    ]
    large = [
        pltpu.make_async_copy(inflow_hbm.at[0, b], landed.at[b], sems.at[b]) for b in range(blocks)
    ]
    rows = (pass_rows, reflect_rows)
    for copy in small + large:
        copy.start()
    rows_copies = start_copies((pass_hbm, reflect_hbm), rows, rows_sems)

    @pl.when(odd)
    def _():
        start_copies((ops_hbm, source_hbm), (ops_ref, source_ref), load_sems)

    for copy in small:
        copy.wait()
    _, sides, listed = ids.shape
    taken = pattern.shape[1]
    for side in range(sides):
        for slot in range(listed):
            plan_ref[side * listed + slot] = ids[0, side, slot]
        plan_ref[sides * listed + side] = count[0, side]
    for b in range(blocks):
        for k in range(taken):
            plan_ref[sides * (listed + 1) + b * taken + k] = pattern[b, k]
    for b, copy in enumerate(large):
        copy.wait()
        wave_ref[b] = landed[b].astype(wave_ref.dtype)
    write_lists(lax.axis_index("lat"), plan_ref, wave_ref, (first_ref, second_ref))

    for copy in rows_copies:
        copy.wait()

    @pl.when(odd)
    def _():
        write_columns(rows, (pass_ref, reflect_ref))
        for copy in copies_of((ops_hbm, source_hbm), (ops_ref, source_ref), load_sems):
            copy.wait()


def load_kernel(ops_hbm, source_hbm, pass_hbm, reflect_hbm, *rest):
    ops_ref, source_ref, pass_ref, reflect_ref, pass_rows, reflect_rows, rows_sems, sems = rest[-8:]

    @pl.when(lax.rem(lax.axis_index("depth"), 2) == 0)
    def _():
        rows = (pass_rows, reflect_rows)
        copies = start_copies((ops_hbm, source_hbm), (ops_ref, source_ref), sems)
        for copy in start_copies((pass_hbm, reflect_hbm), rows, rows_sems):
            copy.wait()
        write_columns(rows, (pass_ref, reflect_ref))
        for copy in copies:
            copy.wait()


def fill_buffer(section, tick, source_ref, wave_refs, first_ref, second_ref, buffer):
    blocks, points = source_ref.shape[1:3]
    listed = (buffer.shape[0] - blocks) // 2

    def fill(start, ref):
        if len(ref.shape) == 2:
            count = min(ref.shape[0] // points, blocks)
            part = ref[: count * points].reshape(count, points, -1)
        else:
            part = ref[0] if len(ref.shape) == 4 else ref[...]
        buffer[pl.ds(start, part.shape[0])] = part
        return start + part.shape[0]

    def fill_wave():
        start = 0
        for wave_ref in wave_refs:
            start = fill(start, wave_ref)

    if tick == 0:
        fill_wave()
    else:
        pl.when(section != 0)(fill_wave)

        @pl.when(section == 0)
        def _():
            buffer[:blocks] = source_ref[tick - 1]

    parity = lax.rem(lax.axis_index("lat"), 2)
    fill(blocks + (1 - parity) * listed, first_ref)
    fill(blocks + parity * listed, second_ref)


def extrapolate_block(plan_ref, pattern_start, ops_ref, buffer, b):
    taken = ops_ref.shape[2]
    points = ops_ref.shape[5]
    left = jnp.concatenate(
        [ops_ref[0, b, k].reshape(2 * points, points) for k in range(taken)], axis=1
    )
    right = jnp.concatenate(
        [buffer[plan_ref[pattern_start + b * taken + k]] for k in range(taken)], axis=0
    )
    products = jnp.dot(left, right, preferred_element_type=jnp.float32)
    half = products.shape[1] // 2
    real_part = products[:points, :half] - products[points:, half:]
    imag_part = products[:points, half:] + products[points:, :half]
    return real_part, imag_part


def ids_of(plan_ref, ops_ref):
    return (plan_ref.shape[0] - ops_ref.shape[1] * ops_ref.shape[2]) // 2 - 1


def acts(section, parity):
    return lax.rem(section, 2) == parity


def tick_kernel(
    parity, tick, sections, plan_ref, ops_ref, source_ref, pass_ref, reflect_ref,
    wave_refs, first_in_ref, second_in_ref, known_refs, out_refs, buffer, onward,
):
    del known_refs
    echo_ref, first_ref, second_ref, *onward_refs = out_refs
    section = lax.axis_index("depth")
    tile = lax.axis_index("lat")
    listed = ids_of(plan_ref, ops_ref)

    @pl.when(acts(section, parity))
    def _():
        fill_buffer(section, tick, source_ref, wave_refs, first_in_ref, second_in_ref, buffer)
        for b in range(echo_ref.shape[0]):
            parts = extrapolate_block(plan_ref, 2 * (listed + 1), ops_ref, buffer, b)
            for i, part in enumerate(parts):
                cols = pl.ds(i * part.shape[1], part.shape[1])
                onward[b, :, cols] = (pass_ref[b] * part).astype(onward.dtype)
                echo_ref[b, :, cols] = (reflect_ref[b] * part).astype(echo_ref.dtype)
        start = 0
        for onward_ref in onward_refs:
            if len(onward_ref.shape) == 2:
                rows = onward.shape[0] * onward.shape[1]
                onward_ref[:rows] = onward[...].reshape(rows, onward.shape[2])
            else:
                slot = onward_ref if len(onward_ref.shape) == 3 else onward_ref.at[1]
                slot[...] = onward[start : start + slot.shape[0]]
                start += slot.shape[0]

        @pl.when(section != sections - 1)
        def _():
            write_lists(tile, plan_ref, onward, (first_ref, second_ref))

        @pl.when(section == sections - 1)
        def _():
            write_lists(tile, plan_ref, source_ref.at[tick], (first_ref, second_ref))


def last_kernel(
    parity, tick, plan_ref, ops_ref, source_ref, pass_ref, reflect_ref,
    wave_refs, first_in_ref, second_in_ref, earlier, known_refs, out_refs,
    buffer, echo, leaving, early_sems, echo_sems, leave_sems,
):
    del known_refs
    reflected_ref, transmitted_ref = out_refs
    section = lax.axis_index("depth")
    listed = ids_of(plan_ref, ops_ref)

    @pl.when(acts(section, parity))
    def _():
        copies = [
            pltpu.make_async_copy(earlier[t], reflected_ref.at[t, 0], early_sems.at[t])
            for t in range(tick)
        ]
        for copy in copies:
            copy.start()
        fill_buffer(section, tick, source_ref, wave_refs, first_in_ref, second_in_ref, buffer)
        for b in range(echo.shape[0]):
            parts = extrapolate_block(plan_ref, 2 * (listed + 1), ops_ref, buffer, b)
            for i, part in enumerate(parts):
                cols = pl.ds(i * part.shape[1], part.shape[1])
                leaving[b, :, cols] = pass_ref[b] * part
                echo[b, :, cols] = (reflect_ref[b] * part).astype(echo.dtype)
            for copy in (
                pltpu.make_async_copy(leaving.at[b], transmitted_ref.at[0, b], leave_sems.at[b]),
                pltpu.make_async_copy(echo.at[b], reflected_ref.at[tick, 0, b], echo_sems.at[b]),
            ):
                copy.start()
                copies.append(copy)
        for copy in copies:
            copy.wait()


def grouped_call(kernel, groups, outs, out_specs, known, **options):
    flat = [array for group in groups for array in (group if isinstance(group, list) else [group])]

    def body(*refs):
        refs = list(refs)
        take = lambda count: [refs.pop(0) for _ in range(count)]
        inputs = [take(len(g)) if isinstance(g, list) else refs.pop(0) for g in groups]
        kernel(*inputs, take(len(known)), take(len(outs)), *refs)

    return pl.pallas_call(
        body,
        out_shape=tuple(outs),
        in_specs=[SMEM_SPEC] + [VMEM_SPEC] * (len(flat) - 1) + list(out_specs[: len(known)]),
        out_specs=tuple(out_specs),
        input_output_aliases={len(flat) + i: i for i in range(len(known))},
        **options,
    )(flat[0], *map(in_vmem, flat[1:]), *known)


def neighbour(j, turn, tiles):
    to = j + (1 if (j + turn) % 2 == 0 else -1)
    return to if 0 <= to < tiles else None


def swap_routes(sections, tiles):
    routes = []
    for turn in (0, 1):
        route = []
        for s in range(sections):
            for j in range(tiles):
                to = neighbour(j, turn, tiles)
                end = ((s ^ 1) * tiles + j) if to is None else (s * tiles + to)
                route.append((s * tiles + j, end))
        routes.append(route)
    return routes


def halo_routes(sections, tiles, senders):
    routes = []
    for turn in (0, 1):
        route = []
        for s in range(sections):
            for j in range(tiles):
                to = neighbour(j, turn, tiles)
                real = to is not None and s % 2 in senders
                end = (s + 1) % sections * tiles + to if real else (s ^ 1) * tiles + j
                route.append((s * tiles + j, end))
        routes.append(route)
    return routes


def per_device(
    inflow, source, operators, transmission, reflectivity, send_ids, send_count, pattern
):
    sections, tiles = lax.axis_size("depth"), lax.axis_size("lat")
    ticks = source.shape[0] + 1
    _, blocks, points, columns = inflow.shape
    listed = send_ids.shape[-1]
    taken = operators.shape[2]
    wave_type = pltpu.VMEM((blocks, points, columns), WAVE)
    list_type = pltpu.VMEM((listed * points, columns), WAVE)
    params = pltpu.CompilerParams(vmem_limit_bytes=VMEM_LIMIT)
    tick_cost = pl.CostEstimate(
        flops=0,
        bytes_accessed=0,
        transcendentals=0,
    )
    both = ("depth", "lat")
    deeper = [(s, (s + 1) % sections) for s in range(sections)]

    column_type = pltpu.VMEM((blocks, points, columns // 2), jnp.float32)
    rows_scratch = [
        pltpu.VMEM(transmission.shape, transmission.dtype),
        pltpu.VMEM(reflectivity.shape, reflectivity.dtype),
        pltpu.SemaphoreType.DMA((2,)),
    ]
    fixed_types = (
        pltpu.VMEM(operators.shape, operators.dtype),
        pltpu.VMEM(source.shape, source.dtype),
        column_type,
        column_type,
    )
    stored = [in_hbm(a) for a in (operators, source, transmission, reflectivity)]
    plan, wave, first, second, *loaded = pl.pallas_call(
        prepare_kernel,
        out_shape=(
            pltpu.SMEM((2 * (listed + 1) + blocks * taken,), jnp.int32),
            wave_type,
            list_type,
            list_type,
            *fixed_types,
        ),
        in_specs=[ANY_SPEC] * 8,
        out_specs=(SMEM_SPEC,) + (VMEM_SPEC,) * 7,
        scratch_shapes=[
            pltpu.SMEM(send_ids.shape, jnp.int32),
            pltpu.SMEM(send_count.shape, jnp.int32),
            pltpu.SMEM(pattern.shape, jnp.int32),
            pltpu.VMEM((blocks, points, columns), inflow.dtype),
            pltpu.SemaphoreType.DMA((3,)),
            pltpu.SemaphoreType.DMA((blocks,)),
            *rows_scratch,
            pltpu.SemaphoreType.DMA((2,)),
        ],
        compiler_params=params,
        cost_estimate=pl.CostEstimate(
            flops=inflow.size, bytes_accessed=8 * inflow.size, transcendentals=0
        ),
        name="prepare",
    )(*map(in_hbm, (send_ids, send_count, pattern, inflow)), *stored)
    listed_first = first
    routes = swap_routes(sections, tiles)
    first = lax.ppermute(first, both, routes[0])
    second = lax.ppermute(second, both, routes[1])

    fixed = pl.pallas_call(
        load_kernel,
        out_shape=fixed_types,
        in_specs=[ANY_SPEC] * 4 + [VMEM_SPEC] * 5,
        out_specs=(VMEM_SPEC,) * 4,
        input_output_aliases={4: 0, 5: 1, 6: 2, 7: 3},
        scratch_shapes=[*rows_scratch, pltpu.SemaphoreType.DMA((2,))],
        compiler_params=params,
        cost_estimate=pl.CostEstimate(
            flops=0, bytes_accessed=4 * (operators.size + source.size), transcendentals=0
        ),
        name="load",
    )(*stored, *map(in_vmem, [*loaded, listed_first]))
    fixed = [plan, *fixed]

    buffer_type = pltpu.VMEM((blocks + 2 * listed, points, columns), WAVE)

    ODD, EVEN = 1, 0
    crossing = [(s, (s + 1) % sections) for s in range(sections)]
    inside = [(s, s ^ 1) for s in range(sections)]
    pairs = [[s, s + 1] for s in range(0, sections, 2)]
    pair_type = pltpu.VMEM((2, blocks, points, columns), WAVE)
    part_types = [pltpu.VMEM((blocks // 2, points, columns), WAVE)] * 2
    half_types = [pltpu.VMEM((n, points, columns), WAVE) for n in (blocks // 2, blocks - blocks // 2)]

    def lists_of(extra):
        return [pltpu.VMEM((listed * points + extra, columns), WAVE)] * 2

    def exchange(lists, senders):
        routes = halo_routes(sections, tiles, senders)
        return [lax.ppermute(a, both, route) for a, route in zip(lists, routes)]

    arrived = {parity: ([wave], first, second) for parity in (ODD, EVEN)}
    echoes = []
    for tick in range(ticks - 1):
        first_step, last_step = tick == 0, tick == ticks - 2
        known = []
        waves, halos = {}, {}
        for parity in (ODD, EVEN):
            if first_step:
                extra = 0
            elif last_step:
                extra = 16 if parity == ODD else 0
            else:
                extra = 0 if parity == ODD else 16
            if parity == ODD:
                long = 0 if first_step or last_step else 16
                to_next = [pltpu.VMEM((blocks * points + long, columns), WAVE)]
            else:
                to_next = [pair_type] if last_step else half_types if first_step else part_types
            outs = [wave_type, *lists_of(extra), *to_next]
            echo, *lists = grouped_call(
                functools.partial(tick_kernel, parity, tick, sections),
                [*fixed, *arrived[parity]],
                outs,
                [VMEM_SPEC] * len(outs),
                [in_vmem(a) for a in known],
                scratch_shapes=[buffer_type, pltpu.VMEM(wave_type.shape, WAVE)],
                compiler_params=params,
                cost_estimate=tick_cost,
                name=f"tick{tick}" + ("_odd" if parity else "_even"),
            )
            lists, onward = lists[:2], lists[2:]
            known = [echo, *lists] if first_step else [echo]
            if parity == ODD:
                waves[EVEN] = [lax.ppermute(onward[0], "depth", crossing)]
            elif last_step:
                waves[ODD] = [lax.all_to_all(onward[0], "depth", 0, 0, axis_index_groups=pairs)]
            else:
                waves[ODD] = [lax.ppermute(a, "depth", inside) for a in onward]
            if not first_step:
                halos[1 - parity] = exchange(lists, (parity,))
        if first_step:
            halos[ODD] = halos[EVEN] = exchange(lists, (ODD, EVEN))
        arrived = {parity: (waves[parity], *halos[parity]) for parity in (ODD, EVEN)}
        echoes.append(echo)

    tick = ticks - 1
    results = []
    result_types = (
        jax.ShapeDtypeStruct((ticks, 1, blocks, points, columns), WAVE),
        jax.ShapeDtypeStruct((1, blocks, points, columns), jnp.float32),
    )
    for parity in (ODD, EVEN):
        results = grouped_call(
            functools.partial(last_kernel, parity, tick),
            [*fixed, *arrived[parity], echoes],
            result_types,
            [ANY_SPEC] * 2,
            list(results),
            scratch_shapes=[
                buffer_type,
                pltpu.VMEM((blocks, points, columns), WAVE),
                pltpu.VMEM((blocks, points, columns), jnp.float32),
                pltpu.SemaphoreType.DMA((tick,)),
                pltpu.SemaphoreType.DMA((blocks,)),
                pltpu.SemaphoreType.DMA((blocks,)),
            ],
            compiler_params=params,
            cost_estimate=tick_cost,
            name="last_tick" + ("_odd" if parity else "_even"),
        )
    return tuple(results)


def solution(mesh):
    return jax.shard_map(
        per_device,
        mesh=mesh,
        in_specs=(
            P("depth", "lat", None, None),
            P(None, "lat", None, None),
            P("depth", "lat", None, None, None, None),
            P("depth", "lat", None),
            P("depth", "lat", None),
            P("lat", None, None),
            P("lat", None),
            P("lat", None),
        ),
        out_specs=(P(None, "depth", "lat", None, None), P("depth", "lat", None, None)),
        check_vma=False,
    )
```

```python
import functools

import jax
import jax.numpy as jnp
from jax import lax
from jax.experimental import pallas as pl
from jax.experimental.pallas import tpu as pltpu
from jax.sharding import PartitionSpec as P

WAVE = jnp.bfloat16
SMEM_SPEC = pl.BlockSpec(memory_space=pltpu.SMEM)
VMEM_SPEC = pl.BlockSpec(memory_space=pltpu.VMEM)
ANY_SPEC = pl.BlockSpec(memory_space=pl.ANY)
VMEM_LIMIT = 8 * 1024 * 1024
LOWER, UPPER = 0, 1


def in_vmem(array):
    return pltpu.with_memory_space_constraint(array, pltpu.VMEM)


def in_hbm(array):
    return pltpu.with_memory_space_constraint(array, pltpu.HBM)


def write_lists(tile, plan_ref, blocks_ref, lists):
    points = blocks_ref.shape[1]
    listed = lists[0].shape[0] // points
    parity = lax.rem(tile, 2)
    for list_ref, side in zip(lists, (UPPER - parity, parity)):
        count = plan_ref[2 * listed + side]
        for slot in range(listed):
            live = slot < count

            @pl.when(live)
            def _():
                list_ref[slot * points : (slot + 1) * points] = blocks_ref[
                    plan_ref[side * listed + slot]
                ]

            @pl.when(jnp.logical_not(live))
            def _():
                list_ref[slot * points : (slot + 1) * points] = jnp.zeros(
                    blocks_ref.shape[1:], list_ref.dtype
                )


def prepare_kernel(
    ids_hbm, count_hbm, pattern_hbm, inflow_hbm, plan_ref, wave_ref, first_ref, second_ref,
    ids, count, pattern, landed, small_sems, sems,
):
    blocks = wave_ref.shape[0]
    small = [
        pltpu.make_async_copy(source, target, small_sems.at[i])
        for i, (source, target) in enumerate(
            ((ids_hbm, ids), (count_hbm, count), (pattern_hbm, pattern))
        )
    ]
    large = [
        pltpu.make_async_copy(inflow_hbm.at[0, b], landed.at[b], sems.at[b]) for b in range(blocks)
    ]
    for copy in small + large:
        copy.start()
    for copy in small:
        copy.wait()
    _, sides, listed = ids.shape
    taken = pattern.shape[1]
    for side in range(sides):
        for slot in range(listed):
            plan_ref[side * listed + slot] = ids[0, side, slot]
        plan_ref[sides * listed + side] = count[0, side]
    for b in range(blocks):
        for k in range(taken):
            plan_ref[sides * (listed + 1) + b * taken + k] = pattern[b, k]
    for b, copy in enumerate(large):
        copy.wait()
        wave_ref[b] = landed[b].astype(wave_ref.dtype)
    write_lists(lax.axis_index("lat"), plan_ref, wave_ref, (first_ref, second_ref))


def load_kernel(
    ops_hbm, source_hbm, pass_hbm, reflect_hbm, after_ref,
    ops_ref, source_ref, pass_ref, reflect_ref, pass_rows, reflect_rows, sems,
):
    del after_ref
    copies = [
        pltpu.make_async_copy(source, target, sems.at[i])
        for i, (source, target) in enumerate(
            (
                (pass_hbm, pass_rows),
                (reflect_hbm, reflect_rows),
                (ops_hbm, ops_ref),
                (source_hbm, source_ref),
            )
        )
    ]
    for copy in copies:
        copy.start()
    for copy, rows, columns_ref in zip(copies, (pass_rows, reflect_rows), (pass_ref, reflect_ref)):
        copy.wait()
        for b in range(columns_ref.shape[0]):
            row = rows[0, pl.ds(b, 1), :]
            columns_ref[b] = jnp.broadcast_to(row, columns_ref.shape[1:]).T
    for copy in copies[2:]:
        copy.wait()


def fill_buffer(section, tick, source_ref, wave_refs, first_ref, second_ref, buffer):
    blocks, points = source_ref.shape[1:3]
    listed = (buffer.shape[0] - blocks) // 2

    def fill(start, ref):
        if len(ref.shape) == 2:
            count = min(ref.shape[0] // points, blocks)
            part = ref[: count * points].reshape(count, points, -1)
        else:
            part = ref[0] if len(ref.shape) == 4 else ref[...]
        buffer[pl.ds(start, part.shape[0])] = part
        return start + part.shape[0]

    def fill_wave():
        start = 0
        for wave_ref in wave_refs:
            start = fill(start, wave_ref)

    if tick == 0:
        fill_wave()
    else:
        pl.when(section != 0)(fill_wave)

        @pl.when(section == 0)
        def _():
            buffer[:blocks] = source_ref[tick - 1]

    parity = lax.rem(lax.axis_index("lat"), 2)
    fill(blocks + (1 - parity) * listed, first_ref)
    fill(blocks + parity * listed, second_ref)


def extrapolate_block(plan_ref, pattern_start, ops_ref, buffer, b):
    taken = ops_ref.shape[2]
    points = ops_ref.shape[5]
    left = jnp.concatenate(
        [ops_ref[0, b, k].reshape(2 * points, points) for k in range(taken)], axis=1
    )
    right = jnp.concatenate(
        [buffer[plan_ref[pattern_start + b * taken + k]] for k in range(taken)], axis=0
    )
    products = jnp.dot(left, right, preferred_element_type=jnp.float32)
    half = products.shape[1] // 2
    real_part = products[:points, :half] - products[points:, half:]
    imag_part = products[:points, half:] + products[points:, :half]
    return real_part, imag_part


def ids_of(plan_ref, ops_ref):
    return (plan_ref.shape[0] - ops_ref.shape[1] * ops_ref.shape[2]) // 2 - 1


def acts(section, parity):
    return lax.rem(section, 2) == parity


def tick_kernel(
    parity, tick, sections, plan_ref, ops_ref, source_ref, pass_ref, reflect_ref,
    wave_refs, first_in_ref, second_in_ref, settled_refs, known_refs, out_refs, buffer, onward,
):
    del known_refs, settled_refs
    echo_ref, first_ref, second_ref, *onward_refs = out_refs
    section = lax.axis_index("depth")
    tile = lax.axis_index("lat")
    listed = ids_of(plan_ref, ops_ref)

    @pl.when(acts(section, parity))
    def _():
        fill_buffer(section, tick, source_ref, wave_refs, first_in_ref, second_in_ref, buffer)
        for b in range(echo_ref.shape[0]):
            parts = extrapolate_block(plan_ref, 2 * (listed + 1), ops_ref, buffer, b)
            for i, part in enumerate(parts):
                cols = pl.ds(i * part.shape[1], part.shape[1])
                onward[b, :, cols] = (pass_ref[b] * part).astype(onward.dtype)
                echo_ref[b, :, cols] = (reflect_ref[b] * part).astype(echo_ref.dtype)
        start = 0
        for onward_ref in onward_refs:
            if len(onward_ref.shape) == 2:
                rows = onward.shape[0] * onward.shape[1]
                onward_ref[:rows] = onward[...].reshape(rows, onward.shape[2])
            else:
                slot = onward_ref if len(onward_ref.shape) == 3 else onward_ref.at[1]
                slot[...] = onward[start : start + slot.shape[0]]
                start += slot.shape[0]

        @pl.when(section != sections - 1)
        def _():
            write_lists(tile, plan_ref, onward, (first_ref, second_ref))

        @pl.when(section == sections - 1)
        def _():
            write_lists(tile, plan_ref, source_ref.at[tick], (first_ref, second_ref))


def last_kernel(
    parity, tick, plan_ref, ops_ref, source_ref, pass_ref, reflect_ref,
    wave_refs, first_in_ref, second_in_ref, earlier, known_refs, out_refs,
    buffer, echo, leaving, early_sems, echo_sems, leave_sems,
):
    del known_refs
    reflected_ref, transmitted_ref = out_refs
    section = lax.axis_index("depth")
    listed = ids_of(plan_ref, ops_ref)

    @pl.when(acts(section, parity))
    def _():
        copies = [
            pltpu.make_async_copy(earlier[t], reflected_ref.at[t, 0], early_sems.at[t])
            for t in range(tick)
        ]
        for copy in copies:
            copy.start()
        fill_buffer(section, tick, source_ref, wave_refs, first_in_ref, second_in_ref, buffer)
        for b in range(echo.shape[0]):
            parts = extrapolate_block(plan_ref, 2 * (listed + 1), ops_ref, buffer, b)
            for i, part in enumerate(parts):
                cols = pl.ds(i * part.shape[1], part.shape[1])
                leaving[b, :, cols] = pass_ref[b] * part
                echo[b, :, cols] = (reflect_ref[b] * part).astype(echo.dtype)
            for copy in (
                pltpu.make_async_copy(leaving.at[b], transmitted_ref.at[0, b], leave_sems.at[b]),
                pltpu.make_async_copy(echo.at[b], reflected_ref.at[tick, 0, b], echo_sems.at[b]),
            ):
                copy.start()
                copies.append(copy)
        for copy in copies:
            copy.wait()


def grouped_call(kernel, groups, outs, out_specs, known, **options):
    flat = [array for group in groups for array in (group if isinstance(group, list) else [group])]

    def body(*refs):
        refs = list(refs)
        take = lambda count: [refs.pop(0) for _ in range(count)]
        inputs = [take(len(g)) if isinstance(g, list) else refs.pop(0) for g in groups]
        kernel(*inputs, take(len(known)), take(len(outs)), *refs)

    return pl.pallas_call(
        body,
        out_shape=tuple(outs),
        in_specs=[SMEM_SPEC] + [VMEM_SPEC] * (len(flat) - 1) + list(out_specs[: len(known)]),
        out_specs=tuple(out_specs),
        input_output_aliases={len(flat) + i: i for i in range(len(known))},
        **options,
    )(flat[0], *map(in_vmem, flat[1:]), *known)


def neighbour(j, turn, tiles):
    to = j + (1 if (j + turn) % 2 == 0 else -1)
    return to if 0 <= to < tiles else None


def swap_routes(sections, tiles):
    routes = []
    for turn in (0, 1):
        route = []
        for s in range(sections):
            for j in range(tiles):
                to = neighbour(j, turn, tiles)
                end = ((s ^ 1) * tiles + j) if to is None else (s * tiles + to)
                route.append((s * tiles + j, end))
        routes.append(route)
    return routes


def halo_routes(sections, tiles, senders):
    routes = []
    for turn in (0, 1):
        route = []
        for s in range(sections):
            for j in range(tiles):
                to = neighbour(j, turn, tiles)
                real = to is not None and s % 2 in senders
                end = (s + 1) % sections * tiles + to if real else (s ^ 1) * tiles + j
                route.append((s * tiles + j, end))
        routes.append(route)
    return routes


def per_device(
    inflow, source, operators, transmission, reflectivity, send_ids, send_count, pattern
):
    sections, tiles = lax.axis_size("depth"), lax.axis_size("lat")
    ticks = source.shape[0] + 1
    _, blocks, points, columns = inflow.shape
    listed = send_ids.shape[-1]
    taken = operators.shape[2]
    wave_type = pltpu.VMEM((blocks, points, columns), WAVE)
    list_type = pltpu.VMEM((listed * points, columns), WAVE)
    params = pltpu.CompilerParams(vmem_limit_bytes=VMEM_LIMIT)
    tick_cost = pl.CostEstimate(
        flops=0,
        bytes_accessed=0,
        transcendentals=0,
    )
    both = ("depth", "lat")
    deeper = [(s, (s + 1) % sections) for s in range(sections)]

    plan, wave, first, second = pl.pallas_call(
        prepare_kernel,
        out_shape=(
            pltpu.SMEM((2 * (listed + 1) + blocks * taken,), jnp.int32),
            wave_type,
            list_type,
            list_type,
        ),
        in_specs=[ANY_SPEC] * 4,
        out_specs=(SMEM_SPEC,) + (VMEM_SPEC,) * 3,
        scratch_shapes=[
            pltpu.SMEM(send_ids.shape, jnp.int32),
            pltpu.SMEM(send_count.shape, jnp.int32),
            pltpu.SMEM(pattern.shape, jnp.int32),
            pltpu.VMEM((blocks, points, columns), inflow.dtype),
            pltpu.SemaphoreType.DMA((3,)),
            pltpu.SemaphoreType.DMA((blocks,)),
        ],
        compiler_params=params,
        cost_estimate=pl.CostEstimate(
            flops=inflow.size, bytes_accessed=8 * inflow.size, transcendentals=0
        ),
        name="prepare",
    )(*map(in_hbm, (send_ids, send_count, pattern, inflow)))
    loaded_first = first
    routes = swap_routes(sections, tiles)
    first = lax.ppermute(first, both, routes[0])
    second = lax.ppermute(second, both, routes[1])

    column_type = pltpu.VMEM((blocks, points, columns // 2), jnp.float32)
    fixed = pl.pallas_call(
        load_kernel,
        out_shape=(
            pltpu.VMEM(operators.shape, operators.dtype),
            pltpu.VMEM(source.shape, source.dtype),
            column_type,
            column_type,
        ),
        in_specs=[ANY_SPEC] * 4 + [VMEM_SPEC],
        out_specs=(VMEM_SPEC,) * 4,
        scratch_shapes=[
            pltpu.VMEM(transmission.shape, transmission.dtype),
            pltpu.VMEM(reflectivity.shape, reflectivity.dtype),
            pltpu.SemaphoreType.DMA((4,)),
        ],
        compiler_params=params,
        cost_estimate=pl.CostEstimate(
            flops=0, bytes_accessed=4 * (operators.size + source.size), transcendentals=0
        ),
        name="load",
    )(*map(in_hbm, (operators, source, transmission, reflectivity)), in_vmem(loaded_first))
    fixed = [plan, *fixed]

    buffer_type = pltpu.VMEM((blocks + 2 * listed, points, columns), WAVE)

    ODD, EVEN = 1, 0
    crossing = [(s, (s + 1) % sections) for s in range(sections)]
    inside = [(s, s ^ 1) for s in range(sections)]
    pairs = [[s, s + 1] for s in range(0, sections, 2)]
    pair_type = pltpu.VMEM((2, blocks, points, columns), WAVE)
    part_types = [pltpu.VMEM((blocks // 2, points, columns), WAVE)] * 2
    half_types = [pltpu.VMEM((n, points, columns), WAVE) for n in (blocks // 2, blocks - blocks // 2)]

    def lists_of(extra):
        return [pltpu.VMEM((listed * points + extra, columns), WAVE)] * 2

    def exchange(lists, senders):
        routes = halo_routes(sections, tiles, senders)
        return [lax.ppermute(a, both, route) for a, route in zip(lists, routes)]

    arrived = {parity: ([wave], first, second) for parity in (ODD, EVEN)}
    echoes = []
    for tick in range(ticks - 1):
        first_step, last_step = tick == 0, tick == ticks - 2
        known = []
        waves, halos = {}, {}
        for parity in (ODD, EVEN):
            if first_step:
                extra = 0
            elif last_step:
                extra = 16 if parity == ODD else 0
            else:
                extra = 0 if parity == ODD else 16
            if parity == ODD:
                long = 0 if last_step else 16
                to_next = [pltpu.VMEM((blocks * points + long, columns), WAVE)]
            else:
                to_next = [pair_type] if last_step else half_types if first_step else part_types
            outs = [wave_type, *lists_of(extra), *to_next]
            settled = arrived[EVEN][0] if last_step and parity == ODD else []
            echo, *lists = grouped_call(
                functools.partial(tick_kernel, parity, tick, sections),
                [*fixed, *arrived[parity], settled],
                outs,
                [VMEM_SPEC] * len(outs),
                [in_vmem(a) for a in known],
                scratch_shapes=[buffer_type, pltpu.VMEM(wave_type.shape, WAVE)],
                compiler_params=params,
                cost_estimate=tick_cost,
                name=f"tick{tick}" + ("_odd" if parity else "_even"),
            )
            lists, onward = lists[:2], lists[2:]
            known = [echo, *lists] if first_step else [echo]
            if parity == ODD:
                waves[EVEN] = [lax.ppermute(onward[0], "depth", crossing)]
            elif last_step:
                waves[ODD] = [lax.all_to_all(onward[0], "depth", 0, 0, axis_index_groups=pairs)]
            else:
                waves[ODD] = [lax.ppermute(a, "depth", inside) for a in onward]
            if not first_step:
                halos[1 - parity] = exchange(lists, (parity,))
        if first_step:
            halos[ODD] = halos[EVEN] = exchange(lists, (ODD, EVEN))
        arrived = {parity: (waves[parity], *halos[parity]) for parity in (ODD, EVEN)}
        echoes.append(echo)

    tick = ticks - 1
    results = []
    result_types = (
        jax.ShapeDtypeStruct((ticks, 1, blocks, points, columns), WAVE),
        jax.ShapeDtypeStruct((1, blocks, points, columns), jnp.float32),
    )
    for parity in (ODD, EVEN):
        results = grouped_call(
            functools.partial(last_kernel, parity, tick),
            [*fixed, *arrived[parity], echoes],
            result_types,
            [ANY_SPEC] * 2,
            list(results),
            scratch_shapes=[
                buffer_type,
                pltpu.VMEM((blocks, points, columns), WAVE),
                pltpu.VMEM((blocks, points, columns), jnp.float32),
                pltpu.SemaphoreType.DMA((tick,)),
                pltpu.SemaphoreType.DMA((blocks,)),
                pltpu.SemaphoreType.DMA((blocks,)),
            ],
            compiler_params=params,
            cost_estimate=tick_cost,
            name="last_tick" + ("_odd" if parity else "_even"),
        )
    return tuple(results)


def solution(mesh):
    return jax.shard_map(
        per_device,
        mesh=mesh,
        in_specs=(
            P("depth", "lat", None, None),
            P(None, "lat", None, None),
            P("depth", "lat", None, None, None, None),
            P("depth", "lat", None),
            P("depth", "lat", None),
            P("lat", None, None),
            P("lat", None),
            P("lat", None),
        ),
        out_specs=(P(None, "depth", "lat", None, None), P("depth", "lat", None, None)),
        check_vma=False,
    )
```

```python
import functools

import jax
import jax.numpy as jnp
from jax import lax
from jax.experimental import pallas as pl
from jax.experimental.pallas import tpu as pltpu
from jax.sharding import PartitionSpec as P

WAVE = jnp.bfloat16
SMEM_SPEC = pl.BlockSpec(memory_space=pltpu.SMEM)
VMEM_SPEC = pl.BlockSpec(memory_space=pltpu.VMEM)
ANY_SPEC = pl.BlockSpec(memory_space=pl.ANY)
VMEM_LIMIT = 8 * 1024 * 1024
LOWER, UPPER = 0, 1


def in_vmem(array):
    return pltpu.with_memory_space_constraint(array, pltpu.VMEM)


def in_hbm(array):
    return pltpu.with_memory_space_constraint(array, pltpu.HBM)


def write_lists(tile, plan_ref, blocks_ref, lists):
    points = blocks_ref.shape[1]
    listed = lists[0].shape[0] // points
    parity = lax.rem(tile, 2)
    for list_ref, side in zip(lists, (UPPER - parity, parity)):
        count = plan_ref[2 * listed + side]
        for slot in range(listed):
            live = slot < count

            @pl.when(live)
            def _():
                list_ref[slot * points : (slot + 1) * points] = blocks_ref[
                    plan_ref[side * listed + slot]
                ]

            @pl.when(jnp.logical_not(live))
            def _():
                list_ref[slot * points : (slot + 1) * points] = jnp.zeros(
                    blocks_ref.shape[1:], list_ref.dtype
                )


def prepare_kernel(
    ids_hbm, count_hbm, pattern_hbm, inflow_hbm, plan_ref, wave_ref, first_ref, second_ref,
    ids, count, pattern, landed, small_sems, sems,
):
    blocks = wave_ref.shape[0]
    small = [
        pltpu.make_async_copy(source, target, small_sems.at[i])
        for i, (source, target) in enumerate(
            ((ids_hbm, ids), (count_hbm, count), (pattern_hbm, pattern))
        )
    ]
    large = [
        pltpu.make_async_copy(inflow_hbm.at[0, b], landed.at[b], sems.at[b]) for b in range(blocks)
    ]
    for copy in small + large:
        copy.start()
    for copy in small:
        copy.wait()
    _, sides, listed = ids.shape
    taken = pattern.shape[1]
    for side in range(sides):
        for slot in range(listed):
            plan_ref[side * listed + slot] = ids[0, side, slot]
        plan_ref[sides * listed + side] = count[0, side]
    for b in range(blocks):
        for k in range(taken):
            plan_ref[sides * (listed + 1) + b * taken + k] = pattern[b, k]
    for b, copy in enumerate(large):
        copy.wait()
        wave_ref[b] = landed[b].astype(wave_ref.dtype)
    write_lists(lax.axis_index("lat"), plan_ref, wave_ref, (first_ref, second_ref))


def load_kernel(
    ops_hbm, source_hbm, pass_hbm, reflect_hbm, after_ref,
    ops_ref, source_ref, pass_ref, reflect_ref, pass_rows, reflect_rows, sems,
):
    del after_ref
    copies = [
        pltpu.make_async_copy(source, target, sems.at[i])
        for i, (source, target) in enumerate(
            (
                (pass_hbm, pass_rows),
                (reflect_hbm, reflect_rows),
                (ops_hbm, ops_ref),
                (source_hbm, source_ref),
            )
        )
    ]
    for copy in copies:
        copy.start()
    for copy, rows, columns_ref in zip(copies, (pass_rows, reflect_rows), (pass_ref, reflect_ref)):
        copy.wait()
        for b in range(columns_ref.shape[0]):
            row = rows[0, pl.ds(b, 1), :]
            columns_ref[b] = jnp.broadcast_to(row, columns_ref.shape[1:]).T
    for copy in copies[2:]:
        copy.wait()


def fill_buffer(section, tick, source_ref, wave_refs, first_ref, second_ref, buffer):
    blocks, points = source_ref.shape[1:3]
    listed = (buffer.shape[0] - blocks) // 2

    def fill(start, ref):
        if len(ref.shape) == 2:
            count = min(ref.shape[0] // points, blocks)
            part = ref[: count * points].reshape(count, points, -1)
        else:
            part = ref[0] if len(ref.shape) == 4 else ref[...]
        buffer[pl.ds(start, part.shape[0])] = part
        return start + part.shape[0]

    def fill_wave():
        start = 0
        for wave_ref in wave_refs:
            start = fill(start, wave_ref)

    if tick == 0:
        fill_wave()
    else:
        pl.when(section != 0)(fill_wave)

        @pl.when(section == 0)
        def _():
            buffer[:blocks] = source_ref[tick - 1]

    parity = lax.rem(lax.axis_index("lat"), 2)
    fill(blocks + (1 - parity) * listed, first_ref)
    fill(blocks + parity * listed, second_ref)


def extrapolate_block(plan_ref, pattern_start, ops_ref, buffer, b):
    taken = ops_ref.shape[2]
    points = ops_ref.shape[5]
    left = jnp.concatenate(
        [ops_ref[0, b, k].reshape(2 * points, points) for k in range(taken)], axis=1
    )
    right = jnp.concatenate(
        [buffer[plan_ref[pattern_start + b * taken + k]] for k in range(taken)], axis=0
    )
    products = jnp.dot(left, right, preferred_element_type=jnp.float32)
    half = products.shape[1] // 2
    real_part = products[:points, :half] - products[points:, half:]
    imag_part = products[:points, half:] + products[points:, :half]
    return real_part, imag_part


def ids_of(plan_ref, ops_ref):
    return (plan_ref.shape[0] - ops_ref.shape[1] * ops_ref.shape[2]) // 2 - 1


def acts(section, parity):
    return lax.rem(section, 2) == parity


def tick_kernel(
    parity, tick, sections, writes, plan_ref, ops_ref, source_ref, pass_ref, reflect_ref,
    wave_refs, first_in_ref, second_in_ref, earlier, known_refs, out_refs,
    buffer, onward, write_sems,
):
    del known_refs
    echo_ref, first_ref, second_ref, *onward_refs = out_refs
    section = lax.axis_index("depth")
    if writes:
        reflected_ref = onward_refs.pop()

        @pl.when(jnp.logical_not(acts(section, parity)))
        def _():
            copies = [
                pltpu.make_async_copy(
                    (earlier[i] if i < len(earlier) else echo_ref).at[...],
                    reflected_ref.at[t, 0],
                    write_sems.at[i],
                )
                for i, t in enumerate(writes)
            ]
            for copy in copies:
                copy.start()
            for copy in copies:
                copy.wait()

    tile = lax.axis_index("lat")
    listed = ids_of(plan_ref, ops_ref)

    @pl.when(acts(section, parity))
    def _():
        fill_buffer(section, tick, source_ref, wave_refs, first_in_ref, second_in_ref, buffer)
        for b in range(echo_ref.shape[0]):
            parts = extrapolate_block(plan_ref, 2 * (listed + 1), ops_ref, buffer, b)
            for i, part in enumerate(parts):
                cols = pl.ds(i * part.shape[1], part.shape[1])
                onward[b, :, cols] = (pass_ref[b] * part).astype(onward.dtype)
                echo_ref[b, :, cols] = (reflect_ref[b] * part).astype(echo_ref.dtype)
        start = 0
        for onward_ref in onward_refs:
            if len(onward_ref.shape) == 2:
                rows = onward.shape[0] * onward.shape[1]
                onward_ref[:rows] = onward[...].reshape(rows, onward.shape[2])
            else:
                slot = onward_ref if len(onward_ref.shape) == 3 else onward_ref.at[1]
                slot[...] = onward[start : start + slot.shape[0]]
                start += slot.shape[0]

        @pl.when(section != sections - 1)
        def _():
            write_lists(tile, plan_ref, onward, (first_ref, second_ref))

        @pl.when(section == sections - 1)
        def _():
            write_lists(tile, plan_ref, source_ref.at[tick], (first_ref, second_ref))


def last_kernel(
    parity, tick, plan_ref, ops_ref, source_ref, pass_ref, reflect_ref,
    wave_refs, first_in_ref, second_in_ref, earlier, known_refs, out_refs,
    buffer, echo, leaving, early_sems, echo_sems, leave_sems,
):
    del known_refs
    reflected_ref, transmitted_ref = out_refs
    section = lax.axis_index("depth")
    listed = ids_of(plan_ref, ops_ref)

    @pl.when(acts(section, parity))
    def _():
        copies = [
            pltpu.make_async_copy(
                ref, reflected_ref.at[tick - len(earlier) + i, 0], early_sems.at[i]
            )
            for i, ref in enumerate(earlier)
        ]
        for copy in copies:
            copy.start()
        fill_buffer(section, tick, source_ref, wave_refs, first_in_ref, second_in_ref, buffer)
        for b in range(echo.shape[0]):
            parts = extrapolate_block(plan_ref, 2 * (listed + 1), ops_ref, buffer, b)
            for i, part in enumerate(parts):
                cols = pl.ds(i * part.shape[1], part.shape[1])
                leaving[b, :, cols] = pass_ref[b] * part
                echo[b, :, cols] = (reflect_ref[b] * part).astype(echo.dtype)
            for copy in (
                pltpu.make_async_copy(leaving.at[b], transmitted_ref.at[0, b], leave_sems.at[b]),
                pltpu.make_async_copy(echo.at[b], reflected_ref.at[tick, 0, b], echo_sems.at[b]),
            ):
                copy.start()
                copies.append(copy)
        for copy in copies:
            copy.wait()


def grouped_call(kernel, groups, outs, out_specs, known, **options):
    flat = [array for group in groups for array in (group if isinstance(group, list) else [group])]
    kept = [(i, array) for i, array in enumerate(known) if array is not None]

    def body(*refs):
        refs = list(refs)
        take = lambda count: [refs.pop(0) for _ in range(count)]
        inputs = [take(len(g)) if isinstance(g, list) else refs.pop(0) for g in groups]
        kernel(*inputs, take(len(kept)), take(len(outs)), *refs)

    return pl.pallas_call(
        body,
        out_shape=tuple(outs),
        in_specs=[SMEM_SPEC] + [VMEM_SPEC] * (len(flat) - 1) + [out_specs[i] for i, _ in kept],
        out_specs=tuple(out_specs),
        input_output_aliases={len(flat) + n: i for n, (i, _) in enumerate(kept)},
        **options,
    )(
        flat[0],
        *map(in_vmem, flat[1:]),
        *[a if out_specs[i] is ANY_SPEC else in_vmem(a) for i, a in kept],
    )


def neighbour(j, turn, tiles):
    to = j + (1 if (j + turn) % 2 == 0 else -1)
    return to if 0 <= to < tiles else None


def swap_routes(sections, tiles):
    routes = []
    for turn in (0, 1):
        route = []
        for s in range(sections):
            for j in range(tiles):
                to = neighbour(j, turn, tiles)
                end = ((s ^ 1) * tiles + j) if to is None else (s * tiles + to)
                route.append((s * tiles + j, end))
        routes.append(route)
    return routes


def halo_routes(sections, tiles, senders):
    routes = []
    for turn in (0, 1):
        route = []
        for s in range(sections):
            for j in range(tiles):
                to = neighbour(j, turn, tiles)
                real = to is not None and s % 2 in senders
                end = (s + 1) % sections * tiles + to if real else (s ^ 1) * tiles + j
                route.append((s * tiles + j, end))
        routes.append(route)
    return routes


def per_device(
    inflow, source, operators, transmission, reflectivity, send_ids, send_count, pattern
):
    sections, tiles = lax.axis_size("depth"), lax.axis_size("lat")
    ticks = source.shape[0] + 1
    _, blocks, points, columns = inflow.shape
    listed = send_ids.shape[-1]
    taken = operators.shape[2]
    wave_type = pltpu.VMEM((blocks, points, columns), WAVE)
    list_type = pltpu.VMEM((listed * points, columns), WAVE)
    params = pltpu.CompilerParams(vmem_limit_bytes=VMEM_LIMIT)
    tick_cost = pl.CostEstimate(
        flops=0,
        bytes_accessed=0,
        transcendentals=0,
    )
    both = ("depth", "lat")
    deeper = [(s, (s + 1) % sections) for s in range(sections)]

    plan, wave, first, second = pl.pallas_call(
        prepare_kernel,
        out_shape=(
            pltpu.SMEM((2 * (listed + 1) + blocks * taken,), jnp.int32),
            wave_type,
            list_type,
            list_type,
        ),
        in_specs=[ANY_SPEC] * 4,
        out_specs=(SMEM_SPEC,) + (VMEM_SPEC,) * 3,
        scratch_shapes=[
            pltpu.SMEM(send_ids.shape, jnp.int32),
            pltpu.SMEM(send_count.shape, jnp.int32),
            pltpu.SMEM(pattern.shape, jnp.int32),
            pltpu.VMEM((blocks, points, columns), inflow.dtype),
            pltpu.SemaphoreType.DMA((3,)),
            pltpu.SemaphoreType.DMA((blocks,)),
        ],
        compiler_params=params,
        cost_estimate=pl.CostEstimate(
            flops=inflow.size, bytes_accessed=8 * inflow.size, transcendentals=0
        ),
        name="prepare",
    )(*map(in_hbm, (send_ids, send_count, pattern, inflow)))
    loaded_first = first
    routes = swap_routes(sections, tiles)
    first = lax.ppermute(first, both, routes[0])
    second = lax.ppermute(second, both, routes[1])

    column_type = pltpu.VMEM((blocks, points, columns // 2), jnp.float32)
    fixed = pl.pallas_call(
        load_kernel,
        out_shape=(
            pltpu.VMEM(operators.shape, operators.dtype),
            pltpu.VMEM(source.shape, source.dtype),
            column_type,
            column_type,
        ),
        in_specs=[ANY_SPEC] * 4 + [VMEM_SPEC],
        out_specs=(VMEM_SPEC,) * 4,
        scratch_shapes=[
            pltpu.VMEM(transmission.shape, transmission.dtype),
            pltpu.VMEM(reflectivity.shape, reflectivity.dtype),
            pltpu.SemaphoreType.DMA((4,)),
        ],
        compiler_params=params,
        cost_estimate=pl.CostEstimate(
            flops=0, bytes_accessed=4 * (operators.size + source.size), transcendentals=0
        ),
        name="load",
    )(*map(in_hbm, (operators, source, transmission, reflectivity)), in_vmem(loaded_first))
    fixed = [plan, *fixed]

    buffer_type = pltpu.VMEM((blocks + 2 * listed, points, columns), WAVE)

    ODD, EVEN = 1, 0
    crossing = [(s, (s + 1) % sections) for s in range(sections)]
    inside = [(s, s ^ 1) for s in range(sections)]
    pairs = [[s, s + 1] for s in range(0, sections, 2)]
    pair_type = pltpu.VMEM((2, blocks, points, columns), WAVE)
    part_types = [pltpu.VMEM((blocks // 2, points, columns), WAVE)] * 2
    half_types = [pltpu.VMEM((n, points, columns), WAVE) for n in (blocks // 2, blocks - blocks // 2)]

    def lists_of(extra):
        return [pltpu.VMEM((listed * points + extra, columns), WAVE)] * 2

    def exchange(lists, senders):
        routes = halo_routes(sections, tiles, senders)
        return [lax.ppermute(a, both, route) for a, route in zip(lists, routes)]

    result_types = (
        jax.ShapeDtypeStruct((ticks, 1, blocks, points, columns), WAVE),
        jax.ShapeDtypeStruct((1, blocks, points, columns), jnp.float32),
    )
    arrived = {parity: ([wave], first, second) for parity in (ODD, EVEN)}
    echoes = []
    reflected = None
    for tick in range(ticks - 1):
        first_step, last_step = tick == 0, tick == ticks - 2
        known = []
        waves, halos = {}, {}
        for parity in (ODD, EVEN):
            if first_step:
                extra = 0
            elif last_step:
                extra = 16 if parity == ODD else 0
            else:
                extra = 0 if parity == ODD else 16
            if parity == ODD:
                long = 0 if first_step or last_step else 16
                to_next = [pltpu.VMEM((blocks * points + long, columns), WAVE)]
            else:
                to_next = [pair_type] if last_step else half_types if first_step else part_types
            outs = [wave_type, *lists_of(extra), *to_next]
            specs = [VMEM_SPEC] * len(outs)
            writes = range(0)
            if parity == EVEN and tick >= 1:
                writes = range(0 if tick == 1 else tick, tick + 1)
            if parity == ODD and tick >= 2:
                writes = range(0 if tick == 2 else tick - 1, tick)
            known = known + [None] * (len(outs) - len(known))
            if writes:
                outs, specs, known = outs + [result_types[0]], specs + [ANY_SPEC], known + [reflected]
            echo, *lists = grouped_call(
                functools.partial(tick_kernel, parity, tick, sections, tuple(writes)),
                [*fixed, *arrived[parity], [echoes[t] for t in writes if t < tick]],
                outs,
                specs,
                known,
                scratch_shapes=[
                    buffer_type,
                    pltpu.VMEM(wave_type.shape, WAVE),
                    pltpu.SemaphoreType.DMA((2,)),
                ],
                compiler_params=params,
                cost_estimate=tick_cost,
                name=f"tick{tick}" + ("_odd" if parity else "_even"),
            )
            if writes:
                reflected = lists.pop()
            lists, onward = lists[:2], lists[2:]
            known = [echo, *lists] if first_step else [echo]
            if parity == ODD:
                waves[EVEN] = [lax.ppermute(onward[0], "depth", crossing)]
            elif last_step:
                waves[ODD] = [lax.all_to_all(onward[0], "depth", 0, 0, axis_index_groups=pairs)]
            else:
                waves[ODD] = [lax.ppermute(a, "depth", inside) for a in onward]
            if not first_step:
                halos[1 - parity] = exchange(lists, (parity,))
        if first_step:
            halos[ODD] = halos[EVEN] = exchange(lists, (ODD, EVEN))
        arrived = {parity: (waves[parity], *halos[parity]) for parity in (ODD, EVEN)}
        echoes.append(echo)

    tick = ticks - 1
    unwritten = {ODD: [], EVEN: echoes[-1:] if ticks > 3 else echoes}
    results = [reflected, None]
    for parity in (ODD, EVEN):
        results = grouped_call(
            functools.partial(last_kernel, parity, tick),
            [*fixed, *arrived[parity], unwritten[parity]],
            result_types,
            [ANY_SPEC] * 2,
            list(results),
            scratch_shapes=[
                buffer_type,
                pltpu.VMEM((blocks, points, columns), WAVE),
                pltpu.VMEM((blocks, points, columns), jnp.float32),
                pltpu.SemaphoreType.DMA((tick,)),
                pltpu.SemaphoreType.DMA((blocks,)),
                pltpu.SemaphoreType.DMA((blocks,)),
            ],
            compiler_params=params,
            cost_estimate=tick_cost,
            name="last_tick" + ("_odd" if parity else "_even"),
        )
    return tuple(results)


def solution(mesh):
    return jax.shard_map(
        per_device,
        mesh=mesh,
        in_specs=(
            P("depth", "lat", None, None),
            P(None, "lat", None, None),
            P("depth", "lat", None, None, None, None),
            P("depth", "lat", None),
            P("depth", "lat", None),
            P("lat", None, None),
            P("lat", None),
            P("lat", None),
        ),
        out_specs=(P(None, "depth", "lat", None, None), P("depth", "lat", None, None)),
        check_vma=False,
    )
```

```python
import functools

import jax
import jax.numpy as jnp
from jax import lax
from jax.experimental import pallas as pl
from jax.experimental.pallas import tpu as pltpu
from jax.sharding import PartitionSpec as P

WAVE = jnp.bfloat16
SMEM_SPEC = pl.BlockSpec(memory_space=pltpu.SMEM)
VMEM_SPEC = pl.BlockSpec(memory_space=pltpu.VMEM)
ANY_SPEC = pl.BlockSpec(memory_space=pl.ANY)
VMEM_LIMIT = 8 * 1024 * 1024
LOWER, UPPER = 0, 1


def in_vmem(array):
    return pltpu.with_memory_space_constraint(array, pltpu.VMEM)


def in_hbm(array):
    return pltpu.with_memory_space_constraint(array, pltpu.HBM)


def write_lists(tile, plan_ref, blocks_ref, lists):
    points = blocks_ref.shape[1]
    listed = lists[0].shape[0] // points
    parity = lax.rem(tile, 2)
    for list_ref, side in zip(lists, (UPPER - parity, parity)):
        count = plan_ref[2 * listed + side]
        for slot in range(listed):
            live = slot < count

            @pl.when(live)
            def _():
                list_ref[slot * points : (slot + 1) * points] = blocks_ref[
                    plan_ref[side * listed + slot]
                ]

            @pl.when(jnp.logical_not(live))
            def _():
                list_ref[slot * points : (slot + 1) * points] = jnp.zeros(
                    blocks_ref.shape[1:], list_ref.dtype
                )


def prepare_kernel(
    ids_hbm, count_hbm, pattern_hbm, inflow_hbm, plan_ref, wave_ref, first_ref, second_ref,
    ids, count, pattern, landed, small_sems, sems,
):
    blocks = wave_ref.shape[0]
    small = [
        pltpu.make_async_copy(source, target, small_sems.at[i])
        for i, (source, target) in enumerate(
            ((ids_hbm, ids), (count_hbm, count), (pattern_hbm, pattern))
        )
    ]
    large = [
        pltpu.make_async_copy(inflow_hbm.at[0, b], landed.at[b], sems.at[b]) for b in range(blocks)
    ]
    for copy in small + large:
        copy.start()
    for copy in small:
        copy.wait()
    _, sides, listed = ids.shape
    taken = pattern.shape[1]
    for side in range(sides):
        for slot in range(listed):
            plan_ref[side * listed + slot] = ids[0, side, slot]
        plan_ref[sides * listed + side] = count[0, side]
    for b in range(blocks):
        for k in range(taken):
            plan_ref[sides * (listed + 1) + b * taken + k] = pattern[b, k]
    for b, copy in enumerate(large):
        copy.wait()
        wave_ref[b] = landed[b].astype(wave_ref.dtype)
    write_lists(lax.axis_index("lat"), plan_ref, wave_ref, (first_ref, second_ref))


def load_kernel(
    ops_hbm, source_hbm, pass_hbm, reflect_hbm, after_ref,
    ops_ref, source_ref, pass_ref, reflect_ref, pass_rows, reflect_rows, sems,
):
    del after_ref
    copies = [
        pltpu.make_async_copy(source, target, sems.at[i])
        for i, (source, target) in enumerate(
            (
                (pass_hbm, pass_rows),
                (reflect_hbm, reflect_rows),
                (ops_hbm, ops_ref),
                (source_hbm, source_ref),
            )
        )
    ]
    for copy in copies:
        copy.start()
    for copy, rows, columns_ref in zip(copies, (pass_rows, reflect_rows), (pass_ref, reflect_ref)):
        copy.wait()
        for b in range(columns_ref.shape[0]):
            row = rows[0, pl.ds(b, 1), :]
            columns_ref[b] = jnp.broadcast_to(row, columns_ref.shape[1:]).T
    for copy in copies[2:]:
        copy.wait()


def fill_buffer(section, tick, source_ref, wave_refs, first_ref, second_ref, buffer):
    blocks, points = source_ref.shape[1:3]
    listed = (buffer.shape[0] - blocks) // 2

    def fill(start, ref):
        if len(ref.shape) == 2:
            count = min(ref.shape[0] // points, blocks)
            part = ref[: count * points].reshape(count, points, -1)
        else:
            part = ref[0] if len(ref.shape) == 4 else ref[...]
        buffer[pl.ds(start, part.shape[0])] = part
        return start + part.shape[0]

    def fill_wave():
        start = 0
        for wave_ref in wave_refs:
            start = fill(start, wave_ref)

    if tick == 0:
        fill_wave()
    else:
        pl.when(section != 0)(fill_wave)

        @pl.when(section == 0)
        def _():
            buffer[:blocks] = source_ref[tick - 1]

    parity = lax.rem(lax.axis_index("lat"), 2)
    fill(blocks + (1 - parity) * listed, first_ref)
    fill(blocks + parity * listed, second_ref)


def extrapolate_block(plan_ref, pattern_start, ops_ref, buffer, b):
    taken = ops_ref.shape[2]
    points = ops_ref.shape[5]
    left = jnp.concatenate(
        [ops_ref[0, b, k].reshape(2 * points, points) for k in range(taken)], axis=1
    )
    right = jnp.concatenate(
        [buffer[plan_ref[pattern_start + b * taken + k]] for k in range(taken)], axis=0
    )
    products = jnp.dot(left, right, preferred_element_type=jnp.float32)
    half = products.shape[1] // 2
    real_part = products[:points, :half] - products[points:, half:]
    imag_part = products[:points, half:] + products[points:, :half]
    return real_part, imag_part


def ids_of(plan_ref, ops_ref):
    return (plan_ref.shape[0] - ops_ref.shape[1] * ops_ref.shape[2]) // 2 - 1


def acts(section, parity):
    return lax.rem(section, 2) == parity


def tick_kernel(
    parity, tick, sections, plan_ref, ops_ref, source_ref, pass_ref, reflect_ref,
    wave_refs, first_in_ref, second_in_ref, known_refs, out_refs, buffer, onward,
):
    del known_refs
    echo_ref, first_ref, second_ref, *onward_refs = out_refs
    section = lax.axis_index("depth")
    tile = lax.axis_index("lat")
    listed = ids_of(plan_ref, ops_ref)

    @pl.when(acts(section, parity))
    def _():
        fill_buffer(section, tick, source_ref, wave_refs, first_in_ref, second_in_ref, buffer)
        for b in range(echo_ref.shape[0]):
            parts = extrapolate_block(plan_ref, 2 * (listed + 1), ops_ref, buffer, b)
            for i, part in enumerate(parts):
                cols = pl.ds(i * part.shape[1], part.shape[1])
                onward[b, :, cols] = (pass_ref[b] * part).astype(onward.dtype)
                echo_ref[b, :, cols] = (reflect_ref[b] * part).astype(echo_ref.dtype)
        start = 0
        for onward_ref in onward_refs:
            if len(onward_ref.shape) == 2:
                rows = onward.shape[0] * onward.shape[1]
                onward_ref[:rows] = onward[...].reshape(rows, onward.shape[2])
            else:
                slot = onward_ref if len(onward_ref.shape) == 3 else onward_ref.at[1]
                slot[...] = onward[start : start + slot.shape[0]]
                start += slot.shape[0]

        @pl.when(section != sections - 1)
        def _():
            write_lists(tile, plan_ref, onward, (first_ref, second_ref))

        @pl.when(section == sections - 1)
        def _():
            write_lists(tile, plan_ref, source_ref.at[tick], (first_ref, second_ref))


def last_kernel(
    parity, tick, plan_ref, ops_ref, source_ref, pass_ref, reflect_ref,
    wave_refs, first_in_ref, second_in_ref, earlier, known_refs, out_refs,
    buffer, echo, leaving, early_sems, echo_sems, leave_sems,
):
    del known_refs
    reflected_ref, transmitted_ref = out_refs
    section = lax.axis_index("depth")
    listed = ids_of(plan_ref, ops_ref)

    @pl.when(acts(section, parity))
    def _():
        copies = [
            pltpu.make_async_copy(earlier[t], reflected_ref.at[t, 0], early_sems.at[t])
            for t in range(tick)
        ]
        for copy in copies:
            copy.start()
        fill_buffer(section, tick, source_ref, wave_refs, first_in_ref, second_in_ref, buffer)
        for b in range(echo.shape[0]):
            parts = extrapolate_block(plan_ref, 2 * (listed + 1), ops_ref, buffer, b)
            for i, part in enumerate(parts):
                cols = pl.ds(i * part.shape[1], part.shape[1])
                leaving[b, :, cols] = pass_ref[b] * part
                echo[b, :, cols] = (reflect_ref[b] * part).astype(echo.dtype)
            for copy in (
                pltpu.make_async_copy(leaving.at[b], transmitted_ref.at[0, b], leave_sems.at[b]),
                pltpu.make_async_copy(echo.at[b], reflected_ref.at[tick, 0, b], echo_sems.at[b]),
            ):
                copy.start()
                copies.append(copy)
        for copy in copies:
            copy.wait()


def grouped_call(kernel, groups, outs, out_specs, known, **options):
    flat = [array for group in groups for array in (group if isinstance(group, list) else [group])]

    def body(*refs):
        refs = list(refs)
        take = lambda count: [refs.pop(0) for _ in range(count)]
        inputs = [take(len(g)) if isinstance(g, list) else refs.pop(0) for g in groups]
        kernel(*inputs, take(len(known)), take(len(outs)), *refs)

    return pl.pallas_call(
        body,
        out_shape=tuple(outs),
        in_specs=[SMEM_SPEC] + [VMEM_SPEC] * (len(flat) - 1) + list(out_specs[: len(known)]),
        out_specs=tuple(out_specs),
        input_output_aliases={len(flat) + i: i for i in range(len(known))},
        **options,
    )(flat[0], *map(in_vmem, flat[1:]), *known)


def neighbour(j, turn, tiles):
    to = j + (1 if (j + turn) % 2 == 0 else -1)
    return to if 0 <= to < tiles else None


def swap_routes(sections, tiles):
    routes = []
    for turn in (0, 1):
        route = []
        for s in range(sections):
            for j in range(tiles):
                to = neighbour(j, turn, tiles)
                end = ((s ^ 1) * tiles + j) if to is None else (s * tiles + to)
                route.append((s * tiles + j, end))
        routes.append(route)
    return routes


def halo_routes(sections, tiles, senders):
    routes = []
    for turn in (0, 1):
        route = []
        for s in range(sections):
            for j in range(tiles):
                to = neighbour(j, turn, tiles)
                real = to is not None and s % 2 in senders
                end = (s + 1) % sections * tiles + to if real else (s ^ 1) * tiles + j
                route.append((s * tiles + j, end))
        routes.append(route)
    return routes


def per_device(
    inflow, source, operators, transmission, reflectivity, send_ids, send_count, pattern
):
    sections, tiles = lax.axis_size("depth"), lax.axis_size("lat")
    ticks = source.shape[0] + 1
    _, blocks, points, columns = inflow.shape
    listed = send_ids.shape[-1]
    taken = operators.shape[2]
    wave_type = pltpu.VMEM((blocks, points, columns), WAVE)
    list_type = pltpu.VMEM((listed * points, columns), WAVE)
    params = pltpu.CompilerParams(vmem_limit_bytes=VMEM_LIMIT)
    tick_cost = pl.CostEstimate(
        flops=0,
        bytes_accessed=0,
        transcendentals=0,
    )
    both = ("depth", "lat")
    deeper = [(s, (s + 1) % sections) for s in range(sections)]

    plan, wave, first, second = pl.pallas_call(
        prepare_kernel,
        out_shape=(
            pltpu.SMEM((2 * (listed + 1) + blocks * taken,), jnp.int32),
            wave_type,
            list_type,
            list_type,
        ),
        in_specs=[ANY_SPEC] * 4,
        out_specs=(SMEM_SPEC,) + (VMEM_SPEC,) * 3,
        scratch_shapes=[
            pltpu.SMEM(send_ids.shape, jnp.int32),
            pltpu.SMEM(send_count.shape, jnp.int32),
            pltpu.SMEM(pattern.shape, jnp.int32),
            pltpu.VMEM((blocks, points, columns), inflow.dtype),
            pltpu.SemaphoreType.DMA((3,)),
            pltpu.SemaphoreType.DMA((blocks,)),
        ],
        compiler_params=params,
        cost_estimate=pl.CostEstimate(
            flops=inflow.size, bytes_accessed=8 * inflow.size, transcendentals=0
        ),
        name="prepare",
    )(*map(in_hbm, (send_ids, send_count, pattern, inflow)))
    loaded_first = first
    routes = swap_routes(sections, tiles)
    first = lax.ppermute(first, both, routes[0])
    second = lax.ppermute(second, both, routes[1])

    column_type = pltpu.VMEM((blocks, points, columns // 2), jnp.float32)
    fixed = pl.pallas_call(
        load_kernel,
        out_shape=(
            pltpu.VMEM(operators.shape, operators.dtype),
            pltpu.VMEM(source.shape, source.dtype),
            column_type,
            column_type,
        ),
        in_specs=[ANY_SPEC] * 4 + [VMEM_SPEC],
        out_specs=(VMEM_SPEC,) * 4,
        scratch_shapes=[
            pltpu.VMEM(transmission.shape, transmission.dtype),
            pltpu.VMEM(reflectivity.shape, reflectivity.dtype),
            pltpu.SemaphoreType.DMA((4,)),
        ],
        compiler_params=params,
        cost_estimate=pl.CostEstimate(
            flops=0, bytes_accessed=4 * (operators.size + source.size), transcendentals=0
        ),
        name="load",
    )(*map(in_hbm, (operators, source, transmission, reflectivity)), in_vmem(loaded_first))
    fixed = [plan, *fixed]

    buffer_type = pltpu.VMEM((blocks + 2 * listed, points, columns), WAVE)

    ODD, EVEN = 1, 0
    crossing = [(s, (s + 1) % sections) for s in range(sections)]
    inside = [(s, s ^ 1) for s in range(sections)]
    pairs = [[s, s + 1] for s in range(0, sections, 2)]
    pair_type = pltpu.VMEM((2, blocks, points, columns), WAVE)
    part_types = [pltpu.VMEM((blocks // 2, points, columns), WAVE)] * 2
    half_types = [pltpu.VMEM((n, points, columns), WAVE) for n in (blocks // 2, blocks - blocks // 2)]

    def lists_of(extra):
        return [pltpu.VMEM((listed * points + extra, columns), WAVE)] * 2

    def exchange(lists, senders):
        routes = halo_routes(sections, tiles, senders)
        return [lax.ppermute(a, both, route) for a, route in zip(lists, routes)]

    arrived = {parity: ([wave], first, second) for parity in (ODD, EVEN)}
    echoes = []
    for tick in range(ticks - 1):
        first_step, last_step = tick == 0, tick == ticks - 2
        known = []
        waves, halos = {}, {}
        for parity in (ODD, EVEN):
            if first_step:
                extra = 0
            elif last_step:
                extra = 16 if parity == ODD else 0
            else:
                extra = 0 if parity == ODD else 32
            if parity == ODD:
                long = 0 if first_step or last_step else 32
                to_next = [pltpu.VMEM((blocks * points + long, columns), WAVE)]
            else:
                to_next = [pair_type] if last_step else half_types if first_step else part_types
            outs = [wave_type, *lists_of(extra), *to_next]
            echo, *lists = grouped_call(
                functools.partial(tick_kernel, parity, tick, sections),
                [*fixed, *arrived[parity]],
                outs,
                [VMEM_SPEC] * len(outs),
                [in_vmem(a) for a in known],
                scratch_shapes=[buffer_type, pltpu.VMEM(wave_type.shape, WAVE)],
                compiler_params=params,
                cost_estimate=tick_cost,
                name=f"tick{tick}" + ("_odd" if parity else "_even"),
            )
            lists, onward = lists[:2], lists[2:]
            known = [echo, *lists] if first_step else [echo]
            if parity == ODD:
                waves[EVEN] = [lax.ppermute(onward[0], "depth", crossing)]
            elif last_step:
                waves[ODD] = [lax.all_to_all(onward[0], "depth", 0, 0, axis_index_groups=pairs)]
            else:
                waves[ODD] = [lax.ppermute(a, "depth", inside) for a in onward]
            if not first_step:
                halos[1 - parity] = exchange(lists, (parity,))
        if first_step:
            halos[ODD] = halos[EVEN] = exchange(lists, (ODD, EVEN))
        arrived = {parity: (waves[parity], *halos[parity]) for parity in (ODD, EVEN)}
        echoes.append(echo)

    tick = ticks - 1
    results = []
    result_types = (
        jax.ShapeDtypeStruct((ticks, 1, blocks, points, columns), WAVE),
        jax.ShapeDtypeStruct((1, blocks, points, columns), jnp.float32),
    )
    for parity in (ODD, EVEN):
        results = grouped_call(
            functools.partial(last_kernel, parity, tick),
            [*fixed, *arrived[parity], echoes],
            result_types,
            [ANY_SPEC] * 2,
            list(results),
            scratch_shapes=[
                buffer_type,
                pltpu.VMEM((blocks, points, columns), WAVE),
                pltpu.VMEM((blocks, points, columns), jnp.float32),
                pltpu.SemaphoreType.DMA((tick,)),
                pltpu.SemaphoreType.DMA((blocks,)),
                pltpu.SemaphoreType.DMA((blocks,)),
            ],
            compiler_params=params,
            cost_estimate=tick_cost,
            name="last_tick" + ("_odd" if parity else "_even"),
        )
    return tuple(results)


def solution(mesh):
    return jax.shard_map(
        per_device,
        mesh=mesh,
        in_specs=(
            P("depth", "lat", None, None),
            P(None, "lat", None, None),
            P("depth", "lat", None, None, None, None),
            P("depth", "lat", None),
            P("depth", "lat", None),
            P("lat", None, None),
            P("lat", None),
            P("lat", None),
        ),
        out_specs=(P(None, "depth", "lat", None, None), P("depth", "lat", None, None)),
        check_vma=False,
    )
```

```python
import functools

import jax
import jax.numpy as jnp
from jax import lax
from jax.experimental import pallas as pl
from jax.experimental.pallas import tpu as pltpu
from jax.sharding import PartitionSpec as P

WAVE = jnp.bfloat16
SMEM_SPEC = pl.BlockSpec(memory_space=pltpu.SMEM)
VMEM_SPEC = pl.BlockSpec(memory_space=pltpu.VMEM)
ANY_SPEC = pl.BlockSpec(memory_space=pl.ANY)
VMEM_LIMIT = 8 * 1024 * 1024
LOWER, UPPER = 0, 1


def in_vmem(array):
    return pltpu.with_memory_space_constraint(array, pltpu.VMEM)


def in_hbm(array):
    return pltpu.with_memory_space_constraint(array, pltpu.HBM)


def write_lists(tile, plan_ref, blocks_ref, lists):
    points = blocks_ref.shape[1]
    listed = lists[0].shape[0] // points
    parity = lax.rem(tile, 2)
    for list_ref, side in zip(lists, (UPPER - parity, parity)):
        count = plan_ref[2 * listed + side]
        for slot in range(listed):
            live = slot < count

            @pl.when(live)
            def _():
                list_ref[slot * points : (slot + 1) * points] = blocks_ref[
                    plan_ref[side * listed + slot]
                ]

            @pl.when(jnp.logical_not(live))
            def _():
                list_ref[slot * points : (slot + 1) * points] = jnp.zeros(
                    blocks_ref.shape[1:], list_ref.dtype
                )


def prepare_kernel(
    ids_hbm, count_hbm, pattern_hbm, inflow_hbm, plan_ref, wave_ref, first_ref, second_ref,
    ids, count, pattern, landed, small_sems, sems,
):
    blocks = wave_ref.shape[0]
    small = [
        pltpu.make_async_copy(source, target, small_sems.at[i])
        for i, (source, target) in enumerate(
            ((ids_hbm, ids), (count_hbm, count), (pattern_hbm, pattern))
        )
    ]
    large = [
        pltpu.make_async_copy(inflow_hbm.at[0, b], landed.at[b], sems.at[b]) for b in range(blocks)
    ]
    for copy in small + large:
        copy.start()
    for copy in small:
        copy.wait()
    _, sides, listed = ids.shape
    taken = pattern.shape[1]
    for side in range(sides):
        for slot in range(listed):
            plan_ref[side * listed + slot] = ids[0, side, slot]
        plan_ref[sides * listed + side] = count[0, side]
    for b in range(blocks):
        for k in range(taken):
            plan_ref[sides * (listed + 1) + b * taken + k] = pattern[b, k]
    for b, copy in enumerate(large):
        copy.wait()
        wave_ref[b] = landed[b].astype(wave_ref.dtype)
    write_lists(lax.axis_index("lat"), plan_ref, wave_ref, (first_ref, second_ref))


def load_kernel(
    ops_hbm, source_hbm, pass_hbm, reflect_hbm, after_ref,
    ops_ref, source_ref, pass_ref, reflect_ref, pass_rows, reflect_rows, sems,
):
    del after_ref
    copies = [
        pltpu.make_async_copy(source, target, sems.at[i])
        for i, (source, target) in enumerate(
            (
                (pass_hbm, pass_rows),
                (reflect_hbm, reflect_rows),
                (ops_hbm, ops_ref),
                (source_hbm, source_ref),
            )
        )
    ]
    for copy in copies:
        copy.start()
    for copy, rows, columns_ref in zip(copies, (pass_rows, reflect_rows), (pass_ref, reflect_ref)):
        copy.wait()
        for b in range(columns_ref.shape[0]):
            row = rows[0, pl.ds(b, 1), :]
            columns_ref[b] = jnp.broadcast_to(row, columns_ref.shape[1:]).T
    for copy in copies[2:]:
        copy.wait()


def fill_buffer(section, tick, source_ref, wave_refs, first_ref, second_ref, buffer):
    blocks, points = source_ref.shape[1:3]
    listed = (buffer.shape[0] - blocks) // 2

    def fill(start, ref):
        if len(ref.shape) == 2:
            count = min(ref.shape[0] // points, blocks)
            part = ref[: count * points].reshape(count, points, -1)
        else:
            part = ref[0] if len(ref.shape) == 4 else ref[...]
        buffer[pl.ds(start, part.shape[0])] = part
        return start + part.shape[0]

    def fill_wave():
        start = 0
        for wave_ref in wave_refs:
            start = fill(start, wave_ref)

    if tick == 0:
        fill_wave()
    else:
        pl.when(section != 0)(fill_wave)

        @pl.when(section == 0)
        def _():
            buffer[:blocks] = source_ref[tick - 1]

    parity = lax.rem(lax.axis_index("lat"), 2)
    fill(blocks + (1 - parity) * listed, first_ref)
    fill(blocks + parity * listed, second_ref)


def extrapolate_block(plan_ref, pattern_start, ops_ref, buffer, b):
    taken = ops_ref.shape[2]
    points = ops_ref.shape[5]
    left = jnp.concatenate(
        [ops_ref[0, b, k].reshape(2 * points, points) for k in range(taken)], axis=1
    )
    right = jnp.concatenate(
        [buffer[plan_ref[pattern_start + b * taken + k]] for k in range(taken)], axis=0
    )
    products = jnp.dot(left, right, preferred_element_type=jnp.float32)
    half = products.shape[1] // 2
    real_part = products[:points, :half] - products[points:, half:]
    imag_part = products[:points, half:] + products[points:, :half]
    return real_part, imag_part


def ids_of(plan_ref, ops_ref):
    return (plan_ref.shape[0] - ops_ref.shape[1] * ops_ref.shape[2]) // 2 - 1


def acts(section, parity):
    return lax.rem(section, 2) == parity


def tick_kernel(
    parity, tick, sections, plan_ref, ops_ref, source_ref, pass_ref, reflect_ref,
    wave_refs, first_in_ref, second_in_ref, known_refs, out_refs, buffer, onward,
):
    del known_refs
    echo_ref, first_ref, second_ref, *onward_refs = out_refs
    section = lax.axis_index("depth")
    tile = lax.axis_index("lat")
    listed = ids_of(plan_ref, ops_ref)

    @pl.when(acts(section, parity))
    def _():
        fill_buffer(section, tick, source_ref, wave_refs, first_in_ref, second_in_ref, buffer)
        for b in range(echo_ref.shape[0]):
            parts = extrapolate_block(plan_ref, 2 * (listed + 1), ops_ref, buffer, b)
            for i, part in enumerate(parts):
                cols = pl.ds(i * part.shape[1], part.shape[1])
                onward[b, :, cols] = (pass_ref[b] * part).astype(onward.dtype)
                echo_ref[b, :, cols] = (reflect_ref[b] * part).astype(echo_ref.dtype)
        start = 0
        for onward_ref in onward_refs:
            if len(onward_ref.shape) == 2:
                rows = onward.shape[0] * onward.shape[1]
                onward_ref[:rows] = onward[...].reshape(rows, onward.shape[2])
            else:
                slot = onward_ref if len(onward_ref.shape) == 3 else onward_ref.at[1]
                slot[...] = onward[start : start + slot.shape[0]]
                start += slot.shape[0]

        @pl.when(section != sections - 1)
        def _():
            write_lists(tile, plan_ref, onward, (first_ref, second_ref))

        @pl.when(section == sections - 1)
        def _():
            write_lists(tile, plan_ref, source_ref.at[tick], (first_ref, second_ref))


def last_kernel(
    parity, tick, plan_ref, ops_ref, source_ref, pass_ref, reflect_ref,
    wave_refs, first_in_ref, second_in_ref, earlier, known_refs, out_refs,
    buffer, echo, leaving, early_sems, echo_sems, leave_sems,
):
    del known_refs
    reflected_ref, transmitted_ref = out_refs
    section = lax.axis_index("depth")
    listed = ids_of(plan_ref, ops_ref)

    @pl.when(acts(section, parity))
    def _():
        copies = [
            pltpu.make_async_copy(earlier[t], reflected_ref.at[t, 0], early_sems.at[t])
            for t in range(tick)
        ]
        for copy in copies:
            copy.start()
        fill_buffer(section, tick, source_ref, wave_refs, first_in_ref, second_in_ref, buffer)
        for b in range(echo.shape[0]):
            parts = extrapolate_block(plan_ref, 2 * (listed + 1), ops_ref, buffer, b)
            for i, part in enumerate(parts):
                cols = pl.ds(i * part.shape[1], part.shape[1])
                leaving[b, :, cols] = pass_ref[b] * part
                echo[b, :, cols] = (reflect_ref[b] * part).astype(echo.dtype)
            for copy in (
                pltpu.make_async_copy(leaving.at[b], transmitted_ref.at[0, b], leave_sems.at[b]),
                pltpu.make_async_copy(echo.at[b], reflected_ref.at[tick, 0, b], echo_sems.at[b]),
            ):
                copy.start()
                copies.append(copy)
        for copy in copies:
            copy.wait()


def grouped_call(kernel, groups, outs, out_specs, known, **options):
    flat = [array for group in groups for array in (group if isinstance(group, list) else [group])]

    def body(*refs):
        refs = list(refs)
        take = lambda count: [refs.pop(0) for _ in range(count)]
        inputs = [take(len(g)) if isinstance(g, list) else refs.pop(0) for g in groups]
        kernel(*inputs, take(len(known)), take(len(outs)), *refs)

    return pl.pallas_call(
        body,
        out_shape=tuple(outs),
        in_specs=[SMEM_SPEC] + [VMEM_SPEC] * (len(flat) - 1) + list(out_specs[: len(known)]),
        out_specs=tuple(out_specs),
        input_output_aliases={len(flat) + i: i for i in range(len(known))},
        **options,
    )(flat[0], *map(in_vmem, flat[1:]), *known)


def neighbour(j, turn, tiles):
    to = j + (1 if (j + turn) % 2 == 0 else -1)
    return to if 0 <= to < tiles else None


def swap_routes(sections, tiles):
    routes = []
    for turn in (0, 1):
        route = []
        for s in range(sections):
            for j in range(tiles):
                to = neighbour(j, turn, tiles)
                end = ((s ^ 1) * tiles + j) if to is None else (s * tiles + to)
                route.append((s * tiles + j, end))
        routes.append(route)
    return routes


def halo_routes(sections, tiles, senders):
    routes = []
    for turn in (0, 1):
        route = []
        for s in range(sections):
            for j in range(tiles):
                to = neighbour(j, turn, tiles)
                real = to is not None and s % 2 in senders
                end = (s + 1) % sections * tiles + to if real else (s ^ 1) * tiles + j
                route.append((s * tiles + j, end))
        routes.append(route)
    return routes


def per_device(
    inflow, source, operators, transmission, reflectivity, send_ids, send_count, pattern
):
    sections, tiles = lax.axis_size("depth"), lax.axis_size("lat")
    ticks = source.shape[0] + 1
    _, blocks, points, columns = inflow.shape
    listed = send_ids.shape[-1]
    taken = operators.shape[2]
    wave_type = pltpu.VMEM((blocks, points, columns), WAVE)
    list_type = pltpu.VMEM((listed * points, columns), WAVE)
    params = pltpu.CompilerParams(vmem_limit_bytes=VMEM_LIMIT)
    tick_cost = pl.CostEstimate(
        flops=0,
        bytes_accessed=0,
        transcendentals=0,
    )
    both = ("depth", "lat")
    deeper = [(s, (s + 1) % sections) for s in range(sections)]

    plan, wave, first, second = pl.pallas_call(
        prepare_kernel,
        out_shape=(
            pltpu.SMEM((2 * (listed + 1) + blocks * taken,), jnp.int32),
            wave_type,
            list_type,
            list_type,
        ),
        in_specs=[ANY_SPEC] * 4,
        out_specs=(SMEM_SPEC,) + (VMEM_SPEC,) * 3,
        scratch_shapes=[
            pltpu.SMEM(send_ids.shape, jnp.int32),
            pltpu.SMEM(send_count.shape, jnp.int32),
            pltpu.SMEM(pattern.shape, jnp.int32),
            pltpu.VMEM((blocks, points, columns), inflow.dtype),
            pltpu.SemaphoreType.DMA((3,)),
            pltpu.SemaphoreType.DMA((blocks,)),
        ],
        compiler_params=params,
        cost_estimate=pl.CostEstimate(
            flops=inflow.size, bytes_accessed=8 * inflow.size, transcendentals=0
        ),
        name="prepare",
    )(*map(in_hbm, (send_ids, send_count, pattern, inflow)))
    loaded_first = first
    routes = swap_routes(sections, tiles)
    first = lax.ppermute(first, both, routes[0])
    second = lax.ppermute(second, both, routes[1])

    column_type = pltpu.VMEM((blocks, points, columns // 2), jnp.float32)
    fixed = pl.pallas_call(
        load_kernel,
        out_shape=(
            pltpu.VMEM(operators.shape, operators.dtype),
            pltpu.VMEM(source.shape, source.dtype),
            column_type,
            column_type,
        ),
        in_specs=[ANY_SPEC] * 4 + [VMEM_SPEC],
        out_specs=(VMEM_SPEC,) * 4,
        scratch_shapes=[
            pltpu.VMEM(transmission.shape, transmission.dtype),
            pltpu.VMEM(reflectivity.shape, reflectivity.dtype),
            pltpu.SemaphoreType.DMA((4,)),
        ],
        compiler_params=params,
        cost_estimate=pl.CostEstimate(
            flops=0, bytes_accessed=4 * (operators.size + source.size), transcendentals=0
        ),
        name="load",
    )(*map(in_hbm, (operators, source, transmission, reflectivity)), in_vmem(loaded_first))
    fixed = [plan, *fixed]

    buffer_type = pltpu.VMEM((blocks + 2 * listed, points, columns), WAVE)

    ODD, EVEN = 1, 0
    crossing = [(s, (s + 1) % sections) for s in range(sections)]
    inside = [(s, s ^ 1) for s in range(sections)]
    pairs = [[s, s + 1] for s in range(0, sections, 2)]
    pair_type = pltpu.VMEM((2, blocks, points, columns), WAVE)
    part_types = [pltpu.VMEM((blocks // 2, points, columns), WAVE)] * 2
    half_types = [pltpu.VMEM((n, points, columns), WAVE) for n in (blocks // 2, blocks - blocks // 2)]

    def lists_of(extra):
        return [pltpu.VMEM((listed * points + extra, columns), WAVE)] * 2

    def exchange(lists, senders):
        routes = halo_routes(sections, tiles, senders)
        return [lax.ppermute(a, both, route) for a, route in zip(lists, routes)]

    arrived = {parity: ([wave], first, second) for parity in (ODD, EVEN)}
    echoes = []
    for tick in range(ticks - 1):
        first_step, last_step = tick in (0, ticks - 2), False
        known = []
        waves, halos = {}, {}
        for parity in (ODD, EVEN):
            if first_step:
                extra = 0
            elif last_step:
                extra = 16 if parity == ODD else 0
            else:
                extra = 0 if parity == ODD else 16
            if parity == ODD:
                long = 0 if first_step or last_step else 16
                to_next = [pltpu.VMEM((blocks * points + long, columns), WAVE)]
            else:
                to_next = [pair_type] if last_step else half_types if first_step else part_types
            outs = [wave_type, *lists_of(extra), *to_next]
            echo, *lists = grouped_call(
                functools.partial(tick_kernel, parity, tick, sections),
                [*fixed, *arrived[parity]],
                outs,
                [VMEM_SPEC] * len(outs),
                [in_vmem(a) for a in known],
                scratch_shapes=[buffer_type, pltpu.VMEM(wave_type.shape, WAVE)],
                compiler_params=params,
                cost_estimate=tick_cost,
                name=f"tick{tick}" + ("_odd" if parity else "_even"),
            )
            lists, onward = lists[:2], lists[2:]
            known = [echo, *lists] if first_step else [echo]
            if parity == ODD:
                waves[EVEN] = [lax.ppermute(onward[0], "depth", crossing)]
            elif last_step:
                waves[ODD] = [lax.all_to_all(onward[0], "depth", 0, 0, axis_index_groups=pairs)]
            else:
                waves[ODD] = [lax.ppermute(a, "depth", inside) for a in onward]
            if not first_step:
                halos[1 - parity] = exchange(lists, (parity,))
        if first_step:
            halos[ODD] = halos[EVEN] = exchange(lists, (ODD, EVEN))
        arrived = {parity: (waves[parity], *halos[parity]) for parity in (ODD, EVEN)}
        echoes.append(echo)

    tick = ticks - 1
    results = []
    result_types = (
        jax.ShapeDtypeStruct((ticks, 1, blocks, points, columns), WAVE),
        jax.ShapeDtypeStruct((1, blocks, points, columns), jnp.float32),
    )
    for parity in (ODD, EVEN):
        results = grouped_call(
            functools.partial(last_kernel, parity, tick),
            [*fixed, *arrived[parity], echoes],
            result_types,
            [ANY_SPEC] * 2,
            list(results),
            scratch_shapes=[
                buffer_type,
                pltpu.VMEM((blocks, points, columns), WAVE),
                pltpu.VMEM((blocks, points, columns), jnp.float32),
                pltpu.SemaphoreType.DMA((tick,)),
                pltpu.SemaphoreType.DMA((blocks,)),
                pltpu.SemaphoreType.DMA((blocks,)),
            ],
            compiler_params=params,
            cost_estimate=tick_cost,
            name="last_tick" + ("_odd" if parity else "_even"),
        )
    return tuple(results)


def solution(mesh):
    return jax.shard_map(
        per_device,
        mesh=mesh,
        in_specs=(
            P("depth", "lat", None, None),
            P(None, "lat", None, None),
            P("depth", "lat", None, None, None, None),
            P("depth", "lat", None),
            P("depth", "lat", None),
            P("lat", None, None),
            P("lat", None),
            P("lat", None),
        ),
        out_specs=(P(None, "depth", "lat", None, None), P("depth", "lat", None, None)),
        check_vma=False,
    )
```

```python
import functools

import jax
import jax.numpy as jnp
from jax import lax
from jax.experimental import pallas as pl
from jax.experimental.pallas import tpu as pltpu
from jax.sharding import PartitionSpec as P

WAVE = jnp.bfloat16
SMEM_SPEC = pl.BlockSpec(memory_space=pltpu.SMEM)
VMEM_SPEC = pl.BlockSpec(memory_space=pltpu.VMEM)
ANY_SPEC = pl.BlockSpec(memory_space=pl.ANY)
VMEM_LIMIT = 8 * 1024 * 1024
LOWER, UPPER = 0, 1


def in_vmem(array):
    return pltpu.with_memory_space_constraint(array, pltpu.VMEM)


def in_hbm(array):
    return pltpu.with_memory_space_constraint(array, pltpu.HBM)


def write_lists(tile, plan_ref, blocks_ref, lists):
    points = blocks_ref.shape[1]
    listed = lists[0].shape[0] // points
    parity = lax.rem(tile, 2)
    for list_ref, side in zip(lists, (UPPER - parity, parity)):
        count = plan_ref[2 * listed + side]
        for slot in range(listed):
            live = slot < count

            @pl.when(live)
            def _():
                list_ref[slot * points : (slot + 1) * points] = blocks_ref[
                    plan_ref[side * listed + slot]
                ]

            @pl.when(jnp.logical_not(live))
            def _():
                list_ref[slot * points : (slot + 1) * points] = jnp.zeros(
                    blocks_ref.shape[1:], list_ref.dtype
                )


def prepare_kernel(
    ids_hbm, count_hbm, pattern_hbm, inflow_hbm, plan_ref, wave_ref, first_ref, second_ref,
    ids, count, pattern, landed, small_sems, sems,
):
    blocks = wave_ref.shape[0]
    small = [
        pltpu.make_async_copy(source, target, small_sems.at[i])
        for i, (source, target) in enumerate(
            ((ids_hbm, ids), (count_hbm, count), (pattern_hbm, pattern))
        )
    ]
    large = [
        pltpu.make_async_copy(inflow_hbm.at[0, b], landed.at[b], sems.at[b]) for b in range(blocks)
    ]
    for copy in small + large:
        copy.start()
    for copy in small:
        copy.wait()
    _, sides, listed = ids.shape
    taken = pattern.shape[1]
    for side in range(sides):
        for slot in range(listed):
            plan_ref[side * listed + slot] = ids[0, side, slot]
        plan_ref[sides * listed + side] = count[0, side]
    for b in range(blocks):
        for k in range(taken):
            plan_ref[sides * (listed + 1) + b * taken + k] = pattern[b, k]
    for b, copy in enumerate(large):
        copy.wait()
        wave_ref[b] = landed[b].astype(wave_ref.dtype)
    write_lists(lax.axis_index("lat"), plan_ref, wave_ref, (first_ref, second_ref))


def load_kernel(
    ops_hbm, source_hbm, pass_hbm, reflect_hbm, after_ref,
    ops_ref, source_ref, pass_ref, reflect_ref, pass_rows, reflect_rows, sems,
):
    del after_ref
    copies = [
        pltpu.make_async_copy(source, target, sems.at[i])
        for i, (source, target) in enumerate(
            (
                (pass_hbm, pass_rows),
                (reflect_hbm, reflect_rows),
                (ops_hbm, ops_ref),
                (source_hbm, source_ref),
            )
        )
    ]
    for copy in copies:
        copy.start()
    for copy, rows, columns_ref in zip(copies, (pass_rows, reflect_rows), (pass_ref, reflect_ref)):
        copy.wait()
        for b in range(columns_ref.shape[0]):
            row = rows[0, pl.ds(b, 1), :]
            columns_ref[b] = jnp.broadcast_to(row, columns_ref.shape[1:]).T
    for copy in copies[2:]:
        copy.wait()


def fill_buffer(section, tick, source_ref, wave_refs, first_ref, second_ref, buffer):
    blocks, points = source_ref.shape[1:3]
    listed = (buffer.shape[0] - blocks) // 2

    def fill(start, ref):
        if len(ref.shape) == 2:
            count = min(ref.shape[0] // points, blocks)
            part = ref[: count * points].reshape(count, points, -1)
        else:
            part = ref[0] if len(ref.shape) == 4 else ref[...]
        buffer[pl.ds(start, part.shape[0])] = part
        return start + part.shape[0]

    def fill_wave():
        start = 0
        for wave_ref in wave_refs:
            start = fill(start, wave_ref)

    if tick == 0:
        fill_wave()
    else:
        pl.when(section != 0)(fill_wave)

        @pl.when(section == 0)
        def _():
            buffer[:blocks] = source_ref[tick - 1]

    parity = lax.rem(lax.axis_index("lat"), 2)
    fill(blocks + (1 - parity) * listed, first_ref)
    fill(blocks + parity * listed, second_ref)


def extrapolate_block(plan_ref, pattern_start, ops_ref, buffer, b):
    taken = ops_ref.shape[2]
    points = ops_ref.shape[5]
    left = jnp.concatenate(
        [ops_ref[0, b, k].reshape(2 * points, points) for k in range(taken)], axis=1
    )
    right = jnp.concatenate(
        [buffer[plan_ref[pattern_start + b * taken + k]] for k in range(taken)], axis=0
    )
    products = jnp.dot(left, right, preferred_element_type=jnp.float32)
    half = products.shape[1] // 2
    real_part = products[:points, :half] - products[points:, half:]
    imag_part = products[:points, half:] + products[points:, :half]
    return real_part, imag_part


def ids_of(plan_ref, ops_ref):
    return (plan_ref.shape[0] - ops_ref.shape[1] * ops_ref.shape[2]) // 2 - 1


def acts(section, parity):
    return lax.rem(section, 2) == parity


def tick_kernel(
    parity, tick, sections, plan_ref, ops_ref, source_ref, pass_ref, reflect_ref,
    wave_refs, first_in_ref, second_in_ref, known_refs, out_refs, buffer, onward,
):
    del known_refs
    echo_ref, first_ref, second_ref, *onward_refs = out_refs
    section = lax.axis_index("depth")
    tile = lax.axis_index("lat")
    listed = ids_of(plan_ref, ops_ref)

    @pl.when(acts(section, parity))
    def _():
        fill_buffer(section, tick, source_ref, wave_refs, first_in_ref, second_in_ref, buffer)
        for b in range(echo_ref.shape[0]):
            parts = extrapolate_block(plan_ref, 2 * (listed + 1), ops_ref, buffer, b)
            for i, part in enumerate(parts):
                cols = pl.ds(i * part.shape[1], part.shape[1])
                onward[b, :, cols] = (pass_ref[b] * part).astype(onward.dtype)
                echo_ref[b, :, cols] = (reflect_ref[b] * part).astype(echo_ref.dtype)
        start = 0
        for onward_ref in onward_refs:
            if len(onward_ref.shape) == 2:
                rows = onward.shape[0] * onward.shape[1]
                onward_ref[:rows] = onward[...].reshape(rows, onward.shape[2])
            else:
                slot = onward_ref if len(onward_ref.shape) == 3 else onward_ref.at[1]
                slot[...] = onward[start : start + slot.shape[0]]
                start += slot.shape[0]

        @pl.when(section != sections - 1)
        def _():
            write_lists(tile, plan_ref, onward, (first_ref, second_ref))

        @pl.when(section == sections - 1)
        def _():
            write_lists(tile, plan_ref, source_ref.at[tick], (first_ref, second_ref))


def last_kernel(
    parity, tick, plan_ref, ops_ref, source_ref, pass_ref, reflect_ref,
    wave_refs, first_in_ref, second_in_ref, earlier, known_refs, out_refs,
    buffer, echo, leaving, early_sems, echo_sems, leave_sems,
):
    del known_refs
    reflected_ref, transmitted_ref = out_refs
    section = lax.axis_index("depth")
    listed = ids_of(plan_ref, ops_ref)

    @pl.when(acts(section, parity))
    def _():
        copies = [
            pltpu.make_async_copy(earlier[t], reflected_ref.at[t, 0], early_sems.at[t])
            for t in range(tick)
        ]
        for copy in copies:
            copy.start()
        fill_buffer(section, tick, source_ref, wave_refs, first_in_ref, second_in_ref, buffer)
        for b in range(echo.shape[0]):
            parts = extrapolate_block(plan_ref, 2 * (listed + 1), ops_ref, buffer, b)
            for i, part in enumerate(parts):
                cols = pl.ds(i * part.shape[1], part.shape[1])
                leaving[b, :, cols] = pass_ref[b] * part
                echo[b, :, cols] = (reflect_ref[b] * part).astype(echo.dtype)
            for copy in (
                pltpu.make_async_copy(leaving.at[b], transmitted_ref.at[0, b], leave_sems.at[b]),
                pltpu.make_async_copy(echo.at[b], reflected_ref.at[tick, 0, b], echo_sems.at[b]),
            ):
                copy.start()
                copies.append(copy)
        for copy in copies:
            copy.wait()


def grouped_call(kernel, groups, outs, out_specs, known, **options):
    flat = [array for group in groups for array in (group if isinstance(group, list) else [group])]

    def body(*refs):
        refs = list(refs)
        take = lambda count: [refs.pop(0) for _ in range(count)]
        inputs = [take(len(g)) if isinstance(g, list) else refs.pop(0) for g in groups]
        kernel(*inputs, take(len(known)), take(len(outs)), *refs)

    return pl.pallas_call(
        body,
        out_shape=tuple(outs),
        in_specs=[SMEM_SPEC] + [VMEM_SPEC] * (len(flat) - 1) + list(out_specs[: len(known)]),
        out_specs=tuple(out_specs),
        input_output_aliases={len(flat) + i: i for i in range(len(known))},
        **options,
    )(flat[0], *map(in_vmem, flat[1:]), *known)


def neighbour(j, turn, tiles):
    to = j + (1 if (j + turn) % 2 == 0 else -1)
    return to if 0 <= to < tiles else None


def swap_routes(sections, tiles):
    routes = []
    for turn in (0, 1):
        route = []
        for s in range(sections):
            for j in range(tiles):
                to = neighbour(j, turn, tiles)
                end = ((s ^ 1) * tiles + j) if to is None else (s * tiles + to)
                route.append((s * tiles + j, end))
        routes.append(route)
    return routes


def halo_routes(sections, tiles, senders):
    routes = []
    for turn in (0, 1):
        route = []
        for s in range(sections):
            for j in range(tiles):
                to = neighbour(j, turn, tiles)
                real = to is not None and s % 2 in senders
                end = (s + 1) % sections * tiles + to if real else (s ^ 1) * tiles + j
                route.append((s * tiles + j, end))
        routes.append(route)
    return routes


def per_device(
    inflow, source, operators, transmission, reflectivity, send_ids, send_count, pattern
):
    sections, tiles = lax.axis_size("depth"), lax.axis_size("lat")
    ticks = source.shape[0] + 1
    _, blocks, points, columns = inflow.shape
    listed = send_ids.shape[-1]
    taken = operators.shape[2]
    wave_type = pltpu.VMEM((blocks, points, columns), WAVE)
    list_type = pltpu.VMEM((listed * points, columns), WAVE)
    params = pltpu.CompilerParams(vmem_limit_bytes=VMEM_LIMIT)
    tick_cost = pl.CostEstimate(
        flops=0,
        bytes_accessed=0,
        transcendentals=0,
    )
    both = ("depth", "lat")
    deeper = [(s, (s + 1) % sections) for s in range(sections)]

    plan, wave, first, second = pl.pallas_call(
        prepare_kernel,
        out_shape=(
            pltpu.SMEM((2 * (listed + 1) + blocks * taken,), jnp.int32),
            wave_type,
            list_type,
            list_type,
        ),
        in_specs=[ANY_SPEC] * 4,
        out_specs=(SMEM_SPEC,) + (VMEM_SPEC,) * 3,
        scratch_shapes=[
            pltpu.SMEM(send_ids.shape, jnp.int32),
            pltpu.SMEM(send_count.shape, jnp.int32),
            pltpu.SMEM(pattern.shape, jnp.int32),
            pltpu.VMEM((blocks, points, columns), inflow.dtype),
            pltpu.SemaphoreType.DMA((3,)),
            pltpu.SemaphoreType.DMA((blocks,)),
        ],
        compiler_params=params,
        cost_estimate=pl.CostEstimate(
            flops=inflow.size, bytes_accessed=8 * inflow.size, transcendentals=0
        ),
        name="prepare",
    )(*map(in_hbm, (send_ids, send_count, pattern, inflow)))
    loaded_first = first
    routes = swap_routes(sections, tiles)
    first = lax.ppermute(first, both, routes[0])
    second = lax.ppermute(second, both, routes[1])

    column_type = pltpu.VMEM((blocks, points, columns // 2), jnp.float32)
    fixed = pl.pallas_call(
        load_kernel,
        out_shape=(
            pltpu.VMEM(operators.shape, operators.dtype),
            pltpu.VMEM(source.shape, source.dtype),
            column_type,
            column_type,
        ),
        in_specs=[ANY_SPEC] * 4 + [VMEM_SPEC],
        out_specs=(VMEM_SPEC,) * 4,
        scratch_shapes=[
            pltpu.VMEM(transmission.shape, transmission.dtype),
            pltpu.VMEM(reflectivity.shape, reflectivity.dtype),
            pltpu.SemaphoreType.DMA((4,)),
        ],
        compiler_params=params,
        cost_estimate=pl.CostEstimate(
            flops=0, bytes_accessed=4 * (operators.size + source.size), transcendentals=0
        ),
        name="load",
    )(*map(in_hbm, (operators, source, transmission, reflectivity)), in_vmem(loaded_first))
    fixed = [plan, *fixed]

    buffer_type = pltpu.VMEM((blocks + 2 * listed, points, columns), WAVE)

    ODD, EVEN = 1, 0
    crossing = [(s, (s + 1) % sections) for s in range(sections)]
    inside = [(s, s ^ 1) for s in range(sections)]
    pairs = [[s, s + 1] for s in range(0, sections, 2)]
    pair_type = pltpu.VMEM((2, blocks, points, columns), WAVE)
    part_types = [pltpu.VMEM((blocks // 2, points, columns), WAVE)] * 2
    half_types = [pltpu.VMEM((n, points, columns), WAVE) for n in (blocks // 2, blocks - blocks // 2)]

    def lists_of(extra):
        return [pltpu.VMEM((listed * points + extra, columns), WAVE)] * 2

    def exchange(lists, senders):
        routes = halo_routes(sections, tiles, senders)
        return [lax.ppermute(a, both, route) for a, route in zip(lists, routes)]

    arrived = {parity: ([wave], first, second) for parity in (ODD, EVEN)}
    echoes = []
    for tick in range(ticks - 1):
        first_step, last_step = False, tick == ticks - 2
        known = []
        waves, halos = {}, {}
        for parity in (ODD, EVEN):
            if first_step:
                extra = 0
            elif last_step:
                extra = 16 if parity == ODD else 0
            else:
                extra = 0 if parity == ODD else 16
            if parity == ODD:
                long = 0 if first_step or last_step else 16
                to_next = [pltpu.VMEM((blocks * points + long, columns), WAVE)]
            else:
                to_next = [pair_type] if last_step else half_types if first_step else part_types
            outs = [wave_type, *lists_of(extra), *to_next]
            echo, *lists = grouped_call(
                functools.partial(tick_kernel, parity, tick, sections),
                [*fixed, *arrived[parity]],
                outs,
                [VMEM_SPEC] * len(outs),
                [in_vmem(a) for a in known],
                scratch_shapes=[buffer_type, pltpu.VMEM(wave_type.shape, WAVE)],
                compiler_params=params,
                cost_estimate=tick_cost,
                name=f"tick{tick}" + ("_odd" if parity else "_even"),
            )
            lists, onward = lists[:2], lists[2:]
            known = [echo, *lists] if first_step else [echo]
            if parity == ODD:
                waves[EVEN] = [lax.ppermute(onward[0], "depth", crossing)]
            elif last_step:
                waves[ODD] = [lax.all_to_all(onward[0], "depth", 0, 0, axis_index_groups=pairs)]
            else:
                waves[ODD] = [lax.ppermute(a, "depth", inside) for a in onward]
            if not first_step:
                halos[1 - parity] = exchange(lists, (parity,))
        if first_step:
            halos[ODD] = halos[EVEN] = exchange(lists, (ODD, EVEN))
        arrived = {parity: (waves[parity], *halos[parity]) for parity in (ODD, EVEN)}
        echoes.append(echo)

    tick = ticks - 1
    results = []
    result_types = (
        jax.ShapeDtypeStruct((ticks, 1, blocks, points, columns), WAVE),
        jax.ShapeDtypeStruct((1, blocks, points, columns), jnp.float32),
    )
    for parity in (ODD, EVEN):
        results = grouped_call(
            functools.partial(last_kernel, parity, tick),
            [*fixed, *arrived[parity], echoes],
            result_types,
            [ANY_SPEC] * 2,
            list(results),
            scratch_shapes=[
                buffer_type,
                pltpu.VMEM((blocks, points, columns), WAVE),
                pltpu.VMEM((blocks, points, columns), jnp.float32),
                pltpu.SemaphoreType.DMA((tick,)),
                pltpu.SemaphoreType.DMA((blocks,)),
                pltpu.SemaphoreType.DMA((blocks,)),
            ],
            compiler_params=params,
            cost_estimate=tick_cost,
            name="last_tick" + ("_odd" if parity else "_even"),
        )
    return tuple(results)


def solution(mesh):
    return jax.shard_map(
        per_device,
        mesh=mesh,
        in_specs=(
            P("depth", "lat", None, None),
            P(None, "lat", None, None),
            P("depth", "lat", None, None, None, None),
            P("depth", "lat", None),
            P("depth", "lat", None),
            P("lat", None, None),
            P("lat", None),
            P("lat", None),
        ),
        out_specs=(P(None, "depth", "lat", None, None), P("depth", "lat", None, None)),
        check_vma=False,
    )
```

```python
import functools

import jax
import jax.numpy as jnp
from jax import lax
from jax.experimental import pallas as pl
from jax.experimental.pallas import tpu as pltpu
from jax.sharding import PartitionSpec as P

WAVE = jnp.bfloat16
SMEM_SPEC = pl.BlockSpec(memory_space=pltpu.SMEM)
VMEM_SPEC = pl.BlockSpec(memory_space=pltpu.VMEM)
ANY_SPEC = pl.BlockSpec(memory_space=pl.ANY)
VMEM_LIMIT = 8 * 1024 * 1024
LOWER, UPPER = 0, 1


def in_vmem(array):
    return pltpu.with_memory_space_constraint(array, pltpu.VMEM)


def in_hbm(array):
    return pltpu.with_memory_space_constraint(array, pltpu.HBM)


def write_lists(tile, plan_ref, blocks_ref, lists):
    points = blocks_ref.shape[1]
    listed = lists[0].shape[0] // points
    parity = lax.rem(tile, 2)
    for list_ref, side in zip(lists, (UPPER - parity, parity)):
        count = plan_ref[2 * listed + side]
        for slot in range(listed):
            live = slot < count

            @pl.when(live)
            def _():
                list_ref[slot * points : (slot + 1) * points] = blocks_ref[
                    plan_ref[side * listed + slot]
                ]

            @pl.when(jnp.logical_not(live))
            def _():
                list_ref[slot * points : (slot + 1) * points] = jnp.zeros(
                    blocks_ref.shape[1:], list_ref.dtype
                )


def prepare_kernel(
    ids_hbm, count_hbm, pattern_hbm, inflow_hbm, plan_ref, wave_ref, first_ref, second_ref,
    ids, count, pattern, landed, small_sems, sems,
):
    blocks = wave_ref.shape[0]
    small = [
        pltpu.make_async_copy(source, target, small_sems.at[i])
        for i, (source, target) in enumerate(
            ((ids_hbm, ids), (count_hbm, count), (pattern_hbm, pattern))
        )
    ]
    large = [
        pltpu.make_async_copy(inflow_hbm.at[0, b], landed.at[b], sems.at[b]) for b in range(blocks)
    ]
    for copy in small + large:
        copy.start()
    for copy in small:
        copy.wait()
    _, sides, listed = ids.shape
    taken = pattern.shape[1]
    for side in range(sides):
        for slot in range(listed):
            plan_ref[side * listed + slot] = ids[0, side, slot]
        plan_ref[sides * listed + side] = count[0, side]
    for b in range(blocks):
        for k in range(taken):
            plan_ref[sides * (listed + 1) + b * taken + k] = pattern[b, k]
    for b, copy in enumerate(large):
        copy.wait()
        wave_ref[b] = landed[b].astype(wave_ref.dtype)
    write_lists(lax.axis_index("lat"), plan_ref, wave_ref, (first_ref, second_ref))


def load_kernel(
    ops_hbm, source_hbm, pass_hbm, reflect_hbm, after_ref,
    ops_ref, source_ref, pass_ref, reflect_ref, pass_rows, reflect_rows, sems,
):
    del after_ref
    copies = [
        pltpu.make_async_copy(source, target, sems.at[i])
        for i, (source, target) in enumerate(
            (
                (pass_hbm, pass_rows),
                (reflect_hbm, reflect_rows),
                (ops_hbm, ops_ref),
                (source_hbm, source_ref),
            )
        )
    ]
    for copy in copies:
        copy.start()
    for copy, rows, columns_ref in zip(copies, (pass_rows, reflect_rows), (pass_ref, reflect_ref)):
        copy.wait()
        for b in range(columns_ref.shape[0]):
            row = rows[0, pl.ds(b, 1), :]
            columns_ref[b] = jnp.broadcast_to(row, columns_ref.shape[1:]).T
    for copy in copies[2:]:
        copy.wait()


def fill_buffer(section, tick, source_ref, wave_refs, first_ref, second_ref, buffer):
    blocks, points = source_ref.shape[1:3]
    listed = (buffer.shape[0] - blocks) // 2

    def fill(start, ref):
        if len(ref.shape) == 2:
            count = min(ref.shape[0] // points, blocks)
            part = ref[: count * points].reshape(count, points, -1)
        else:
            part = ref[0] if len(ref.shape) == 4 else ref[...]
        buffer[pl.ds(start, part.shape[0])] = part
        return start + part.shape[0]

    def fill_wave():
        start = 0
        for wave_ref in wave_refs:
            start = fill(start, wave_ref)

    if tick == 0:
        fill_wave()
    else:
        pl.when(section != 0)(fill_wave)

        @pl.when(section == 0)
        def _():
            buffer[:blocks] = source_ref[tick - 1]

    parity = lax.rem(lax.axis_index("lat"), 2)
    fill(blocks + (1 - parity) * listed, first_ref)
    fill(blocks + parity * listed, second_ref)


def extrapolate_block(plan_ref, pattern_start, ops_ref, buffer, b):
    taken = ops_ref.shape[2]
    points = ops_ref.shape[5]
    products = None
    for start in range(0, taken, 2):
        pair = range(start, min(start + 2, taken))
        left = jnp.concatenate(
            [ops_ref[0, b, k].reshape(2 * points, points) for k in pair], axis=1
        )
        right = jnp.concatenate(
            [buffer[plan_ref[pattern_start + b * taken + k]] for k in pair], axis=0
        )
        part = jnp.dot(left, right, preferred_element_type=jnp.float32)
        products = part if products is None else products + part
    half = products.shape[1] // 2
    real_part = products[:points, :half] - products[points:, half:]
    imag_part = products[:points, half:] + products[points:, :half]
    return real_part, imag_part


def ids_of(plan_ref, ops_ref):
    return (plan_ref.shape[0] - ops_ref.shape[1] * ops_ref.shape[2]) // 2 - 1


def acts(section, parity):
    return lax.rem(section, 2) == parity


def tick_kernel(
    parity, tick, sections, plan_ref, ops_ref, source_ref, pass_ref, reflect_ref,
    wave_refs, first_in_ref, second_in_ref, known_refs, out_refs, buffer, onward,
):
    del known_refs
    echo_ref, first_ref, second_ref, *onward_refs = out_refs
    section = lax.axis_index("depth")
    tile = lax.axis_index("lat")
    listed = ids_of(plan_ref, ops_ref)

    @pl.when(acts(section, parity))
    def _():
        fill_buffer(section, tick, source_ref, wave_refs, first_in_ref, second_in_ref, buffer)
        for b in range(echo_ref.shape[0]):
            parts = extrapolate_block(plan_ref, 2 * (listed + 1), ops_ref, buffer, b)
            for i, part in enumerate(parts):
                cols = pl.ds(i * part.shape[1], part.shape[1])
                onward[b, :, cols] = (pass_ref[b] * part).astype(onward.dtype)
                echo_ref[b, :, cols] = (reflect_ref[b] * part).astype(echo_ref.dtype)
        start = 0
        for onward_ref in onward_refs:
            if len(onward_ref.shape) == 2:
                rows = onward.shape[0] * onward.shape[1]
                onward_ref[:rows] = onward[...].reshape(rows, onward.shape[2])
            else:
                slot = onward_ref if len(onward_ref.shape) == 3 else onward_ref.at[1]
                slot[...] = onward[start : start + slot.shape[0]]
                start += slot.shape[0]

        @pl.when(section != sections - 1)
        def _():
            write_lists(tile, plan_ref, onward, (first_ref, second_ref))

        @pl.when(section == sections - 1)
        def _():
            write_lists(tile, plan_ref, source_ref.at[tick], (first_ref, second_ref))


def last_kernel(
    parity, tick, plan_ref, ops_ref, source_ref, pass_ref, reflect_ref,
    wave_refs, first_in_ref, second_in_ref, earlier, known_refs, out_refs,
    buffer, echo, leaving, early_sems, echo_sems, leave_sems,
):
    del known_refs
    reflected_ref, transmitted_ref = out_refs
    section = lax.axis_index("depth")
    listed = ids_of(plan_ref, ops_ref)

    @pl.when(acts(section, parity))
    def _():
        copies = [
            pltpu.make_async_copy(earlier[t], reflected_ref.at[t, 0], early_sems.at[t])
            for t in range(tick)
        ]
        for copy in copies:
            copy.start()
        fill_buffer(section, tick, source_ref, wave_refs, first_in_ref, second_in_ref, buffer)
        for b in range(echo.shape[0]):
            parts = extrapolate_block(plan_ref, 2 * (listed + 1), ops_ref, buffer, b)
            for i, part in enumerate(parts):
                cols = pl.ds(i * part.shape[1], part.shape[1])
                leaving[b, :, cols] = pass_ref[b] * part
                echo[b, :, cols] = (reflect_ref[b] * part).astype(echo.dtype)
            for copy in (
                pltpu.make_async_copy(leaving.at[b], transmitted_ref.at[0, b], leave_sems.at[b]),
                pltpu.make_async_copy(echo.at[b], reflected_ref.at[tick, 0, b], echo_sems.at[b]),
            ):
                copy.start()
                copies.append(copy)
        for copy in copies:
            copy.wait()


def grouped_call(kernel, groups, outs, out_specs, known, **options):
    flat = [array for group in groups for array in (group if isinstance(group, list) else [group])]

    def body(*refs):
        refs = list(refs)
        take = lambda count: [refs.pop(0) for _ in range(count)]
        inputs = [take(len(g)) if isinstance(g, list) else refs.pop(0) for g in groups]
        kernel(*inputs, take(len(known)), take(len(outs)), *refs)

    return pl.pallas_call(
        body,
        out_shape=tuple(outs),
        in_specs=[SMEM_SPEC] + [VMEM_SPEC] * (len(flat) - 1) + list(out_specs[: len(known)]),
        out_specs=tuple(out_specs),
        input_output_aliases={len(flat) + i: i for i in range(len(known))},
        **options,
    )(flat[0], *map(in_vmem, flat[1:]), *known)


def neighbour(j, turn, tiles):
    to = j + (1 if (j + turn) % 2 == 0 else -1)
    return to if 0 <= to < tiles else None


def swap_routes(sections, tiles):
    routes = []
    for turn in (0, 1):
        route = []
        for s in range(sections):
            for j in range(tiles):
                to = neighbour(j, turn, tiles)
                end = ((s ^ 1) * tiles + j) if to is None else (s * tiles + to)
                route.append((s * tiles + j, end))
        routes.append(route)
    return routes


def halo_routes(sections, tiles, senders):
    routes = []
    for turn in (0, 1):
        route = []
        for s in range(sections):
            for j in range(tiles):
                to = neighbour(j, turn, tiles)
                real = to is not None and s % 2 in senders
                end = (s + 1) % sections * tiles + to if real else (s ^ 1) * tiles + j
                route.append((s * tiles + j, end))
        routes.append(route)
    return routes


def per_device(
    inflow, source, operators, transmission, reflectivity, send_ids, send_count, pattern
):
    sections, tiles = lax.axis_size("depth"), lax.axis_size("lat")
    ticks = source.shape[0] + 1
    _, blocks, points, columns = inflow.shape
    listed = send_ids.shape[-1]
    taken = operators.shape[2]
    wave_type = pltpu.VMEM((blocks, points, columns), WAVE)
    list_type = pltpu.VMEM((listed * points, columns), WAVE)
    params = pltpu.CompilerParams(vmem_limit_bytes=VMEM_LIMIT)
    tick_cost = pl.CostEstimate(
        flops=0,
        bytes_accessed=0,
        transcendentals=0,
    )
    both = ("depth", "lat")
    deeper = [(s, (s + 1) % sections) for s in range(sections)]

    plan, wave, first, second = pl.pallas_call(
        prepare_kernel,
        out_shape=(
            pltpu.SMEM((2 * (listed + 1) + blocks * taken,), jnp.int32),
            wave_type,
            list_type,
            list_type,
        ),
        in_specs=[ANY_SPEC] * 4,
        out_specs=(SMEM_SPEC,) + (VMEM_SPEC,) * 3,
        scratch_shapes=[
            pltpu.SMEM(send_ids.shape, jnp.int32),
            pltpu.SMEM(send_count.shape, jnp.int32),
            pltpu.SMEM(pattern.shape, jnp.int32),
            pltpu.VMEM((blocks, points, columns), inflow.dtype),
            pltpu.SemaphoreType.DMA((3,)),
            pltpu.SemaphoreType.DMA((blocks,)),
        ],
        compiler_params=params,
        cost_estimate=pl.CostEstimate(
            flops=inflow.size, bytes_accessed=8 * inflow.size, transcendentals=0
        ),
        name="prepare",
    )(*map(in_hbm, (send_ids, send_count, pattern, inflow)))
    loaded_first = first
    routes = swap_routes(sections, tiles)
    first = lax.ppermute(first, both, routes[0])
    second = lax.ppermute(second, both, routes[1])

    column_type = pltpu.VMEM((blocks, points, columns // 2), jnp.float32)
    fixed = pl.pallas_call(
        load_kernel,
        out_shape=(
            pltpu.VMEM(operators.shape, operators.dtype),
            pltpu.VMEM(source.shape, source.dtype),
            column_type,
            column_type,
        ),
        in_specs=[ANY_SPEC] * 4 + [VMEM_SPEC],
        out_specs=(VMEM_SPEC,) * 4,
        scratch_shapes=[
            pltpu.VMEM(transmission.shape, transmission.dtype),
            pltpu.VMEM(reflectivity.shape, reflectivity.dtype),
            pltpu.SemaphoreType.DMA((4,)),
        ],
        compiler_params=params,
        cost_estimate=pl.CostEstimate(
            flops=0, bytes_accessed=4 * (operators.size + source.size), transcendentals=0
        ),
        name="load",
    )(*map(in_hbm, (operators, source, transmission, reflectivity)), in_vmem(loaded_first))
    fixed = [plan, *fixed]

    buffer_type = pltpu.VMEM((blocks + 2 * listed, points, columns), WAVE)

    ODD, EVEN = 1, 0
    crossing = [(s, (s + 1) % sections) for s in range(sections)]
    inside = [(s, s ^ 1) for s in range(sections)]
    pairs = [[s, s + 1] for s in range(0, sections, 2)]
    pair_type = pltpu.VMEM((2, blocks, points, columns), WAVE)
    part_types = [pltpu.VMEM((blocks // 2, points, columns), WAVE)] * 2
    half_types = [pltpu.VMEM((n, points, columns), WAVE) for n in (blocks // 2, blocks - blocks // 2)]

    def lists_of(extra):
        return [pltpu.VMEM((listed * points + extra, columns), WAVE)] * 2

    def exchange(lists, senders):
        routes = halo_routes(sections, tiles, senders)
        return [lax.ppermute(a, both, route) for a, route in zip(lists, routes)]

    arrived = {parity: ([wave], first, second) for parity in (ODD, EVEN)}
    echoes = []
    for tick in range(ticks - 1):
        first_step, last_step = tick == 0, tick == ticks - 2
        known = []
        waves, halos = {}, {}
        for parity in (ODD, EVEN):
            if first_step:
                extra = 0
            elif last_step:
                extra = 16 if parity == ODD else 0
            else:
                extra = 0 if parity == ODD else 16
            if parity == ODD:
                long = 0 if first_step or last_step else 16
                to_next = [pltpu.VMEM((blocks * points + long, columns), WAVE)]
            else:
                to_next = [pair_type] if last_step else half_types if first_step else part_types
            outs = [wave_type, *lists_of(extra), *to_next]
            echo, *lists = grouped_call(
                functools.partial(tick_kernel, parity, tick, sections),
                [*fixed, *arrived[parity]],
                outs,
                [VMEM_SPEC] * len(outs),
                [in_vmem(a) for a in known],
                scratch_shapes=[buffer_type, pltpu.VMEM(wave_type.shape, WAVE)],
                compiler_params=params,
                cost_estimate=tick_cost,
                name=f"tick{tick}" + ("_odd" if parity else "_even"),
            )
            lists, onward = lists[:2], lists[2:]
            known = [echo, *lists] if first_step else [echo]
            if parity == ODD:
                waves[EVEN] = [lax.ppermute(onward[0], "depth", crossing)]
            elif last_step:
                waves[ODD] = [lax.all_to_all(onward[0], "depth", 0, 0, axis_index_groups=pairs)]
            else:
                waves[ODD] = [lax.ppermute(a, "depth", inside) for a in onward]
            if not first_step:
                halos[1 - parity] = exchange(lists, (parity,))
        if first_step:
            halos[ODD] = halos[EVEN] = exchange(lists, (ODD, EVEN))
        arrived = {parity: (waves[parity], *halos[parity]) for parity in (ODD, EVEN)}
        echoes.append(echo)

    tick = ticks - 1
    results = []
    result_types = (
        jax.ShapeDtypeStruct((ticks, 1, blocks, points, columns), WAVE),
        jax.ShapeDtypeStruct((1, blocks, points, columns), jnp.float32),
    )
    for parity in (ODD, EVEN):
        results = grouped_call(
            functools.partial(last_kernel, parity, tick),
            [*fixed, *arrived[parity], echoes],
            result_types,
            [ANY_SPEC] * 2,
            list(results),
            scratch_shapes=[
                buffer_type,
                pltpu.VMEM((blocks, points, columns), WAVE),
                pltpu.VMEM((blocks, points, columns), jnp.float32),
                pltpu.SemaphoreType.DMA((tick,)),
                pltpu.SemaphoreType.DMA((blocks,)),
                pltpu.SemaphoreType.DMA((blocks,)),
            ],
            compiler_params=params,
            cost_estimate=tick_cost,
            name="last_tick" + ("_odd" if parity else "_even"),
        )
    return tuple(results)


def solution(mesh):
    return jax.shard_map(
        per_device,
        mesh=mesh,
        in_specs=(
            P("depth", "lat", None, None),
            P(None, "lat", None, None),
            P("depth", "lat", None, None, None, None),
            P("depth", "lat", None),
            P("depth", "lat", None),
            P("lat", None, None),
            P("lat", None),
            P("lat", None),
        ),
        out_specs=(P(None, "depth", "lat", None, None), P("depth", "lat", None, None)),
        check_vma=False,
    )
```

```python
import functools

import jax
import jax.numpy as jnp
from jax import lax
from jax.experimental import pallas as pl
from jax.experimental.pallas import tpu as pltpu
from jax.sharding import PartitionSpec as P

WAVE = jnp.bfloat16
SMEM_SPEC = pl.BlockSpec(memory_space=pltpu.SMEM)
VMEM_SPEC = pl.BlockSpec(memory_space=pltpu.VMEM)
ANY_SPEC = pl.BlockSpec(memory_space=pl.ANY)
VMEM_LIMIT = 8 * 1024 * 1024
LOWER, UPPER = 0, 1


def in_vmem(array):
    return pltpu.with_memory_space_constraint(array, pltpu.VMEM)


def in_hbm(array):
    return pltpu.with_memory_space_constraint(array, pltpu.HBM)


def block_of(ref, index, points):
    if len(ref.shape) == 2:
        return ref[pl.ds(pl.multiple_of(index * points, points), points)]
    return ref[index]


def write_lists(tile, plan_ref, blocks_ref, lists, points):
    listed = lists[0].shape[0] // points
    parity = lax.rem(tile, 2)
    for list_ref, side in zip(lists, (UPPER - parity, parity)):
        count = plan_ref[2 * listed + side]
        for slot in range(listed):
            live = slot < count

            @pl.when(live)
            def _():
                list_ref[slot * points : (slot + 1) * points] = block_of(
                    blocks_ref, plan_ref[side * listed + slot], points
                )

            @pl.when(jnp.logical_not(live))
            def _():
                list_ref[slot * points : (slot + 1) * points] = jnp.zeros(
                    (points, list_ref.shape[1]), list_ref.dtype
                )


def prepare_kernel(
    ids_hbm, count_hbm, pattern_hbm, inflow_hbm, plan_ref, wave_ref, first_ref, second_ref,
    ids, count, pattern, landed, small_sems, sems,
):
    blocks, points = wave_ref.shape[:2]
    small = [
        pltpu.make_async_copy(source, target, small_sems.at[i])
        for i, (source, target) in enumerate(
            ((ids_hbm, ids), (count_hbm, count), (pattern_hbm, pattern))
        )
    ]
    large = [
        pltpu.make_async_copy(inflow_hbm.at[0, b], landed.at[b], sems.at[b]) for b in range(blocks)
    ]
    for copy in small + large:
        copy.start()
    for copy in small:
        copy.wait()
    _, sides, listed = ids.shape
    taken = pattern.shape[1]
    for side in range(sides):
        for slot in range(listed):
            plan_ref[side * listed + slot] = ids[0, side, slot]
        plan_ref[sides * listed + side] = count[0, side]
    for b in range(blocks):
        for k in range(taken):
            plan_ref[sides * (listed + 1) + b * taken + k] = pattern[b, k]
    for b, copy in enumerate(large):
        copy.wait()
        wave_ref[b] = landed[b].astype(wave_ref.dtype)
    write_lists(lax.axis_index("lat"), plan_ref, wave_ref, (first_ref, second_ref), points)


def load_kernel(
    ops_hbm, source_hbm, pass_hbm, reflect_hbm, after_ref,
    ops_ref, source_ref, pass_ref, reflect_ref, pass_rows, reflect_rows, sems,
):
    del after_ref
    copies = [
        pltpu.make_async_copy(source, target, sems.at[i])
        for i, (source, target) in enumerate(
            (
                (pass_hbm, pass_rows),
                (reflect_hbm, reflect_rows),
                (ops_hbm, ops_ref),
                (source_hbm, source_ref),
            )
        )
    ]
    for copy in copies:
        copy.start()
    for copy, rows, columns_ref in zip(copies, (pass_rows, reflect_rows), (pass_ref, reflect_ref)):
        copy.wait()
        for b in range(columns_ref.shape[0]):
            row = rows[0, pl.ds(b, 1), :]
            columns_ref[b] = jnp.broadcast_to(row, columns_ref.shape[1:]).T
    for copy in copies[2:]:
        copy.wait()


def fill_buffer(section, tick, source_ref, wave_refs, first_ref, second_ref, buffer):
    blocks, points = source_ref.shape[1:3]
    listed = (buffer.shape[0] - blocks) // 2

    def fill(start, ref):
        if len(ref.shape) == 2:
            count = min(ref.shape[0] // points, blocks)
            part = ref[: count * points].reshape(count, points, -1)
        else:
            part = ref[0] if len(ref.shape) == 4 else ref[...]
        buffer[pl.ds(start, part.shape[0])] = part
        return start + part.shape[0]

    def fill_wave():
        start = 0
        for wave_ref in wave_refs:
            start = fill(start, wave_ref)

    if tick == 0:
        fill_wave()
    else:
        pl.when(section != 0)(fill_wave)

        @pl.when(section == 0)
        def _():
            buffer[:blocks] = source_ref[tick - 1]

    parity = lax.rem(lax.axis_index("lat"), 2)
    fill(blocks + (1 - parity) * listed, first_ref)
    fill(blocks + parity * listed, second_ref)


def extrapolate_block(plan_ref, pattern_start, ops_ref, buffer, b):
    taken = ops_ref.shape[2]
    points = ops_ref.shape[5]
    left = jnp.concatenate(
        [ops_ref[0, b, k].reshape(2 * points, points) for k in range(taken)], axis=1
    )
    right = jnp.concatenate(
        [buffer[plan_ref[pattern_start + b * taken + k]] for k in range(taken)], axis=0
    )
    products = jnp.dot(left, right, preferred_element_type=jnp.float32)
    half = products.shape[1] // 2
    real_part = products[:points, :half] - products[points:, half:]
    imag_part = products[:points, half:] + products[points:, :half]
    return real_part, imag_part


def ids_of(plan_ref, ops_ref):
    return (plan_ref.shape[0] - ops_ref.shape[1] * ops_ref.shape[2]) // 2 - 1


def acts(section, parity):
    return lax.rem(section, 2) == parity


def wave_of(onward_refs, onward):
    if len(onward_refs) > 1:
        return onward
    ref = onward_refs[0]
    return ref.at[1] if len(ref.shape) == 4 else ref


def targets_of(onward_refs, onward, b):
    whole = wave_of(onward_refs, onward)
    points = onward.shape[1]
    if len(whole.shape) == 2:
        return [whole.at[pl.ds(b * points, points)]]
    targets = [whole.at[b]]
    start = 0
    for ref in onward_refs if len(onward_refs) > 1 else []:
        if start <= b < start + ref.shape[0]:
            targets.append(ref.at[b - start])
        start += ref.shape[0]
    return targets


def tick_kernel(
    parity, tick, sections, plan_ref, ops_ref, source_ref, pass_ref, reflect_ref,
    wave_refs, first_in_ref, second_in_ref, known_refs, out_refs, buffer, onward,
):
    del known_refs
    echo_ref, first_ref, second_ref, *onward_refs = out_refs
    section = lax.axis_index("depth")
    tile = lax.axis_index("lat")
    points = onward.shape[1]
    listed = ids_of(plan_ref, ops_ref)

    @pl.when(acts(section, parity))
    def _():
        fill_buffer(section, tick, source_ref, wave_refs, first_in_ref, second_in_ref, buffer)
        for b in range(echo_ref.shape[0]):
            parts = extrapolate_block(plan_ref, 2 * (listed + 1), ops_ref, buffer, b)
            for i, part in enumerate(parts):
                cols = pl.ds(i * part.shape[1], part.shape[1])
                leaving = (pass_ref[b] * part).astype(onward.dtype)
                for target in targets_of(onward_refs, onward, b):
                    target[:, cols] = leaving
                echo_ref[b, :, cols] = (reflect_ref[b] * part).astype(echo_ref.dtype)
        @pl.when(section != sections - 1)
        def _():
            write_lists(tile, plan_ref, wave_of(onward_refs, onward), (first_ref, second_ref), points)

        @pl.when(section == sections - 1)
        def _():
            write_lists(tile, plan_ref, source_ref.at[tick], (first_ref, second_ref), points)


def last_kernel(
    parity, tick, plan_ref, ops_ref, source_ref, pass_ref, reflect_ref,
    wave_refs, first_in_ref, second_in_ref, earlier, known_refs, out_refs,
    buffer, echo, leaving, early_sems, echo_sems, leave_sems,
):
    del known_refs
    reflected_ref, transmitted_ref = out_refs
    section = lax.axis_index("depth")
    listed = ids_of(plan_ref, ops_ref)

    @pl.when(acts(section, parity))
    def _():
        copies = [
            pltpu.make_async_copy(earlier[t], reflected_ref.at[t, 0], early_sems.at[t])
            for t in range(tick)
        ]
        for copy in copies:
            copy.start()
        fill_buffer(section, tick, source_ref, wave_refs, first_in_ref, second_in_ref, buffer)
        for b in range(echo.shape[0]):
            parts = extrapolate_block(plan_ref, 2 * (listed + 1), ops_ref, buffer, b)
            for i, part in enumerate(parts):
                cols = pl.ds(i * part.shape[1], part.shape[1])
                leaving[b, :, cols] = pass_ref[b] * part
                echo[b, :, cols] = (reflect_ref[b] * part).astype(echo.dtype)
            for copy in (
                pltpu.make_async_copy(leaving.at[b], transmitted_ref.at[0, b], leave_sems.at[b]),
                pltpu.make_async_copy(echo.at[b], reflected_ref.at[tick, 0, b], echo_sems.at[b]),
            ):
                copy.start()
                copies.append(copy)
        for copy in copies:
            copy.wait()


def grouped_call(kernel, groups, outs, out_specs, known, **options):
    flat = [array for group in groups for array in (group if isinstance(group, list) else [group])]

    def body(*refs):
        refs = list(refs)
        take = lambda count: [refs.pop(0) for _ in range(count)]
        inputs = [take(len(g)) if isinstance(g, list) else refs.pop(0) for g in groups]
        kernel(*inputs, take(len(known)), take(len(outs)), *refs)

    return pl.pallas_call(
        body,
        out_shape=tuple(outs),
        in_specs=[SMEM_SPEC] + [VMEM_SPEC] * (len(flat) - 1) + list(out_specs[: len(known)]),
        out_specs=tuple(out_specs),
        input_output_aliases={len(flat) + i: i for i in range(len(known))},
        **options,
    )(flat[0], *map(in_vmem, flat[1:]), *known)


def neighbour(j, turn, tiles):
    to = j + (1 if (j + turn) % 2 == 0 else -1)
    return to if 0 <= to < tiles else None


def swap_routes(sections, tiles):
    routes = []
    for turn in (0, 1):
        route = []
        for s in range(sections):
            for j in range(tiles):
                to = neighbour(j, turn, tiles)
                end = ((s ^ 1) * tiles + j) if to is None else (s * tiles + to)
                route.append((s * tiles + j, end))
        routes.append(route)
    return routes


def halo_routes(sections, tiles, senders):
    routes = []
    for turn in (0, 1):
        route = []
        for s in range(sections):
            for j in range(tiles):
                to = neighbour(j, turn, tiles)
                real = to is not None and s % 2 in senders
                end = (s + 1) % sections * tiles + to if real else (s ^ 1) * tiles + j
                route.append((s * tiles + j, end))
        routes.append(route)
    return routes


def per_device(
    inflow, source, operators, transmission, reflectivity, send_ids, send_count, pattern
):
    sections, tiles = lax.axis_size("depth"), lax.axis_size("lat")
    ticks = source.shape[0] + 1
    _, blocks, points, columns = inflow.shape
    listed = send_ids.shape[-1]
    taken = operators.shape[2]
    wave_type = pltpu.VMEM((blocks, points, columns), WAVE)
    list_type = pltpu.VMEM((listed * points, columns), WAVE)
    params = pltpu.CompilerParams(vmem_limit_bytes=VMEM_LIMIT)
    tick_cost = pl.CostEstimate(
        flops=0,
        bytes_accessed=0,
        transcendentals=0,
    )
    both = ("depth", "lat")
    deeper = [(s, (s + 1) % sections) for s in range(sections)]

    plan, wave, first, second = pl.pallas_call(
        prepare_kernel,
        out_shape=(
            pltpu.SMEM((2 * (listed + 1) + blocks * taken,), jnp.int32),
            wave_type,
            list_type,
            list_type,
        ),
        in_specs=[ANY_SPEC] * 4,
        out_specs=(SMEM_SPEC,) + (VMEM_SPEC,) * 3,
        scratch_shapes=[
            pltpu.SMEM(send_ids.shape, jnp.int32),
            pltpu.SMEM(send_count.shape, jnp.int32),
            pltpu.SMEM(pattern.shape, jnp.int32),
            pltpu.VMEM((blocks, points, columns), inflow.dtype),
            pltpu.SemaphoreType.DMA((3,)),
            pltpu.SemaphoreType.DMA((blocks,)),
        ],
        compiler_params=params,
        cost_estimate=pl.CostEstimate(
            flops=inflow.size, bytes_accessed=8 * inflow.size, transcendentals=0
        ),
        name="prepare",
    )(*map(in_hbm, (send_ids, send_count, pattern, inflow)))
    loaded_first = first
    routes = swap_routes(sections, tiles)
    first = lax.ppermute(first, both, routes[0])
    second = lax.ppermute(second, both, routes[1])

    column_type = pltpu.VMEM((blocks, points, columns // 2), jnp.float32)
    fixed = pl.pallas_call(
        load_kernel,
        out_shape=(
            pltpu.VMEM(operators.shape, operators.dtype),
            pltpu.VMEM(source.shape, source.dtype),
            column_type,
            column_type,
        ),
        in_specs=[ANY_SPEC] * 4 + [VMEM_SPEC],
        out_specs=(VMEM_SPEC,) * 4,
        scratch_shapes=[
            pltpu.VMEM(transmission.shape, transmission.dtype),
            pltpu.VMEM(reflectivity.shape, reflectivity.dtype),
            pltpu.SemaphoreType.DMA((4,)),
        ],
        compiler_params=params,
        cost_estimate=pl.CostEstimate(
            flops=0, bytes_accessed=4 * (operators.size + source.size), transcendentals=0
        ),
        name="load",
    )(*map(in_hbm, (operators, source, transmission, reflectivity)), in_vmem(loaded_first))
    fixed = [plan, *fixed]

    buffer_type = pltpu.VMEM((blocks + 2 * listed, points, columns), WAVE)

    ODD, EVEN = 1, 0
    crossing = [(s, (s + 1) % sections) for s in range(sections)]
    inside = [(s, s ^ 1) for s in range(sections)]
    pairs = [[s, s + 1] for s in range(0, sections, 2)]
    pair_type = pltpu.VMEM((2, blocks, points, columns), WAVE)
    part_types = [pltpu.VMEM((blocks // 2, points, columns), WAVE)] * 2
    half_types = [pltpu.VMEM((n, points, columns), WAVE) for n in (blocks // 2, blocks - blocks // 2)]

    def lists_of(extra):
        return [pltpu.VMEM((listed * points + extra, columns), WAVE)] * 2

    def exchange(lists, senders):
        routes = halo_routes(sections, tiles, senders)
        return [lax.ppermute(a, both, route) for a, route in zip(lists, routes)]

    arrived = {parity: ([wave], first, second) for parity in (ODD, EVEN)}
    echoes = []
    for tick in range(ticks - 1):
        first_step, last_step = tick == 0, tick == ticks - 2
        known = []
        waves, halos = {}, {}
        for parity in (ODD, EVEN):
            if first_step:
                extra = 0
            elif last_step:
                extra = 16 if parity == ODD else 0
            else:
                extra = 0 if parity == ODD else 16
            if parity == ODD:
                long = 0 if first_step or last_step else 16
                to_next = [pltpu.VMEM((blocks * points + long, columns), WAVE)]
            else:
                to_next = [pair_type] if last_step else half_types if first_step else part_types
            outs = [wave_type, *lists_of(extra), *to_next]
            echo, *lists = grouped_call(
                functools.partial(tick_kernel, parity, tick, sections),
                [*fixed, *arrived[parity]],
                outs,
                [VMEM_SPEC] * len(outs),
                [in_vmem(a) for a in known],
                scratch_shapes=[buffer_type, pltpu.VMEM(wave_type.shape, WAVE)],
                compiler_params=params,
                cost_estimate=tick_cost,
                name=f"tick{tick}" + ("_odd" if parity else "_even"),
            )
            lists, onward = lists[:2], lists[2:]
            known = [echo, *lists] if first_step else [echo]
            if parity == ODD:
                waves[EVEN] = [lax.ppermute(onward[0], "depth", crossing)]
            elif last_step:
                waves[ODD] = [lax.all_to_all(onward[0], "depth", 0, 0, axis_index_groups=pairs)]
            else:
                waves[ODD] = [lax.ppermute(a, "depth", inside) for a in onward]
            if not first_step:
                halos[1 - parity] = exchange(lists, (parity,))
        if first_step:
            halos[ODD] = halos[EVEN] = exchange(lists, (ODD, EVEN))
        arrived = {parity: (waves[parity], *halos[parity]) for parity in (ODD, EVEN)}
        echoes.append(echo)

    tick = ticks - 1
    results = []
    result_types = (
        jax.ShapeDtypeStruct((ticks, 1, blocks, points, columns), WAVE),
        jax.ShapeDtypeStruct((1, blocks, points, columns), jnp.float32),
    )
    for parity in (ODD, EVEN):
        results = grouped_call(
            functools.partial(last_kernel, parity, tick),
            [*fixed, *arrived[parity], echoes],
            result_types,
            [ANY_SPEC] * 2,
            list(results),
            scratch_shapes=[
                buffer_type,
                pltpu.VMEM((blocks, points, columns), WAVE),
                pltpu.VMEM((blocks, points, columns), jnp.float32),
                pltpu.SemaphoreType.DMA((tick,)),
                pltpu.SemaphoreType.DMA((blocks,)),
                pltpu.SemaphoreType.DMA((blocks,)),
            ],
            compiler_params=params,
            cost_estimate=tick_cost,
            name="last_tick" + ("_odd" if parity else "_even"),
        )
    return tuple(results)


def solution(mesh):
    return jax.shard_map(
        per_device,
        mesh=mesh,
        in_specs=(
            P("depth", "lat", None, None),
            P(None, "lat", None, None),
            P("depth", "lat", None, None, None, None),
            P("depth", "lat", None),
            P("depth", "lat", None),
            P("lat", None, None),
            P("lat", None),
            P("lat", None),
        ),
        out_specs=(P(None, "depth", "lat", None, None), P("depth", "lat", None, None)),
        check_vma=False,
    )
```

```python
import functools

import jax
import jax.numpy as jnp
from jax import lax
from jax.experimental import pallas as pl
from jax.experimental.pallas import tpu as pltpu
from jax.sharding import PartitionSpec as P

WAVE = jnp.bfloat16
SMEM_SPEC = pl.BlockSpec(memory_space=pltpu.SMEM)
VMEM_SPEC = pl.BlockSpec(memory_space=pltpu.VMEM)
ANY_SPEC = pl.BlockSpec(memory_space=pl.ANY)
VMEM_LIMIT = 8 * 1024 * 1024
LOWER, UPPER = 0, 1


def in_vmem(array):
    return pltpu.with_memory_space_constraint(array, pltpu.VMEM)


def in_hbm(array):
    return pltpu.with_memory_space_constraint(array, pltpu.HBM)


def block_of(ref, index, points):
    if len(ref.shape) == 2:
        return ref[pl.ds(pl.multiple_of(index * points, points), points)]
    return ref[index]


def write_lists(tile, plan_ref, blocks_ref, lists, points):
    listed = lists[0].shape[0] // points
    parity = lax.rem(tile, 2)
    for list_ref, side in zip(lists, (UPPER - parity, parity)):
        count = plan_ref[2 * listed + side]
        for slot in range(listed):
            live = slot < count

            @pl.when(live)
            def _():
                list_ref[slot * points : (slot + 1) * points] = block_of(
                    blocks_ref, plan_ref[side * listed + slot], points
                )

            @pl.when(jnp.logical_not(live))
            def _():
                list_ref[slot * points : (slot + 1) * points] = jnp.zeros(
                    (points, list_ref.shape[1]), list_ref.dtype
                )


def prepare_kernel(
    ids_hbm, count_hbm, pattern_hbm, inflow_hbm, plan_ref, wave_ref, first_ref, second_ref,
    ids, count, pattern, landed, small_sems, sems,
):
    blocks, points = wave_ref.shape[:2]
    small = [
        pltpu.make_async_copy(source, target, small_sems.at[i])
        for i, (source, target) in enumerate(
            ((ids_hbm, ids), (count_hbm, count), (pattern_hbm, pattern))
        )
    ]
    large = [
        pltpu.make_async_copy(inflow_hbm.at[0, b], landed.at[b], sems.at[b]) for b in range(blocks)
    ]
    for copy in small + large:
        copy.start()
    for copy in small:
        copy.wait()
    _, sides, listed = ids.shape
    taken = pattern.shape[1]
    for side in range(sides):
        for slot in range(listed):
            plan_ref[side * listed + slot] = ids[0, side, slot]
        plan_ref[sides * listed + side] = count[0, side]
    for b in range(blocks):
        for k in range(taken):
            plan_ref[sides * (listed + 1) + b * taken + k] = pattern[b, k]
    for b, copy in enumerate(large):
        copy.wait()
        wave_ref[b] = landed[b].astype(wave_ref.dtype)
    write_lists(lax.axis_index("lat"), plan_ref, wave_ref, (first_ref, second_ref), points)


def load_kernel(
    ops_hbm, source_hbm, pass_hbm, reflect_hbm, after_ref,
    ops_ref, source_ref, pass_ref, reflect_ref, pass_rows, reflect_rows, sems,
):
    del after_ref
    copies = [
        pltpu.make_async_copy(source, target, sems.at[i])
        for i, (source, target) in enumerate(
            (
                (pass_hbm, pass_rows),
                (reflect_hbm, reflect_rows),
                (ops_hbm, ops_ref),
                (source_hbm, source_ref),
            )
        )
    ]
    for copy in copies:
        copy.start()
    for copy, rows, columns_ref in zip(copies, (pass_rows, reflect_rows), (pass_ref, reflect_ref)):
        copy.wait()
        for b in range(columns_ref.shape[0]):
            row = rows[0, pl.ds(b, 1), :]
            columns_ref[b] = jnp.broadcast_to(row, columns_ref.shape[1:]).T
    for copy in copies[2:]:
        copy.wait()


def fill_buffer(section, tick, source_ref, wave_refs, first_ref, second_ref, buffer):
    blocks, points = source_ref.shape[1:3]
    listed = (buffer.shape[0] - blocks) // 2

    def fill(start, ref):
        if len(ref.shape) == 2:
            count = min(ref.shape[0] // points, blocks)
            part = ref[: count * points].reshape(count, points, -1)
        else:
            part = ref[0] if len(ref.shape) == 4 else ref[...]
        buffer[pl.ds(start, part.shape[0])] = part
        return start + part.shape[0]

    def fill_wave():
        start = 0
        for wave_ref in wave_refs:
            start = fill(start, wave_ref)

    if tick == 0:
        fill_wave()
    else:
        pl.when(section != 0)(fill_wave)

        @pl.when(section == 0)
        def _():
            buffer[:blocks] = source_ref[tick - 1]

    parity = lax.rem(lax.axis_index("lat"), 2)
    fill(blocks + (1 - parity) * listed, first_ref)
    fill(blocks + parity * listed, second_ref)


def extrapolate_block(plan_ref, pattern_start, ops_ref, buffer, b):
    taken = ops_ref.shape[2]
    points = ops_ref.shape[5]
    left = jnp.concatenate(
        [ops_ref[0, b, k].reshape(2 * points, points) for k in range(taken)], axis=1
    )
    right = jnp.concatenate(
        [buffer[plan_ref[pattern_start + b * taken + k]] for k in range(taken)], axis=0
    )
    products = jnp.dot(left, right, preferred_element_type=jnp.float32)
    half = products.shape[1] // 2
    real_part = products[:points, :half] - products[points:, half:]
    imag_part = products[:points, half:] + products[points:, :half]
    return real_part, imag_part


def ids_of(plan_ref, ops_ref):
    return (plan_ref.shape[0] - ops_ref.shape[1] * ops_ref.shape[2]) // 2 - 1


def acts(section, parity):
    return lax.rem(section, 2) == parity


def wave_of(onward_refs, onward):
    if len(onward_refs) > 1:
        return onward
    ref = onward_refs[0]
    return ref.at[1] if len(ref.shape) == 4 else ref


def targets_of(onward_refs, onward, b):
    whole = wave_of(onward_refs, onward)
    points = onward.shape[1]
    if len(whole.shape) == 2:
        return [whole.at[pl.ds(b * points, points)]]
    targets = [whole.at[b]]
    start = 0
    for ref in onward_refs if len(onward_refs) > 1 else []:
        if start <= b < start + ref.shape[0]:
            targets.append(ref.at[b - start])
        start += ref.shape[0]
    return targets


def tick_kernel(
    parity, tick, sections, plan_ref, ops_ref, source_ref, pass_ref, reflect_ref,
    wave_refs, first_in_ref, second_in_ref, known_refs, out_refs, buffer, onward,
):
    del known_refs
    echo_ref, first_ref, second_ref, *onward_refs = out_refs
    section = lax.axis_index("depth")
    tile = lax.axis_index("lat")
    points = onward.shape[1]
    listed = ids_of(plan_ref, ops_ref)

    @pl.when(acts(section, parity))
    def _():
        fill_buffer(section, tick, source_ref, wave_refs, first_in_ref, second_in_ref, buffer)
        for b in range(echo_ref.shape[0]):
            parts = extrapolate_block(plan_ref, 2 * (listed + 1), ops_ref, buffer, b)
            for i, part in enumerate(parts):
                cols = pl.ds(i * part.shape[1], part.shape[1])
                leaving = (pass_ref[b] * part).astype(onward.dtype)
                for target in targets_of(onward_refs, onward, b):
                    target[:, cols] = leaving
                echo_ref[b, :, cols] = (reflect_ref[b] * part).astype(echo_ref.dtype)
        @pl.when(section != sections - 1)
        def _():
            write_lists(tile, plan_ref, wave_of(onward_refs, onward), (first_ref, second_ref), points)

        @pl.when(section == sections - 1)
        def _():
            write_lists(tile, plan_ref, source_ref.at[tick], (first_ref, second_ref), points)


def last_kernel(
    parity, tick, plan_ref, ops_ref, source_ref, pass_ref, reflect_ref,
    wave_refs, first_in_ref, second_in_ref, earlier, known_refs, out_refs,
    buffer, echo, leaving, early_sems, echo_sems, leave_sems,
):
    del known_refs
    reflected_ref, transmitted_ref = out_refs
    section = lax.axis_index("depth")
    listed = ids_of(plan_ref, ops_ref)

    @pl.when(acts(section, parity))
    def _():
        copies = [
            pltpu.make_async_copy(earlier[t], reflected_ref.at[t, 0], early_sems.at[t])
            for t in range(tick)
        ]
        for copy in copies:
            copy.start()
        fill_buffer(section, tick, source_ref, wave_refs, first_in_ref, second_in_ref, buffer)
        for b in range(echo.shape[0]):
            parts = extrapolate_block(plan_ref, 2 * (listed + 1), ops_ref, buffer, b)
            for i, part in enumerate(parts):
                cols = pl.ds(i * part.shape[1], part.shape[1])
                leaving[b, :, cols] = pass_ref[b] * part
                echo[b, :, cols] = (reflect_ref[b] * part).astype(echo.dtype)
            for copy in (
                pltpu.make_async_copy(leaving.at[b], transmitted_ref.at[0, b], leave_sems.at[b]),
                pltpu.make_async_copy(echo.at[b], reflected_ref.at[tick, 0, b], echo_sems.at[b]),
            ):
                copy.start()
                copies.append(copy)
        for copy in copies:
            copy.wait()


def grouped_call(kernel, groups, outs, out_specs, known, **options):
    flat = [array for group in groups for array in (group if isinstance(group, list) else [group])]

    def body(*refs):
        refs = list(refs)
        take = lambda count: [refs.pop(0) for _ in range(count)]
        inputs = [take(len(g)) if isinstance(g, list) else refs.pop(0) for g in groups]
        kernel(*inputs, take(len(known)), take(len(outs)), *refs)

    return pl.pallas_call(
        body,
        out_shape=tuple(outs),
        in_specs=[SMEM_SPEC] + [VMEM_SPEC] * (len(flat) - 1) + list(out_specs[: len(known)]),
        out_specs=tuple(out_specs),
        input_output_aliases={len(flat) + i: i for i in range(len(known))},
        **options,
    )(flat[0], *map(in_vmem, flat[1:]), *known)


def neighbour(j, turn, tiles):
    to = j + (1 if (j + turn) % 2 == 0 else -1)
    return to if 0 <= to < tiles else None


def swap_routes(sections, tiles):
    routes = []
    for turn in (0, 1):
        route = []
        for s in range(sections):
            for j in range(tiles):
                to = neighbour(j, turn, tiles)
                end = ((s ^ 1) * tiles + j) if to is None else (s * tiles + to)
                route.append((s * tiles + j, end))
        routes.append(route)
    return routes


def halo_routes(sections, tiles, senders):
    routes = []
    for turn in (0, 1):
        route = []
        for s in range(sections):
            for j in range(tiles):
                to = neighbour(j, turn, tiles)
                real = to is not None and s % 2 in senders
                end = (s + 1) % sections * tiles + to if real else (s ^ 1) * tiles + j
                route.append((s * tiles + j, end))
        routes.append(route)
    return routes


def per_device(
    inflow, source, operators, transmission, reflectivity, send_ids, send_count, pattern
):
    sections, tiles = lax.axis_size("depth"), lax.axis_size("lat")
    ticks = source.shape[0] + 1
    _, blocks, points, columns = inflow.shape
    listed = send_ids.shape[-1]
    taken = operators.shape[2]
    wave_type = pltpu.VMEM((blocks, points, columns), WAVE)
    list_type = pltpu.VMEM((listed * points, columns), WAVE)
    params = pltpu.CompilerParams(vmem_limit_bytes=VMEM_LIMIT)
    tick_cost = pl.CostEstimate(
        flops=0,
        bytes_accessed=0,
        transcendentals=0,
    )
    both = ("depth", "lat")
    deeper = [(s, (s + 1) % sections) for s in range(sections)]

    plan, wave, first, second = pl.pallas_call(
        prepare_kernel,
        out_shape=(
            pltpu.SMEM((2 * (listed + 1) + blocks * taken,), jnp.int32),
            wave_type,
            list_type,
            list_type,
        ),
        in_specs=[ANY_SPEC] * 4,
        out_specs=(SMEM_SPEC,) + (VMEM_SPEC,) * 3,
        scratch_shapes=[
            pltpu.SMEM(send_ids.shape, jnp.int32),
            pltpu.SMEM(send_count.shape, jnp.int32),
            pltpu.SMEM(pattern.shape, jnp.int32),
            pltpu.VMEM((blocks, points, columns), inflow.dtype),
            pltpu.SemaphoreType.DMA((3,)),
            pltpu.SemaphoreType.DMA((blocks,)),
        ],
        compiler_params=params,
        cost_estimate=pl.CostEstimate(
            flops=inflow.size, bytes_accessed=8 * inflow.size, transcendentals=0
        ),
        name="prepare",
    )(*map(in_hbm, (send_ids, send_count, pattern, inflow)))
    loaded_first = first
    routes = swap_routes(sections, tiles)
    first = lax.ppermute(first, both, routes[0])
    second = lax.ppermute(second, both, routes[1])

    column_type = pltpu.VMEM((blocks, points, columns // 2), jnp.float32)
    fixed = pl.pallas_call(
        load_kernel,
        out_shape=(
            pltpu.VMEM(operators.shape, operators.dtype),
            pltpu.VMEM(source.shape, source.dtype),
            column_type,
            column_type,
        ),
        in_specs=[ANY_SPEC] * 4 + [VMEM_SPEC],
        out_specs=(VMEM_SPEC,) * 4,
        scratch_shapes=[
            pltpu.VMEM(transmission.shape, transmission.dtype),
            pltpu.VMEM(reflectivity.shape, reflectivity.dtype),
            pltpu.SemaphoreType.DMA((4,)),
        ],
        compiler_params=params,
        cost_estimate=pl.CostEstimate(
            flops=0, bytes_accessed=4 * (operators.size + source.size), transcendentals=0
        ),
        name="load",
    )(*map(in_hbm, (operators, source, transmission, reflectivity)), in_vmem(loaded_first))
    fixed = [plan, *fixed]

    buffer_type = pltpu.VMEM((blocks + 2 * listed, points, columns), WAVE)

    ODD, EVEN = 1, 0
    crossing = [(s, (s + 1) % sections) for s in range(sections)]
    inside = [(s, s ^ 1) for s in range(sections)]
    pairs = [[s, s + 1] for s in range(0, sections, 2)]
    pair_type = pltpu.VMEM((2, blocks, points, columns), WAVE)
    part_types = [pltpu.VMEM((blocks // 2, points, columns), WAVE)] * 2
    half_types = [pltpu.VMEM((n, points, columns), WAVE) for n in (blocks // 2, blocks - blocks // 2)]

    def lists_of(extra):
        return [pltpu.VMEM((listed * points + extra, columns), WAVE)] * 2

    def exchange(lists, senders):
        routes = halo_routes(sections, tiles, senders)
        return [lax.ppermute(a, both, route) for a, route in zip(lists, routes)]

    arrived = {parity: ([wave], first, second) for parity in (ODD, EVEN)}
    echoes = []
    for tick in range(ticks - 1):
        first_step, last_step = tick == 0, tick == ticks - 2
        known = []
        waves, halos = {}, {}
        for parity in (ODD, EVEN):
            if first_step:
                extra = 0
            elif last_step:
                extra = 16 if parity == ODD else 0
            else:
                extra = 0 if parity == ODD else 16
            if parity == ODD:
                long = 0 if first_step or last_step else 16
                to_next = [pltpu.VMEM((blocks * points + long, columns), WAVE)]
            else:
                to_next = [pair_type] if last_step else half_types if first_step else part_types
            outs = [wave_type, *lists_of(extra), *to_next]
            if first_step:
                outs[2] = lists_of(16)[1]
            echo, *lists = grouped_call(
                functools.partial(tick_kernel, parity, tick, sections),
                [*fixed, *arrived[parity]],
                outs,
                [VMEM_SPEC] * len(outs),
                [in_vmem(a) for a in known],
                scratch_shapes=[buffer_type, pltpu.VMEM(wave_type.shape, WAVE)],
                compiler_params=params,
                cost_estimate=tick_cost,
                name=f"tick{tick}" + ("_odd" if parity else "_even"),
            )
            lists, onward = lists[:2], lists[2:]
            known = [echo, *lists] if first_step else [echo]
            if parity == ODD:
                waves[EVEN] = [lax.ppermute(onward[0], "depth", crossing)]
            elif last_step:
                waves[ODD] = [lax.all_to_all(onward[0], "depth", 0, 0, axis_index_groups=pairs)]
            else:
                waves[ODD] = [lax.ppermute(a, "depth", inside) for a in onward]
            if not first_step:
                halos[1 - parity] = exchange(lists, (parity,))
        if first_step:
            halos[ODD] = halos[EVEN] = exchange(lists, (ODD, EVEN))
        arrived = {parity: (waves[parity], *halos[parity]) for parity in (ODD, EVEN)}
        echoes.append(echo)

    tick = ticks - 1
    results = []
    result_types = (
        jax.ShapeDtypeStruct((ticks, 1, blocks, points, columns), WAVE),
        jax.ShapeDtypeStruct((1, blocks, points, columns), jnp.float32),
    )
    for parity in (ODD, EVEN):
        results = grouped_call(
            functools.partial(last_kernel, parity, tick),
            [*fixed, *arrived[parity], echoes],
            result_types,
            [ANY_SPEC] * 2,
            list(results),
            scratch_shapes=[
                buffer_type,
                pltpu.VMEM((blocks, points, columns), WAVE),
                pltpu.VMEM((blocks, points, columns), jnp.float32),
                pltpu.SemaphoreType.DMA((tick,)),
                pltpu.SemaphoreType.DMA((blocks,)),
                pltpu.SemaphoreType.DMA((blocks,)),
            ],
            compiler_params=params,
            cost_estimate=tick_cost,
            name="last_tick" + ("_odd" if parity else "_even"),
        )
    return tuple(results)


def solution(mesh):
    return jax.shard_map(
        per_device,
        mesh=mesh,
        in_specs=(
            P("depth", "lat", None, None),
            P(None, "lat", None, None),
            P("depth", "lat", None, None, None, None),
            P("depth", "lat", None),
            P("depth", "lat", None),
            P("lat", None, None),
            P("lat", None),
            P("lat", None),
        ),
        out_specs=(P(None, "depth", "lat", None, None), P("depth", "lat", None, None)),
        check_vma=False,
    )
```
